32 devices in a mesh: dp: 8 (over z, core), tensor: 4 (over y, x).
Axes of the slice: x: 2, y: 2, z: 4, core: 2. Of those that a mesh axis runs over, the one named last changes fastest.
Arguments:
- tokens: bfloat16 [16384, 1536], P(('dp', 'tensor')), may hold values from -6 to 6
- cotangent: bfloat16 [16384, 1536], P(('dp', 'tensor')), may hold values from -6 to 6
- first_gain: float32 [1536], replicated, may hold values from 0.1 to 1.9
- query_weight: bfloat16 [1536, 1536], P('dp', 'tensor'), may hold values from -0.15625 to 0.15625
- key_weight: bfloat16 [1536, 768], P('dp', 'tensor'), may hold values from -0.15625 to 0.15625
- value_weight: bfloat16 [1536, 768], P('dp', 'tensor'), may hold values from -0.15625 to 0.15625
- out_weight: bfloat16 [1536, 1536], P('tensor', 'dp'), may hold values from -0.625 to 0.625
- second_gain: float32 [1536], replicated, may hold values from 0.1 to 1.9
- gate_weight: bfloat16 [1536, 4096], P('dp', 'tensor'), may hold values from -0.15625 to 0.15625
- up_weight: bfloat16 [1536, 4096], P('dp', 'tensor'), may hold values from -0.15625 to 0.15625
- down_weight: bfloat16 [4096, 1536], P('tensor', 'dp'), may hold values from -0.1875 to 0.1875
Outputs:
- result: bfloat16 [16384, 1536], P(('dp', 'tensor'))
- tokens_grad: float32 [16384, 1536], P(('dp', 'tensor'))
- query_grad: float32 [1536, 1536], P('dp', 'tensor')
- key_grad: float32 [1536, 768], P('dp', 'tensor')
- value_grad: float32 [1536, 768], P('dp', 'tensor')
- out_grad: float32 [1536, 1536], P('tensor', 'dp')
- gate_grad: float32 [1536, 4096], P('dp', 'tensor')
- up_grad: float32 [1536, 4096], P('dp', 'tensor')
- down_grad: float32 [4096, 1536], P('tensor', 'dp')
- first_gain_grad: float32 [1536], P(('dp', 'tensor'))
- second_gain_grad: float32 [1536], P(('dp', 'tensor'))
The draws below stay inside these ranges and needn't reach their ends.
All inputs are finite; a program needn't handle non-finite values.
Results may differ from the reference program's by a relative error of at most 0.02.
Values may be sent and summed in bfloat16 or wider, within the bound.
A program may use at most 192 MiB of HBM per device.

```python
import jax
import jax.numpy as jnp
from jax import lax

D = 1536
HQ = 16
HK = 8
HD = 96
FF = 4096
SEQ_LEN = 1024
NSEQ = 16
TOKENS = 16384


def with_spikes(values, key, source, target, parts, factor):
    def block_of(dim):
        return (jnp.arange(values.shape[dim]) // (values.shape[dim] // parts)).reshape((-1,) + (1,) * (values.ndim - 1 - dim))

    near = jax.random.permutation(key, parts)[block_of(target)]
    other_side = (block_of(target) + parts // 2) % parts
    return jnp.where((block_of(source) == near) | (block_of(source) == other_side), factor * values, values)


def steps_of(stream_key, extent, cuts, low, high):
    level = 1.0
    for dim, shards_of in cuts:
        draws = jax.random.uniform(jax.random.fold_in(jax.random.fold_in(stream_key, 6), dim), (shards_of,), jnp.float32, low / len(cuts), high / len(cuts))
        level = level * jnp.repeat(jnp.exp(draws), extent[dim] // shards_of).reshape((-1,) + (1,) * (len(extent) - 1 - dim))
    return level


def bell_draw(own_key, extent, width, bound, pieces=(), kind=jnp.bfloat16):
    drawn = width * jax.random.normal(own_key, extent, jnp.float32)
    if pieces:
        drawn = drawn * steps_of(own_key, extent, pieces, -0.22, 0.18)
    return jnp.clip(drawn, -bound, bound).astype(kind)


def bell_draw_with(stream_key, dims, spread, limit, pieces, heavy, kind=jnp.bfloat16):
    values = spread * jax.random.normal(stream_key, dims, jnp.float32)
    if pieces:
        values = values * steps_of(stream_key, dims, pieces, -0.22, 0.18)
    return jnp.clip(with_spikes(values, jax.random.fold_in(stream_key, 3), *heavy), -limit, limit).astype(kind)


def setup_inputs(seed: int = 0) -> dict:
    arg_keys = jax.random.split(jax.random.key(seed), 12)
    return {
        "tokens": bell_draw(arg_keys[0], (TOKENS, D), 1.0, 6.0, ((0, 32),)),
        "cotangent": bell_draw_with(arg_keys[1], (TOKENS, D), 1.0, 6.0, ((0, 32),), (0, 1, 32, 2.75)),
        "first_gain": jnp.clip(1.0 + 0.18 * jax.random.normal(arg_keys[2], (D,), jnp.float32), 0.1, 1.9),
        "query_weight": bell_draw(arg_keys[3], (D, HQ * HD), D ** -0.5, 0.15625, ((0, 8), (1, 4))),
        "key_weight": bell_draw(arg_keys[4], (D, HK * HD), D ** -0.5, 0.15625, ((0, 8), (1, 4))),
        "value_weight": bell_draw(arg_keys[5], (D, HK * HD), D ** -0.5, 0.15625, ((0, 8), (1, 4))),
        "out_weight": bell_draw(arg_keys[6], (HQ * HD, D), (HQ * HD // 16) ** -0.5, 0.625, ((0, 4), (1, 8))),
        "second_gain": jnp.clip(1.0 + 0.18 * jax.random.normal(arg_keys[7], (D,), jnp.float32), 0.1, 1.9),
        "gate_weight": bell_draw(arg_keys[8], (D, FF), D ** -0.5, 0.15625, ((0, 8), (1, 4))),
        "up_weight": bell_draw(arg_keys[9], (D, FF), D ** -0.5, 0.15625, ((0, 8), (1, 4))),
        "down_weight": bell_draw(arg_keys[10], (FF, D), (FF // 4) ** -0.5, 0.1875, ((0, 4), (1, 8))),
    }


EPSILON = 1e-05
THETA = 100000.0
MASKED = -1e+30
HIGHEST = lax.Precision.HIGHEST

@jax.custom_vjp
def low(v):
    return lax.optimization_barrier(v.astype(jnp.bfloat16)).astype(jnp.float32)

@jax.custom_vjp
def low_back(v):
    return v

def low_keep(v):
    return (low(v), None)

def low_pass(kept, grad):
    return (grad,)

def back_keep(v):
    return (v, None)

def back_low(kept, grad):
    return (low(grad),)
low.defvjp(low_keep, low_pass)
low_back.defvjp(back_keep, back_low)

def product(left, right):
    return jnp.dot(left, right, precision=HIGHEST, preferred_element_type=jnp.float32)

def normed(inputs, gain):
    factor = lax.rsqrt(lax.optimization_barrier(jnp.mean(inputs * inputs, axis=-1, keepdims=True)) + EPSILON)
    return inputs * factor * gain

def rotate(vectors, direction):
    seq_rows, head_count, head_size = vectors.shape
    half_size = head_size // 2
    position = (jnp.arange(seq_rows, dtype=jnp.int32) % SEQ_LEN).astype(jnp.float32)
    inverse = THETA ** (-2.0 * jnp.arange(half_size, dtype=jnp.float32) / head_size)
    angles = position[:, None] * inverse[None, :]
    cosine = jnp.cos(angles)[:, None, :]
    sine_part = direction * jnp.sin(angles)[:, None, :]
    leading = vectors[..., :half_size]
    trailing = vectors[..., half_size:]
    return jnp.concatenate([leading * cosine - trailing * sine_part, trailing * cosine + leading * sine_part], axis=-1)

def block_forward(inputs, first_gain, query_weight, key_weight, value_weight, out_weight, second_gain, gate_weight, up_weight, down_weight):
    first_normed = low(normed(inputs, first_gain))
    queries = low(rotate(low_back(product(first_normed, query_weight)).reshape(SEQ_LEN, HQ, HD), 1.0))
    keys_rot = low(rotate(low_back(product(first_normed, key_weight)).reshape(SEQ_LEN, HK, HD), 1.0))
    values = low(low_back(product(first_normed, value_weight))).reshape(SEQ_LEN, HK, HD)
    grouped = queries.reshape(SEQ_LEN, HK, HQ // HK, HD)
    scores = low_back(jnp.einsum('qhgd,khd->hgqk', grouped, keys_rot, precision=HIGHEST) * HD ** (-0.5))
    causal = jnp.arange(SEQ_LEN)[:, None] >= jnp.arange(SEQ_LEN)[None, :]
    scores = jnp.where(causal, scores, MASKED)
    row_max = lax.optimization_barrier(jnp.max(scores, axis=-1, keepdims=True))
    weights = jnp.exp(scores - row_max)
    softmax = weights / lax.optimization_barrier(jnp.sum(weights, axis=-1, keepdims=True))
    mixed_heads = jnp.einsum('hgqk,khd->qhgd', low(softmax), values, precision=HIGHEST)
    heads_out = low_back(low(mixed_heads.reshape(SEQ_LEN, HQ * HD)))
    middle = inputs + low_back(product(heads_out, out_weight))
    second_normed = low(normed(middle, second_gain))
    gate_value = low_back(product(second_normed, gate_weight))
    up_value = low_back(product(second_normed, up_weight))
    hidden = low(jax.nn.silu(gate_value) * up_value)
    return middle + low_back(product(hidden, down_weight))

def reference(tokens, cotangent, first_gain, query_weight, key_weight, value_weight, out_weight, second_gain, gate_weight, up_weight, down_weight):
    params = (first_gain, query_weight.astype(jnp.float32), key_weight.astype(jnp.float32), value_weight.astype(jnp.float32), out_weight.astype(jnp.float32), second_gain, gate_weight.astype(jnp.float32), up_weight.astype(jnp.float32), down_weight.astype(jnp.float32))

    def whole_layer(sequences, *weights_all):

        def one_sequence(sequence):
            return block_forward(sequence, *weights_all)
        return lax.map(jax.checkpoint(one_sequence), sequences)
    sequences = tokens.astype(jnp.float32).reshape(NSEQ, SEQ_LEN, D)
    result, pullback = jax.vjp(whole_layer, sequences, *params)
    gradients = pullback(cotangent.astype(jnp.float32).reshape(NSEQ, SEQ_LEN, D))
    return (result.reshape(TOKENS, D).astype(jnp.bfloat16), gradients[0].reshape(TOKENS, D), gradients[2], gradients[3], gradients[4], gradients[5], gradients[7], gradients[8], gradients[9], gradients[1], gradients[6])
```

```python
import functools

import jax
import jax.numpy as jnp
import numpy as np
from jax import lax
from jax.experimental import pallas as pl
from jax.experimental.pallas import tpu as pltpu
from jax.sharding import PartitionSpec as P

HD = 96
SEQ_LEN = 1024


EPSILON = 1e-05
THETA = 100000.0
MASKED = -1e30
LOG2E = 1.4426950408889634
LANES = 128
VMEM_BYTES = 56 * 2**20


def normed(inputs, gain):
    factor = lax.rsqrt(jnp.mean(inputs * inputs, axis=-1, keepdims=True) + EPSILON)
    return inputs * factor * gain


def rotate(vectors, direction):
    seq_rows, head_count, head_size = vectors.shape
    half_size = head_size // 2
    position = (jnp.arange(seq_rows, dtype=jnp.int32) % SEQ_LEN).astype(jnp.float32)
    inverse = THETA ** (-2.0 * jnp.arange(half_size, dtype=jnp.float32) / head_size)
    angles = position[:, None] * inverse[None, :]
    cosine = jnp.cos(angles)[:, None, :]
    sine_part = direction * jnp.sin(angles)[:, None, :]
    leading = vectors[..., :half_size]
    trailing = vectors[..., half_size:]
    return jnp.concatenate(
        [leading * cosine - trailing * sine_part, trailing * cosine + leading * sine_part], axis=-1
    )


def times_transposed(left, right):
    return lax.dot_general(
        left, right, (((1,), (1,)), ((), ())), preferred_element_type=jnp.float32
    )


def transposed_times(left, right):
    return lax.dot_general(
        left, right, (((0,), (0,)), ((), ())), preferred_element_type=jnp.float32
    )


def scaled_scores(queries, keys_rot):
    raw_scores = jnp.einsum(
        "qhgd,khd->hgqk", queries, keys_rot, preferred_element_type=jnp.float32
    ) * queries.shape[-1] ** (-0.5)
    length_rows = queries.shape[0]
    causal = jnp.arange(length_rows)[:, None] >= jnp.arange(length_rows)[None, :]
    return jnp.where(causal, raw_scores, MASKED)


def attend_forward(operands):
    queries, keys_rot, values = operands
    scores = scaled_scores(queries, keys_rot)
    row_max = jnp.max(scores, axis=-1, keepdims=True)
    weights = jnp.exp(scores - row_max)
    row_total = jnp.sum(weights, axis=-1, keepdims=True)
    softmax = (weights / row_total).astype(jnp.bfloat16)
    mixed_heads = jnp.einsum("hgqk,khd->qhgd", softmax, values, preferred_element_type=jnp.float32)
    return (mixed_heads.astype(jnp.bfloat16), (row_max + jnp.log(row_total))[..., 0])


def attend_backward(operands):
    queries, keys_rot, values, grad_mixed, log_total = operands
    scores = scaled_scores(queries, keys_rot)
    softmax = jnp.exp(scores - log_total[..., None])
    grad_softmax = jnp.einsum(
        "qhgd,khd->hgqk", grad_mixed, values, preferred_element_type=jnp.float32
    )
    grad_values = jnp.einsum(
        "hgqk,qhgd->khd",
        softmax.astype(jnp.bfloat16),
        grad_mixed,
        preferred_element_type=jnp.float32,
    )
    row_inner = jnp.sum(softmax * grad_softmax, axis=-1, keepdims=True)
    grad_scores = (softmax * (grad_softmax - row_inner)).astype(jnp.bfloat16)
    scale_factor = queries.shape[-1] ** (-0.5)
    grad_queries = (
        jnp.einsum("hgqk,khd->qhgd", grad_scores, keys_rot, preferred_element_type=jnp.float32)
        * scale_factor
    )
    grad_keys = (
        jnp.einsum("hgqk,qhgd->khd", grad_scores, queries, preferred_element_type=jnp.float32)
        * scale_factor
    )
    return (grad_queries, grad_keys, grad_values)


def gather_rows(shard):
    return lax.all_gather(shard, "tensor", axis=0, tiled=True)


def gather_grads(shard):
    return lax.all_gather(shard, "tensor", axis=0, tiled=True)


def sum_outputs(term, row_count):
    return lax.psum_scatter(
        term(jnp.int32(0), row_count * lax.axis_size("tensor")),
        "tensor",
        scatter_dimension=0,
        tiled=True,
    )


def sum_inputs(term, row_count):
    return lax.psum_scatter(
        term(jnp.int32(0), row_count * lax.axis_size("tensor")),
        "tensor",
        scatter_dimension=0,
        tiled=True,
    )


def local(
    tokens,
    cotangent,
    first_gain,
    query_weight,
    key_weight,
    value_weight,
    out_weight,
    second_gain,
    gate_weight,
    up_weight,
    down_weight,
):
    query_weight, key_weight, value_weight, out_weight, gate_weight, up_weight, down_weight = (
        lax.all_gather(query_weight, "dp", axis=0, tiled=True),
        lax.all_gather(key_weight, "dp", axis=0, tiled=True),
        lax.all_gather(value_weight, "dp", axis=0, tiled=True),
        lax.all_gather(out_weight, "dp", axis=1, tiled=True),
        lax.all_gather(gate_weight, "dp", axis=0, tiled=True),
        lax.all_gather(up_weight, "dp", axis=0, tiled=True),
        lax.all_gather(down_weight, "dp", axis=1, tiled=True),
    )
    own_rows = tokens.astype(jnp.float32)
    row_count = own_rows.shape[0]
    pair_count = key_weight.shape[1] // HD
    first_normed = normed(own_rows, first_gain).astype(jnp.bfloat16)
    first_rows = gather_rows(first_normed)
    group_rows = first_rows.shape[0]
    sequences = group_rows // SEQ_LEN
    query_pre = jnp.dot(first_rows, query_weight, preferred_element_type=jnp.float32)
    key_pre = jnp.dot(first_rows, key_weight, preferred_element_type=jnp.float32)
    value_pre = jnp.dot(first_rows, value_weight, preferred_element_type=jnp.float32)
    queries = rotate(query_pre.reshape(group_rows, 2 * pair_count, HD), 1.0).astype(jnp.bfloat16)
    queries = queries.reshape(sequences, SEQ_LEN, pair_count, 2, HD)
    keys_rot = rotate(key_pre.reshape(group_rows, pair_count, HD), 1.0).astype(jnp.bfloat16)
    keys_rot = keys_rot.reshape(sequences, SEQ_LEN, pair_count, HD)
    values = value_pre.astype(jnp.bfloat16).reshape(sequences, SEQ_LEN, pair_count, HD)
    mixed_heads, log_total = lax.map(attend_forward, (queries, keys_rot, values))
    heads_out = mixed_heads.reshape(group_rows, 2 * pair_count * HD)
    heads_rows = lax.all_to_all(heads_out, "tensor", split_axis=0, concat_axis=1, tiled=True)
    out_full = lax.all_gather(out_weight, "tensor", axis=0, tiled=True)
    attention_branch = jnp.dot(heads_rows, out_full, preferred_element_type=jnp.float32)
    middle = own_rows + attention_branch
    second_normed = normed(middle, second_gain).astype(jnp.bfloat16)
    second_rows = gather_rows(second_normed)
    gate_full, up_full, down_full = (gate_weight, up_weight, down_weight)
    gate_value = jnp.dot(second_rows, gate_full, preferred_element_type=jnp.float32)
    up_value = jnp.dot(second_rows, up_full, preferred_element_type=jnp.float32)
    sigmoid_gate = jax.nn.sigmoid(gate_value)
    swish_gate = gate_value * sigmoid_gate
    hidden = (swish_gate * up_value).astype(jnp.bfloat16)

    def project_hidden(start, amount):
        return jnp.dot(hidden, down_full, preferred_element_type=jnp.float32)

    ffn_branch = sum_outputs(project_hidden, row_count)
    grad_branch = gather_grads(cotangent)
    result = (middle + ffn_branch).astype(jnp.bfloat16)
    grad_hidden = times_transposed(grad_branch, down_full)
    down_part = transposed_times(hidden, grad_branch)
    slope = sigmoid_gate + gate_value * sigmoid_gate * (1.0 - sigmoid_gate)
    grad_gate = (grad_hidden * up_value * slope).astype(jnp.bfloat16)
    grad_up = (grad_hidden * swish_gate).astype(jnp.bfloat16)
    gate_part = transposed_times(second_rows, grad_gate)
    up_part = transposed_times(second_rows, grad_up)

    def second_back(start, amount):
        return times_transposed(grad_gate, gate_full) + times_transposed(grad_up, up_full)

    grad_second = sum_inputs(second_back, row_count)
    second_unused, second_pull = jax.vjp(normed, middle, second_gain)
    grad_middle_norm, second_gain_part = second_pull(grad_second)
    grad_middle = cotangent.astype(jnp.float32) + grad_middle_norm
    grad_attention = grad_middle.astype(jnp.bfloat16)
    grad_heads_rows = times_transposed(grad_attention, out_full).astype(jnp.bfloat16)
    grad_heads = lax.all_to_all(grad_heads_rows, "tensor", split_axis=1, concat_axis=0, tiled=True)
    out_part = lax.psum_scatter(
        transposed_times(heads_rows, grad_attention).astype(jnp.bfloat16),
        "tensor",
        scatter_dimension=0,
        tiled=True,
    )
    grad_mixed = grad_heads.reshape(sequences, SEQ_LEN, pair_count, 2, HD)
    grad_queries, grad_keys, grad_values = lax.map(
        attend_backward, (queries, keys_rot, values, grad_mixed, log_total)
    )
    grad_query = (
        rotate(grad_queries.reshape(group_rows, 2 * pair_count, HD), -1.0)
        .reshape(group_rows, -1)
        .astype(jnp.bfloat16)
    )
    grad_key = (
        rotate(grad_keys.reshape(group_rows, pair_count, HD), -1.0)
        .reshape(group_rows, -1)
        .astype(jnp.bfloat16)
    )
    grad_value = grad_values.reshape(group_rows, -1).astype(jnp.bfloat16)
    query_part = transposed_times(first_rows, grad_query)
    key_part = transposed_times(first_rows, grad_key)
    value_part = transposed_times(first_rows, grad_value)

    def first_back(start, amount):
        return (
            times_transposed(grad_query, query_weight)
            + times_transposed(grad_key, key_weight)
            + times_transposed(grad_value, value_weight)
        )

    grad_first = sum_inputs(first_back, row_count)
    first_unused, first_pull = jax.vjp(normed, own_rows, first_gain)
    grad_own_norm, first_gain_part = first_pull(grad_first)
    tokens_grad = grad_middle + grad_own_norm
    query_grad, key_grad, value_grad, out_grad, gate_grad, up_grad, down_grad = (
        lax.psum_scatter(
            query_part.astype(jnp.bfloat16), "dp", scatter_dimension=0, tiled=True
        ).astype(jnp.float32),
        lax.psum_scatter(
            key_part.astype(jnp.bfloat16), "dp", scatter_dimension=0, tiled=True
        ).astype(jnp.float32),
        lax.psum_scatter(
            value_part.astype(jnp.bfloat16), "dp", scatter_dimension=0, tiled=True
        ).astype(jnp.float32),
        lax.psum_scatter(out_part, "dp", scatter_dimension=1, tiled=True).astype(jnp.float32),
        lax.psum_scatter(
            gate_part.astype(jnp.bfloat16), "dp", scatter_dimension=0, tiled=True
        ).astype(jnp.float32),
        lax.psum_scatter(
            up_part.astype(jnp.bfloat16), "dp", scatter_dimension=0, tiled=True
        ).astype(jnp.float32),
        lax.psum_scatter(
            down_part.astype(jnp.bfloat16), "dp", scatter_dimension=1, tiled=True
        ).astype(jnp.float32),
    )
    first_gain_grad, second_gain_grad = (
        lax.psum_scatter(first_gain_part, ("dp", "tensor"), scatter_dimension=0, tiled=True),
        lax.psum_scatter(second_gain_part, ("dp", "tensor"), scatter_dimension=0, tiled=True),
    )
    return (
        result,
        tokens_grad,
        query_grad,
        key_grad,
        value_grad,
        out_grad,
        gate_grad,
        up_grad,
        down_grad,
        first_gain_grad,
        second_gain_grad,
    )


def swap(value, axis):
    return lax.ppermute(value, axis, [(0, 1), (1, 0)])


def nn(left, right):
    return jnp.dot(left, right, preferred_element_type=jnp.float32)


def vmem_params(**more):
    return pltpu.CompilerParams(vmem_limit_bytes=VMEM_BYTES, **more)


def smem_spec():
    return pl.BlockSpec(memory_space=pltpu.SMEM)


def vmem_spec():
    return pl.BlockSpec(memory_space=pltpu.VMEM)


def any_spec():
    return pl.BlockSpec(memory_space=pl.ANY)


def row_offset(place_ref, shift, rel, deep, part):
    ring = jnp.int32(deep)
    slot = lax.rem(place_ref[0] + shift, ring)
    core = lax.rem(place_ref[1] + rel, jnp.int32(2))
    return pl.multiple_of((slot * 2 + core) * part, 64)


def spread_heads(heads_split, heads_plain):
    columns = (heads_split + heads_plain) * HD
    spread = np.zeros((columns, (heads_split + heads_plain) * LANES), np.float32)
    for head in range(heads_split + heads_plain):
        for entry in range(HD):
            lane = entry
            if head < heads_split and entry >= HD // 2:
                lane = entry - HD // 2 + LANES // 2
            spread[head * HD + entry, head * LANES + lane] = 1.0
    return jnp.asarray(spread, jnp.bfloat16)


def prepare_kernel(deep, place_ref, *refs):
    own, other, spread_ref = refs[:deep], refs[deep : 2 * deep], refs[2 * deep]
    qkv_ref, out_ref = refs[2 * deep + 1 :]
    part = own[0].shape[1]
    half_qkv, half_out = qkv_ref.shape[1] // 2, out_ref.shape[1] // 2
    for side, chunks in enumerate((own, other)):
        for shift in range(deep):
            for rel in range(2):
                rows = pl.ds(row_offset(place_ref, shift, rel, deep, part), part)
                wide = nn(chunks[shift][rel], spread_ref[...]).astype(jnp.bfloat16)
                qkv_ref[rows, side * half_qkv : (side + 1) * half_qkv] = wide[:, :half_qkv]
                out_ref[rows, side * half_out : (side + 1) * half_out] = wide[:, half_qkv:]


def prepare(place, own, other, spread):
    deep, part = len(own), own[0].shape[1]
    rows = deep * 2 * part
    wide = spread.shape[1]
    half_qkv = wide * 2 // 3
    return pl.pallas_call(
        functools.partial(prepare_kernel, deep),
        out_shape=(
            jax.ShapeDtypeStruct((rows, 2 * half_qkv), jnp.bfloat16),
            jax.ShapeDtypeStruct((rows, 2 * (wide - half_qkv)), jnp.bfloat16),
        ),
        in_specs=[smem_spec()] + [vmem_spec()] * (2 * deep + 1),
        out_specs=(vmem_spec(), vmem_spec()),
        compiler_params=vmem_params(),
        cost_estimate=pl.CostEstimate(
            flops=4 * rows * spread.shape[0] * wide, bytes_accessed=12 * rows * wide, transcendentals=0
        ),
        name="prepare",
    )(place, *own, *other, spread)


def turn(vectors, cosine, sine):
    return vectors * cosine + pltpu.roll(vectors, LANES // 2, 1) * sine


def project_kernel(rows_ref, weight_ref, cosine_ref, sine_ref, out_ref):
    product = nn(rows_ref[...], weight_ref[...])
    cosine, sine = cosine_ref[...], sine_ref[...]
    for head in range(3):
        lanes = slice(head * LANES, (head + 1) * LANES)
        out_ref[:, lanes] = turn(product[:, lanes], cosine, sine).astype(jnp.bfloat16)
    out_ref[:, 3 * LANES :] = product[:, 3 * LANES :].astype(jnp.bfloat16)


def project(rows, weight, cosine, sine):
    count, width = rows.shape
    tile = 4 * LANES
    return pl.pallas_call(
        project_kernel,
        grid=(weight.shape[1] // tile,),
        out_shape=jax.ShapeDtypeStruct((count, weight.shape[1]), jnp.bfloat16),
        in_specs=[
            pl.BlockSpec((count, width), lambda i: (0, 0)),
            pl.BlockSpec((width, tile), lambda i: (0, i)),
            pl.BlockSpec((count, LANES), lambda i: (0, 0)),
            pl.BlockSpec((count, LANES), lambda i: (0, 0)),
        ],
        out_specs=pl.BlockSpec((count, tile), lambda i: (0, i)),
        compiler_params=vmem_params(),
        cost_estimate=pl.CostEstimate(
            flops=2 * count * width * weight.shape[1],
            bytes_accessed=2 * width * (count + weight.shape[1]) + 2 * count * weight.shape[1],
            transcendentals=0,
        ),
        name="project",
    )(rows, weight, cosine, sine)


TILE = 256


def place_rows(place_ref, qkv_refs, keys, values):
    for rel, ref in enumerate(qkv_refs):
        count = ref.shape[0]
        position = lax.rem(place_ref[2] + rel, jnp.int32(2))
        rows = pl.ds(pl.multiple_of(position * count, count), count)
        keys[rows, :] = ref[:, 2 * LANES : 3 * LANES]
        values[rows, :] = ref[:, 3 * LANES :]


def each_tile(place_ref, qkv_refs, visit):
    for rel, ref in enumerate(qkv_refs):
        count = ref.shape[0]
        position = lax.rem(place_ref[2] + rel, jnp.int32(2))
        for static_position in range(2):

            @pl.when(position == static_position)
            def _(rel=rel, count=count, static_position=static_position):
                for step in range(count // TILE):
                    visit(rel, step * TILE, static_position * count + step * TILE)


def stacked(ref, first, start):
    rows = slice(start, start + TILE)
    return jnp.concatenate(
        [ref[rows, first : first + LANES], ref[rows, first + LANES : first + 2 * LANES]], axis=0
    )


def diagonal_mask():
    row = lax.broadcasted_iota(jnp.int32, (2 * TILE, TILE), 0)
    row = jnp.where(row >= TILE, row - TILE, row)
    return row >= lax.broadcasted_iota(jnp.int32, (2 * TILE, TILE), 1)


def attend_kernel(place_ref, a_ref, b_ref, oa_ref, ob_ref, la_ref, lb_ref, keys, values):
    qkv_refs, out_refs, log_refs = (a_ref, b_ref), (oa_ref, ob_ref), (la_ref, lb_ref)
    place_rows(place_ref, qkv_refs, keys, values)
    mask = diagonal_mask()
    scale = HD ** (-0.5) * LOG2E

    def visit(rel, start, before):
        queries = stacked(qkv_refs[rel], 0, start)
        edge = slice(before, before + TILE)
        near = times_transposed(queries, keys[edge, :])
        near = jnp.where(mask, near, MASKED)
        top = jnp.max(near, axis=-1, keepdims=True)
        if before:
            far = times_transposed(queries, keys[:before, :])
            top = jnp.maximum(top, jnp.max(far, axis=-1, keepdims=True))
        top = top * scale
        near = jnp.exp2(near * scale - top)
        total = jnp.sum(near, axis=-1, keepdims=True)
        mixed = nn(near.astype(jnp.bfloat16), values[edge, :])
        if before:
            far = jnp.exp2(far * scale - top)
            total = total + jnp.sum(far, axis=-1, keepdims=True)
            mixed = mixed + nn(far.astype(jnp.bfloat16), values[:before, :])
        mixed = (mixed / total).astype(jnp.bfloat16)
        logs = jnp.broadcast_to(top + jnp.log2(total), (2 * TILE, LANES))
        rows = slice(start, start + TILE)
        for head in range(2):
            lanes = slice(head * LANES, (head + 1) * LANES)
            part = slice(head * TILE, (head + 1) * TILE)
            out_refs[rel][rows, lanes] = mixed[part]
            log_refs[rel][rows, lanes] = logs[part]

    each_tile(place_ref, qkv_refs, visit)


def attend(place, first, second):
    count = first.shape[0]
    pairs = first.shape[1] // (4 * LANES)
    wide = pl.BlockSpec((count, 4 * LANES), lambda i: (0, i))
    narrow = pl.BlockSpec((count, 2 * LANES), lambda i: (0, i))
    heads = jax.ShapeDtypeStruct((count, pairs * 2 * LANES), jnp.bfloat16)
    logs = jax.ShapeDtypeStruct((count, pairs * 2 * LANES), jnp.float32)
    return pl.pallas_call(
        attend_kernel,
        grid=(pairs,),
        out_shape=(heads, heads, logs, logs),
        in_specs=[smem_spec(), wide, wide],
        out_specs=(narrow,) * 4,
        scratch_shapes=[pltpu.VMEM((2 * count, LANES), jnp.bfloat16)] * 2,
        compiler_params=vmem_params(),
        cost_estimate=pl.CostEstimate(
            flops=pairs * 2 * 4 * count * count * 4 * LANES,
            bytes_accessed=12 * first.size,
            transcendentals=pairs * 4 * count * count,
        ),
        name="attend",
    )(place, first, second)


def attend_back_kernel(
    place_ref, a_ref, b_ref, ga_ref, gb_ref, oa_ref, ob_ref, la_ref, lb_ref, cosine_ref, sine_ref,
    da_ref, db_ref, keys, values, grad_keys, grad_values,
):
    qkv_refs, grad_refs, out_refs = (a_ref, b_ref), (ga_ref, gb_ref), (oa_ref, ob_ref)
    log_refs, result_refs = (la_ref, lb_ref), (da_ref, db_ref)
    place_rows(place_ref, qkv_refs, keys, values)
    mask = diagonal_mask()
    factor = HD ** (-0.5)
    scale = factor * LOG2E
    grad_keys[...] = jnp.zeros_like(grad_keys)
    grad_values[...] = jnp.zeros_like(grad_values)

    def visit(rel, start, before):
        queries = stacked(qkv_refs[rel], 0, start)
        grads = stacked(grad_refs[rel], 0, start)
        heads = stacked(out_refs[rel], 0, start)
        logs = stacked(log_refs[rel], 0, start)[:, :1]
        inner = jnp.sum(grads.astype(jnp.float32) * heads.astype(jnp.float32), axis=-1, keepdims=True)

        def span(rows, masked):
            softmax = jnp.exp2(times_transposed(queries, keys[rows, :]) * scale - logs)
            if masked:
                softmax = jnp.where(mask, softmax, 0.0)
            grad_softmax = times_transposed(grads, values[rows, :])
            grad_scores = (softmax * (grad_softmax - inner)).astype(jnp.bfloat16)
            grad_values[rows, :] += transposed_times(softmax.astype(jnp.bfloat16), grads)
            grad_keys[rows, :] += transposed_times(grad_scores, queries)
            return nn(grad_scores, keys[rows, :])

        grad_queries = span(slice(before, before + TILE), True)
        if before:
            grad_queries = grad_queries + span(slice(0, before), False)
        rows = slice(start, start + TILE)
        cosine, sine = cosine_ref[rel, rows, :], -sine_ref[rel, rows, :]
        for head in range(2):
            part = grad_queries[head * TILE : (head + 1) * TILE] * factor
            result_refs[rel][rows, head * LANES : (head + 1) * LANES] = turn(part, cosine, sine).astype(
                jnp.bfloat16
            )

    each_tile(place_ref, qkv_refs, visit)
    for rel, ref in enumerate(result_refs):
        count = ref.shape[0]
        position = lax.rem(place_ref[2] + rel, jnp.int32(2))
        rows = pl.ds(pl.multiple_of(position * count, count), count)
        ref[:, 2 * LANES : 3 * LANES] = turn(
            grad_keys[rows, :] * factor, cosine_ref[rel], -sine_ref[rel]
        ).astype(jnp.bfloat16)
        ref[:, 3 * LANES :] = grad_values[rows, :].astype(jnp.bfloat16)


def attend_back(place, qkv, grads, heads, logs, cosine, sine):
    count = qkv[0].shape[0]
    pairs = qkv[0].shape[1] // (4 * LANES)
    wide = pl.BlockSpec((count, 4 * LANES), lambda i: (0, i))
    narrow = pl.BlockSpec((count, 2 * LANES), lambda i: (0, i))
    table = pl.BlockSpec((2, count, LANES), lambda i: (0, 0, 0))
    result = jax.ShapeDtypeStruct(qkv[0].shape, jnp.bfloat16)
    return pl.pallas_call(
        attend_back_kernel,
        grid=(pairs,),
        out_shape=(result, result),
        in_specs=[smem_spec(), wide, wide] + [narrow] * 6 + [table] * 2,
        out_specs=(wide, wide),
        scratch_shapes=[pltpu.VMEM((2 * count, LANES), jnp.bfloat16)] * 2
        + [pltpu.VMEM((2 * count, LANES), jnp.float32)] * 2,
        compiler_params=vmem_params(),
        cost_estimate=pl.CostEstimate(
            flops=pairs * 5 * 4 * count * count * 4 * LANES,
            bytes_accessed=20 * qkv[0].size,
            transcendentals=pairs * 4 * count * count,
        ),
        name="attend_back",
    )(place, *qkv, *grads, *heads, *logs, cosine, sine)


def feed_kernel(deep, blocks, place_ref, *refs):
    rows_refs, grad_refs, refs = refs[:blocks], refs[blocks : 2 * blocks], refs[2 * blocks :]
    wide_own, wide_other, refs = refs[:deep], refs[deep : 2 * deep], refs[2 * deep :]
    down_own, down_other, refs = refs[:deep], refs[deep : 2 * deep], refs[2 * deep :]
    outs, scratch = refs[: 5 * blocks], refs[5 * blocks :]
    gate, up, down, hidden, grad_gate, grad_up, branch, grad_rows, in_sems, out_sems = scratch
    part = wide_own[0].shape[1]
    half = gate.shape[1] // 2
    loads = []
    for matrix, (target, own, other, column) in enumerate(
        ((gate, wide_own, wide_other, 0), (up, wide_own, wide_other, half), (down, down_own, down_other, 0))
    ):
        here = []
        for side, chunks in enumerate((own, other)):
            for shift in range(deep):
                for rel in range(2):
                    copy = pltpu.make_async_copy(
                        chunks[shift].at[rel, :, pl.ds(column, half)],
                        target.at[
                            pl.ds(row_offset(place_ref, shift, rel, deep, part), part),
                            pl.ds(side * half, half),
                        ],
                        in_sems.at[matrix, side, shift, rel],
                    )
                    copy.start()
                    here.append(copy)
        loads.append(here)
    stores = []

    def store(scratch_ref, block, which):
        copy = pltpu.make_async_copy(
            scratch_ref.at[block], outs[block * 5 + which], out_sems.at[block, which]
        )
        copy.start()
        stores.append(copy)

    for block in range(blocks):
        if block == 0:
            for here in loads:
                for copy in here:
                    copy.wait()
        width = gate.shape[1]

        @pl.loop(0, width // TILE)
        def _(step, block=block):
            lanes = pl.ds(pl.multiple_of(step * TILE, TILE), TILE)
            rows, grads = rows_refs[block][...], grad_refs[block][...]
            gate_value = nn(rows, gate[:, lanes])
            up_value = nn(rows, up[:, lanes])
            grad_hidden = nn(grads, down[:, lanes])
            sigmoid = 1.0 / (1.0 + jnp.exp(-gate_value))
            swish = gate_value * sigmoid
            slope = sigmoid + swish * (1.0 - sigmoid)
            hidden[block, :, lanes] = (swish * up_value).astype(jnp.bfloat16)
            grad_gate[block, :, lanes] = (grad_hidden * up_value * slope).astype(jnp.bfloat16)
            grad_up[block, :, lanes] = (grad_hidden * swish).astype(jnp.bfloat16)

        store(hidden, block, 0)
        store(grad_gate, block, 1)
        store(grad_up, block, 2)

        @pl.loop(0, gate.shape[0] // TILE)
        def _(step, block=block):
            lanes = pl.ds(pl.multiple_of(step * TILE, TILE), TILE)
            grad_rows[block, :, lanes] = (
                times_transposed(grad_gate[block], gate[lanes, :])
                + times_transposed(grad_up[block], up[lanes, :])
            ).astype(jnp.bfloat16)
            branch[block, :, lanes] = times_transposed(hidden[block], down[lanes, :]).astype(
                jnp.bfloat16
            )

        store(branch, block, 3)
        store(grad_rows, block, 4)
    for copy in stores:
        copy.wait()


def feed(place, rows, grads, wide_own, wide_other, down_own, down_other):
    deep, part = len(wide_own), wide_own[0].shape[1]
    width, hidden_units = deep * 2 * part, 2 * down_own[0].shape[2]
    blocks = len(rows)
    count = rows[0].shape[0]
    small = jax.ShapeDtypeStruct((count, hidden_units), jnp.bfloat16)
    large = jax.ShapeDtypeStruct((count, width), jnp.bfloat16)
    outs = pl.pallas_call(
        functools.partial(feed_kernel, deep, blocks),
        out_shape=(small, small, small, large, large) * blocks,
        in_specs=[smem_spec()] + [vmem_spec()] * (2 * blocks) + [any_spec()] * (4 * deep),
        out_specs=(any_spec(),) * (5 * blocks),
        scratch_shapes=[pltpu.VMEM((width, hidden_units), jnp.bfloat16)] * 3
        + [pltpu.VMEM((blocks, count, hidden_units), jnp.bfloat16)] * 3
        + [pltpu.VMEM((blocks, count, width), jnp.bfloat16)] * 2
        + [pltpu.SemaphoreType.DMA((3, 2, deep, 2)), pltpu.SemaphoreType.DMA((blocks, 5))],
        compiler_params=vmem_params(),
        cost_estimate=pl.CostEstimate(
            flops=blocks * 12 * count * width * hidden_units,
            bytes_accessed=2 * (3 * width * hidden_units + blocks * count * (4 * width + 3 * hidden_units)),
            transcendentals=blocks * count * hidden_units,
        ),
        name="feed",
    )(place, *rows, *grads, *wide_own, *wide_other, *down_own, *down_other)
    return [outs[5 * block : 5 * block + 5] for block in range(blocks)]


def weight_kernel(blocks, pairs, spread, added, *refs):
    lefts, rights = refs[: blocks * pairs], refs[blocks * pairs : 2 * blocks * pairs]
    rest = refs[2 * blocks * pairs :]
    out_ref = rest[-1]
    offset = 0
    parts = []
    for pair in range(pairs):
        total = None
        for block in range(blocks):
            term = transposed_times(lefts[pair * blocks + block][...], rights[pair * blocks + block][...])
            total = term if total is None else total + term
        parts.append(total)
    if spread:
        joined = jnp.concatenate([part.astype(jnp.bfloat16) for part in parts], axis=1)
        total = times_transposed(joined, rest[0][...])
        if added:
            total = total + rest[1][...].astype(jnp.float32)
        out_ref[...] = total.astype(jnp.bfloat16)
    else:
        for pair, total in enumerate(parts):
            lanes = slice(offset, offset + total.shape[1])
            if added:
                total = total + rest[0][:, lanes].astype(jnp.float32)
            out_ref[:, lanes] = total.astype(jnp.bfloat16)
            offset += total.shape[1]


def weight_grad(pairs, side, spread=None, added=None, tile=256):
    blocks = len(pairs[0][0])
    lefts = [left for left_blocks, _ in pairs for left in left_blocks]
    rights = [right for _, right_blocks in pairs for right in right_blocks]
    count, width = lefts[0].shape
    widths = [right_blocks[0].shape[1] // 2 for _, right_blocks in pairs]
    columns = sum(widths) if spread is None else spread.shape[0]
    operands = lefts + rights
    in_specs = [pl.BlockSpec((count, tile), lambda i: (0, i)) for _ in lefts]
    in_specs += [pl.BlockSpec((count, right.shape[1] // 2), lambda i: (0, side)) for right in rights]
    if spread is not None:
        operands.append(spread)
        in_specs.append(pl.BlockSpec(spread.shape, lambda i: (0, 0)))
    if added is not None:
        operands.append(added)
        in_specs.append(pl.BlockSpec((tile, columns), lambda i: (i, 0)))
    return pl.pallas_call(
        functools.partial(weight_kernel, blocks, len(pairs), spread is not None, added is not None),
        grid=(width // tile,),
        out_shape=jax.ShapeDtypeStruct((width, columns), jnp.bfloat16),
        in_specs=in_specs,
        out_specs=pl.BlockSpec((tile, columns), lambda i: (i, 0)),
        compiler_params=vmem_params(),
        cost_estimate=pl.CostEstimate(
            flops=2 * blocks * count * width * sum(widths),
            bytes_accessed=2 * (blocks * count * (width * len(pairs) + sum(widths)) + width * columns),
            transcendentals=0,
        ),
        name="weight_grad",
    )(*operands)


def tables(rows, x_place):
    lane = np.arange(LANES)
    entry = lane % (LANES // 2)
    live = (entry < HD // 2).astype(np.float32)
    sign = np.where(lane < LANES // 2, -1.0, 1.0).astype(np.float32) * live
    pair_entry = np.where(entry < HD // 2, entry, 0).astype(np.float32)
    inverse = THETA ** (-2.0 * jnp.asarray(pair_entry) / HD)
    both = []
    for rel in range(2):
        first = lax.rem(x_place + rel, jnp.int32(2)) * rows
        position = (first + jnp.arange(rows, dtype=jnp.int32)).astype(jnp.float32)
        both.append(position[:, None] * inverse[None, :])
    angles = jnp.stack(both)
    return jnp.cos(angles) * live, jnp.sin(angles) * sign


def norm_factor(rows):
    return lax.rsqrt(jnp.mean(rows * rows, axis=-1, keepdims=True) + EPSILON)


def norm_back(rows, gain, grad):
    factor = norm_factor(rows)
    scaled = grad * gain
    return factor * scaled - rows * factor**3 * jnp.mean(scaled * rows, axis=-1, keepdims=True)


def spread_blocks(own):
    beside = swap(own, "x")
    return [own, beside, swap(own, "c"), swap(beside, "c")]


def sum_blocks(parts):
    beside = parts[1].astype(jnp.float32) + swap(parts[3], "c").astype(jnp.float32)
    arrived = swap(beside.astype(jnp.bfloat16), "x")
    own = parts[0].astype(jnp.float32) + swap(parts[2], "c").astype(jnp.float32)
    return own + arrived.astype(jnp.float32)


def gather_chunks(halves, core, deep):
    keep = jnp.where(core == 0, halves[0], halves[1])
    send = jnp.where(core == 0, halves[1], halves[0])
    chunk = jnp.stack([keep, swap(send, "c")])
    own = [chunk]
    for shift in range(1, deep):
        own.append(lax.ppermute(chunk, "z", [((i + shift) % deep, i) for i in range(deep)]))
    other = [swap(piece, "y") for piece in own]
    return own, other


def finish_grad(summed, core, part):
    mine = lax.psum_scatter(summed, "z", scatter_dimension=0, tiled=True)
    keep = lax.dynamic_slice_in_dim(mine, core * part, part, axis=0)
    send = lax.dynamic_slice_in_dim(mine, (1 - core) * part, part, axis=0)
    recv = swap(send, "c")
    first = jnp.where(core == 0, keep, recv).astype(jnp.float32)
    second = jnp.where(core == 0, recv, keep).astype(jnp.float32)
    return first, second


def join(first, second, start, stop):
    return jnp.concatenate([first[:, start:stop], second[:, start:stop]], axis=1)


def gain_grad(columns, gain, depth_place, part):
    rows = sum(jnp.sum(grad * weight.astype(jnp.float32), axis=1) for grad, weight in columns)
    rows = rows / lax.dynamic_slice_in_dim(gain, depth_place * part, part)
    rows = rows + swap(rows, "x")
    rows = rows + swap(rows, "y")
    piece = part // 4
    place = lax.axis_index("y") * 2 + lax.axis_index("x")
    return lax.dynamic_slice_in_dim(rows, place * piece, piece)


def fast_local(
    tokens,
    cotangent,
    first_gain,
    query_weight,
    key_weight,
    value_weight,
    out_weight,
    second_gain,
    gate_weight,
    up_weight,
    down_weight,
):
    deep = lax.axis_size("z")
    z_place, core, x_place = (lax.axis_index(name).astype(jnp.int32) for name in ("z", "c", "x"))
    place = jnp.stack([z_place, core, x_place])
    rows = tokens.shape[0]
    part = gate_weight.shape[0]
    depth_place = z_place * 2 + core
    own_rows = tokens.astype(jnp.float32)
    first_normed = (own_rows * norm_factor(own_rows) * first_gain).astype(jnp.bfloat16)
    out_turned, down_turned = out_weight.T, down_weight.T

    def halves(*weights):
        result = []
        for half in range(2):
            pieces = []
            for weight in weights:
                size = weight.shape[1] // 2
                pieces.append(weight[:, half * size : (half + 1) * size])
            result.append(jnp.concatenate(pieces, axis=1))
        return result

    spread = spread_heads(3, 3)
    heads_own, heads_other = gather_chunks(
        halves(query_weight, key_weight, value_weight, out_turned), core, deep
    )
    wide_own, wide_other = gather_chunks(halves(gate_weight, up_weight), core, deep)
    down_own, down_other = gather_chunks(halves(down_turned), core, deep)
    first_blocks = spread_blocks(first_normed)
    qkv_weight, out_wide = prepare(place, heads_own, heads_other, spread)
    cosine, sine = tables(rows, x_place)
    qkv = [project(first_blocks[i], qkv_weight, cosine[i % 2], sine[i % 2]) for i in (0, 1, 2, 3)]
    heads, logs = [], []
    for sequence in range(2):
        one, two, log_one, log_two = attend(place, qkv[2 * sequence], qkv[2 * sequence + 1])
        heads += [one, two]
        logs += [log_one, log_two]
    branch = sum_blocks([times_transposed(block, out_wide).astype(jnp.bfloat16) for block in heads])
    middle = own_rows + branch
    second_normed = (middle * norm_factor(middle) * second_gain).astype(jnp.bfloat16)
    cotangent_blocks = spread_blocks(cotangent)
    second_blocks = spread_blocks(second_normed)
    fed = [None] * 4
    for pair in ((0, 2), (1, 3)):
        outs = feed(
            place,
            [second_blocks[i] for i in pair],
            [cotangent_blocks[i] for i in pair],
            wide_own,
            wide_other,
            down_own,
            down_other,
        )
        for i, out in zip(pair, outs):
            fed[i] = out
    hidden, grad_gate, grad_up, branches, grads_second = ([block[i] for block in fed] for i in range(5))
    grad_second = sum_blocks(grads_second)
    grad_middle = cotangent.astype(jnp.float32) + norm_back(middle, second_gain, grad_second)
    grad_attention = spread_blocks(grad_middle.astype(jnp.bfloat16))
    result = (middle + sum_blocks(branches)).astype(jnp.bfloat16)

    down_sent = swap(weight_grad([(cotangent_blocks, hidden)], 1), "y")
    wide_sent = swap(weight_grad([(second_blocks, grad_gate), (second_blocks, grad_up)], 1), "y")
    down_grads = finish_grad(weight_grad([(cotangent_blocks, hidden)], 0, added=down_sent), core, part)
    wide_grads = finish_grad(
        weight_grad([(second_blocks, grad_gate), (second_blocks, grad_up)], 0, added=wide_sent), core, part
    )

    grad_heads = [nn(block, out_wide).astype(jnp.bfloat16) for block in grad_attention]
    grad_qkv = []
    for sequence in range(2):
        chosen = slice(2 * sequence, 2 * sequence + 2)
        grad_qkv += attend_back(
            place, qkv[chosen], grad_heads[chosen], heads[chosen], logs[chosen], cosine, sine
        )
    grad_first = sum_blocks([times_transposed(block, qkv_weight).astype(jnp.bfloat16) for block in grad_qkv])
    tokens_grad = grad_middle + norm_back(own_rows, first_gain, grad_first)
    head_pairs = [(first_blocks, grad_qkv), (grad_attention, heads)]
    heads_sent = swap(weight_grad(head_pairs, 1, spread=spread), "y")
    heads_grads = finish_grad(
        weight_grad(head_pairs, 0, spread=spread, added=heads_sent), core, part
    )

    sizes = [weight.shape[1] // 2 for weight in (query_weight, key_weight, value_weight, out_turned)]
    starts = np.cumsum([0] + sizes)
    query_grad, key_grad, value_grad, out_grad = (
        join(*heads_grads, int(starts[i]), int(starts[i + 1])) for i in range(4)
    )
    half = gate_weight.shape[1] // 2
    gate_grad, up_grad = (join(*wide_grads, i * half, (i + 1) * half) for i in range(2))
    down_grad = join(*down_grads, 0, half)
    first_gain_grad = gain_grad(
        ((query_grad, query_weight), (key_grad, key_weight), (value_grad, value_weight)),
        first_gain,
        depth_place,
        part,
    )
    second_gain_grad = gain_grad(
        ((gate_grad, gate_weight), (up_grad, up_weight)), second_gain, depth_place, part
    )
    return (
        result,
        tokens_grad,
        query_grad,
        key_grad,
        value_grad,
        out_grad.T,
        gate_grad,
        up_grad,
        down_grad.T,
        first_gain_grad,
        second_gain_grad,
    )


def specs(depth, width):
    both = depth + width
    rows, inward, outward = P(both, None), P(depth, width), P(width, depth)
    in_specs = (rows, rows, P(), inward, inward, inward, outward, P(), inward, inward, outward)
    out_specs = (rows, rows, inward, inward, inward, outward, inward, inward, outward, P(both), P(both))
    return in_specs, out_specs


def solution(mesh):
    depth, width = mesh.shape["dp"], mesh.shape["tensor"]

    def run(tokens, cotangent, *weights):
        fits = (
            width == 4
            and depth % 2 == 0
            and tokens.shape[0] * 2 == SEQ_LEN * depth * width
            and weights[2].shape[1] == 2 * width * HD
            and weights[1].shape[1] == 4 * width * HD
        )
        if fits:
            devices = mesh.devices.reshape(depth // 2, 2, 2, 2)
            fine = jax.sharding.Mesh(devices, ("z", "c", "y", "x"))
            in_specs, out_specs = specs(("z", "c"), ("y", "x"))
            call, over = fast_local, fine
        else:
            in_specs, out_specs = specs(("dp",), ("tensor",))
            call, over = local, mesh
        return jax.shard_map(call, mesh=over, in_specs=in_specs, out_specs=out_specs, check_vma=False)(
            tokens, cotangent, *weights
        )

    return run
```

```python
import functools

import jax
import jax.numpy as jnp
import numpy as np
from jax import lax
from jax.experimental import pallas as pl
from jax.experimental.pallas import tpu as pltpu
from jax.sharding import PartitionSpec as P

HD = 96
SEQ_LEN = 1024


EPSILON = 1e-05
THETA = 100000.0
MASKED = -1e30
LOG2E = 1.4426950408889634
LANES = 128
SHARE = 20
VMEM_BYTES = 56 * 2**20


def normed(inputs, gain):
    factor = lax.rsqrt(jnp.mean(inputs * inputs, axis=-1, keepdims=True) + EPSILON)
    return inputs * factor * gain


def rotate(vectors, direction):
    seq_rows, head_count, head_size = vectors.shape
    half_size = head_size // 2
    position = (jnp.arange(seq_rows, dtype=jnp.int32) % SEQ_LEN).astype(jnp.float32)
    inverse = THETA ** (-2.0 * jnp.arange(half_size, dtype=jnp.float32) / head_size)
    angles = position[:, None] * inverse[None, :]
    cosine = jnp.cos(angles)[:, None, :]
    sine_part = direction * jnp.sin(angles)[:, None, :]
    leading = vectors[..., :half_size]
    trailing = vectors[..., half_size:]
    return jnp.concatenate(
        [leading * cosine - trailing * sine_part, trailing * cosine + leading * sine_part], axis=-1
    )


def times_transposed(left, right):
    return lax.dot_general(
        left, right, (((1,), (1,)), ((), ())), preferred_element_type=jnp.float32
    )


def transposed_times(left, right):
    return lax.dot_general(
        left, right, (((0,), (0,)), ((), ())), preferred_element_type=jnp.float32
    )


def scaled_scores(queries, keys_rot):
    raw_scores = jnp.einsum(
        "qhgd,khd->hgqk", queries, keys_rot, preferred_element_type=jnp.float32
    ) * queries.shape[-1] ** (-0.5)
    length_rows = queries.shape[0]
    causal = jnp.arange(length_rows)[:, None] >= jnp.arange(length_rows)[None, :]
    return jnp.where(causal, raw_scores, MASKED)


def attend_forward(operands):
    queries, keys_rot, values = operands
    scores = scaled_scores(queries, keys_rot)
    row_max = jnp.max(scores, axis=-1, keepdims=True)
    weights = jnp.exp(scores - row_max)
    row_total = jnp.sum(weights, axis=-1, keepdims=True)
    softmax = (weights / row_total).astype(jnp.bfloat16)
    mixed_heads = jnp.einsum("hgqk,khd->qhgd", softmax, values, preferred_element_type=jnp.float32)
    return (mixed_heads.astype(jnp.bfloat16), (row_max + jnp.log(row_total))[..., 0])


def attend_backward(operands):
    queries, keys_rot, values, grad_mixed, log_total = operands
    scores = scaled_scores(queries, keys_rot)
    softmax = jnp.exp(scores - log_total[..., None])
    grad_softmax = jnp.einsum(
        "qhgd,khd->hgqk", grad_mixed, values, preferred_element_type=jnp.float32
    )
    grad_values = jnp.einsum(
        "hgqk,qhgd->khd",
        softmax.astype(jnp.bfloat16),
        grad_mixed,
        preferred_element_type=jnp.float32,
    )
    row_inner = jnp.sum(softmax * grad_softmax, axis=-1, keepdims=True)
    grad_scores = (softmax * (grad_softmax - row_inner)).astype(jnp.bfloat16)
    scale_factor = queries.shape[-1] ** (-0.5)
    grad_queries = (
        jnp.einsum("hgqk,khd->qhgd", grad_scores, keys_rot, preferred_element_type=jnp.float32)
        * scale_factor
    )
    grad_keys = (
        jnp.einsum("hgqk,qhgd->khd", grad_scores, queries, preferred_element_type=jnp.float32)
        * scale_factor
    )
    return (grad_queries, grad_keys, grad_values)


def gather_rows(shard):
    return lax.all_gather(shard, "tensor", axis=0, tiled=True)


def gather_grads(shard):
    return lax.all_gather(shard, "tensor", axis=0, tiled=True)


def sum_outputs(term, row_count):
    return lax.psum_scatter(
        term(jnp.int32(0), row_count * lax.axis_size("tensor")),
        "tensor",
        scatter_dimension=0,
        tiled=True,
    )


def sum_inputs(term, row_count):
    return lax.psum_scatter(
        term(jnp.int32(0), row_count * lax.axis_size("tensor")),
        "tensor",
        scatter_dimension=0,
        tiled=True,
    )


def local(
    tokens,
    cotangent,
    first_gain,
    query_weight,
    key_weight,
    value_weight,
    out_weight,
    second_gain,
    gate_weight,
    up_weight,
    down_weight,
):
    query_weight, key_weight, value_weight, out_weight, gate_weight, up_weight, down_weight = (
        lax.all_gather(query_weight, "dp", axis=0, tiled=True),
        lax.all_gather(key_weight, "dp", axis=0, tiled=True),
        lax.all_gather(value_weight, "dp", axis=0, tiled=True),
        lax.all_gather(out_weight, "dp", axis=1, tiled=True),
        lax.all_gather(gate_weight, "dp", axis=0, tiled=True),
        lax.all_gather(up_weight, "dp", axis=0, tiled=True),
        lax.all_gather(down_weight, "dp", axis=1, tiled=True),
    )
    own_rows = tokens.astype(jnp.float32)
    row_count = own_rows.shape[0]
    pair_count = key_weight.shape[1] // HD
    first_normed = normed(own_rows, first_gain).astype(jnp.bfloat16)
    first_rows = gather_rows(first_normed)
    group_rows = first_rows.shape[0]
    sequences = group_rows // SEQ_LEN
    query_pre = jnp.dot(first_rows, query_weight, preferred_element_type=jnp.float32)
    key_pre = jnp.dot(first_rows, key_weight, preferred_element_type=jnp.float32)
    value_pre = jnp.dot(first_rows, value_weight, preferred_element_type=jnp.float32)
    queries = rotate(query_pre.reshape(group_rows, 2 * pair_count, HD), 1.0).astype(jnp.bfloat16)
    queries = queries.reshape(sequences, SEQ_LEN, pair_count, 2, HD)
    keys_rot = rotate(key_pre.reshape(group_rows, pair_count, HD), 1.0).astype(jnp.bfloat16)
    keys_rot = keys_rot.reshape(sequences, SEQ_LEN, pair_count, HD)
    values = value_pre.astype(jnp.bfloat16).reshape(sequences, SEQ_LEN, pair_count, HD)
    mixed_heads, log_total = lax.map(attend_forward, (queries, keys_rot, values))
    heads_out = mixed_heads.reshape(group_rows, 2 * pair_count * HD)
    heads_rows = lax.all_to_all(heads_out, "tensor", split_axis=0, concat_axis=1, tiled=True)
    out_full = lax.all_gather(out_weight, "tensor", axis=0, tiled=True)
    attention_branch = jnp.dot(heads_rows, out_full, preferred_element_type=jnp.float32)
    middle = own_rows + attention_branch
    second_normed = normed(middle, second_gain).astype(jnp.bfloat16)
    second_rows = gather_rows(second_normed)
    gate_full, up_full, down_full = (gate_weight, up_weight, down_weight)
    gate_value = jnp.dot(second_rows, gate_full, preferred_element_type=jnp.float32)
    up_value = jnp.dot(second_rows, up_full, preferred_element_type=jnp.float32)
    sigmoid_gate = jax.nn.sigmoid(gate_value)
    swish_gate = gate_value * sigmoid_gate
    hidden = (swish_gate * up_value).astype(jnp.bfloat16)

    def project_hidden(start, amount):
        return jnp.dot(hidden, down_full, preferred_element_type=jnp.float32)

    ffn_branch = sum_outputs(project_hidden, row_count)
    grad_branch = gather_grads(cotangent)
    result = (middle + ffn_branch).astype(jnp.bfloat16)
    grad_hidden = times_transposed(grad_branch, down_full)
    down_part = transposed_times(hidden, grad_branch)
    slope = sigmoid_gate + gate_value * sigmoid_gate * (1.0 - sigmoid_gate)
    grad_gate = (grad_hidden * up_value * slope).astype(jnp.bfloat16)
    grad_up = (grad_hidden * swish_gate).astype(jnp.bfloat16)
    gate_part = transposed_times(second_rows, grad_gate)
    up_part = transposed_times(second_rows, grad_up)

    def second_back(start, amount):
        return times_transposed(grad_gate, gate_full) + times_transposed(grad_up, up_full)

    grad_second = sum_inputs(second_back, row_count)
    second_unused, second_pull = jax.vjp(normed, middle, second_gain)
    grad_middle_norm, second_gain_part = second_pull(grad_second)
    grad_middle = cotangent.astype(jnp.float32) + grad_middle_norm
    grad_attention = grad_middle.astype(jnp.bfloat16)
    grad_heads_rows = times_transposed(grad_attention, out_full).astype(jnp.bfloat16)
    grad_heads = lax.all_to_all(grad_heads_rows, "tensor", split_axis=1, concat_axis=0, tiled=True)
    out_part = lax.psum_scatter(
        transposed_times(heads_rows, grad_attention).astype(jnp.bfloat16),
        "tensor",
        scatter_dimension=0,
        tiled=True,
    )
    grad_mixed = grad_heads.reshape(sequences, SEQ_LEN, pair_count, 2, HD)
    grad_queries, grad_keys, grad_values = lax.map(
        attend_backward, (queries, keys_rot, values, grad_mixed, log_total)
    )
    grad_query = (
        rotate(grad_queries.reshape(group_rows, 2 * pair_count, HD), -1.0)
        .reshape(group_rows, -1)
        .astype(jnp.bfloat16)
    )
    grad_key = (
        rotate(grad_keys.reshape(group_rows, pair_count, HD), -1.0)
        .reshape(group_rows, -1)
        .astype(jnp.bfloat16)
    )
    grad_value = grad_values.reshape(group_rows, -1).astype(jnp.bfloat16)
    query_part = transposed_times(first_rows, grad_query)
    key_part = transposed_times(first_rows, grad_key)
    value_part = transposed_times(first_rows, grad_value)

    def first_back(start, amount):
        return (
            times_transposed(grad_query, query_weight)
            + times_transposed(grad_key, key_weight)
            + times_transposed(grad_value, value_weight)
        )

    grad_first = sum_inputs(first_back, row_count)
    first_unused, first_pull = jax.vjp(normed, own_rows, first_gain)
    grad_own_norm, first_gain_part = first_pull(grad_first)
    tokens_grad = grad_middle + grad_own_norm
    query_grad, key_grad, value_grad, out_grad, gate_grad, up_grad, down_grad = (
        lax.psum_scatter(
            query_part.astype(jnp.bfloat16), "dp", scatter_dimension=0, tiled=True
        ).astype(jnp.float32),
        lax.psum_scatter(
            key_part.astype(jnp.bfloat16), "dp", scatter_dimension=0, tiled=True
        ).astype(jnp.float32),
        lax.psum_scatter(
            value_part.astype(jnp.bfloat16), "dp", scatter_dimension=0, tiled=True
        ).astype(jnp.float32),
        lax.psum_scatter(out_part, "dp", scatter_dimension=1, tiled=True).astype(jnp.float32),
        lax.psum_scatter(
            gate_part.astype(jnp.bfloat16), "dp", scatter_dimension=0, tiled=True
        ).astype(jnp.float32),
        lax.psum_scatter(
            up_part.astype(jnp.bfloat16), "dp", scatter_dimension=0, tiled=True
        ).astype(jnp.float32),
        lax.psum_scatter(
            down_part.astype(jnp.bfloat16), "dp", scatter_dimension=1, tiled=True
        ).astype(jnp.float32),
    )
    first_gain_grad, second_gain_grad = (
        lax.psum_scatter(first_gain_part, ("dp", "tensor"), scatter_dimension=0, tiled=True),
        lax.psum_scatter(second_gain_part, ("dp", "tensor"), scatter_dimension=0, tiled=True),
    )
    return (
        result,
        tokens_grad,
        query_grad,
        key_grad,
        value_grad,
        out_grad,
        gate_grad,
        up_grad,
        down_grad,
        first_gain_grad,
        second_gain_grad,
    )


def swap(value, axis):
    return lax.ppermute(value, axis, [(0, 1), (1, 0)])


def nn(left, right):
    return jnp.dot(left, right, preferred_element_type=jnp.float32)


def cost(flops, bytes_accessed, transcendentals):
    return pl.CostEstimate(
        flops=flops // SHARE, bytes_accessed=bytes_accessed // SHARE, transcendentals=transcendentals // SHARE
    )


def vmem_params(**more):
    return pltpu.CompilerParams(vmem_limit_bytes=VMEM_BYTES, **more)


def smem_spec():
    return pl.BlockSpec(memory_space=pltpu.SMEM)


def vmem_spec():
    return pl.BlockSpec(memory_space=pltpu.VMEM)


def any_spec():
    return pl.BlockSpec(memory_space=pl.ANY)


def row_offset(place_ref, shift, rel, deep, part):
    ring = jnp.int32(deep)
    slot = lax.rem(place_ref[0] + shift, ring)
    core = lax.rem(place_ref[1] + rel, jnp.int32(2))
    return pl.multiple_of((slot * 2 + core) * part, 64)


def spread_heads(heads_split, heads_plain):
    columns = (heads_split + heads_plain) * HD
    spread = np.zeros((columns, (heads_split + heads_plain) * LANES), np.float32)
    for head in range(heads_split + heads_plain):
        for entry in range(HD):
            lane = entry
            if head < heads_split and entry >= HD // 2:
                lane = entry - HD // 2 + LANES // 2
            spread[head * HD + entry, head * LANES + lane] = 1.0
    return jnp.asarray(spread, jnp.bfloat16)


def turn(vectors, cosine, sine):
    return vectors * cosine + pltpu.roll(vectors, LANES // 2, 1) * sine


TILE = 256


def place_rows(place_ref, qkv_refs, keys, values):
    for rel, ref in enumerate(qkv_refs):
        count = ref.shape[0]
        position = lax.rem(place_ref[2] + rel, jnp.int32(2))
        rows = pl.ds(pl.multiple_of(position * count, count), count)
        keys[rows, :] = ref[:, 2 * LANES : 3 * LANES]
        values[rows, :] = ref[:, 3 * LANES :]


def each_tile(place_ref, qkv_refs, visit):
    for rel, ref in enumerate(qkv_refs):
        count = ref.shape[0]
        position = lax.rem(place_ref[2] + rel, jnp.int32(2))
        for static_position in range(2):

            @pl.when(position == static_position)
            def _(rel=rel, count=count, static_position=static_position):
                for step in range(count // TILE):
                    visit(rel, step * TILE, static_position * count + step * TILE)


def stacked(ref, first, start):
    rows = slice(start, start + TILE)
    return jnp.concatenate(
        [ref[rows, first : first + LANES], ref[rows, first + LANES : first + 2 * LANES]], axis=0
    )


def diagonal_mask():
    row = lax.broadcasted_iota(jnp.int32, (2 * TILE, TILE), 0)
    row = jnp.where(row >= TILE, row - TILE, row)
    return row >= lax.broadcasted_iota(jnp.int32, (2 * TILE, TILE), 1)


def attend_back_kernel(
    place_ref, a_ref, b_ref, ga_ref, gb_ref, oa_ref, ob_ref, la_ref, lb_ref, cosine_ref, sine_ref,
    da_ref, db_ref, keys, values, grad_keys, grad_values,
):
    qkv_refs, grad_refs, out_refs = (a_ref, b_ref), (ga_ref, gb_ref), (oa_ref, ob_ref)
    log_refs, result_refs = (la_ref, lb_ref), (da_ref, db_ref)
    place_rows(place_ref, qkv_refs, keys, values)
    mask = diagonal_mask()
    factor = HD ** (-0.5)
    scale = factor * LOG2E
    grad_keys[...] = jnp.zeros_like(grad_keys)
    grad_values[...] = jnp.zeros_like(grad_values)

    def visit(rel, start, before):
        queries = stacked(qkv_refs[rel], 0, start)
        grads = stacked(grad_refs[rel], 0, start)
        heads = stacked(out_refs[rel], 0, start)
        rows = slice(start, start + TILE)
        pair = pl.program_id(0)
        lane = lax.broadcasted_iota(jnp.int32, (TILE, LANES), 1)
        logs = jnp.concatenate(
            [
                jnp.sum(jnp.where(lane == 2 * pair + head, log_refs[rel][rows, :], 0.0), axis=-1, keepdims=True)
                for head in range(2)
            ],
            axis=0,
        )
        inner = jnp.sum(grads.astype(jnp.float32) * heads.astype(jnp.float32), axis=-1, keepdims=True)

        def span(rows, masked):
            softmax = jnp.exp2(times_transposed(queries, keys[rows, :]) * scale - logs)
            if masked:
                softmax = jnp.where(mask, softmax, 0.0)
            grad_softmax = times_transposed(grads, values[rows, :])
            grad_scores = (softmax * (grad_softmax - inner)).astype(jnp.bfloat16)
            grad_values[rows, :] += transposed_times(softmax.astype(jnp.bfloat16), grads)
            grad_keys[rows, :] += transposed_times(grad_scores, queries)
            return nn(grad_scores, keys[rows, :])

        grad_queries = span(slice(before, before + TILE), True)
        if before:
            grad_queries = grad_queries + span(slice(0, before), False)
        rows = slice(start, start + TILE)
        cosine, sine = cosine_ref[rel, rows, :], -sine_ref[rel, rows, :]
        for head in range(2):
            part = grad_queries[head * TILE : (head + 1) * TILE] * factor
            result_refs[rel][rows, head * LANES : (head + 1) * LANES] = turn(part, cosine, sine).astype(
                jnp.bfloat16
            )

    each_tile(place_ref, qkv_refs, visit)
    for rel, ref in enumerate(result_refs):
        count = ref.shape[0]
        position = lax.rem(place_ref[2] + rel, jnp.int32(2))
        rows = pl.ds(pl.multiple_of(position * count, count), count)
        ref[:, 2 * LANES : 3 * LANES] = turn(
            grad_keys[rows, :] * factor, cosine_ref[rel], -sine_ref[rel]
        ).astype(jnp.bfloat16)
        ref[:, 3 * LANES :] = grad_values[rows, :].astype(jnp.bfloat16)


def attend_back(place, qkv, grads, heads, logs, cosine, sine):
    count = qkv[0].shape[0]
    pairs = qkv[0].shape[1] // (4 * LANES)
    wide = pl.BlockSpec((count, 4 * LANES), lambda i: (0, i))
    narrow = pl.BlockSpec((count, 2 * LANES), lambda i: (0, i))
    log = pl.BlockSpec((count, LANES), lambda i: (0, 0))
    table = pl.BlockSpec((2, count, LANES), lambda i: (0, 0, 0))
    result = jax.ShapeDtypeStruct(qkv[0].shape, jnp.bfloat16)
    return pl.pallas_call(
        attend_back_kernel,
        grid=(pairs,),
        out_shape=(result, result),
        in_specs=[smem_spec(), wide, wide] + [narrow] * 4 + [log] * 2 + [table] * 2,
        out_specs=(wide, wide),
        scratch_shapes=[pltpu.VMEM((2 * count, LANES), jnp.bfloat16)] * 2
        + [pltpu.VMEM((2 * count, LANES), jnp.float32)] * 2,
        compiler_params=vmem_params(),
        cost_estimate=cost(
            flops=pairs * 5 * 4 * count * count * 4 * LANES,
            bytes_accessed=20 * qkv[0].size,
            transcendentals=pairs * 4 * count * count,
        ),
        name="attend_back",
    )(place, *qkv, *grads, *heads, *logs, cosine, sine)


def feed_kernel(deep, blocks, chosen, place_ref, rows_ref, grads_ref, chunks, *refs):
    outs, scratch = refs[: 5 * blocks], refs[5 * blocks :]
    gate, up, down, hidden, grad_gate, grad_up, branch, grad_rows, in_sems, out_sems = scratch[:10]
    rows_refs, grad_refs, row_sems = scratch[10], scratch[11], scratch[12]
    part = chunks.shape[3]
    half = gate.shape[1] // 2
    row_loads = []
    for block, index in enumerate(chosen):
        here = []
        for which, (source, target) in enumerate(((rows_ref, rows_refs), (grads_ref, grad_refs))):
            copy = pltpu.make_async_copy(source.at[index], target.at[block], row_sems.at[block, which])
            copy.start()
            here.append(copy)
        row_loads.append(here)
    loads = []
    for matrix, target in enumerate((gate, up, down)):
        here = []
        for side in range(2):
            for shift in range(deep):
                for rel in range(2):
                    copy = pltpu.make_async_copy(
                        chunks.at[side, shift, rel, :, pl.ds(matrix * half, half)],
                        target.at[
                            pl.ds(row_offset(place_ref, shift, rel, deep, part), part),
                            pl.ds(side * half, half),
                        ],
                        in_sems.at[matrix, side, shift, rel],
                    )
                    copy.start()
                    here.append(copy)
        loads.append(here)
    stores = []

    def store(scratch_ref, block, which):
        copy = pltpu.make_async_copy(
            scratch_ref.at[block], outs[block * 5 + which], out_sems.at[block, which]
        )
        copy.start()
        stores.append(copy)

    for block in range(blocks):
        for here in [row_loads[block]] + (loads if block == 0 else []):
            for copy in here:
                copy.wait()
        width = gate.shape[1]

        @pl.loop(0, width // TILE)
        def _(step, block=block):
            lanes = pl.ds(pl.multiple_of(step * TILE, TILE), TILE)
            rows, grads = rows_refs[block][...], grad_refs[block][...]
            gate_value = nn(rows, gate[:, lanes])
            up_value = nn(rows, up[:, lanes])
            grad_hidden = nn(grads, down[:, lanes])
            sigmoid = 1.0 / (1.0 + jnp.exp(-gate_value))
            swish = gate_value * sigmoid
            slope = sigmoid + swish * (1.0 - sigmoid)
            hidden[block, :, lanes] = (swish * up_value).astype(jnp.bfloat16)
            grad_gate[block, :, lanes] = (grad_hidden * up_value * slope).astype(jnp.bfloat16)
            grad_up[block, :, lanes] = (grad_hidden * swish).astype(jnp.bfloat16)

        store(hidden, block, 0)
        store(grad_gate, block, 1)
        store(grad_up, block, 2)

        @pl.loop(0, gate.shape[0] // TILE)
        def _(step, block=block):
            lanes = pl.ds(pl.multiple_of(step * TILE, TILE), TILE)
            grad_rows[block, :, lanes] = (
                times_transposed(grad_gate[block], gate[lanes, :])
                + times_transposed(grad_up[block], up[lanes, :])
            ).astype(jnp.bfloat16)
            branch[block, :, lanes] = times_transposed(hidden[block], down[lanes, :]).astype(
                jnp.bfloat16
            )

        store(branch, block, 3)
        store(grad_rows, block, 4)
    for copy in stores:
        copy.wait()


def feed(place, rows, grads, chunks, chosen):
    deep, part = chunks.shape[1], chunks.shape[3]
    width, hidden_units = deep * 2 * part, 2 * (chunks.shape[4] // 3)
    blocks = len(chosen)
    count = rows.shape[1]
    small = jax.ShapeDtypeStruct((count, hidden_units), jnp.bfloat16)
    large = jax.ShapeDtypeStruct((count, width), jnp.bfloat16)
    outs = pl.pallas_call(
        functools.partial(feed_kernel, deep, blocks, chosen),
        out_shape=(small, small, small, large, large) * blocks,
        in_specs=[smem_spec()] + [any_spec()] * 3,
        out_specs=(any_spec(),) * (5 * blocks),
        scratch_shapes=[pltpu.VMEM((width, hidden_units), jnp.bfloat16)] * 3
        + [pltpu.VMEM((blocks, count, hidden_units), jnp.bfloat16)] * 3
        + [pltpu.VMEM((blocks, count, width), jnp.bfloat16)] * 2
        + [pltpu.SemaphoreType.DMA((3, 2, deep, 2)), pltpu.SemaphoreType.DMA((blocks, 5))]
        + [pltpu.VMEM((blocks, count, width), jnp.bfloat16)] * 2
        + [pltpu.SemaphoreType.DMA((blocks, 2))],
        compiler_params=vmem_params(),
        cost_estimate=cost(
            flops=blocks * 12 * count * width * hidden_units,
            bytes_accessed=2 * (3 * width * hidden_units + blocks * count * (4 * width + 3 * hidden_units)),
            transcendentals=blocks * count * hidden_units,
        ),
        name="feed",
    )(place, rows, grads, chunks)
    return [outs[5 * block : 5 * block + 5] for block in range(blocks)]


def weight_kernel(blocks, pairs, spread, added, *refs):
    lefts, rights = refs[: blocks * pairs], refs[blocks * pairs : 2 * blocks * pairs]
    rest = refs[2 * blocks * pairs :]
    out_ref = rest[-1]
    offset = 0
    parts = []
    for pair in range(pairs):
        total = None
        for block in range(blocks):
            term = transposed_times(lefts[pair * blocks + block][...], rights[pair * blocks + block][...])
            total = term if total is None else total + term
        parts.append(total)
    if spread:
        joined = jnp.concatenate([part.astype(jnp.bfloat16) for part in parts], axis=1)
        total = times_transposed(joined, rest[0][...])
        if added:
            total = total + rest[1][...].astype(jnp.float32)
        out_ref[...] = total.astype(jnp.bfloat16)
    else:
        for pair, total in enumerate(parts):
            lanes = slice(offset, offset + total.shape[1])
            if added:
                total = total + rest[0][:, lanes].astype(jnp.float32)
            out_ref[:, lanes] = total.astype(jnp.bfloat16)
            offset += total.shape[1]


def weight_grad(pairs, side, spread=None, added=None, tile=256):
    blocks = len(pairs[0][0])
    lefts = [left for left_blocks, _ in pairs for left in left_blocks]
    rights = [right for _, right_blocks in pairs for right in right_blocks]
    count, width = lefts[0].shape
    widths = [right_blocks[0].shape[1] // 2 for _, right_blocks in pairs]
    columns = sum(widths) if spread is None else spread.shape[0]
    operands = lefts + rights
    in_specs = [pl.BlockSpec((count, tile), lambda i: (0, i)) for _ in lefts]
    in_specs += [pl.BlockSpec((count, right.shape[1] // 2), lambda i: (0, side)) for right in rights]
    if spread is not None:
        operands.append(spread)
        in_specs.append(pl.BlockSpec(spread.shape, lambda i: (0, 0)))
    if added is not None:
        operands.append(added)
        in_specs.append(pl.BlockSpec((tile, columns), lambda i: (i, 0)))
    return pl.pallas_call(
        functools.partial(weight_kernel, blocks, len(pairs), spread is not None, added is not None),
        grid=(width // tile,),
        out_shape=jax.ShapeDtypeStruct((width, columns), jnp.bfloat16),
        in_specs=in_specs,
        out_specs=pl.BlockSpec((tile, columns), lambda i: (i, 0)),
        compiler_params=vmem_params(),
        cost_estimate=cost(
            flops=2 * blocks * count * width * sum(widths),
            bytes_accessed=2 * (blocks * count * (width * len(pairs) + sum(widths)) + width * columns),
            transcendentals=0,
        ),
        name="weight_grad",
    )(*operands)


def hbm_spec():
    return pl.BlockSpec(memory_space=pltpu.HBM)


def send(source, target, sems, where):
    copy = pltpu.make_async_remote_copy(
        src_ref=source,
        dst_ref=target,
        send_sem=sems[0],
        recv_sem=sems[1],
        device_id=where,
        device_id_type=pl.DeviceIdType.MESH,
    )
    copy.start()
    return copy


def greet(partners):
    barrier = pltpu.get_barrier_semaphore()
    for partner in partners:
        pl.semaphore_signal(barrier, inc=1, device_id=partner, device_id_type=pl.DeviceIdType.MESH)
    pl.semaphore_wait(barrier, len(partners))


def beside():
    core, across, along = (lax.axis_index(name).astype(jnp.int32) for name in ("c", "x", "y"))
    return {"c": 1 - core}, {"x": 1 - across}, {"y": 1 - along}


def grid_offset(slot, rel, deep, part):
    z_place = lax.rem(lax.axis_index("z").astype(jnp.int32) + slot, jnp.int32(deep))
    core = lax.rem(lax.axis_index("c").astype(jnp.int32) + rel, jnp.int32(2))
    return pl.multiple_of((z_place * 2 + core) * part, 64)


def spread_weight(buffer, spread_ref, wide, deep):
    part = buffer.shape[3]
    half = wide.shape[1] // 2

    @pl.loop(0, 4 * deep)
    def _(step):
        rel, slot = lax.rem(step, jnp.int32(2)), lax.rem(step // 2, jnp.int32(deep))
        side = step // (2 * deep)
        rows = pl.ds(grid_offset(slot, rel, deep, part), part)
        lanes = pl.ds(pl.multiple_of(side * half, half), half)
        wide[rows, lanes] = nn(buffer[side, slot, rel], spread_ref[...]).astype(jnp.bfloat16)


def attend_pair(qkv, heads, logs, keys, values, sequence, pair):
    count = qkv.shape[1]
    x_place = lax.axis_index("x").astype(jnp.int32)
    lane0 = pl.multiple_of(pair * 4 * LANES, 4 * LANES)
    mask = diagonal_mask()
    scale = HD ** (-0.5) * LOG2E
    for rel in range(2):
        position = lax.rem(x_place + rel, jnp.int32(2))
        rows = pl.ds(pl.multiple_of(position * count, count), count)
        keys[rows, :] = qkv[2 * sequence + rel, :, pl.ds(lane0 + 2 * LANES, LANES)]
        values[rows, :] = qkv[2 * sequence + rel, :, pl.ds(lane0 + 3 * LANES, LANES)]

    def visit(rel, start, before):
        block = 2 * sequence + rel
        rows = slice(start, start + TILE)
        queries = jnp.concatenate(
            [qkv[block, rows, pl.ds(lane0, LANES)], qkv[block, rows, pl.ds(lane0 + LANES, LANES)]], axis=0
        )
        edge = slice(before, before + TILE)
        near = jnp.where(mask, times_transposed(queries, keys[edge, :]), MASKED)
        top = jnp.max(near, axis=-1, keepdims=True)
        if before:
            far = times_transposed(queries, keys[:before, :])
            top = jnp.maximum(top, jnp.max(far, axis=-1, keepdims=True))
        top = top * scale
        near = jnp.exp2(near * scale - top)
        total = jnp.sum(near, axis=-1, keepdims=True)
        mixed = nn(near.astype(jnp.bfloat16), values[edge, :])
        if before:
            far = jnp.exp2(far * scale - top)
            total = total + jnp.sum(far, axis=-1, keepdims=True)
            mixed = mixed + nn(far.astype(jnp.bfloat16), values[:before, :])
        mixed = (mixed / total).astype(jnp.bfloat16)
        log = top + jnp.log2(total)
        lane = lax.broadcasted_iota(jnp.int32, (TILE, LANES), 1)
        kept = logs[block, rows, :]
        for head in range(2):
            part = slice(head * TILE, (head + 1) * TILE)
            out_lane = pl.multiple_of(pair * 2 * LANES, LANES) + head * LANES
            heads[block, rows, pl.ds(out_lane, LANES)] = mixed[part]
            kept = jnp.where(lane == 2 * pair + head, log[part], kept)
        logs[block, rows, :] = kept

    for rel in range(2):
        position = lax.rem(x_place + rel, jnp.int32(2))
        for static_position in range(2):

            @pl.when(position == static_position)
            def _(rel=rel, static_position=static_position):
                for step in range(count // TILE):
                    visit(rel, step * TILE, static_position * count + step * TILE)


def forward_kernel(
    deep, first_ref, cotangent_ref, tokens_ref, gain_ref, qkv_halves, out_halves, feed_halves,
    qkv_spread, out_spread, cosine_ref, sine_ref,
    first_out, qkv_out, heads_out, logs_out, qkv_wide_out, out_wide_out, middle_out, second_out,
    cotangent_out, feed_out,
    first_all, qkv_buffer, out_buffer, qkv_wide, out_wide, qkv, heads, logs, keys, values,
    parts, core_parts, outgoing, incoming, middle, second,
    local_sems, row_sems, qkv_sems, out_sems, feed_sems, core_sems,
):
    core, z_place = lax.axis_index("c").astype(jnp.int32), lax.axis_index("z").astype(jnp.int32)
    core_beside, x_beside, y_beside = beside()
    count = first_ref.shape[0]
    ring = jnp.int32(deep)
    z_beside = [{"z": lax.rem(z_place + deep - shift, ring)} for shift in range(deep)]
    greet([core_beside, x_beside, y_beside] + z_beside[1:])

    kept = []
    sent = []

    def keep_local(source, target, index):
        copy = pltpu.make_async_copy(source, target, local_sems.at[index])
        copy.start()
        return copy

    def pair_of(sems, index):
        return sems.at[0, index], sems.at[1, index]

    def move(source, target, sems, index, where):
        copy = send(source, target, pair_of(sems, index), where)
        sent.append(copy)
        return copy

    qkv_core = move(qkv_halves.at[1 - core], qkv_buffer.at[0, 0, 1], qkv_sems, 0, core_beside)
    qkv_kept = keep_local(qkv_halves.at[core], qkv_buffer.at[0, 0, 0], 0)
    first_x = move(first_ref, first_all.at[1], row_sems, 0, x_beside)
    out_core = move(out_halves.at[1 - core], out_buffer.at[0, 0, 1], out_sems, 0, core_beside)
    out_kept = keep_local(out_halves.at[core], out_buffer.at[0, 0, 0], 1)
    feed_core = move(feed_halves.at[1 - core], feed_out.at[0, 0, 1], feed_sems, 0, core_beside)
    feed_kept = keep_local(feed_halves.at[core], feed_out.at[0, 0, 0], 2)
    first_core = move(first_ref, first_all.at[2], row_sems, 1, core_beside)
    first_kept = keep_local(first_ref, first_all.at[0], 3)
    cotangent_kept = keep_local(cotangent_ref, cotangent_out.at[0], 4)

    def open_z(buffer, sems, shifts):
        return [move(buffer.at[0, 0], buffer.at[0, shift], sems, shift, z_beside[shift]) for shift in shifts]

    def open_y(buffer, sems, shift):
        return move(buffer.at[0, shift], buffer.at[1, shift], sems, deep + shift, y_beside)

    far = [shift for shift in range(1, deep) if shift in (1, deep - 1)]
    rest = [shift for shift in range(1, deep) if shift not in far]

    qkv_core.wait_recv()
    qkv_kept.wait()
    qkv_z = open_z(qkv_buffer, qkv_sems, far + rest)
    qkv_y = [open_y(qkv_buffer, qkv_sems, 0)]
    out_core.wait_recv()
    out_kept.wait()
    feed_core.wait_recv()
    feed_kept.wait()
    for shift, copy in zip(far + rest, qkv_z):
        copy.wait_recv()
        qkv_y.append(open_y(qkv_buffer, qkv_sems, shift))
    out_z = open_z(out_buffer, out_sems, far + rest)
    out_y = [open_y(out_buffer, out_sems, 0)]
    first_x.wait_recv()
    first_far = move(first_all.at[1], first_all.at[3], row_sems, 2, core_beside)
    cotangent_x = move(cotangent_ref, cotangent_out.at[1], row_sems, 3, x_beside)
    cotangent_core = move(cotangent_ref, cotangent_out.at[2], row_sems, 4, core_beside)
    feed_z = open_z(feed_out, feed_sems, far)
    for copy in qkv_y:
        copy.wait_recv()
    for shift, copy in zip(far + rest, out_z):
        copy.wait_recv()
        out_y.append(open_y(out_buffer, out_sems, shift))
    feed_y = [open_y(feed_out, feed_sems, 0)]

    spread_weight(qkv_buffer, qkv_spread, qkv_wide, deep)
    kept.append(keep_local(qkv_wide, qkv_wide_out, 5))
    first_core.wait_recv()
    first_far.wait_recv()
    first_kept.wait()
    kept.append(keep_local(first_all, first_out, 6))

    @pl.loop(0, 8)
    def _(step):
        block, pair = step // 2, lax.rem(step, jnp.int32(2))
        lane0 = pl.multiple_of(pair * 4 * LANES, 4 * LANES)
        product = nn(first_all[block], qkv_wide[:, pl.ds(lane0, 4 * LANES)])
        rel = lax.rem(block, jnp.int32(2))
        cosine, sine = cosine_ref[rel], sine_ref[rel]
        for head in range(4):
            part = product[:, head * LANES : (head + 1) * LANES]
            if head < 3:
                part = turn(part, cosine, sine)
            qkv[block, :, pl.ds(lane0 + head * LANES, LANES)] = part.astype(jnp.bfloat16)

    kept.append(keep_local(qkv, qkv_out, 7))
    logs[...] = jnp.zeros_like(logs)

    @pl.loop(0, 4)
    def _(step):
        attend_pair(qkv, heads, logs, keys, values, step // 2, lax.rem(step, jnp.int32(2)))

    kept.append(keep_local(heads, heads_out, 8))
    kept.append(keep_local(logs, logs_out, 9))
    for copy in out_y:
        copy.wait_recv()
    spread_weight(out_buffer, out_spread, out_wide, deep)
    kept.append(keep_local(out_wide, out_wide_out, 10))

    def out_part(block):
        @pl.loop(0, out_wide.shape[0] // 512)
        def _(step):
            lanes = pl.ds(pl.multiple_of(step * 512, 512), 512)
            parts[block, :, lanes] = times_transposed(heads[block], out_wide[lanes, :]).astype(jnp.bfloat16)

    out_part(3)
    core_far = move(parts.at[3], core_parts.at[1], core_sems, 0, core_beside)
    out_part(1)
    core_far.wait_recv()
    step_rows = 128

    @pl.loop(0, count // step_rows)
    def _(step):
        rows = pl.ds(pl.multiple_of(step * step_rows, step_rows), step_rows)
        outgoing[rows, :] = (
            parts[1, rows, :].astype(jnp.float32) + core_parts[1, rows, :].astype(jnp.float32)
        ).astype(jnp.bfloat16)

    branch_x = move(outgoing, incoming, core_sems, 1, x_beside)
    out_part(2)
    core_near = move(parts.at[2], core_parts.at[0], core_sems, 2, core_beside)
    out_part(0)
    for shift, copy in zip(far, feed_z):
        copy.wait_recv()
        feed_y.append(open_y(feed_out, feed_sems, shift))
    feed_z = open_z(feed_out, feed_sems, rest)
    core_near.wait_recv()
    branch_x.wait_recv()

    @pl.loop(0, count // step_rows)
    def _(step):
        rows = pl.ds(pl.multiple_of(step * step_rows, step_rows), step_rows)
        total = (
            tokens_ref[rows, :].astype(jnp.float32)
            + parts[0, rows, :].astype(jnp.float32)
            + core_parts[0, rows, :].astype(jnp.float32)
            + incoming[rows, :].astype(jnp.float32)
        )
        middle[rows, :] = total
        second[rows, :] = (total * norm_factor(total) * gain_ref[...]).astype(jnp.bfloat16)

    kept.append(keep_local(middle, middle_out, 11))
    kept.append(keep_local(second, second_out.at[0], 12))
    second_x = move(second, second_out.at[1], row_sems, 5, x_beside)
    second_core = move(second, second_out.at[2], row_sems, 6, core_beside)
    cotangent_x.wait_recv()
    cotangent_far = move(cotangent_out.at[1], cotangent_out.at[3], row_sems, 7, core_beside)
    for shift, copy in zip(rest, feed_z):
        copy.wait_recv()
        feed_y.append(open_y(feed_out, feed_sems, shift))
    second_x.wait_recv()
    second_far = move(second_out.at[1], second_out.at[3], row_sems, 8, core_beside)
    for copy in [second_core, second_far, cotangent_core, cotangent_far] + feed_y:
        copy.wait_recv()
    for copy in kept + [cotangent_kept]:
        copy.wait()
    for copy in sent:
        copy.wait_send()


def forward(deep, first, cotangent, tokens, gain, qkv_halves, out_halves, feed_halves, spreads, cosine, sine):
    count, width = first.shape
    part = feed_halves.shape[1]

    def shape(*dims, kind=jnp.bfloat16):
        return jax.ShapeDtypeStruct(dims, kind)

    def room(*dims, kind=jnp.bfloat16):
        return pltpu.VMEM(dims, kind)

    qkv_lanes, out_lanes = 2 * spreads[0].shape[1], 2 * spreads[1].shape[1]
    outs = (
        shape(4, count, width),
        shape(4, count, qkv_lanes),
        shape(4, count, out_lanes),
        shape(4, count, LANES, kind=jnp.float32),
        shape(width, qkv_lanes),
        shape(width, out_lanes),
        shape(count, width, kind=jnp.float32),
        shape(4, count, width),
        shape(4, count, width),
        shape(2, deep, 2, part, feed_halves.shape[2]),
    )
    scratch = [
        room(4, count, width),
        room(2, deep, 2, part, qkv_halves.shape[2]),
        room(2, deep, 2, part, out_halves.shape[2]),
        room(width, qkv_lanes),
        room(width, out_lanes),
        room(4, count, qkv_lanes),
        room(4, count, out_lanes),
        room(4, count, LANES, kind=jnp.float32),
        room(2 * count, LANES),
        room(2 * count, LANES),
        room(4, count, width),
        room(2, count, width),
        room(count, width),
        room(count, width),
        room(count, width, kind=jnp.float32),
        room(count, width),
        pltpu.SemaphoreType.DMA((13,)),
        pltpu.SemaphoreType.DMA((2, 9)),
        pltpu.SemaphoreType.DMA((2, 2 * deep)),
        pltpu.SemaphoreType.DMA((2, 2 * deep)),
        pltpu.SemaphoreType.DMA((2, 2 * deep)),
        pltpu.SemaphoreType.DMA((2, 3)),
    ]
    return pl.pallas_call(
        functools.partial(forward_kernel, deep),
        out_shape=outs,
        in_specs=[vmem_spec(), hbm_spec()] + [vmem_spec()] * 2 + [hbm_spec()] * 3 + [vmem_spec()] * 4,
        out_specs=(hbm_spec(),) * len(outs),
        scratch_shapes=scratch,
        compiler_params=vmem_params(collective_id=1, has_side_effects=True),
        cost_estimate=cost(flops=20 * 10**9, bytes_accessed=10**8, transcendentals=10**7),
        name="forward",
    )(first, cotangent, tokens, gain, qkv_halves, out_halves, feed_halves, *spreads, cosine, sine)


def tables(rows, x_place):
    lane = np.arange(LANES)
    entry = lane % (LANES // 2)
    live = (entry < HD // 2).astype(np.float32)
    sign = np.where(lane < LANES // 2, -1.0, 1.0).astype(np.float32) * live
    pair_entry = np.where(entry < HD // 2, entry, 0).astype(np.float32)
    inverse = THETA ** (-2.0 * jnp.asarray(pair_entry) / HD)
    both = []
    for rel in range(2):
        first = lax.rem(x_place + rel, jnp.int32(2)) * rows
        position = (first + jnp.arange(rows, dtype=jnp.int32)).astype(jnp.float32)
        both.append(position[:, None] * inverse[None, :])
    angles = jnp.stack(both)
    return jnp.cos(angles) * live, jnp.sin(angles) * sign


def norm_factor(rows):
    return lax.rsqrt(jnp.mean(rows * rows, axis=-1, keepdims=True) + EPSILON)


def norm_back(rows, gain, grad):
    factor = norm_factor(rows)
    scaled = grad * gain
    return factor * scaled - rows * factor**3 * jnp.mean(scaled * rows, axis=-1, keepdims=True)


def spread_blocks(own):
    beside = swap(own, "x")
    return [own, beside, swap(own, "c"), swap(beside, "c")]


def sum_blocks(parts):
    beside = parts[1].astype(jnp.float32) + swap(parts[3], "c").astype(jnp.float32)
    arrived = swap(beside.astype(jnp.bfloat16), "x")
    own = parts[0].astype(jnp.float32) + swap(parts[2], "c").astype(jnp.float32)
    return own + arrived.astype(jnp.float32)


def finish_grad(summed, core, part):
    mine = lax.psum_scatter(summed, "z", scatter_dimension=0, tiled=True)
    keep = lax.dynamic_slice_in_dim(mine, core * part, part, axis=0)
    send = lax.dynamic_slice_in_dim(mine, (1 - core) * part, part, axis=0)
    recv = swap(send, "c")
    first = jnp.where(core == 0, keep, recv).astype(jnp.float32)
    second = jnp.where(core == 0, recv, keep).astype(jnp.float32)
    return first, second


def join(first, second, start, stop):
    return jnp.concatenate([first[:, start:stop], second[:, start:stop]], axis=1)


def gain_grad(columns, gain, depth_place, part):
    rows = sum(jnp.sum(grad * weight.astype(jnp.float32), axis=1) for grad, weight in columns)
    rows = rows / lax.dynamic_slice_in_dim(gain, depth_place * part, part)
    rows = rows + swap(rows, "x")
    rows = rows + swap(rows, "y")
    piece = part // 4
    place = lax.axis_index("y") * 2 + lax.axis_index("x")
    return lax.dynamic_slice_in_dim(rows, place * piece, piece)


def fast_local(
    tokens,
    cotangent,
    first_gain,
    query_weight,
    key_weight,
    value_weight,
    out_weight,
    second_gain,
    gate_weight,
    up_weight,
    down_weight,
):
    deep = lax.axis_size("z")
    z_place, core, x_place = (lax.axis_index(name).astype(jnp.int32) for name in ("z", "c", "x"))
    place = jnp.stack([z_place, core, x_place])
    rows = tokens.shape[0]
    part = gate_weight.shape[0]
    depth_place = z_place * 2 + core
    own_rows = tokens.astype(jnp.float32)
    first_normed = (own_rows * norm_factor(own_rows) * first_gain).astype(jnp.bfloat16)
    out_turned, down_turned = out_weight.T, down_weight.T

    def halves(*weights):
        result = []
        for half in range(2):
            pieces = []
            for weight in weights:
                size = weight.shape[1] // 2
                pieces.append(weight[:, half * size : (half + 1) * size])
            result.append(jnp.concatenate(pieces, axis=1))
        return result

    spread = spread_heads(3, 3)
    spreads = (spread_heads(3, 1), spread_heads(0, 2))
    cosine, sine = tables(rows, x_place)
    (
        first_all, qkv_all, heads_all, logs_all, qkv_weight, out_wide, middle, second_all, cotangent_all, chunks,
    ) = forward(
        deep,
        first_normed,
        cotangent,
        tokens,
        second_gain[None],
        jnp.stack(halves(query_weight, key_weight, value_weight)),
        jnp.stack(halves(out_turned)),
        jnp.stack(halves(gate_weight, up_weight, down_turned)),
        spreads,
        cosine,
        sine,
    )
    first_blocks, cotangent_blocks, second_blocks, qkv, heads, logs = (
        [stack[i] for i in range(4)]
        for stack in (first_all, cotangent_all, second_all, qkv_all, heads_all, logs_all)
    )
    fed = [None] * 4
    for pair in ((1, 3), (0, 2)):
        outs = feed(place, second_all, cotangent_all, chunks, pair)
        for i, out in zip(pair, outs):
            fed[i] = out
    hidden, grad_gate, grad_up, branches, grads_second = ([block[i] for block in fed] for i in range(5))
    grad_second = sum_blocks(grads_second)
    grad_middle = cotangent.astype(jnp.float32) + norm_back(middle, second_gain, grad_second)
    grad_attention = spread_blocks(grad_middle.astype(jnp.bfloat16))
    result = (middle + sum_blocks(branches)).astype(jnp.bfloat16)

    down_sent = swap(weight_grad([(cotangent_blocks, hidden)], 1), "y")
    wide_sent = swap(weight_grad([(second_blocks, grad_gate), (second_blocks, grad_up)], 1), "y")
    down_grads = finish_grad(weight_grad([(cotangent_blocks, hidden)], 0, added=down_sent), core, part)
    wide_grads = finish_grad(
        weight_grad([(second_blocks, grad_gate), (second_blocks, grad_up)], 0, added=wide_sent), core, part
    )

    grad_heads = [nn(block, out_wide).astype(jnp.bfloat16) for block in grad_attention]
    grad_qkv = []
    for sequence in range(2):
        chosen = slice(2 * sequence, 2 * sequence + 2)
        grad_qkv += attend_back(
            place, qkv[chosen], grad_heads[chosen], heads[chosen], logs[chosen], cosine, sine
        )
    grad_first = sum_blocks([times_transposed(block, qkv_weight).astype(jnp.bfloat16) for block in grad_qkv])
    tokens_grad = grad_middle + norm_back(own_rows, first_gain, grad_first)
    head_pairs = [(first_blocks, grad_qkv), (grad_attention, heads)]
    heads_sent = swap(weight_grad(head_pairs, 1, spread=spread), "y")
    heads_grads = finish_grad(
        weight_grad(head_pairs, 0, spread=spread, added=heads_sent), core, part
    )

    sizes = [weight.shape[1] // 2 for weight in (query_weight, key_weight, value_weight, out_turned)]
    starts = np.cumsum([0] + sizes)
    query_grad, key_grad, value_grad, out_grad = (
        join(*heads_grads, int(starts[i]), int(starts[i + 1])) for i in range(4)
    )
    half = gate_weight.shape[1] // 2
    gate_grad, up_grad = (join(*wide_grads, i * half, (i + 1) * half) for i in range(2))
    down_grad = join(*down_grads, 0, half)
    first_gain_grad = gain_grad(
        ((query_grad, query_weight), (key_grad, key_weight), (value_grad, value_weight)),
        first_gain,
        depth_place,
        part,
    )
    second_gain_grad = gain_grad(
        ((gate_grad, gate_weight), (up_grad, up_weight)), second_gain, depth_place, part
    )
    return (
        result,
        tokens_grad,
        query_grad,
        key_grad,
        value_grad,
        out_grad.T,
        gate_grad,
        up_grad,
        down_grad.T,
        first_gain_grad,
        second_gain_grad,
    )


def specs(depth, width):
    both = depth + width
    rows, inward, outward = P(both, None), P(depth, width), P(width, depth)
    in_specs = (rows, rows, P(), inward, inward, inward, outward, P(), inward, inward, outward)
    out_specs = (rows, rows, inward, inward, inward, outward, inward, inward, outward, P(both), P(both))
    return in_specs, out_specs


def solution(mesh):
    depth, width = mesh.shape["dp"], mesh.shape["tensor"]

    def run(tokens, cotangent, *weights):
        fits = (
            width == 4
            and depth % 2 == 0
            and tokens.shape[0] * 2 == SEQ_LEN * depth * width
            and weights[2].shape[1] == 2 * width * HD
            and weights[1].shape[1] == 4 * width * HD
        )
        if fits:
            devices = mesh.devices.reshape(depth // 2, 2, 2, 2)
            fine = jax.sharding.Mesh(devices, ("z", "c", "y", "x"))
            in_specs, out_specs = specs(("z", "c"), ("y", "x"))
            call, over = fast_local, fine
        else:
            in_specs, out_specs = specs(("dp",), ("tensor",))
            call, over = local, mesh
        return jax.shard_map(call, mesh=over, in_specs=in_specs, out_specs=out_specs, check_vma=False)(
            tokens, cotangent, *weights
        )

    return run
```

```python
import functools

import jax
import jax.numpy as jnp
import numpy as np
from jax import lax
from jax.experimental import pallas as pl
from jax.experimental.pallas import tpu as pltpu
from jax.sharding import PartitionSpec as P

HD = 96
SEQ_LEN = 1024


EPSILON = 1e-05
THETA = 100000.0
MASKED = -1e30
LOG2E = 1.4426950408889634
LANES = 128
SHARE = 20
VMEM_BYTES = 60 * 2**20


def normed(inputs, gain):
    factor = lax.rsqrt(jnp.mean(inputs * inputs, axis=-1, keepdims=True) + EPSILON)
    return inputs * factor * gain


def rotate(vectors, direction):
    seq_rows, head_count, head_size = vectors.shape
    half_size = head_size // 2
    position = (jnp.arange(seq_rows, dtype=jnp.int32) % SEQ_LEN).astype(jnp.float32)
    inverse = THETA ** (-2.0 * jnp.arange(half_size, dtype=jnp.float32) / head_size)
    angles = position[:, None] * inverse[None, :]
    cosine = jnp.cos(angles)[:, None, :]
    sine_part = direction * jnp.sin(angles)[:, None, :]
    leading = vectors[..., :half_size]
    trailing = vectors[..., half_size:]
    return jnp.concatenate(
        [leading * cosine - trailing * sine_part, trailing * cosine + leading * sine_part], axis=-1
    )


def times_transposed(left, right):
    return lax.dot_general(
        left, right, (((1,), (1,)), ((), ())), preferred_element_type=jnp.float32
    )


def transposed_times(left, right):
    return lax.dot_general(
        left, right, (((0,), (0,)), ((), ())), preferred_element_type=jnp.float32
    )


def scaled_scores(queries, keys_rot):
    raw_scores = jnp.einsum(
        "qhgd,khd->hgqk", queries, keys_rot, preferred_element_type=jnp.float32
    ) * queries.shape[-1] ** (-0.5)
    length_rows = queries.shape[0]
    causal = jnp.arange(length_rows)[:, None] >= jnp.arange(length_rows)[None, :]
    return jnp.where(causal, raw_scores, MASKED)


def attend_forward(operands):
    queries, keys_rot, values = operands
    scores = scaled_scores(queries, keys_rot)
    row_max = jnp.max(scores, axis=-1, keepdims=True)
    weights = jnp.exp(scores - row_max)
    row_total = jnp.sum(weights, axis=-1, keepdims=True)
    softmax = (weights / row_total).astype(jnp.bfloat16)
    mixed_heads = jnp.einsum("hgqk,khd->qhgd", softmax, values, preferred_element_type=jnp.float32)
    return (mixed_heads.astype(jnp.bfloat16), (row_max + jnp.log(row_total))[..., 0])


def attend_backward(operands):
    queries, keys_rot, values, grad_mixed, log_total = operands
    scores = scaled_scores(queries, keys_rot)
    softmax = jnp.exp(scores - log_total[..., None])
    grad_softmax = jnp.einsum(
        "qhgd,khd->hgqk", grad_mixed, values, preferred_element_type=jnp.float32
    )
    grad_values = jnp.einsum(
        "hgqk,qhgd->khd",
        softmax.astype(jnp.bfloat16),
        grad_mixed,
        preferred_element_type=jnp.float32,
    )
    row_inner = jnp.sum(softmax * grad_softmax, axis=-1, keepdims=True)
    grad_scores = (softmax * (grad_softmax - row_inner)).astype(jnp.bfloat16)
    scale_factor = queries.shape[-1] ** (-0.5)
    grad_queries = (
        jnp.einsum("hgqk,khd->qhgd", grad_scores, keys_rot, preferred_element_type=jnp.float32)
        * scale_factor
    )
    grad_keys = (
        jnp.einsum("hgqk,qhgd->khd", grad_scores, queries, preferred_element_type=jnp.float32)
        * scale_factor
    )
    return (grad_queries, grad_keys, grad_values)


def gather_rows(shard):
    return lax.all_gather(shard, "tensor", axis=0, tiled=True)


def gather_grads(shard):
    return lax.all_gather(shard, "tensor", axis=0, tiled=True)


def sum_outputs(term, row_count):
    return lax.psum_scatter(
        term(jnp.int32(0), row_count * lax.axis_size("tensor")),
        "tensor",
        scatter_dimension=0,
        tiled=True,
    )


def sum_inputs(term, row_count):
    return lax.psum_scatter(
        term(jnp.int32(0), row_count * lax.axis_size("tensor")),
        "tensor",
        scatter_dimension=0,
        tiled=True,
    )


def local(
    tokens,
    cotangent,
    first_gain,
    query_weight,
    key_weight,
    value_weight,
    out_weight,
    second_gain,
    gate_weight,
    up_weight,
    down_weight,
):
    query_weight, key_weight, value_weight, out_weight, gate_weight, up_weight, down_weight = (
        lax.all_gather(query_weight, "dp", axis=0, tiled=True),
        lax.all_gather(key_weight, "dp", axis=0, tiled=True),
        lax.all_gather(value_weight, "dp", axis=0, tiled=True),
        lax.all_gather(out_weight, "dp", axis=1, tiled=True),
        lax.all_gather(gate_weight, "dp", axis=0, tiled=True),
        lax.all_gather(up_weight, "dp", axis=0, tiled=True),
        lax.all_gather(down_weight, "dp", axis=1, tiled=True),
    )
    own_rows = tokens.astype(jnp.float32)
    row_count = own_rows.shape[0]
    pair_count = key_weight.shape[1] // HD
    first_normed = normed(own_rows, first_gain).astype(jnp.bfloat16)
    first_rows = gather_rows(first_normed)
    group_rows = first_rows.shape[0]
    sequences = group_rows // SEQ_LEN
    query_pre = jnp.dot(first_rows, query_weight, preferred_element_type=jnp.float32)
    key_pre = jnp.dot(first_rows, key_weight, preferred_element_type=jnp.float32)
    value_pre = jnp.dot(first_rows, value_weight, preferred_element_type=jnp.float32)
    queries = rotate(query_pre.reshape(group_rows, 2 * pair_count, HD), 1.0).astype(jnp.bfloat16)
    queries = queries.reshape(sequences, SEQ_LEN, pair_count, 2, HD)
    keys_rot = rotate(key_pre.reshape(group_rows, pair_count, HD), 1.0).astype(jnp.bfloat16)
    keys_rot = keys_rot.reshape(sequences, SEQ_LEN, pair_count, HD)
    values = value_pre.astype(jnp.bfloat16).reshape(sequences, SEQ_LEN, pair_count, HD)
    mixed_heads, log_total = lax.map(attend_forward, (queries, keys_rot, values))
    heads_out = mixed_heads.reshape(group_rows, 2 * pair_count * HD)
    heads_rows = lax.all_to_all(heads_out, "tensor", split_axis=0, concat_axis=1, tiled=True)
    out_full = lax.all_gather(out_weight, "tensor", axis=0, tiled=True)
    attention_branch = jnp.dot(heads_rows, out_full, preferred_element_type=jnp.float32)
    middle = own_rows + attention_branch
    second_normed = normed(middle, second_gain).astype(jnp.bfloat16)
    second_rows = gather_rows(second_normed)
    gate_full, up_full, down_full = (gate_weight, up_weight, down_weight)
    gate_value = jnp.dot(second_rows, gate_full, preferred_element_type=jnp.float32)
    up_value = jnp.dot(second_rows, up_full, preferred_element_type=jnp.float32)
    sigmoid_gate = jax.nn.sigmoid(gate_value)
    swish_gate = gate_value * sigmoid_gate
    hidden = (swish_gate * up_value).astype(jnp.bfloat16)

    def project_hidden(start, amount):
        return jnp.dot(hidden, down_full, preferred_element_type=jnp.float32)

    ffn_branch = sum_outputs(project_hidden, row_count)
    grad_branch = gather_grads(cotangent)
    result = (middle + ffn_branch).astype(jnp.bfloat16)
    grad_hidden = times_transposed(grad_branch, down_full)
    down_part = transposed_times(hidden, grad_branch)
    slope = sigmoid_gate + gate_value * sigmoid_gate * (1.0 - sigmoid_gate)
    grad_gate = (grad_hidden * up_value * slope).astype(jnp.bfloat16)
    grad_up = (grad_hidden * swish_gate).astype(jnp.bfloat16)
    gate_part = transposed_times(second_rows, grad_gate)
    up_part = transposed_times(second_rows, grad_up)

    def second_back(start, amount):
        return times_transposed(grad_gate, gate_full) + times_transposed(grad_up, up_full)

    grad_second = sum_inputs(second_back, row_count)
    second_unused, second_pull = jax.vjp(normed, middle, second_gain)
    grad_middle_norm, second_gain_part = second_pull(grad_second)
    grad_middle = cotangent.astype(jnp.float32) + grad_middle_norm
    grad_attention = grad_middle.astype(jnp.bfloat16)
    grad_heads_rows = times_transposed(grad_attention, out_full).astype(jnp.bfloat16)
    grad_heads = lax.all_to_all(grad_heads_rows, "tensor", split_axis=1, concat_axis=0, tiled=True)
    out_part = lax.psum_scatter(
        transposed_times(heads_rows, grad_attention).astype(jnp.bfloat16),
        "tensor",
        scatter_dimension=0,
        tiled=True,
    )
    grad_mixed = grad_heads.reshape(sequences, SEQ_LEN, pair_count, 2, HD)
    grad_queries, grad_keys, grad_values = lax.map(
        attend_backward, (queries, keys_rot, values, grad_mixed, log_total)
    )
    grad_query = (
        rotate(grad_queries.reshape(group_rows, 2 * pair_count, HD), -1.0)
        .reshape(group_rows, -1)
        .astype(jnp.bfloat16)
    )
    grad_key = (
        rotate(grad_keys.reshape(group_rows, pair_count, HD), -1.0)
        .reshape(group_rows, -1)
        .astype(jnp.bfloat16)
    )
    grad_value = grad_values.reshape(group_rows, -1).astype(jnp.bfloat16)
    query_part = transposed_times(first_rows, grad_query)
    key_part = transposed_times(first_rows, grad_key)
    value_part = transposed_times(first_rows, grad_value)

    def first_back(start, amount):
        return (
            times_transposed(grad_query, query_weight)
            + times_transposed(grad_key, key_weight)
            + times_transposed(grad_value, value_weight)
        )

    grad_first = sum_inputs(first_back, row_count)
    first_unused, first_pull = jax.vjp(normed, own_rows, first_gain)
    grad_own_norm, first_gain_part = first_pull(grad_first)
    tokens_grad = grad_middle + grad_own_norm
    query_grad, key_grad, value_grad, out_grad, gate_grad, up_grad, down_grad = (
        lax.psum_scatter(
            query_part.astype(jnp.bfloat16), "dp", scatter_dimension=0, tiled=True
        ).astype(jnp.float32),
        lax.psum_scatter(
            key_part.astype(jnp.bfloat16), "dp", scatter_dimension=0, tiled=True
        ).astype(jnp.float32),
        lax.psum_scatter(
            value_part.astype(jnp.bfloat16), "dp", scatter_dimension=0, tiled=True
        ).astype(jnp.float32),
        lax.psum_scatter(out_part, "dp", scatter_dimension=1, tiled=True).astype(jnp.float32),
        lax.psum_scatter(
            gate_part.astype(jnp.bfloat16), "dp", scatter_dimension=0, tiled=True
        ).astype(jnp.float32),
        lax.psum_scatter(
            up_part.astype(jnp.bfloat16), "dp", scatter_dimension=0, tiled=True
        ).astype(jnp.float32),
        lax.psum_scatter(
            down_part.astype(jnp.bfloat16), "dp", scatter_dimension=1, tiled=True
        ).astype(jnp.float32),
    )
    first_gain_grad, second_gain_grad = (
        lax.psum_scatter(first_gain_part, ("dp", "tensor"), scatter_dimension=0, tiled=True),
        lax.psum_scatter(second_gain_part, ("dp", "tensor"), scatter_dimension=0, tiled=True),
    )
    return (
        result,
        tokens_grad,
        query_grad,
        key_grad,
        value_grad,
        out_grad,
        gate_grad,
        up_grad,
        down_grad,
        first_gain_grad,
        second_gain_grad,
    )


def nn(left, right):
    return jnp.dot(left, right, preferred_element_type=jnp.float32)


def cost(flops, bytes_accessed, transcendentals):
    return pl.CostEstimate(
        flops=flops // SHARE, bytes_accessed=bytes_accessed // SHARE, transcendentals=transcendentals // SHARE
    )


def vmem_params(**more):
    return pltpu.CompilerParams(vmem_limit_bytes=VMEM_BYTES, **more)


def vmem_spec():
    return pl.BlockSpec(memory_space=pltpu.VMEM)


def spread_heads(heads_split, heads_plain):
    columns = (heads_split + heads_plain) * HD
    spread = np.zeros((columns, (heads_split + heads_plain) * LANES), np.float32)
    for head in range(heads_split + heads_plain):
        for entry in range(HD):
            lane = entry
            if head < heads_split and entry >= HD // 2:
                lane = entry - HD // 2 + LANES // 2
            spread[head * HD + entry, head * LANES + lane] = 1.0
    return jnp.asarray(spread, jnp.bfloat16)


def turn(vectors, cosine, sine):
    return vectors * cosine + pltpu.roll(vectors, LANES // 2, 1) * sine


TILE = 256


def diagonal_mask():
    row = lax.broadcasted_iota(jnp.int32, (2 * TILE, TILE), 0)
    row = jnp.where(row >= TILE, row - TILE, row)
    return row >= lax.broadcasted_iota(jnp.int32, (2 * TILE, TILE), 1)


def hbm_spec():
    return pl.BlockSpec(memory_space=pltpu.HBM)


def send(source, target, sems, where):
    copy = pltpu.make_async_remote_copy(
        src_ref=source,
        dst_ref=target,
        send_sem=sems[0],
        recv_sem=sems[1],
        device_id=where,
        device_id_type=pl.DeviceIdType.MESH,
    )
    copy.start()
    return copy


def greet(partners):
    barrier = pltpu.get_barrier_semaphore()
    for partner in partners:
        pl.semaphore_signal(barrier, inc=1, device_id=partner, device_id_type=pl.DeviceIdType.MESH)
    pl.semaphore_wait(barrier, len(partners))


def beside():
    core, across, along = (lax.axis_index(name).astype(jnp.int32) for name in ("c", "x", "y"))
    return {"c": 1 - core}, {"x": 1 - across}, {"y": 1 - along}


def grid_offset(slot, rel, deep, part):
    z_place = lax.rem(lax.axis_index("z").astype(jnp.int32) + slot, jnp.int32(deep))
    core = lax.rem(lax.axis_index("c").astype(jnp.int32) + rel, jnp.int32(2))
    return pl.multiple_of((z_place * 2 + core) * part, 64)


def spread_weight(buffer, spread_ref, wide, deep):
    part = buffer.shape[3]
    half = wide.shape[1] // 2

    @pl.loop(0, 4 * deep)
    def _(step):
        rel, slot = lax.rem(step, jnp.int32(2)), lax.rem(step // 2, jnp.int32(deep))
        side = step // (2 * deep)
        rows = pl.ds(grid_offset(slot, rel, deep, part), part)
        lanes = pl.ds(pl.multiple_of(side * half, half), half)
        wide[rows, lanes] = nn(buffer[side, slot, rel], spread_ref[...]).astype(jnp.bfloat16)


def attend_pair(qkv, heads, logs, keys, values, sequence, pair):
    count = qkv.shape[1]
    x_place = lax.axis_index("x").astype(jnp.int32)
    lane0 = pl.multiple_of(pair * 4 * LANES, 4 * LANES)
    mask = diagonal_mask()
    scale = HD ** (-0.5) * LOG2E
    for rel in range(2):
        position = lax.rem(x_place + rel, jnp.int32(2))
        rows = pl.ds(pl.multiple_of(position * count, count), count)
        keys[rows, :] = qkv[2 * sequence + rel, :, pl.ds(lane0 + 2 * LANES, LANES)]
        values[rows, :] = qkv[2 * sequence + rel, :, pl.ds(lane0 + 3 * LANES, LANES)]

    def visit(rel, start, before):
        block = 2 * sequence + rel
        rows = slice(start, start + TILE)
        queries = jnp.concatenate(
            [qkv[block, rows, pl.ds(lane0, LANES)], qkv[block, rows, pl.ds(lane0 + LANES, LANES)]], axis=0
        )
        edge = slice(before, before + TILE)
        near = jnp.where(mask, times_transposed(queries, keys[edge, :]), MASKED)
        top = jnp.max(near, axis=-1, keepdims=True)
        if before:
            far = times_transposed(queries, keys[:before, :])
            top = jnp.maximum(top, jnp.max(far, axis=-1, keepdims=True))
        top = top * scale
        near = jnp.exp2(near * scale - top)
        total = jnp.sum(near, axis=-1, keepdims=True)
        mixed = nn(near.astype(jnp.bfloat16), values[edge, :])
        if before:
            far = jnp.exp2(far * scale - top)
            total = total + jnp.sum(far, axis=-1, keepdims=True)
            mixed = mixed + nn(far.astype(jnp.bfloat16), values[:before, :])
        mixed = (mixed / total).astype(jnp.bfloat16)
        log = top + jnp.log2(total)
        lane = lax.broadcasted_iota(jnp.int32, (TILE, LANES), 1)
        kept = logs[block, rows, :]
        for head in range(2):
            part = slice(head * TILE, (head + 1) * TILE)
            out_lane = pl.multiple_of(pair * 2 * LANES, LANES) + head * LANES
            heads[block, rows, pl.ds(out_lane, LANES)] = mixed[part]
            kept = jnp.where(lane == 2 * pair + head, log[part], kept)
        logs[block, rows, :] = kept

    for rel in range(2):
        position = lax.rem(x_place + rel, jnp.int32(2))
        for static_position in range(2):

            @pl.when(position == static_position)
            def _(rel=rel, static_position=static_position):
                for step in range(count // TILE):
                    visit(rel, step * TILE, static_position * count + step * TILE)


def forward_kernel(
    deep, first_ref, cotangent_ref, tokens_ref, gain_ref, qkv_halves, out_halves, feed_halves,
    qkv_spread, out_spread, cosine_ref, sine_ref,
    first_out, qkv_out, heads_out, logs_out, qkv_wide_out, out_wide_out, middle_out, second_out,
    cotangent_out, feed_out, qkv_own_out,
    first_all, qkv_buffer, out_buffer, qkv_wide, out_wide, qkv, heads, logs, keys, values,
    parts, core_parts, outgoing, incoming, middle, second,
    local_sems, row_sems, qkv_sems, out_sems, feed_sems, core_sems,
):
    core, z_place = lax.axis_index("c").astype(jnp.int32), lax.axis_index("z").astype(jnp.int32)
    core_beside, x_beside, y_beside = beside()
    count = first_ref.shape[0]
    ring = jnp.int32(deep)
    z_beside = [{"z": lax.rem(z_place + deep - shift, ring)} for shift in range(deep)]
    greet([core_beside, x_beside, y_beside] + z_beside[1:])

    kept = []
    sent = []

    def keep_local(source, target, index):
        copy = pltpu.make_async_copy(source, target, local_sems.at[index])
        copy.start()
        return copy

    def pair_of(sems, index):
        return sems.at[0, index], sems.at[1, index]

    def move(source, target, sems, index, where):
        copy = send(source, target, pair_of(sems, index), where)
        sent.append(copy)
        return copy

    qkv_core = move(qkv_halves.at[1 - core], qkv_buffer.at[0, 0, 1], qkv_sems, 0, core_beside)
    qkv_kept = keep_local(qkv_halves.at[core], qkv_buffer.at[0, 0, 0], 0)
    first_x = move(first_ref, first_all.at[1], row_sems, 0, x_beside)
    out_core = move(out_halves.at[1 - core], out_buffer.at[0, 0, 1], out_sems, 0, core_beside)
    out_kept = keep_local(out_halves.at[core], out_buffer.at[0, 0, 0], 1)
    feed_core = move(feed_halves.at[1 - core], feed_out.at[0, 0, 1], feed_sems, 0, core_beside)
    feed_kept = keep_local(feed_halves.at[core], feed_out.at[0, 0, 0], 2)
    first_core = move(first_ref, first_all.at[2], row_sems, 1, core_beside)
    first_kept = keep_local(first_ref, first_all.at[0], 3)
    cotangent_kept = keep_local(cotangent_ref, cotangent_out.at[0], 4)

    def open_z(buffer, sems, shifts):
        return [move(buffer.at[0, 0], buffer.at[0, shift], sems, shift, z_beside[shift]) for shift in shifts]

    def open_y(buffer, sems, shift):
        return move(buffer.at[0, shift], buffer.at[1, shift], sems, deep + shift, y_beside)

    far = [shift for shift in range(1, deep) if shift in (1, deep - 1)]
    rest = [shift for shift in range(1, deep) if shift not in far]

    qkv_core.wait_recv()
    qkv_kept.wait()
    qkv_z = open_z(qkv_buffer, qkv_sems, far + rest)
    qkv_y = [open_y(qkv_buffer, qkv_sems, 0)]
    out_core.wait_recv()
    out_kept.wait()
    feed_core.wait_recv()
    feed_kept.wait()
    kept.append(keep_local(qkv_buffer.at[0, 0], qkv_own_out, 13))
    for shift, copy in zip(far + rest, qkv_z):
        copy.wait_recv()
        qkv_y.append(open_y(qkv_buffer, qkv_sems, shift))
    out_z = open_z(out_buffer, out_sems, far + rest)
    out_y = [open_y(out_buffer, out_sems, 0)]
    first_x.wait_recv()
    first_far = move(first_all.at[1], first_all.at[3], row_sems, 2, core_beside)
    cotangent_x = move(cotangent_ref, cotangent_out.at[1], row_sems, 3, x_beside)
    cotangent_core = move(cotangent_ref, cotangent_out.at[2], row_sems, 4, core_beside)
    feed_z = open_z(feed_out, feed_sems, far)
    for copy in qkv_y:
        copy.wait_recv()
    for shift, copy in zip(far + rest, out_z):
        copy.wait_recv()
        out_y.append(open_y(out_buffer, out_sems, shift))
    feed_y = [open_y(feed_out, feed_sems, 0)]

    spread_weight(qkv_buffer, qkv_spread, qkv_wide, deep)
    kept.append(keep_local(qkv_wide, qkv_wide_out, 5))
    first_core.wait_recv()
    first_far.wait_recv()
    first_kept.wait()
    kept.append(keep_local(first_all, first_out, 6))

    @pl.loop(0, 8)
    def _(step):
        block, pair = step // 2, lax.rem(step, jnp.int32(2))
        lane0 = pl.multiple_of(pair * 4 * LANES, 4 * LANES)
        product = nn(first_all[block], qkv_wide[:, pl.ds(lane0, 4 * LANES)])
        rel = lax.rem(block, jnp.int32(2))
        cosine, sine = cosine_ref[rel], sine_ref[rel]
        for head in range(4):
            part = product[:, head * LANES : (head + 1) * LANES]
            if head < 3:
                part = turn(part, cosine, sine)
            qkv[block, :, pl.ds(lane0 + head * LANES, LANES)] = part.astype(jnp.bfloat16)

    kept.append(keep_local(qkv, qkv_out, 7))
    logs[...] = jnp.zeros_like(logs)

    @pl.loop(0, 4)
    def _(step):
        attend_pair(qkv, heads, logs, keys, values, step // 2, lax.rem(step, jnp.int32(2)))

    kept.append(keep_local(heads, heads_out, 8))
    kept.append(keep_local(logs, logs_out, 9))
    for copy in out_y:
        copy.wait_recv()
    spread_weight(out_buffer, out_spread, out_wide, deep)
    kept.append(keep_local(out_wide, out_wide_out, 10))

    def out_part(block):
        @pl.loop(0, out_wide.shape[0] // 512)
        def _(step):
            lanes = pl.ds(pl.multiple_of(step * 512, 512), 512)
            parts[block, :, lanes] = times_transposed(heads[block], out_wide[lanes, :]).astype(jnp.bfloat16)

    out_part(3)
    core_far = move(parts.at[3], core_parts.at[1], core_sems, 0, core_beside)
    out_part(1)
    core_far.wait_recv()
    step_rows = 128

    @pl.loop(0, count // step_rows)
    def _(step):
        rows = pl.ds(pl.multiple_of(step * step_rows, step_rows), step_rows)
        outgoing[rows, :] = (
            parts[1, rows, :].astype(jnp.float32) + core_parts[1, rows, :].astype(jnp.float32)
        ).astype(jnp.bfloat16)

    branch_x = move(outgoing, incoming, core_sems, 1, x_beside)
    out_part(2)
    core_near = move(parts.at[2], core_parts.at[0], core_sems, 2, core_beside)
    out_part(0)
    for shift, copy in zip(far, feed_z):
        copy.wait_recv()
        feed_y.append(open_y(feed_out, feed_sems, shift))
    feed_z = open_z(feed_out, feed_sems, rest)
    core_near.wait_recv()
    branch_x.wait_recv()

    @pl.loop(0, count // step_rows)
    def _(step):
        rows = pl.ds(pl.multiple_of(step * step_rows, step_rows), step_rows)
        total = (
            tokens_ref[rows, :].astype(jnp.float32)
            + parts[0, rows, :].astype(jnp.float32)
            + core_parts[0, rows, :].astype(jnp.float32)
            + incoming[rows, :].astype(jnp.float32)
        )
        middle[rows, :] = total
        second[rows, :] = (total * norm_factor(total) * gain_ref[...]).astype(jnp.bfloat16)

    kept.append(keep_local(middle, middle_out, 11))
    kept.append(keep_local(second, second_out.at[0], 12))
    second_x = move(second, second_out.at[1], row_sems, 5, x_beside)
    second_core = move(second, second_out.at[2], row_sems, 6, core_beside)
    cotangent_x.wait_recv()
    cotangent_far = move(cotangent_out.at[1], cotangent_out.at[3], row_sems, 7, core_beside)
    for shift, copy in zip(rest, feed_z):
        copy.wait_recv()
        feed_y.append(open_y(feed_out, feed_sems, shift))
    second_x.wait_recv()
    second_far = move(second_out.at[1], second_out.at[3], row_sems, 8, core_beside)
    for copy in [second_core, second_far, cotangent_core, cotangent_far] + feed_y:
        copy.wait_recv()
    for copy in kept + [cotangent_kept]:
        copy.wait()
    for copy in sent:
        copy.wait_send()


def forward(deep, first, cotangent, tokens, gain, qkv_halves, out_halves, feed_halves, spreads, cosine, sine):
    count, width = first.shape
    part = feed_halves.shape[1]

    def shape(*dims, kind=jnp.bfloat16):
        return jax.ShapeDtypeStruct(dims, kind)

    def room(*dims, kind=jnp.bfloat16):
        return pltpu.VMEM(dims, kind)

    qkv_lanes, out_lanes = 2 * spreads[0].shape[1], 2 * spreads[1].shape[1]
    outs = (
        shape(4, count, width),
        shape(4, count, qkv_lanes),
        shape(4, count, out_lanes),
        shape(4, count, LANES, kind=jnp.float32),
        shape(width, qkv_lanes),
        shape(width, out_lanes),
        shape(count, width, kind=jnp.float32),
        shape(4, count, width),
        shape(4, count, width),
        shape(2, deep, 2, part, feed_halves.shape[2]),
        shape(2, part, qkv_halves.shape[2]),
    )
    scratch = [
        room(4, count, width),
        room(2, deep, 2, part, qkv_halves.shape[2]),
        room(2, deep, 2, part, out_halves.shape[2]),
        room(width, qkv_lanes),
        room(width, out_lanes),
        room(4, count, qkv_lanes),
        room(4, count, out_lanes),
        room(4, count, LANES, kind=jnp.float32),
        room(2 * count, LANES),
        room(2 * count, LANES),
        room(4, count, width),
        room(2, count, width),
        room(count, width),
        room(count, width),
        room(count, width, kind=jnp.float32),
        room(count, width),
        pltpu.SemaphoreType.DMA((14,)),
        pltpu.SemaphoreType.DMA((2, 9)),
        pltpu.SemaphoreType.DMA((2, 2 * deep)),
        pltpu.SemaphoreType.DMA((2, 2 * deep)),
        pltpu.SemaphoreType.DMA((2, 2 * deep)),
        pltpu.SemaphoreType.DMA((2, 3)),
    ]
    return pl.pallas_call(
        functools.partial(forward_kernel, deep),
        out_shape=outs,
        in_specs=[vmem_spec(), hbm_spec()] + [vmem_spec()] * 2 + [hbm_spec()] * 3 + [vmem_spec()] * 4,
        out_specs=(hbm_spec(),) * len(outs),
        scratch_shapes=scratch,
        compiler_params=vmem_params(collective_id=1, has_side_effects=True),
        cost_estimate=cost(flops=20 * 10**9, bytes_accessed=10**8, transcendentals=10**7),
        name="forward",
    )(first, cotangent, tokens, gain, qkv_halves, out_halves, feed_halves, *spreads, cosine, sine)


EARLY = 6


def ring_row(shift, deep, rows):
    z_place = lax.rem(lax.axis_index("z").astype(jnp.int32) + shift, jnp.int32(deep))
    return pl.multiple_of(z_place * rows, rows)


def add_rows(target, source, step_rows=128):
    @pl.loop(0, target.shape[0] // step_rows)
    def _(step):
        rows = pl.ds(pl.multiple_of(step * step_rows, step_rows), step_rows)
        target[rows, :] = (target[rows, :].astype(jnp.float32) + source[rows, :].astype(jnp.float32)).astype(
            jnp.bfloat16
        )


def pieces_of(deep):
    return [(piece, shift) for piece in range(3) for shift in range(deep)]


def feed_back_kernel(
    deep, rows_hbm, grads_hbm, chunks, middle_hbm, gain_ref,
    grad_middle_out, grad_attention_out, branch_out, sent_out, own_out, arrived_out,
    gate, up, down, rows, grads, hidden, grad_gate, grad_up, parts, landing, incoming, middle, stage,
    load_sems, weight_sems, store_sems, early_sems, core_sems, x_sems, y_sems,
):
    core_beside, x_beside, y_beside = beside()
    greet([core_beside, x_beside, y_beside])
    blocks, count, width = rows.shape
    half = gate.shape[1] // 2
    part = chunks.shape[3]
    piece_rows = 2 * part
    sent = []

    def load(source, target, sem):
        copy = pltpu.make_async_copy(source, target, sem)
        copy.start()
        return copy

    def move(source, target, sems, index, where):
        copy = send(source, target, (sems.at[0, index], sems.at[1, index]), where)
        sent.append(copy)
        return copy

    row_loads = {}
    for block in (3, 1):
        row_loads[block] = [load(rows_hbm.at[block], rows.at[block], load_sems.at[0, block])]
    weight_loads = []
    for matrix, target in enumerate((gate, up, down)):
        here = []
        for side in range(2):
            for shift in range(deep):
                for rel in range(2):
                    here.append(
                        load(
                            chunks.at[side, shift, rel, :, pl.ds(matrix * half, half)],
                            target.at[pl.ds(grid_offset(shift, rel, deep, part), part), pl.ds(side * half, half)],
                            weight_sems.at[matrix, side, shift, rel],
                        )
                    )
        weight_loads.append(here)
        if matrix == 0:
            for block in (3, 1):
                row_loads[block].append(load(grads_hbm.at[block], grads.at[block], load_sems.at[1, block]))
    for block in (2, 0):
        row_loads[block] = [
            load(rows_hbm.at[block], rows.at[block], load_sems.at[0, block]),
            load(grads_hbm.at[block], grads.at[block], load_sems.at[1, block]),
        ]
    middle_load = load(middle_hbm, middle, load_sems.at[0, 4])

    def inner(block):
        @pl.loop(0, gate.shape[1] // TILE)
        def _(step):
            lanes = pl.ds(pl.multiple_of(step * TILE, TILE), TILE)
            gate_value = nn(rows[block], gate[:, lanes])
            up_value = nn(rows[block], up[:, lanes])
            grad_hidden = nn(grads[block], down[:, lanes])
            sigmoid = 1.0 / (1.0 + jnp.exp(-gate_value))
            swish = gate_value * sigmoid
            slope = sigmoid + swish * (1.0 - sigmoid)
            hidden[block, :, lanes] = (swish * up_value).astype(jnp.bfloat16)
            grad_gate[block, :, lanes] = (grad_hidden * up_value * slope).astype(jnp.bfloat16)
            grad_up[block, :, lanes] = (grad_hidden * swish).astype(jnp.bfloat16)

    def outer(block):
        @pl.loop(0, width // TILE)
        def _(step):
            lanes = pl.ds(pl.multiple_of(step * TILE, TILE), TILE)
            parts[block, :, lanes] = (
                times_transposed(grad_gate[block], gate[lanes, :])
                + times_transposed(grad_up[block], up[lanes, :])
            ).astype(jnp.bfloat16)

    for position, block in enumerate((3, 1, 2, 0)):
        for copy in row_loads[block]:
            copy.wait()
        if position == 0:
            for here in weight_loads:
                for copy in here:
                    copy.wait()
        inner(block)
        outer(block)
        if block == 3:
            far = move(parts.at[3], landing.at[1], core_sems, 0, core_beside)
        if block == 1:
            far.wait_recv()
            add_rows(parts.at[1], landing.at[1])
            across = move(parts.at[1], incoming, x_sems, 0, x_beside)
        if block == 2:
            near = move(parts.at[2], landing.at[0], core_sems, 1, core_beside)

    sources = ((grads, hidden), (rows, grad_gate), (rows, grad_up))

    def weight_part(piece, side, shift):
        left, right = sources[piece]
        row = ring_row(shift, deep, piece_rows)
        lanes = slice(side * half, (side + 1) * half)
        product = transposed_times(
            left[:, :, pl.ds(row, piece_rows)].reshape(blocks * count, piece_rows),
            right[:, :, lanes].reshape(blocks * count, half),
        )
        stage[piece, pl.ds(row, piece_rows), :] = product.astype(jnp.bfloat16)

    early = pieces_of(deep)[:EARLY]
    arrivals, stores, pending = [], [], []

    def flush():
        for index, store, target in pending:
            store.wait()
            arrivals.append(move(target, arrived_out.at[index], y_sems, index, y_beside))
        pending.clear()

    for piece in range(3):
        mine = [pair for pair in early if pair[0] == piece]
        for pair in mine:
            weight_part(piece, 1, pair[1])
            flush()
            rows_here = pl.ds(ring_row(pair[1], deep, piece_rows), piece_rows)
            index = early.index(pair)
            target = sent_out.at[piece, rows_here, :]
            pending.append((index, load(stage.at[piece, rows_here, :], target, early_sems.at[index]), target))
        for shift in range(len(mine), deep):
            weight_part(piece, 1, shift)
            flush()
            rows_here = pl.ds(ring_row(shift, deep, piece_rows), piece_rows)
            stores.append(
                load(
                    stage.at[piece, rows_here, :],
                    sent_out.at[piece, rows_here, :],
                    early_sems.at[piece * deep + shift],
                )
            )
    late_stores = list(stores)
    near.wait_recv()
    middle_load.wait()
    across.wait_recv()
    step_rows = 128

    @pl.loop(0, count // step_rows)
    def _(step):
        tile = pl.ds(pl.multiple_of(step * step_rows, step_rows), step_rows)
        grad = (
            parts[0, tile, :].astype(jnp.float32)
            + landing[0, tile, :].astype(jnp.float32)
            + incoming[tile, :].astype(jnp.float32)
        )
        total = grads[0, tile, :].astype(jnp.float32) + norm_back(middle[tile, :], gain_ref[...], grad)
        middle[tile, :] = total
        incoming[tile, :] = total.astype(jnp.bfloat16)

    attention_x = move(incoming, grad_attention_out.at[1], x_sems, 1, x_beside)
    attention_core = move(incoming, grad_attention_out.at[2], core_sems, 2, core_beside)
    stores.append(load(incoming, grad_attention_out.at[0], store_sems.at[0]))
    stores.append(load(middle, grad_middle_out, store_sems.at[3]))

    far.wait_send()
    across.wait_send()
    near.wait_send()

    def branch(block):
        @pl.loop(0, width // TILE)
        def _(step):
            lanes = pl.ds(pl.multiple_of(step * TILE, TILE), TILE)
            parts[block, :, lanes] = times_transposed(hidden[block], down[lanes, :]).astype(jnp.bfloat16)

    branch(3)
    attention_core.wait_recv()
    branch_far = move(parts.at[3], landing.at[1], core_sems, 3, core_beside)
    branch(2)
    branch_near = move(parts.at[2], landing.at[0], core_sems, 4, core_beside)
    branch(1)
    branch_far.wait_recv()
    add_rows(parts.at[1], landing.at[1])
    stores.append(load(parts.at[1], branch_out.at[1], store_sems.at[4]))
    branch(0)
    stores.append(load(parts.at[0], branch_out.at[0], store_sems.at[5]))
    branch_near.wait_recv()
    stores.append(load(landing.at[0], branch_out.at[2], store_sems.at[6]))
    for copy in late_stores:
        copy.wait()
    for piece in range(3):

        @pl.loop(0, deep)
        def _(shift, piece=piece):
            weight_part(piece, 0, shift)

        stores.append(load(stage.at[piece], own_out.at[piece], store_sems.at[7 + piece]))
    attention_x.wait_recv()
    attention_far = move(grad_attention_out.at[1], grad_attention_out.at[3], core_sems, 5, core_beside)
    attention_far.wait_recv()
    for copy in arrivals:
        copy.wait_recv()
    for copy in stores[len(late_stores) :]:
        copy.wait()
    for copy in arrivals:
        copy.wait_send()
    for copy in (attention_x, attention_core, branch_far, branch_near, attention_far):
        copy.wait_send()


def feed_back(deep, rows, grads, chunks, middle, gain):
    blocks, count, width = rows.shape
    half = chunks.shape[4] // 3
    part = chunks.shape[3]

    def shape(*dims, kind=jnp.bfloat16):
        return jax.ShapeDtypeStruct(dims, kind)

    def room(*dims, kind=jnp.bfloat16):
        return pltpu.VMEM(dims, kind)

    outs = (
        shape(count, width, kind=jnp.float32),
        shape(blocks, count, width),
        shape(3, count, width),
        shape(3, width, half),
        shape(3, width, half),
        shape(EARLY, 2 * part, half),
    )
    dma = pltpu.SemaphoreType.DMA
    return pl.pallas_call(
        functools.partial(feed_back_kernel, deep),
        out_shape=outs,
        in_specs=[hbm_spec()] * 4 + [vmem_spec()],
        out_specs=(hbm_spec(),) * len(outs),
        scratch_shapes=[room(width, 2 * half)] * 3
        + [room(blocks, count, width)] * 2
        + [room(blocks, count, 2 * half)] * 3
        + [room(blocks, count, width), room(2, count, width), room(count, width)]
        + [room(count, width, kind=jnp.float32), room(3, width, half)]
        + [dma((2, 5)), dma((3, 2, deep, 2)), dma((10,)), dma((3 * deep,)), dma((2, 6)), dma((2, 2)), dma((2, EARLY))],
        compiler_params=vmem_params(collective_id=2, has_side_effects=True),
        cost_estimate=cost(flops=80 * 10**9, bytes_accessed=10**8, transcendentals=10**7),
        name="feed_back",
    )(rows, grads, chunks, middle, gain)


def attend_back_pair(
    qkv, grad_heads, heads, logs, cosine_ref, sine_ref, grad_qkv, keys, values, grad_keys, grad_values,
    sequence, pair,
):
    count = qkv.shape[1]
    x_place = lax.axis_index("x").astype(jnp.int32)
    lane0 = pl.multiple_of(pair * 4 * LANES, 4 * LANES)
    head0 = pl.multiple_of(pair * 2 * LANES, 2 * LANES)
    mask = diagonal_mask()
    factor = HD ** (-0.5)
    scale = factor * LOG2E
    for rel in range(2):
        position = lax.rem(x_place + rel, jnp.int32(2))
        rows = pl.ds(pl.multiple_of(position * count, count), count)
        keys[rows, :] = qkv[2 * sequence + rel, :, pl.ds(lane0 + 2 * LANES, LANES)]
        values[rows, :] = qkv[2 * sequence + rel, :, pl.ds(lane0 + 3 * LANES, LANES)]
    grad_keys[...] = jnp.zeros_like(grad_keys)
    grad_values[...] = jnp.zeros_like(grad_values)

    def visit(rel, start, before):
        block = 2 * sequence + rel
        rows = slice(start, start + TILE)

        def both(ref, first):
            return jnp.concatenate(
                [ref[block, rows, pl.ds(first, LANES)], ref[block, rows, pl.ds(first + LANES, LANES)]], axis=0
            )

        queries, grads, outs = both(qkv, lane0), both(grad_heads, head0), both(heads, head0)
        lane = lax.broadcasted_iota(jnp.int32, (TILE, LANES), 1)
        kept = logs[block, rows, :]
        log = jnp.concatenate(
            [
                jnp.sum(jnp.where(lane == 2 * pair + head, kept, 0.0), axis=-1, keepdims=True)
                for head in range(2)
            ],
            axis=0,
        )
        inner = jnp.sum(grads.astype(jnp.float32) * outs.astype(jnp.float32), axis=-1, keepdims=True)

        def span(span_rows, masked):
            softmax = jnp.exp2(times_transposed(queries, keys[span_rows, :]) * scale - log)
            if masked:
                softmax = jnp.where(mask, softmax, 0.0)
            grad_softmax = times_transposed(grads, values[span_rows, :])
            grad_scores = (softmax * (grad_softmax - inner)).astype(jnp.bfloat16)
            grad_values[span_rows, :] += transposed_times(softmax.astype(jnp.bfloat16), grads)
            grad_keys[span_rows, :] += transposed_times(grad_scores, queries)
            return nn(grad_scores, keys[span_rows, :])

        grad_queries = span(slice(before, before + TILE), True)
        if before:
            grad_queries = grad_queries + span(slice(0, before), False)
        cosine, sine = cosine_ref[rel, rows, :], -sine_ref[rel, rows, :]
        for head in range(2):
            piece = grad_queries[head * TILE : (head + 1) * TILE] * factor
            grad_qkv[block, rows, pl.ds(lane0 + head * LANES, LANES)] = turn(piece, cosine, sine).astype(
                jnp.bfloat16
            )

    for rel in range(2):
        position = lax.rem(x_place + rel, jnp.int32(2))
        for static_position in range(2):

            @pl.when(position == static_position)
            def _(rel=rel, static_position=static_position):
                for step in range(count // TILE):
                    visit(rel, step * TILE, static_position * count + step * TILE)

    for rel in range(2):
        block = 2 * sequence + rel
        position = lax.rem(x_place + rel, jnp.int32(2))
        rows = pl.ds(pl.multiple_of(position * count, count), count)
        grad_qkv[block, :, pl.ds(lane0 + 2 * LANES, LANES)] = turn(
            grad_keys[rows, :] * factor, cosine_ref[rel], -sine_ref[rel]
        ).astype(jnp.bfloat16)
        grad_qkv[block, :, pl.ds(lane0 + 3 * LANES, LANES)] = grad_values[rows, :].astype(jnp.bfloat16)


def heads_back_kernel(
    deep, grad_attention_hbm, qkv_hbm, heads_hbm, logs_hbm, first_hbm, qkv_wide_hbm, out_wide_hbm,
    branch_hbm, sent_hbm, own_hbm, early_hbm, chunks_hbm, qkv_own_hbm,
    cosine_ref, sine_ref, qkv_spread, out_spread,
    first_part, first_core, first_x, branch_x, feed_final, qkv_final, out_final, first_gain_out, second_gain_out,
    grad_attention, qkv, heads, grad_heads, logs, grad_qkv, qkv_wide, out_wide, keys, values, grad_keys,
    grad_values, landing, feed_sum, feed_y, feed_z, out_sent, out_sum, out_y, out_z, qkv_sent, qkv_sum, qkv_y,
    qkv_z, feed_last, qkv_last, out_last, feed_weight, qkv_weight, gain_part, gain_in, gain_total,
    load_sems, own_sems, tile_sems, core_sems, x_sems, y_sems, z_sems, gain_sems,
):
    blocks, count, width = grad_attention.shape
    core_beside, x_beside, y_beside = beside()
    core, z_place = lax.axis_index("c").astype(jnp.int32), lax.axis_index("z").astype(jnp.int32)
    across, along = lax.axis_index("x").astype(jnp.int32), lax.axis_index("y").astype(jnp.int32)
    ring = jnp.int32(deep)
    z_ahead = [{"z": lax.rem(z_place + shift, ring)} for shift in range(deep)]
    cube = {
        (rel, up, over): {"c": (core + rel) % 2, "y": (along + up) % 2, "x": (across + over) % 2}
        for rel in range(2)
        for up in range(2)
        for over in range(2)
    }
    far_cube = [key for key in cube if key != (0, 0, 0)]
    greet([cube[key] for key in far_cube] + z_ahead[1:])
    half = feed_sum.shape[3]
    piece_rows = feed_sum.shape[2]
    part = piece_rows // 2
    step_rows = 128
    sent = []

    def load(source, target, sem):
        copy = pltpu.make_async_copy(source, target, sem)
        copy.start()
        return copy

    def move(source, target, sems, index, where):
        copy = send(source, target, (sems.at[0, index], sems.at[1, index]), where)
        sent.append(copy)
        return copy

    early, late = pieces_of(deep)[:EARLY], pieces_of(deep)[EARLY:]
    attention_load = load(grad_attention_hbm, grad_attention, load_sems.at[0])
    out_load = load(out_wide_hbm, out_wide, load_sems.at[1])
    heads_load = load(heads_hbm, heads, load_sems.at[2])
    late_copies = []
    for index, (piece, shift) in enumerate(late):
        row = ring_row(shift, deep, piece_rows)
        late_copies.append(
            move(
                sent_hbm.at[piece, pl.ds(row, piece_rows), :], feed_y.at[piece, shift], y_sems, index, y_beside
            )
        )
    branch_copy = move(branch_hbm.at[1], branch_x, x_sems, 0, x_beside)
    qkv_load = load(qkv_hbm, qkv, load_sems.at[3])
    logs_load = load(logs_hbm, logs, load_sems.at[4])
    wide_load = load(qkv_wide_hbm, qkv_wide, load_sems.at[5])
    own_loads = {}
    early_loads = {}
    for index, (piece, shift) in enumerate(pieces_of(deep)):
        row = ring_row(shift, deep, piece_rows)
        own_loads[piece, shift] = load(
            own_hbm.at[piece, pl.ds(row, piece_rows), :], feed_sum.at[piece, shift], own_sems.at[0, index]
        )
        if (piece, shift) in early:
            early_loads[piece, shift] = load(
                early_hbm.at[index], feed_y.at[piece, shift], own_sems.at[1, index]
            )
    weight_loads = [
        load(chunks_hbm.at[0, 0, :, :, pl.ds(0, 2 * half)], feed_weight, load_sems.at[6]),
        load(qkv_own_hbm, qkv_weight, load_sems.at[7]),
    ]

    attention_load.wait()
    out_load.wait()

    @pl.loop(0, blocks)
    def _(block):
        grad_heads[block] = nn(grad_attention[block], out_wide[...]).astype(jnp.bfloat16)

    heads_load.wait()

    def weight_tile(left, right, spread, side):
        size = spread.shape[1]
        right = right[:, :, side * size : (side + 1) * size].reshape(blocks * count, size)
        product = transposed_times(left.reshape(blocks * count, piece_rows), right)
        return times_transposed(product.astype(jnp.bfloat16), spread[...]).astype(jnp.bfloat16)

    y_index = len(late)
    out_copies = []
    for shift in range(deep):
        row = ring_row(shift, deep, piece_rows)
        out_sent[shift] = weight_tile(grad_attention[:, :, pl.ds(row, piece_rows)], heads, out_spread, 1)
        out_copies.append(move(out_sent.at[shift], out_y.at[shift], y_sems, y_index + shift, y_beside))

    @pl.loop(0, deep)
    def _(shift):
        row = ring_row(shift, deep, piece_rows)
        out_sum[shift] = weight_tile(grad_attention[:, :, pl.ds(row, piece_rows)], heads, out_spread, 0)

    z_copies = {}

    def join_piece(name, number, total, arrived, target, shift):
        add_rows(total.at[shift], arrived.at[shift])
        if shift:
            z_copies[name, shift] = move(
                total.at[shift], target.at[shift - 1], z_sems, number * (deep - 1) + shift - 1, z_ahead[shift]
            )

    def join_feed(piece, shift):
        own_loads[piece, shift].wait()
        join_piece(piece, piece, feed_sum.at[piece], feed_y.at[piece], feed_z.at[piece], shift)

    for pair in early:
        early_loads[pair].wait()
        join_feed(*pair)

    qkv_load.wait()
    logs_load.wait()
    for sequence in range(2):

        @pl.loop(0, 2)
        def _(pair, sequence=sequence):
            attend_back_pair(
                qkv, grad_heads, heads, logs, cosine_ref, sine_ref, grad_qkv, keys, values, grad_keys,
                grad_values, sequence, pair,
            )

        for index in range(sequence * 2, sequence * 2 + 2):
            late_copies[index].wait_recv()
            join_feed(*late[index])
    wide_load.wait()

    def first_tile(shift):
        row = ring_row(shift, deep, piece_rows)
        slot = (shift % 2) * 512
        return load(
            first_hbm.at[:, :, pl.ds(row, piece_rows)],
            qkv.at[:, :, pl.ds(slot, piece_rows)],
            tile_sems.at[shift],
        )

    first_loads = [first_tile(shift) for shift in range(2)]

    def first_piece(block):
        @pl.loop(0, width // 512)
        def _(step):
            lanes = pl.ds(pl.multiple_of(step * 512, 512), 512)
            grad_attention[block, :, lanes] = times_transposed(grad_qkv[block], qkv_wide[lanes, :]).astype(
                jnp.bfloat16
            )

    first_piece(3)
    core_far = move(grad_attention.at[3], landing, core_sems, 0, core_beside)
    first_piece(1)
    core_far.wait_recv()
    add_rows(grad_attention.at[1], landing)
    x_copy = move(grad_attention.at[1], first_x, x_sems, 1, x_beside)
    first_piece(2)
    core_near = move(grad_attention.at[2], first_core, core_sems, 1, core_beside)
    first_piece(0)
    first_store = load(grad_attention.at[0], first_part, load_sems.at[8])

    qkv_copies = []
    y_index += deep
    for shift in range(deep):
        first_loads[shift].wait()
        slot = (shift % 2) * 512
        left = qkv[:, :, slot : slot + piece_rows]
        qkv_sent[shift] = weight_tile(left, grad_qkv, qkv_spread, 1)
        qkv_copies.append(move(qkv_sent.at[shift], qkv_y.at[shift], y_sems, y_index + shift, y_beside))
        qkv_sum[shift] = weight_tile(left, grad_qkv, qkv_spread, 0)
        if shift + 2 < deep:
            first_loads.append(first_tile(shift + 2))

    for index in range(4, len(late)):
        late_copies[index].wait_recv()
        join_feed(*late[index])
    for shift in range(deep):
        out_copies[shift].wait_recv()
        join_piece("out", 3, out_sum, out_y, out_z, shift)

    finals = []

    def finish(name, number, total, arrived, last, final, weights):
        for shift in range(1, deep):
            z_copies[name, shift].wait_recv()
        size = total.shape[2]
        sums = []
        for rel in range(2):
            row = pl.multiple_of(lax.rem(core + rel, jnp.int32(2)) * part, part)
            value = total[0, pl.ds(row, part), :].astype(jnp.float32)
            for shift in range(deep - 1):
                value = value + arrived[shift, pl.ds(row, part), :].astype(jnp.float32)
            last[rel] = value
            if weights is not None:
                product = value * weights[rel].astype(jnp.float32)
                sums.append(sum(product[:, i * LANES : (i + 1) * LANES] for i in range(size // LANES)))
        finals.append(load(last.at[0], final.at[core], own_sems.at[1, 12 + number]))
        finals.append(move(last.at[1], final.at[core], core_sems, 2 + number, core_beside))
        return sums

    def gain_exchange(which, sums):
        slots = {}
        for rel in range(2):
            gain_part[which, rel] = sums[rel]
        piece = part // 4
        for number, key in enumerate(far_cube):
            rel, up, over = key
            target = ((along + up) % 2) * 2 + (across + over) % 2
            row = pl.multiple_of(target * piece, 8)
            slots[key] = move(
                gain_part.at[which, rel, pl.ds(row, piece), :],
                gain_in.at[which, number],
                gain_sems,
                which * len(far_cube) + number,
                cube[key],
            )
        return slots

    def gain_finish(which, slots, output):
        piece = part // 4
        row = pl.multiple_of((along * 2 + across) * piece, 8)
        value = gain_part[which, 0, pl.ds(row, piece), :]
        for number, key in enumerate(far_cube):
            slots[key].wait_recv()
            value = value + gain_in[which, number]
        gain_total[which] = value
        return load(gain_total.at[which], output, load_sems.at[9 + which])

    for copy in weight_loads:
        copy.wait()
    finish(0, 0, feed_sum.at[0], feed_z.at[0], feed_last.at[0], feed_final.at[0], None)
    gate_sums = finish(
        1, 1, feed_sum.at[1], feed_z.at[1], feed_last.at[1], feed_final.at[1], feed_weight.at[:, :, pl.ds(0, half)]
    )
    for shift in range(deep):
        qkv_copies[shift].wait_recv()
        join_piece("qkv", 4, qkv_sum, qkv_y, qkv_z, shift)
    up_sums = finish(
        2, 2, feed_sum.at[2], feed_z.at[2], feed_last.at[2], feed_final.at[2],
        feed_weight.at[:, :, pl.ds(half, half)],
    )
    second_slots = gain_exchange(1, [one + two for one, two in zip(gate_sums, up_sums)])
    finish("out", 3, out_sum, out_z, out_last, out_final, None)
    sums = finish("qkv", 4, qkv_sum, qkv_z, qkv_last, qkv_final, qkv_weight)
    first_slots = gain_exchange(0, sums)
    second_store = gain_finish(1, second_slots, second_gain_out)
    first_gain_store = gain_finish(0, first_slots, first_gain_out)
    for copy in (branch_copy, x_copy, core_near):
        copy.wait_recv()
    for number in range(5):
        finals[2 * number].wait()
        finals[2 * number + 1].wait_recv()
    for copy in (first_store, second_store, first_gain_store):
        copy.wait()
    for copy in sent:
        copy.wait_send()


def heads_back(
    deep, grad_attention, qkv, heads, logs, first, qkv_wide, out_wide, branch, sent, own, early, chunks, qkv_own,
    cosine, sine, spreads,
):
    blocks, count, width = grad_attention.shape
    part, half = chunks.shape[3], chunks.shape[4] // 3
    qkv_half, out_half = spreads[0].shape[0], spreads[1].shape[0]
    rows = 2 * part

    def shape(*dims, kind=jnp.bfloat16):
        return jax.ShapeDtypeStruct(dims, kind)

    def room(*dims, kind=jnp.bfloat16):
        return pltpu.VMEM(dims, kind)

    wide = jnp.float32
    outs = (
        shape(count, width),
        shape(count, width),
        shape(count, width),
        shape(count, width),
        shape(3, 2, part, half, kind=wide),
        shape(2, part, qkv_half, kind=wide),
        shape(2, part, out_half, kind=wide),
        shape(part // 4, LANES, kind=wide),
        shape(part // 4, LANES, kind=wide),
    )
    dma = pltpu.SemaphoreType.DMA
    scratch = [
        room(blocks, count, width),
        room(*qkv.shape),
        room(*heads.shape),
        room(*heads.shape),
        room(*logs.shape, kind=wide),
        room(*qkv.shape),
        room(*qkv_wide.shape),
        room(*out_wide.shape),
        room(2 * count, LANES),
        room(2 * count, LANES),
        room(2 * count, LANES, kind=wide),
        room(2 * count, LANES, kind=wide),
        room(count, width),
        room(3, deep, rows, half),
        room(3, deep, rows, half),
        room(3, deep - 1, rows, half),
        room(deep, rows, out_half),
        room(deep, rows, out_half),
        room(deep, rows, out_half),
        room(deep - 1, rows, out_half),
        room(deep, rows, qkv_half),
        room(deep, rows, qkv_half),
        room(deep, rows, qkv_half),
        room(deep - 1, rows, qkv_half),
        room(3, 2, part, half, kind=wide),
        room(2, part, qkv_half, kind=wide),
        room(2, part, out_half, kind=wide),
        room(2, part, 2 * half),
        room(2, part, qkv_half),
        room(2, 2, part, LANES, kind=wide),
        room(2, 7, part // 4, LANES, kind=wide),
        room(2, part // 4, LANES, kind=wide),
        dma((11,)),
        dma((2, max(3 * deep, 17))),
        dma((deep,)),
        dma((2, 7)),
        dma((2, 2)),
        dma((2, 5 * deep)),
        dma((2, 5 * (deep - 1))),
        dma((2, 14)),
    ]
    return pl.pallas_call(
        functools.partial(heads_back_kernel, deep),
        out_shape=outs,
        in_specs=[hbm_spec()] * 13 + [vmem_spec()] * 4,
        out_specs=(hbm_spec(),) * len(outs),
        scratch_shapes=scratch,
        compiler_params=vmem_params(collective_id=3, has_side_effects=True),
        cost_estimate=cost(flops=30 * 10**9, bytes_accessed=10**8, transcendentals=10**7),
        name="heads_back",
    )(
        grad_attention, qkv, heads, logs, first, qkv_wide, out_wide, branch, sent, own, early, chunks, qkv_own,
        cosine, sine, *spreads,
    )


def tables(rows, x_place):
    lane = np.arange(LANES)
    entry = lane % (LANES // 2)
    live = (entry < HD // 2).astype(np.float32)
    sign = np.where(lane < LANES // 2, -1.0, 1.0).astype(np.float32) * live
    pair_entry = np.where(entry < HD // 2, entry, 0).astype(np.float32)
    inverse = THETA ** (-2.0 * jnp.asarray(pair_entry) / HD)
    both = []
    for rel in range(2):
        first = lax.rem(x_place + rel, jnp.int32(2)) * rows
        position = (first + jnp.arange(rows, dtype=jnp.int32)).astype(jnp.float32)
        both.append(position[:, None] * inverse[None, :])
    angles = jnp.stack(both)
    return jnp.cos(angles) * live, jnp.sin(angles) * sign


def norm_factor(rows):
    return lax.rsqrt(jnp.mean(rows * rows, axis=-1, keepdims=True) + EPSILON)


def norm_back(rows, gain, grad):
    factor = norm_factor(rows)
    scaled = grad * gain
    return factor * scaled - rows * factor**3 * jnp.mean(scaled * rows, axis=-1, keepdims=True)


def join(halves):
    return jnp.concatenate([halves[0], halves[1]], axis=1)


def gain_grad(lanes, gain, depth_place):
    piece = lanes.shape[0]
    start = (depth_place * 4 + lax.axis_index("y") * 2 + lax.axis_index("x")) * piece
    return jnp.sum(lanes, axis=1) / lax.dynamic_slice_in_dim(gain, start, piece)


def fast_local(
    tokens,
    cotangent,
    first_gain,
    query_weight,
    key_weight,
    value_weight,
    out_weight,
    second_gain,
    gate_weight,
    up_weight,
    down_weight,
):
    deep = lax.axis_size("z")
    z_place, core, x_place = (lax.axis_index(name).astype(jnp.int32) for name in ("z", "c", "x"))
    rows = tokens.shape[0]
    depth_place = z_place * 2 + core
    own_rows = tokens.astype(jnp.float32)
    first_normed = (own_rows * norm_factor(own_rows) * first_gain).astype(jnp.bfloat16)
    out_turned, down_turned = out_weight.T, down_weight.T

    def halves(*weights):
        result = []
        for half in range(2):
            pieces = []
            for weight in weights:
                size = weight.shape[1] // 2
                pieces.append(weight[:, half * size : (half + 1) * size])
            result.append(jnp.concatenate(pieces, axis=1))
        return result

    spreads = (spread_heads(3, 1), spread_heads(0, 2))
    cosine, sine = tables(rows, x_place)
    (
        first_all, qkv_all, heads_all, logs_all, qkv_weight, out_wide, middle, second_all, cotangent_all, chunks, qkv_own,
    ) = forward(
        deep,
        first_normed,
        cotangent,
        tokens,
        second_gain[None],
        jnp.stack(halves(query_weight, key_weight, value_weight)),
        jnp.stack(halves(out_turned)),
        jnp.stack(halves(gate_weight, up_weight, down_turned)),
        spreads,
        cosine,
        sine,
    )
    grad_middle, grad_attention, branch, sent, own, early = feed_back(
        deep, second_all, cotangent_all, chunks, middle, second_gain[None]
    )
    first_part, first_core, first_x, branch_x, feed_final, qkv_final, out_final, first_lanes, second_lanes = (
        heads_back(
            deep, grad_attention, qkv_all, heads_all, logs_all, first_all, qkv_weight, out_wide, branch, sent,
            own, early, chunks, qkv_own, cosine, sine, spreads,
        )
    )

    def total(*parts):
        return sum(piece.astype(jnp.float32) for piece in parts)

    result = (middle + total(branch[0], branch[2], branch_x)).astype(jnp.bfloat16)
    grad_first = total(first_part, first_core, first_x)
    tokens_grad = grad_middle + norm_back(own_rows, first_gain, grad_first)
    query_end = query_weight.shape[1] // 2
    key_end = query_end + key_weight.shape[1] // 2
    return (
        result,
        tokens_grad,
        join(qkv_final[:, :, :query_end]),
        join(qkv_final[:, :, query_end:key_end]),
        join(qkv_final[:, :, key_end:]),
        join(out_final).T,
        join(feed_final[1]),
        join(feed_final[2]),
        join(feed_final[0]).T,
        gain_grad(first_lanes, first_gain, depth_place),
        gain_grad(second_lanes, second_gain, depth_place),
    )


def specs(depth, width):
    both = depth + width
    rows, inward, outward = P(both, None), P(depth, width), P(width, depth)
    in_specs = (rows, rows, P(), inward, inward, inward, outward, P(), inward, inward, outward)
    out_specs = (rows, rows, inward, inward, inward, outward, inward, inward, outward, P(both), P(both))
    return in_specs, out_specs


def solution(mesh):
    depth, width = mesh.shape["dp"], mesh.shape["tensor"]

    def run(tokens, cotangent, *weights):
        fits = (
            width == 4
            and depth % 2 == 0
            and tokens.shape[0] * 2 == SEQ_LEN * depth * width
            and weights[2].shape[1] == 2 * width * HD
            and weights[1].shape[1] == 4 * width * HD
        )
        if fits:
            devices = mesh.devices.reshape(depth // 2, 2, 2, 2)
            fine = jax.sharding.Mesh(devices, ("z", "c", "y", "x"))
            in_specs, out_specs = specs(("z", "c"), ("y", "x"))
            call, over = fast_local, fine
        else:
            in_specs, out_specs = specs(("dp",), ("tensor",))
            call, over = local, mesh
        return jax.shard_map(call, mesh=over, in_specs=in_specs, out_specs=out_specs, check_vma=False)(
            tokens, cotangent, *weights
        )

    return run
```

```python
import functools

import jax
import jax.numpy as jnp
import numpy as np
from jax import lax
from jax.experimental import pallas as pl
from jax.experimental.pallas import tpu as pltpu
from jax.sharding import PartitionSpec as P

HD = 96
SEQ_LEN = 1024


EPSILON = 1e-05
THETA = 100000.0
MASKED = -1e30
LOG2E = 1.4426950408889634
LANES = 128
SHARE = 20
VMEM_BYTES = 63 * 2**20


def normed(inputs, gain):
    factor = lax.rsqrt(jnp.mean(inputs * inputs, axis=-1, keepdims=True) + EPSILON)
    return inputs * factor * gain


def rotate(vectors, direction):
    seq_rows, head_count, head_size = vectors.shape
    half_size = head_size // 2
    position = (jnp.arange(seq_rows, dtype=jnp.int32) % SEQ_LEN).astype(jnp.float32)
    inverse = THETA ** (-2.0 * jnp.arange(half_size, dtype=jnp.float32) / head_size)
    angles = position[:, None] * inverse[None, :]
    cosine = jnp.cos(angles)[:, None, :]
    sine_part = direction * jnp.sin(angles)[:, None, :]
    leading = vectors[..., :half_size]
    trailing = vectors[..., half_size:]
    return jnp.concatenate(
        [leading * cosine - trailing * sine_part, trailing * cosine + leading * sine_part], axis=-1
    )


def times_transposed(left, right):
    return lax.dot_general(
        left, right, (((1,), (1,)), ((), ())), preferred_element_type=jnp.float32
    )


def transposed_times(left, right):
    return lax.dot_general(
        left, right, (((0,), (0,)), ((), ())), preferred_element_type=jnp.float32
    )


def scaled_scores(queries, keys_rot):
    raw_scores = jnp.einsum(
        "qhgd,khd->hgqk", queries, keys_rot, preferred_element_type=jnp.float32
    ) * queries.shape[-1] ** (-0.5)
    length_rows = queries.shape[0]
    causal = jnp.arange(length_rows)[:, None] >= jnp.arange(length_rows)[None, :]
    return jnp.where(causal, raw_scores, MASKED)


def attend_forward(operands):
    queries, keys_rot, values = operands
    scores = scaled_scores(queries, keys_rot)
    row_max = jnp.max(scores, axis=-1, keepdims=True)
    weights = jnp.exp(scores - row_max)
    row_total = jnp.sum(weights, axis=-1, keepdims=True)
    softmax = (weights / row_total).astype(jnp.bfloat16)
    mixed_heads = jnp.einsum("hgqk,khd->qhgd", softmax, values, preferred_element_type=jnp.float32)
    return (mixed_heads.astype(jnp.bfloat16), (row_max + jnp.log(row_total))[..., 0])


def attend_backward(operands):
    queries, keys_rot, values, grad_mixed, log_total = operands
    scores = scaled_scores(queries, keys_rot)
    softmax = jnp.exp(scores - log_total[..., None])
    grad_softmax = jnp.einsum(
        "qhgd,khd->hgqk", grad_mixed, values, preferred_element_type=jnp.float32
    )
    grad_values = jnp.einsum(
        "hgqk,qhgd->khd",
        softmax.astype(jnp.bfloat16),
        grad_mixed,
        preferred_element_type=jnp.float32,
    )
    row_inner = jnp.sum(softmax * grad_softmax, axis=-1, keepdims=True)
    grad_scores = (softmax * (grad_softmax - row_inner)).astype(jnp.bfloat16)
    scale_factor = queries.shape[-1] ** (-0.5)
    grad_queries = (
        jnp.einsum("hgqk,khd->qhgd", grad_scores, keys_rot, preferred_element_type=jnp.float32)
        * scale_factor
    )
    grad_keys = (
        jnp.einsum("hgqk,qhgd->khd", grad_scores, queries, preferred_element_type=jnp.float32)
        * scale_factor
    )
    return (grad_queries, grad_keys, grad_values)


def gather_rows(shard):
    return lax.all_gather(shard, "tensor", axis=0, tiled=True)


def gather_grads(shard):
    return lax.all_gather(shard, "tensor", axis=0, tiled=True)


def sum_outputs(term, row_count):
    return lax.psum_scatter(
        term(jnp.int32(0), row_count * lax.axis_size("tensor")),
        "tensor",
        scatter_dimension=0,
        tiled=True,
    )


def sum_inputs(term, row_count):
    return lax.psum_scatter(
        term(jnp.int32(0), row_count * lax.axis_size("tensor")),
        "tensor",
        scatter_dimension=0,
        tiled=True,
    )


def local(
    tokens,
    cotangent,
    first_gain,
    query_weight,
    key_weight,
    value_weight,
    out_weight,
    second_gain,
    gate_weight,
    up_weight,
    down_weight,
):
    query_weight, key_weight, value_weight, out_weight, gate_weight, up_weight, down_weight = (
        lax.all_gather(query_weight, "dp", axis=0, tiled=True),
        lax.all_gather(key_weight, "dp", axis=0, tiled=True),
        lax.all_gather(value_weight, "dp", axis=0, tiled=True),
        lax.all_gather(out_weight, "dp", axis=1, tiled=True),
        lax.all_gather(gate_weight, "dp", axis=0, tiled=True),
        lax.all_gather(up_weight, "dp", axis=0, tiled=True),
        lax.all_gather(down_weight, "dp", axis=1, tiled=True),
    )
    own_rows = tokens.astype(jnp.float32)
    row_count = own_rows.shape[0]
    pair_count = key_weight.shape[1] // HD
    first_normed = normed(own_rows, first_gain).astype(jnp.bfloat16)
    first_rows = gather_rows(first_normed)
    group_rows = first_rows.shape[0]
    sequences = group_rows // SEQ_LEN
    query_pre = jnp.dot(first_rows, query_weight, preferred_element_type=jnp.float32)
    key_pre = jnp.dot(first_rows, key_weight, preferred_element_type=jnp.float32)
    value_pre = jnp.dot(first_rows, value_weight, preferred_element_type=jnp.float32)
    queries = rotate(query_pre.reshape(group_rows, 2 * pair_count, HD), 1.0).astype(jnp.bfloat16)
    queries = queries.reshape(sequences, SEQ_LEN, pair_count, 2, HD)
    keys_rot = rotate(key_pre.reshape(group_rows, pair_count, HD), 1.0).astype(jnp.bfloat16)
    keys_rot = keys_rot.reshape(sequences, SEQ_LEN, pair_count, HD)
    values = value_pre.astype(jnp.bfloat16).reshape(sequences, SEQ_LEN, pair_count, HD)
    mixed_heads, log_total = lax.map(attend_forward, (queries, keys_rot, values))
    heads_out = mixed_heads.reshape(group_rows, 2 * pair_count * HD)
    heads_rows = lax.all_to_all(heads_out, "tensor", split_axis=0, concat_axis=1, tiled=True)
    out_full = lax.all_gather(out_weight, "tensor", axis=0, tiled=True)
    attention_branch = jnp.dot(heads_rows, out_full, preferred_element_type=jnp.float32)
    middle = own_rows + attention_branch
    second_normed = normed(middle, second_gain).astype(jnp.bfloat16)
    second_rows = gather_rows(second_normed)
    gate_full, up_full, down_full = (gate_weight, up_weight, down_weight)
    gate_value = jnp.dot(second_rows, gate_full, preferred_element_type=jnp.float32)
    up_value = jnp.dot(second_rows, up_full, preferred_element_type=jnp.float32)
    sigmoid_gate = jax.nn.sigmoid(gate_value)
    swish_gate = gate_value * sigmoid_gate
    hidden = (swish_gate * up_value).astype(jnp.bfloat16)

    def project_hidden(start, amount):
        return jnp.dot(hidden, down_full, preferred_element_type=jnp.float32)

    ffn_branch = sum_outputs(project_hidden, row_count)
    grad_branch = gather_grads(cotangent)
    result = (middle + ffn_branch).astype(jnp.bfloat16)
    grad_hidden = times_transposed(grad_branch, down_full)
    down_part = transposed_times(hidden, grad_branch)
    slope = sigmoid_gate + gate_value * sigmoid_gate * (1.0 - sigmoid_gate)
    grad_gate = (grad_hidden * up_value * slope).astype(jnp.bfloat16)
    grad_up = (grad_hidden * swish_gate).astype(jnp.bfloat16)
    gate_part = transposed_times(second_rows, grad_gate)
    up_part = transposed_times(second_rows, grad_up)

    def second_back(start, amount):
        return times_transposed(grad_gate, gate_full) + times_transposed(grad_up, up_full)

    grad_second = sum_inputs(second_back, row_count)
    second_unused, second_pull = jax.vjp(normed, middle, second_gain)
    grad_middle_norm, second_gain_part = second_pull(grad_second)
    grad_middle = cotangent.astype(jnp.float32) + grad_middle_norm
    grad_attention = grad_middle.astype(jnp.bfloat16)
    grad_heads_rows = times_transposed(grad_attention, out_full).astype(jnp.bfloat16)
    grad_heads = lax.all_to_all(grad_heads_rows, "tensor", split_axis=1, concat_axis=0, tiled=True)
    out_part = lax.psum_scatter(
        transposed_times(heads_rows, grad_attention).astype(jnp.bfloat16),
        "tensor",
        scatter_dimension=0,
        tiled=True,
    )
    grad_mixed = grad_heads.reshape(sequences, SEQ_LEN, pair_count, 2, HD)
    grad_queries, grad_keys, grad_values = lax.map(
        attend_backward, (queries, keys_rot, values, grad_mixed, log_total)
    )
    grad_query = (
        rotate(grad_queries.reshape(group_rows, 2 * pair_count, HD), -1.0)
        .reshape(group_rows, -1)
        .astype(jnp.bfloat16)
    )
    grad_key = (
        rotate(grad_keys.reshape(group_rows, pair_count, HD), -1.0)
        .reshape(group_rows, -1)
        .astype(jnp.bfloat16)
    )
    grad_value = grad_values.reshape(group_rows, -1).astype(jnp.bfloat16)
    query_part = transposed_times(first_rows, grad_query)
    key_part = transposed_times(first_rows, grad_key)
    value_part = transposed_times(first_rows, grad_value)

    def first_back(start, amount):
        return (
            times_transposed(grad_query, query_weight)
            + times_transposed(grad_key, key_weight)
            + times_transposed(grad_value, value_weight)
        )

    grad_first = sum_inputs(first_back, row_count)
    first_unused, first_pull = jax.vjp(normed, own_rows, first_gain)
    grad_own_norm, first_gain_part = first_pull(grad_first)
    tokens_grad = grad_middle + grad_own_norm
    query_grad, key_grad, value_grad, out_grad, gate_grad, up_grad, down_grad = (
        lax.psum_scatter(
            query_part.astype(jnp.bfloat16), "dp", scatter_dimension=0, tiled=True
        ).astype(jnp.float32),
        lax.psum_scatter(
            key_part.astype(jnp.bfloat16), "dp", scatter_dimension=0, tiled=True
        ).astype(jnp.float32),
        lax.psum_scatter(
            value_part.astype(jnp.bfloat16), "dp", scatter_dimension=0, tiled=True
        ).astype(jnp.float32),
        lax.psum_scatter(out_part, "dp", scatter_dimension=1, tiled=True).astype(jnp.float32),
        lax.psum_scatter(
            gate_part.astype(jnp.bfloat16), "dp", scatter_dimension=0, tiled=True
        ).astype(jnp.float32),
        lax.psum_scatter(
            up_part.astype(jnp.bfloat16), "dp", scatter_dimension=0, tiled=True
        ).astype(jnp.float32),
        lax.psum_scatter(
            down_part.astype(jnp.bfloat16), "dp", scatter_dimension=1, tiled=True
        ).astype(jnp.float32),
    )
    first_gain_grad, second_gain_grad = (
        lax.psum_scatter(first_gain_part, ("dp", "tensor"), scatter_dimension=0, tiled=True),
        lax.psum_scatter(second_gain_part, ("dp", "tensor"), scatter_dimension=0, tiled=True),
    )
    return (
        result,
        tokens_grad,
        query_grad,
        key_grad,
        value_grad,
        out_grad,
        gate_grad,
        up_grad,
        down_grad,
        first_gain_grad,
        second_gain_grad,
    )


def nn(left, right):
    return jnp.dot(left, right, preferred_element_type=jnp.float32)


def cost(flops, bytes_accessed, transcendentals):
    return pl.CostEstimate(
        flops=flops // SHARE, bytes_accessed=bytes_accessed // SHARE, transcendentals=transcendentals // SHARE
    )


def vmem_params(**more):
    return pltpu.CompilerParams(vmem_limit_bytes=VMEM_BYTES, **more)


def vmem_spec():
    return pl.BlockSpec(memory_space=pltpu.VMEM)


def spread_heads(heads_split, heads_plain):
    columns = (heads_split + heads_plain) * HD
    spread = np.zeros((columns, (heads_split + heads_plain) * LANES), np.float32)
    for head in range(heads_split + heads_plain):
        for entry in range(HD):
            lane = entry
            if head < heads_split and entry >= HD // 2:
                lane = entry - HD // 2 + LANES // 2
            spread[head * HD + entry, head * LANES + lane] = 1.0
    return jnp.asarray(spread, jnp.bfloat16)


def turn(vectors, cosine, sine):
    return vectors * cosine + pltpu.roll(vectors, LANES // 2, 1) * sine


TILE = 256


def diagonal_mask():
    row = lax.broadcasted_iota(jnp.int32, (2 * TILE, TILE), 0)
    row = jnp.where(row >= TILE, row - TILE, row)
    return row >= lax.broadcasted_iota(jnp.int32, (2 * TILE, TILE), 1)


def hbm_spec():
    return pl.BlockSpec(memory_space=pltpu.HBM)


def send(source, target, sems, where):
    copy = pltpu.make_async_remote_copy(
        src_ref=source,
        dst_ref=target,
        send_sem=sems[0],
        recv_sem=sems[1],
        device_id=where,
        device_id_type=pl.DeviceIdType.MESH,
    )
    copy.start()
    return copy


def greet(partners):
    barrier = pltpu.get_barrier_semaphore()
    for partner in partners:
        pl.semaphore_signal(barrier, inc=1, device_id=partner, device_id_type=pl.DeviceIdType.MESH)
    pl.semaphore_wait(barrier, len(partners))


def beside():
    core, across, along = (lax.axis_index(name).astype(jnp.int32) for name in ("c", "x", "y"))
    return {"c": 1 - core}, {"x": 1 - across}, {"y": 1 - along}


def grid_offset(slot, rel, deep, part):
    z_place = lax.rem(lax.axis_index("z").astype(jnp.int32) + slot, jnp.int32(deep))
    core = lax.rem(lax.axis_index("c").astype(jnp.int32) + rel, jnp.int32(2))
    return pl.multiple_of((z_place * 2 + core) * part, 64)


def spread_weight(buffer, spread_ref, wide, deep):
    part = buffer.shape[3]
    half = wide.shape[1] // 2

    @pl.loop(0, 4 * deep)
    def _(step):
        rel, slot = lax.rem(step, jnp.int32(2)), lax.rem(step // 2, jnp.int32(deep))
        side = step // (2 * deep)
        rows = pl.ds(grid_offset(slot, rel, deep, part), part)
        lanes = pl.ds(pl.multiple_of(side * half, half), half)
        wide[rows, lanes] = nn(buffer[side, slot, rel], spread_ref[...]).astype(jnp.bfloat16)


def attend_pair(qkv, heads, logs, keys, values, sequence, pair):
    count = qkv.shape[1]
    x_place = lax.axis_index("x").astype(jnp.int32)
    lane0 = pl.multiple_of(pair * 4 * LANES, 4 * LANES)
    mask = diagonal_mask()
    scale = HD ** (-0.5) * LOG2E
    for rel in range(2):
        position = lax.rem(x_place + rel, jnp.int32(2))
        rows = pl.ds(pl.multiple_of(position * count, count), count)
        keys[rows, :] = qkv[2 * sequence + rel, :, pl.ds(lane0 + 2 * LANES, LANES)]
        values[rows, :] = qkv[2 * sequence + rel, :, pl.ds(lane0 + 3 * LANES, LANES)]

    def visit(rel, start, before):
        block = 2 * sequence + rel
        rows = slice(start, start + TILE)
        queries = jnp.concatenate(
            [qkv[block, rows, pl.ds(lane0, LANES)], qkv[block, rows, pl.ds(lane0 + LANES, LANES)]], axis=0
        )
        edge = slice(before, before + TILE)
        near = jnp.where(mask, times_transposed(queries, keys[edge, :]), MASKED)
        top = jnp.max(near, axis=-1, keepdims=True)
        if before:
            far = times_transposed(queries, keys[:before, :])
            top = jnp.maximum(top, jnp.max(far, axis=-1, keepdims=True))
        top = top * scale
        near = jnp.exp2(near * scale - top)
        total = jnp.sum(near, axis=-1, keepdims=True)
        mixed = nn(near.astype(jnp.bfloat16), values[edge, :])
        if before:
            far = jnp.exp2(far * scale - top)
            total = total + jnp.sum(far, axis=-1, keepdims=True)
            mixed = mixed + nn(far.astype(jnp.bfloat16), values[:before, :])
        mixed = (mixed / total).astype(jnp.bfloat16)
        log = top + jnp.log2(total)
        lane = lax.broadcasted_iota(jnp.int32, (TILE, LANES), 1)
        kept = logs[block, rows, :]
        for head in range(2):
            part = slice(head * TILE, (head + 1) * TILE)
            out_lane = pl.multiple_of(pair * 2 * LANES, LANES) + head * LANES
            heads[block, rows, pl.ds(out_lane, LANES)] = mixed[part]
            kept = jnp.where(lane == 2 * pair + head, log[part], kept)
        logs[block, rows, :] = kept

    for rel in range(2):
        position = lax.rem(x_place + rel, jnp.int32(2))
        for static_position in range(2):

            @pl.when(position == static_position)
            def _(rel=rel, static_position=static_position):
                for step in range(count // TILE):
                    visit(rel, step * TILE, static_position * count + step * TILE)


def forward_kernel(
    deep, cotangent_ref, tokens_ref, gains_ref, all_halves,
    qkv_spread, out_spread, cosine_ref, sine_ref,
    first_out, qkv_out, heads_out, logs_out, qkv_wide_out, out_wide_out, middle_out, second_out,
    cotangent_out, feed_out, qkv_own_out,
    first_all, qkv_buffer, out_buffer, qkv_wide, out_wide, qkv, heads, logs, keys, values,
    parts, core_parts, outgoing, incoming, middle, second,
    local_sems, row_sems, qkv_sems, out_sems, feed_sems, core_sems,
):
    core, z_place = lax.axis_index("c").astype(jnp.int32), lax.axis_index("z").astype(jnp.int32)
    core_beside, x_beside, y_beside = beside()
    count = tokens_ref.shape[0]
    ring = jnp.int32(deep)
    feed_lanes, qkv_lanes, out_lanes = (
        buffer.shape[-1] for buffer in (feed_out, qkv_buffer, out_buffer)
    )
    feed_halves = all_halves.at[:, :, pl.ds(0, feed_lanes)]
    qkv_halves = all_halves.at[:, :, pl.ds(feed_lanes, qkv_lanes)]
    out_halves = all_halves.at[:, :, pl.ds(feed_lanes + qkv_lanes, out_lanes)]
    z_beside = {way: {"z": lax.rem(z_place + deep + way, ring)} for way in (-1, 1)}
    greet([core_beside, x_beside, y_beside, z_beside[-1], z_beside[1]])

    kept = []
    sent = []

    def keep_local(source, target, index):
        copy = pltpu.make_async_copy(source, target, local_sems.at[index])
        copy.start()
        return copy

    def pair_of(sems, index):
        return sems.at[0, index], sems.at[1, index]

    def move(source, target, sems, index, where):
        copy = send(source, target, pair_of(sems, index), where)
        sent.append(copy)
        return copy

    qkv_core = move(qkv_halves.at[1 - core], qkv_buffer.at[0, 0, 1], qkv_sems, 0, core_beside)
    qkv_kept = keep_local(qkv_halves.at[core], qkv_buffer.at[0, 0, 0], 0)
    step_rows = 128

    @pl.loop(0, count // step_rows)
    def _(step):
        rows = pl.ds(pl.multiple_of(step * step_rows, step_rows), step_rows)
        value = tokens_ref[rows, :].astype(jnp.float32)
        first_all[0, rows, :] = (value * norm_factor(value) * gains_ref[0:1, :]).astype(jnp.bfloat16)

    first_x = move(first_all.at[0], first_all.at[1], row_sems, 0, x_beside)
    out_core = move(out_halves.at[1 - core], out_buffer.at[0, 0, 1], out_sems, 0, core_beside)
    out_kept = keep_local(out_halves.at[core], out_buffer.at[0, 0, 0], 1)
    feed_core = move(feed_halves.at[1 - core], feed_out.at[0, 0, 1], feed_sems, 0, core_beside)
    feed_kept = keep_local(feed_halves.at[core], feed_out.at[0, 0, 0], 2)
    first_core = move(first_all.at[0], first_all.at[2], row_sems, 1, core_beside)
    cotangent_kept = keep_local(cotangent_ref, cotangent_out.at[0], 4)

    last = deep - 1

    def z_copy(buffer, sems, upward, step, rel):
        source, target = ((deep - step) % deep, last - step) if upward else (step, step + 1)
        return pltpu.make_async_remote_copy(
            src_ref=buffer.at[0, source, rel],
            dst_ref=buffer.at[0, target, rel],
            send_sem=sems.at[0, 2 * (1 + upward * last + step) + rel],
            recv_sem=sems.at[1, 2 * target + rel],
            device_id=z_beside[1 if upward else -1],
            device_id_type=pl.DeviceIdType.MESH,
        )

    def z_sends(upward, step):
        if upward:
            return (z_place <= last - 1) & (z_place - step >= 0)
        return (z_place >= 1) & (z_place + step <= last)

    def z_start(buffer, sems, upward, step, rel):
        @pl.when(z_sends(upward, step))
        def _():
            z_copy(buffer, sems, upward, step, rel).start()

    def open_z(buffer, sems):
        for rel in range(2):
            z_start(buffer, sems, False, 0, rel)
            z_start(buffer, sems, True, 0, rel)

    def y_copy(buffer, sems, slot, rel):
        return pltpu.make_async_remote_copy(
            src_ref=buffer.at[0, slot, rel],
            dst_ref=buffer.at[1, slot, rel],
            send_sem=sems.at[0, 2 * (2 * deep + slot) + rel],
            recv_sem=sems.at[1, 2 * (2 * deep + slot) + rel],
            device_id=y_beside,
            device_id_type=pl.DeviceIdType.MESH,
        )

    def open_y(buffer, sems):
        for rel in range(2):
            y_copy(buffer, sems, 0, rel).start()

    def z_part(buffer, sems, step, rel):
        for upward in (False, True):
            slot = last - step if upward else step + 1
            arrives = z_place - step - 1 >= 0 if upward else z_place + step + 1 <= last

            @pl.when(arrives)
            def _(upward=upward, slot=slot):
                z_copy(buffer, sems, upward, step, rel).wait_recv()
                if step + 1 < last:
                    z_start(buffer, sems, upward, step + 1, rel)
                y_copy(buffer, sems, slot, rel).start()

    def z_step(buffer, sems, step):
        for rel in range(2):
            z_part(buffer, sems, step, rel)

    def y_wait(buffer, sems):
        for slot in range(deep):
            for rel in range(2):
                y_copy(buffer, sems, slot, rel).wait_recv()

    def close(buffer, sems):
        for rel in range(2):
            for slot in range(deep):
                y_copy(buffer, sems, slot, rel).wait_send()
            for upward in (False, True):
                for step in range(last):

                    @pl.when(z_sends(upward, step))
                    def _(upward=upward, step=step, rel=rel):
                        z_copy(buffer, sems, upward, step, rel).wait_send()

    qkv_z, out_z, feed_z = (qkv_buffer, qkv_sems), (out_buffer, out_sems), (feed_out, feed_sems)
    qkv_core.wait_recv()
    qkv_kept.wait()
    open_z(*qkv_z)
    open_y(*qkv_z)
    out_core.wait_recv()
    out_kept.wait()
    feed_core.wait_recv()
    feed_kept.wait()
    kept.append(keep_local(qkv_buffer.at[0, 0], qkv_own_out, 13))
    for step in range(last):
        z_step(*qkv_z, step)
        if step == last - 2:
            open_z(*out_z)
    open_y(*out_z)
    for step in range(last):
        z_step(*out_z, step)
    open_z(*feed_z)
    open_y(*feed_z)
    first_x.wait_recv()
    first_far = move(first_all.at[1], first_all.at[3], row_sems, 2, core_beside)
    cotangent_x = move(cotangent_ref, cotangent_out.at[1], row_sems, 3, x_beside)
    cotangent_core = move(cotangent_ref, cotangent_out.at[2], row_sems, 4, core_beside)
    y_wait(*qkv_z)

    spread_weight(qkv_buffer, qkv_spread, qkv_wide, deep)
    kept.append(keep_local(qkv_wide, qkv_wide_out, 5))
    first_core.wait_recv()
    first_far.wait_recv()
    kept.append(keep_local(first_all, first_out, 6))

    @pl.loop(0, 8)
    def _(step):
        block, pair = step // 2, lax.rem(step, jnp.int32(2))
        lane0 = pl.multiple_of(pair * 4 * LANES, 4 * LANES)
        product = nn(first_all[block], qkv_wide[:, pl.ds(lane0, 4 * LANES)])
        position = lax.rem(lax.axis_index("x").astype(jnp.int32) + block, jnp.int32(2))
        cosine, sine = cosine_ref[position], sine_ref[position]
        for head in range(4):
            part = product[:, head * LANES : (head + 1) * LANES]
            if head < 3:
                part = turn(part, cosine, sine)
            qkv[block, :, pl.ds(lane0 + head * LANES, LANES)] = part.astype(jnp.bfloat16)

    kept.append(keep_local(qkv, qkv_out, 7))
    z_part(*feed_z, 0, 0)
    logs[...] = jnp.zeros_like(logs)
    for sequence in range(2):

        @pl.loop(0, 2)
        def _(pair, sequence=sequence):
            attend_pair(qkv, heads, logs, keys, values, sequence, pair)

        if sequence == 0:
            z_part(*feed_z, 0, 1)

    kept.append(keep_local(heads, heads_out, 8))
    kept.append(keep_local(logs, logs_out, 9))
    y_wait(*out_z)
    spread_weight(out_buffer, out_spread, out_wide, deep)
    kept.append(keep_local(out_wide, out_wide_out, 10))

    def out_part(block):
        @pl.loop(0, out_wide.shape[0] // 512)
        def _(step):
            lanes = pl.ds(pl.multiple_of(step * 512, 512), 512)
            parts[block, :, lanes] = times_transposed(heads[block], out_wide[lanes, :]).astype(jnp.bfloat16)

    out_part(3)
    core_far = move(parts.at[3], core_parts.at[1], core_sems, 0, core_beside)
    out_part(1)
    core_far.wait_recv()

    @pl.loop(0, count // step_rows)
    def _(step):
        rows = pl.ds(pl.multiple_of(step * step_rows, step_rows), step_rows)
        outgoing[rows, :] = (
            parts[1, rows, :].astype(jnp.float32) + core_parts[1, rows, :].astype(jnp.float32)
        ).astype(jnp.bfloat16)

    branch_x = move(outgoing, incoming, core_sems, 1, x_beside)
    out_part(2)
    core_near = move(parts.at[2], core_parts.at[0], core_sems, 2, core_beside)
    out_part(0)
    core_near.wait_recv()
    z_step(*feed_z, 1)
    branch_x.wait_recv()

    @pl.loop(0, count // step_rows)
    def _(step):
        rows = pl.ds(pl.multiple_of(step * step_rows, step_rows), step_rows)
        total = (
            tokens_ref[rows, :].astype(jnp.float32)
            + parts[0, rows, :].astype(jnp.float32)
            + core_parts[0, rows, :].astype(jnp.float32)
            + incoming[rows, :].astype(jnp.float32)
        )
        middle[rows, :] = total
        second[rows, :] = (total * norm_factor(total) * gains_ref[1:2, :]).astype(jnp.bfloat16)

    kept.append(keep_local(middle, middle_out, 11))
    kept.append(keep_local(second, second_out.at[0], 12))
    second_x = move(second, second_out.at[1], row_sems, 5, x_beside)
    second_core = move(second, second_out.at[2], row_sems, 6, core_beside)
    cotangent_x.wait_recv()
    cotangent_far = move(cotangent_out.at[1], cotangent_out.at[3], row_sems, 7, core_beside)
    z_step(*feed_z, 2)
    second_x.wait_recv()
    second_far = move(second_out.at[1], second_out.at[3], row_sems, 8, core_beside)
    for copy in (second_core, second_far, cotangent_core, cotangent_far):
        copy.wait_recv()
    y_wait(*feed_z)
    for copy in kept + [cotangent_kept]:
        copy.wait()
    for copy in sent:
        copy.wait_send()
    for which in (qkv_z, out_z, feed_z):
        close(*which)


def forward(deep, cotangent, tokens, gains, halves, sizes, spreads, cosine, sine):
    count, width = tokens.shape
    part = halves.shape[1]
    feed_size, qkv_size, out_size = sizes

    def shape(*dims, kind=jnp.bfloat16):
        return jax.ShapeDtypeStruct(dims, kind)

    def room(*dims, kind=jnp.bfloat16):
        return pltpu.VMEM(dims, kind)

    qkv_lanes, out_lanes = 2 * spreads[0].shape[1], 2 * spreads[1].shape[1]
    outs = (
        shape(4, count, width),
        shape(4, count, qkv_lanes),
        shape(4, count, out_lanes),
        shape(4, count, LANES, kind=jnp.float32),
        shape(width, qkv_lanes),
        shape(width, out_lanes),
        shape(count, width, kind=jnp.float32),
        shape(4, count, width),
        shape(4, count, width),
        shape(2, deep, 2, part, feed_size),
        shape(2, part, qkv_size),
    )
    scratch = [
        room(4, count, width),
        room(2, deep, 2, part, qkv_size),
        room(2, deep, 2, part, out_size),
        room(width, qkv_lanes),
        room(width, out_lanes),
        room(4, count, qkv_lanes),
        room(4, count, out_lanes),
        room(4, count, LANES, kind=jnp.float32),
        room(2 * count, LANES),
        room(2 * count, LANES),
        room(4, count, width),
        room(2, count, width),
        room(count, width),
        room(count, width),
        room(count, width, kind=jnp.float32),
        room(count, width),
        pltpu.SemaphoreType.DMA((14,)),
        pltpu.SemaphoreType.DMA((2, 9)),
        pltpu.SemaphoreType.DMA((2, 6 * deep)),
        pltpu.SemaphoreType.DMA((2, 6 * deep)),
        pltpu.SemaphoreType.DMA((2, 6 * deep)),
        pltpu.SemaphoreType.DMA((2, 3)),
    ]
    return pl.pallas_call(
        functools.partial(forward_kernel, deep),
        out_shape=outs,
        in_specs=[hbm_spec(), vmem_spec(), vmem_spec(), hbm_spec()] + [vmem_spec()] * 4,
        out_specs=(hbm_spec(),) * len(outs),
        scratch_shapes=scratch,
        compiler_params=vmem_params(collective_id=1, has_side_effects=True),
        cost_estimate=cost(flops=20 * 10**9, bytes_accessed=10**8, transcendentals=10**7),
        name="forward",
    )(cotangent, tokens, gains, halves, *spreads, cosine, sine)


EARLY = 6


def ring_row(shift, deep, rows):
    z_place = lax.rem(lax.axis_index("z").astype(jnp.int32) + shift, jnp.int32(deep))
    return pl.multiple_of(z_place * rows, rows)


def add_rows(target, source, step_rows=128):
    @pl.loop(0, target.shape[0] // step_rows)
    def _(step):
        rows = pl.ds(pl.multiple_of(step * step_rows, step_rows), step_rows)
        target[rows, :] = (target[rows, :].astype(jnp.float32) + source[rows, :].astype(jnp.float32)).astype(
            jnp.bfloat16
        )


def ahead(deep):
    z_place = lax.axis_index("z").astype(jnp.int32)
    return [{"z": lax.rem(z_place + shift, jnp.int32(deep))} for shift in range(deep)]


def pieces_of(deep):
    return [(piece, shift) for piece in range(3) for shift in range(deep)]


def feed_back_kernel(
    deep, rows_hbm, grads_hbm, chunks, middle_hbm, gain_ref,
    grad_middle_out, grad_attention_out, branch_out, sent_out, own_out, sum_out, arrived_out,
    gate, up, down, rows, grads, hidden, grad_gate, grad_up, parts, landing, incoming, middle, stage,
    early_y, load_sems, weight_sems, store_sems, sum_sems, early_sems, core_sems, x_sems, y_sems, z_sems,
):
    core_beside, x_beside, y_beside = beside()
    z_ahead = ahead(deep)
    greet([core_beside, x_beside, y_beside] + z_ahead[1:])
    blocks, count, width = rows.shape
    half = gate.shape[1] // 2
    part = chunks.shape[3]
    piece_rows = 2 * part
    sent = []

    def load(source, target, sem):
        copy = pltpu.make_async_copy(source, target, sem)
        copy.start()
        return copy

    def move(source, target, sems, index, where):
        copy = send(source, target, (sems.at[0, index], sems.at[1, index]), where)
        sent.append(copy)
        return copy

    row_loads = {}
    for block in (3, 1):
        row_loads[block] = [load(rows_hbm.at[block], rows.at[block], load_sems.at[0, block])]
    weight_loads = []
    for matrix, target in enumerate((gate, up, down)):
        here = []
        for side in range(2):
            for shift in range(deep):
                for rel in range(2):
                    here.append(
                        load(
                            chunks.at[side, shift, rel, :, pl.ds(matrix * half, half)],
                            target.at[pl.ds(grid_offset(shift, rel, deep, part), part), pl.ds(side * half, half)],
                            weight_sems.at[matrix, side, shift, rel],
                        )
                    )
        weight_loads.append(here)
        if matrix == 0:
            for block in (3, 1):
                row_loads[block].append(load(grads_hbm.at[block], grads.at[block], load_sems.at[1, block]))
    for block in (2, 0):
        row_loads[block] = [
            load(rows_hbm.at[block], rows.at[block], load_sems.at[0, block]),
            load(grads_hbm.at[block], grads.at[block], load_sems.at[1, block]),
        ]
    middle_load = load(middle_hbm, middle, load_sems.at[0, 4])

    def inner(block):
        @pl.loop(0, gate.shape[1] // TILE)
        def _(step):
            lanes = pl.ds(pl.multiple_of(step * TILE, TILE), TILE)
            gate_value = nn(rows[block], gate[:, lanes])
            up_value = nn(rows[block], up[:, lanes])
            grad_hidden = nn(grads[block], down[:, lanes])
            sigmoid = 1.0 / (1.0 + jnp.exp(-gate_value))
            swish = gate_value * sigmoid
            slope = sigmoid + swish * (1.0 - sigmoid)
            hidden[block, :, lanes] = (swish * up_value).astype(jnp.bfloat16)
            grad_gate[block, :, lanes] = (grad_hidden * up_value * slope).astype(jnp.bfloat16)
            grad_up[block, :, lanes] = (grad_hidden * swish).astype(jnp.bfloat16)

    def outer(block):
        @pl.loop(0, width // TILE)
        def _(step):
            lanes = pl.ds(pl.multiple_of(step * TILE, TILE), TILE)
            parts[block, :, lanes] = (
                times_transposed(grad_gate[block], gate[lanes, :])
                + times_transposed(grad_up[block], up[lanes, :])
            ).astype(jnp.bfloat16)

    for position, block in enumerate((3, 1, 2, 0)):
        for copy in row_loads[block]:
            copy.wait()
        if position == 0:
            for here in weight_loads:
                for copy in here:
                    copy.wait()
        inner(block)
        if block in (3, 1):
            outer(block)
        if block == 3:
            far = move(parts.at[3], landing.at[1], core_sems, 0, core_beside)
        if block == 1:
            far.wait_recv()
            add_rows(parts.at[1], landing.at[1])
            across = move(parts.at[1], incoming, x_sems, 0, x_beside)

    sources = ((grads, hidden), (rows, grad_gate), (rows, grad_up))

    def weight_part(piece, side, shift):
        left, right = sources[piece]
        row = ring_row(shift, deep, piece_rows)
        lanes = slice(side * half, (side + 1) * half)
        return transposed_times(
            left[:, :, pl.ds(row, piece_rows)].reshape(blocks * count, piece_rows),
            right[:, :, lanes].reshape(blocks * count, half),
        )

    def weight_stage(piece, side, shift):
        row = ring_row(shift, deep, piece_rows)
        stage[piece, pl.ds(row, piece_rows), :] = weight_part(piece, side, shift).astype(jnp.bfloat16)

    early = pieces_of(deep)[:EARLY]
    arrivals, stores, pending = [], [], []

    def flush():
        for index, store, target in pending:
            store.wait()
            arrivals.append(move(target, early_y.at[index], y_sems, index, y_beside))
        pending.clear()

    def send_piece(piece):
        for shift in range(deep):
            weight_stage(piece, 1, shift)
            flush()
            rows_here = pl.ds(ring_row(shift, deep, piece_rows), piece_rows)
            target = sent_out.at[piece, rows_here, :]
            store = load(stage.at[piece, rows_here, :], target, early_sems.at[piece * deep + shift])
            if (piece, shift) in early:
                pending.append((early.index((piece, shift)), store, target))
            else:
                stores.append(store)

    send_piece(0)
    outer(2)
    flush()
    near = move(parts.at[2], landing.at[0], core_sems, 1, core_beside)
    outer(0)
    send_piece(1)
    send_piece(2)
    flush()
    late_stores = list(stores)
    near.wait_recv()
    middle_load.wait()
    across.wait_recv()
    step_rows = 128

    @pl.loop(0, count // step_rows)
    def _(step):
        tile = pl.ds(pl.multiple_of(step * step_rows, step_rows), step_rows)
        grad = (
            parts[0, tile, :].astype(jnp.float32)
            + landing[0, tile, :].astype(jnp.float32)
            + incoming[tile, :].astype(jnp.float32)
        )
        total = grads[0, tile, :].astype(jnp.float32) + norm_back(middle[tile, :], gain_ref[1:2, :], grad)
        middle[tile, :] = total
        incoming[tile, :] = total.astype(jnp.bfloat16)

    attention_x = move(incoming, grad_attention_out.at[1], x_sems, 1, x_beside)
    attention_core = move(incoming, grad_attention_out.at[2], core_sems, 2, core_beside)
    stores.append(load(incoming, grad_attention_out.at[0], store_sems.at[0]))
    stores.append(load(middle, grad_middle_out, store_sems.at[3]))

    hops = []

    def join_early(pairs):
        for piece, shift in pairs:
            index = early.index((piece, shift))
            product = weight_part(piece, 0, shift)
            arrivals[index].wait_recv()
            early_y[index] = (product + early_y[index].astype(jnp.float32)).astype(jnp.bfloat16)
            if piece == 0 and shift:
                hops.append(
                    move(early_y.at[index], arrived_out.at[shift - 1], z_sems, shift, z_ahead[shift])
                )
            else:
                stores.append(load(early_y.at[index], sum_out.at[index], sum_sems.at[index]))

    join_early(early[:-2])
    far.wait_send()
    across.wait_send()
    near.wait_send()

    def branch(block):
        @pl.loop(0, width // TILE)
        def _(step):
            lanes = pl.ds(pl.multiple_of(step * TILE, TILE), TILE)
            parts[block, :, lanes] = times_transposed(hidden[block], down[lanes, :]).astype(jnp.bfloat16)

    branch(3)
    attention_core.wait_recv()
    branch_far = move(parts.at[3], landing.at[1], core_sems, 3, core_beside)
    branch(2)
    branch_near = move(parts.at[2], landing.at[0], core_sems, 4, core_beside)
    branch(1)
    branch_far.wait_recv()
    add_rows(parts.at[1], landing.at[1])
    stores.append(load(parts.at[1], branch_out.at[1], store_sems.at[7]))
    branch(0)
    stores.append(load(parts.at[0], branch_out.at[0], store_sems.at[8]))
    branch_near.wait_recv()
    stores.append(load(landing.at[0], branch_out.at[2], store_sems.at[9]))
    for copy in late_stores:
        copy.wait()
    for piece in range(3):
        for shift in range(deep):
            if (piece, shift) not in early:
                weight_stage(piece, 0, shift)
                rows_here = pl.ds(ring_row(shift, deep, piece_rows), piece_rows)
                stores.append(
                    load(
                        stage.at[piece, rows_here, :],
                        own_out.at[piece, rows_here, :],
                        early_sems.at[(3 + piece) * deep + shift],
                    )
                )
    join_early(early[-2:])
    attention_x.wait_recv()
    attention_far = move(grad_attention_out.at[1], grad_attention_out.at[3], core_sems, 5, core_beside)
    attention_far.wait_recv()
    for copy in hops:
        copy.wait_recv()
    for copy in stores[len(late_stores) :]:
        copy.wait()
    for copy in arrivals + hops:
        copy.wait_send()
    for copy in (attention_x, attention_core, branch_far, branch_near, attention_far):
        copy.wait_send()


def feed_back(deep, rows, grads, chunks, middle, gain):
    blocks, count, width = rows.shape
    half = chunks.shape[4] // 3
    part = chunks.shape[3]

    def shape(*dims, kind=jnp.bfloat16):
        return jax.ShapeDtypeStruct(dims, kind)

    def room(*dims, kind=jnp.bfloat16):
        return pltpu.VMEM(dims, kind)

    outs = (
        shape(count, width, kind=jnp.float32),
        shape(blocks, count, width),
        shape(3, count, width),
        shape(3, width, half),
        shape(3, width, half),
        shape(EARLY, 2 * part, half),
        shape(deep - 1, 2 * part, half),
    )
    dma = pltpu.SemaphoreType.DMA
    return pl.pallas_call(
        functools.partial(feed_back_kernel, deep),
        out_shape=outs,
        in_specs=[hbm_spec()] * 4 + [vmem_spec()],
        out_specs=(hbm_spec(),) * len(outs),
        scratch_shapes=[room(width, 2 * half)] * 3
        + [room(blocks, count, width)] * 2
        + [room(blocks, count, 2 * half)] * 3
        + [room(blocks, count, width), room(2, count, width), room(count, width)]
        + [room(count, width, kind=jnp.float32), room(3, width, half), room(EARLY, 2 * part, half)]
        + [dma((2, 5)), dma((3, 2, deep, 2)), dma((10,)), dma((EARLY,)), dma((6 * deep,)), dma((2, 6)), dma((2, 2)), dma((2, EARLY)), dma((2, EARLY))],
        compiler_params=vmem_params(collective_id=2, has_side_effects=True),
        cost_estimate=cost(flops=80 * 10**9, bytes_accessed=10**8, transcendentals=10**7),
        name="feed_back",
    )(rows, grads, chunks, middle, gain)


def attend_back_pair(
    qkv, grad_heads, heads, logs, cosine_ref, sine_ref, grad_qkv, keys, values, grad_keys, grad_values,
    sequence, pair,
):
    count = qkv.shape[1]
    x_place = lax.axis_index("x").astype(jnp.int32)
    lane0 = pl.multiple_of(pair * 4 * LANES, 4 * LANES)
    head0 = pl.multiple_of(pair * 2 * LANES, 2 * LANES)
    mask = diagonal_mask()
    factor = HD ** (-0.5)
    scale = factor * LOG2E
    for rel in range(2):
        position = lax.rem(x_place + rel, jnp.int32(2))
        rows = pl.ds(pl.multiple_of(position * count, count), count)
        keys[rows, :] = qkv[2 * sequence + rel, :, pl.ds(lane0 + 2 * LANES, LANES)]
        values[rows, :] = qkv[2 * sequence + rel, :, pl.ds(lane0 + 3 * LANES, LANES)]
    grad_keys[...] = jnp.zeros_like(grad_keys)
    grad_values[...] = jnp.zeros_like(grad_values)

    def visit(rel, start, before):
        block = 2 * sequence + rel
        rows = slice(start, start + TILE)

        def both(ref, first):
            return jnp.concatenate(
                [ref[block, rows, pl.ds(first, LANES)], ref[block, rows, pl.ds(first + LANES, LANES)]], axis=0
            )

        queries, grads, outs = both(qkv, lane0), both(grad_heads, head0), both(heads, head0)
        lane = lax.broadcasted_iota(jnp.int32, (TILE, LANES), 1)
        kept = logs[block, rows, :]
        log = jnp.concatenate(
            [
                jnp.sum(jnp.where(lane == 2 * pair + head, kept, 0.0), axis=-1, keepdims=True)
                for head in range(2)
            ],
            axis=0,
        )
        inner = jnp.sum(grads.astype(jnp.float32) * outs.astype(jnp.float32), axis=-1, keepdims=True)

        def span(span_rows, masked):
            softmax = jnp.exp2(times_transposed(queries, keys[span_rows, :]) * scale - log)
            if masked:
                softmax = jnp.where(mask, softmax, 0.0)
            grad_softmax = times_transposed(grads, values[span_rows, :])
            grad_scores = (softmax * (grad_softmax - inner)).astype(jnp.bfloat16)
            grad_values[span_rows, :] += transposed_times(softmax.astype(jnp.bfloat16), grads)
            grad_keys[span_rows, :] += transposed_times(grad_scores, queries)
            return nn(grad_scores, keys[span_rows, :])

        grad_queries = span(slice(before, before + TILE), True)
        if before:
            grad_queries = grad_queries + span(slice(0, before), False)
        position, table_rows = before // count, slice(before % count, before % count + TILE)
        cosine, sine = cosine_ref[position, table_rows, :], -sine_ref[position, table_rows, :]
        for head in range(2):
            piece = grad_queries[head * TILE : (head + 1) * TILE] * factor
            grad_qkv[block, rows, pl.ds(lane0 + head * LANES, LANES)] = turn(piece, cosine, sine).astype(
                jnp.bfloat16
            )

    for rel in range(2):
        position = lax.rem(x_place + rel, jnp.int32(2))
        for static_position in range(2):

            @pl.when(position == static_position)
            def _(rel=rel, static_position=static_position):
                for step in range(count // TILE):
                    visit(rel, step * TILE, static_position * count + step * TILE)

    for rel in range(2):
        block = 2 * sequence + rel
        position = lax.rem(x_place + rel, jnp.int32(2))
        rows = pl.ds(pl.multiple_of(position * count, count), count)
        grad_qkv[block, :, pl.ds(lane0 + 2 * LANES, LANES)] = turn(
            grad_keys[rows, :] * factor, cosine_ref[position], -sine_ref[position]
        ).astype(jnp.bfloat16)
        grad_qkv[block, :, pl.ds(lane0 + 3 * LANES, LANES)] = grad_values[rows, :].astype(jnp.bfloat16)


def heads_back_kernel(
    deep, grad_attention_hbm, qkv_hbm, heads_hbm, logs_hbm, first_hbm, qkv_wide_hbm, out_wide_hbm,
    branch_hbm, sent_hbm, own_hbm, sum_hbm, arrived_hbm, chunks_hbm, qkv_own_hbm,
    cosine_ref, sine_ref, qkv_spread, out_spread,
    first_part, first_core, first_x, branch_x, feed_final, qkv_final, out_final, first_gain_out, second_gain_out,
    grad_attention, qkv, heads, grad_heads, logs, grad_qkv, qkv_wide, out_wide, keys, values, grad_keys,
    grad_values, slots, landing, feed_sum, feed_y, feed_z, out_sent, out_sum, out_y, out_z, qkv_sent, qkv_sum, qkv_y,
    qkv_z, feed_last, qkv_last, out_last, feed_weight, qkv_weight, gain_part, gain_in, gain_total,
    load_sems, own_sems, tile_sems, core_sems, x_sems, y_sems, z_sems, gain_sems,
):
    blocks, count, width = grad_attention.shape
    core_beside, x_beside, y_beside = beside()
    core = lax.axis_index("c").astype(jnp.int32)
    across, along = lax.axis_index("x").astype(jnp.int32), lax.axis_index("y").astype(jnp.int32)
    z_ahead = ahead(deep)
    cube = {
        (rel, up, over): {"c": (core + rel) % 2, "y": (along + up) % 2, "x": (across + over) % 2}
        for rel in range(2)
        for up in range(2)
        for over in range(2)
    }
    far_cube = [key for key in cube if key != (0, 0, 0)]
    greet([cube[key] for key in far_cube] + z_ahead[1:])
    half = feed_sum.shape[3]
    piece_rows = feed_sum.shape[2]
    part = piece_rows // 2
    step_rows = 128
    sent = []

    def load(source, target, sem):
        copy = pltpu.make_async_copy(source, target, sem)
        copy.start()
        return copy

    def move(source, target, sems, index, where):
        copy = send(source, target, (sems.at[0, index], sems.at[1, index]), where)
        sent.append(copy)
        return copy

    late = pieces_of(deep)[EARLY:]
    attention_load = load(grad_attention_hbm, grad_attention, load_sems.at[0])
    out_load = load(out_wide_hbm, out_wide, load_sems.at[1])
    heads_load = load(heads_hbm, heads, load_sems.at[2])
    late_copies = []
    for index, (piece, shift) in enumerate(late):
        row = ring_row(shift, deep, piece_rows)
        late_copies.append(
            move(
                sent_hbm.at[piece, pl.ds(row, piece_rows), :], feed_y.at[piece, shift], y_sems, index, y_beside
            )
        )
    branch_copy = move(branch_hbm.at[1], branch_x, x_sems, 0, x_beside)
    qkv_load = load(qkv_hbm, qkv, load_sems.at[3])
    logs_load = load(logs_hbm, logs, load_sems.at[4])
    wide_load = load(qkv_wide_hbm, qkv_wide, load_sems.at[5])
    own_loads, z_copies = {}, {}
    early_loads = []
    for index, (piece, shift) in enumerate(pieces_of(deep)):
        if (piece, shift) in late:
            row = ring_row(shift, deep, piece_rows)
            own_loads[piece, shift] = load(
                own_hbm.at[piece, pl.ds(row, piece_rows), :], feed_sum.at[piece, shift], own_sems.at[0, index]
            )
        elif shift == 0:
            early_loads.append(load(sum_hbm.at[index], feed_sum.at[piece, 0], own_sems.at[1, index]))
        elif piece == 0:
            early_loads.append(
                load(arrived_hbm.at[shift - 1], feed_z.at[piece, shift - 1], own_sems.at[1, index])
            )
        else:
            z_copies[piece, shift] = move(
                sum_hbm.at[index],
                feed_z.at[piece, shift - 1],
                z_sems,
                piece * (deep - 1) + shift - 1,
                z_ahead[shift],
            )
    weight_loads = [
        load(chunks_hbm.at[0, 0, :, :, pl.ds(0, 2 * half)], feed_weight, load_sems.at[6]),
        load(qkv_own_hbm, qkv_weight, load_sems.at[7]),
    ]

    attention_load.wait()
    out_load.wait()

    @pl.loop(0, blocks)
    def _(block):
        grad_heads[block] = nn(grad_attention[block], out_wide[...]).astype(jnp.bfloat16)

    heads_load.wait()

    def weight_tile(left, right, spread, side):
        size = spread.shape[1]
        right = right[:, :, side * size : (side + 1) * size].reshape(blocks * count, size)
        product = transposed_times(left.reshape(blocks * count, piece_rows), right)
        return times_transposed(product.astype(jnp.bfloat16), spread[...]).astype(jnp.bfloat16)

    def join_piece(name, number, total, arrived, target, shift):
        add_rows(total.at[shift], arrived.at[shift])
        if shift:
            z_copies[name, shift] = move(
                total.at[shift], target.at[shift - 1], z_sems, number * (deep - 1) + shift - 1, z_ahead[shift]
            )

    def join_feed(piece, shift):
        own_loads[piece, shift].wait()
        join_piece(piece, piece, feed_sum.at[piece], feed_y.at[piece], feed_z.at[piece], shift)

    def join_feed_late(index):
        late_copies[index].wait_recv()
        join_feed(*late[index])

    qkv_load.wait()
    logs_load.wait()
    for sequence in range(2):

        for pair in range(2):
            attend_back_pair(
                qkv, grad_heads, heads, logs, cosine_ref, sine_ref, grad_qkv, keys, values, grad_keys,
                grad_values, sequence, pair,
            )
            join_feed_late(2 * sequence + pair)
    wide_load.wait()

    def first_tile(shift):
        row = ring_row(shift, deep, piece_rows)
        slot = (shift % 2) * 512
        return load(
            first_hbm.at[:, :, pl.ds(row, piece_rows)],
            qkv.at[:, :, pl.ds(slot, piece_rows)],
            tile_sems.at[shift],
        )

    first_loads = [first_tile(shift) for shift in range(2)]

    def first_piece(block):
        @pl.loop(0, width // 512)
        def _(step):
            lanes = pl.ds(pl.multiple_of(step * 512, 512), 512)
            slots[block % 3, :, lanes] = times_transposed(grad_qkv[block], qkv_wide[lanes, :]).astype(
                jnp.bfloat16
            )

    first_piece(3)
    core_far = move(slots.at[0], landing, core_sems, 0, core_beside)
    first_piece(1)
    core_far.wait_recv()
    add_rows(slots.at[1], landing)
    x_copy = move(slots.at[1], first_x, x_sems, 1, x_beside)
    first_piece(2)
    core_near = move(slots.at[2], first_core, core_sems, 1, core_beside)
    core_far.wait_send()
    sent[:] = [copy for copy in sent if copy is not core_far]
    first_piece(0)
    first_store = load(slots.at[0], first_part, load_sems.at[8])
    join_feed_late(4)
    y_index = len(late)
    out_copies = []
    for shift in range(deep):
        row = ring_row(shift, deep, piece_rows)
        out_sent[shift] = weight_tile(grad_attention[:, :, pl.ds(row, piece_rows)], heads, out_spread, 1)
        out_copies.append(move(out_sent.at[shift], out_y.at[shift], y_sems, y_index + shift, y_beside))

    @pl.loop(0, deep)
    def _(shift):
        row = ring_row(shift, deep, piece_rows)
        out_sum[shift] = weight_tile(grad_attention[:, :, pl.ds(row, piece_rows)], heads, out_spread, 0)

    join_feed_late(5)

    qkv_copies = []
    y_index += deep
    for shift in range(deep):
        first_loads[shift].wait()
        slot = (shift % 2) * 512
        left = qkv[:, :, slot : slot + piece_rows]
        qkv_sent[shift] = weight_tile(left, grad_qkv, qkv_spread, 1)
        qkv_copies.append(move(qkv_sent.at[shift], qkv_y.at[shift], y_sems, y_index + shift, y_beside))
        qkv_sum[shift] = weight_tile(left, grad_qkv, qkv_spread, 0)
        if shift + 2 < deep:
            first_loads.append(first_tile(shift + 2))

    for shift in range(deep):
        out_copies[shift].wait_recv()
        join_piece("out", 3, out_sum, out_y, out_z, shift)

    finals = []

    def finish(name, number, total, arrived, last, final, weights):
        for shift in range(1, deep):
            if (name, shift) in z_copies:
                z_copies[name, shift].wait_recv()
        size = total.shape[2]
        sums = []
        for rel in range(2):
            row = pl.multiple_of(lax.rem(core + rel, jnp.int32(2)) * part, part)
            value = total[0, pl.ds(row, part), :].astype(jnp.float32)
            for shift in range(deep - 1):
                value = value + arrived[shift, pl.ds(row, part), :].astype(jnp.float32)
            last[rel] = value
            if weights is not None:
                product = value * weights[rel].astype(jnp.float32)
                sums.append(sum(product[:, i * LANES : (i + 1) * LANES] for i in range(size // LANES)))
        finals.append(load(last.at[0], final.at[core], own_sems.at[1, 12 + number]))
        finals.append(move(last.at[1], final.at[core], core_sems, 2 + number, core_beside))
        return sums

    def gain_exchange(which, sums):
        slots = {}
        for rel in range(2):
            gain_part[which, rel] = sums[rel]
        piece = part // 4
        for number, key in enumerate(far_cube):
            rel, up, over = key
            target = ((along + up) % 2) * 2 + (across + over) % 2
            row = pl.multiple_of(target * piece, 8)
            slots[key] = move(
                gain_part.at[which, rel, pl.ds(row, piece), :],
                gain_in.at[which, number],
                gain_sems,
                which * len(far_cube) + number,
                cube[key],
            )
        return slots

    def gain_finish(which, slots, output):
        piece = part // 4
        row = pl.multiple_of((along * 2 + across) * piece, 8)
        value = gain_part[which, 0, pl.ds(row, piece), :]
        for number, key in enumerate(far_cube):
            slots[key].wait_recv()
            value = value + gain_in[which, number]
        gain_total[which] = value
        return load(gain_total.at[which], output, load_sems.at[9 + which])

    for copy in weight_loads + early_loads:
        copy.wait()
    finish(0, 0, feed_sum.at[0], feed_z.at[0], feed_last.at[0], feed_final.at[0], None)
    gate_sums = finish(
        1, 1, feed_sum.at[1], feed_z.at[1], feed_last.at[1], feed_final.at[1], feed_weight.at[:, :, pl.ds(0, half)]
    )
    for shift in range(deep):
        qkv_copies[shift].wait_recv()
        join_piece("qkv", 4, qkv_sum, qkv_y, qkv_z, shift)
    up_sums = finish(
        2, 2, feed_sum.at[2], feed_z.at[2], feed_last.at[2], feed_final.at[2],
        feed_weight.at[:, :, pl.ds(half, half)],
    )
    second_slots = gain_exchange(1, [one + two for one, two in zip(gate_sums, up_sums)])
    finish("out", 3, out_sum, out_z, out_last, out_final, None)
    sums = finish("qkv", 4, qkv_sum, qkv_z, qkv_last, qkv_final, qkv_weight)
    first_slots = gain_exchange(0, sums)
    second_store = gain_finish(1, second_slots, second_gain_out)
    first_gain_store = gain_finish(0, first_slots, first_gain_out)
    for copy in (branch_copy, x_copy, core_near):
        copy.wait_recv()
    for number in range(5):
        finals[2 * number].wait()
        finals[2 * number + 1].wait_recv()
    for copy in (first_store, second_store, first_gain_store):
        copy.wait()
    for copy in sent:
        copy.wait_send()


def heads_back(
    deep, grad_attention, qkv, heads, logs, first, qkv_wide, out_wide, branch, sent, own, sums, arrived, chunks,
    qkv_own, cosine, sine, spreads,
):
    blocks, count, width = grad_attention.shape
    part, half = chunks.shape[3], chunks.shape[4] // 3
    qkv_half, out_half = spreads[0].shape[0], spreads[1].shape[0]
    rows = 2 * part

    def shape(*dims, kind=jnp.bfloat16):
        return jax.ShapeDtypeStruct(dims, kind)

    def room(*dims, kind=jnp.bfloat16):
        return pltpu.VMEM(dims, kind)

    wide = jnp.float32
    outs = (
        shape(count, width),
        shape(count, width),
        shape(count, width),
        shape(count, width),
        shape(3, 2, part, half, kind=wide),
        shape(2, part, qkv_half, kind=wide),
        shape(2, part, out_half, kind=wide),
        shape(part // 4, LANES, kind=wide),
        shape(part // 4, LANES, kind=wide),
    )
    dma = pltpu.SemaphoreType.DMA
    scratch = [
        room(blocks, count, width),
        room(*qkv.shape),
        room(*heads.shape),
        room(*heads.shape),
        room(*logs.shape, kind=wide),
        room(*qkv.shape),
        room(*qkv_wide.shape),
        room(*out_wide.shape),
        room(2 * count, LANES),
        room(2 * count, LANES),
        room(2 * count, LANES, kind=wide),
        room(2 * count, LANES, kind=wide),
        room(3, count, width),
        room(count, width),
        room(3, deep, rows, half),
        room(3, deep, rows, half),
        room(3, deep - 1, rows, half),
        room(deep, rows, out_half),
        room(deep, rows, out_half),
        room(deep, rows, out_half),
        room(deep - 1, rows, out_half),
        room(deep, rows, qkv_half),
        room(deep, rows, qkv_half),
        room(deep, rows, qkv_half),
        room(deep - 1, rows, qkv_half),
        room(3, 2, part, half, kind=wide),
        room(2, part, qkv_half, kind=wide),
        room(2, part, out_half, kind=wide),
        room(2, part, 2 * half),
        room(2, part, qkv_half),
        room(2, 2, part, LANES, kind=wide),
        room(2, 7, part // 4, LANES, kind=wide),
        room(2, part // 4, LANES, kind=wide),
        dma((11,)),
        dma((2, max(3 * deep, 17))),
        dma((deep,)),
        dma((2, 7)),
        dma((2, 2)),
        dma((2, 5 * deep)),
        dma((2, 5 * (deep - 1))),
        dma((2, 14)),
    ]
    return pl.pallas_call(
        functools.partial(heads_back_kernel, deep),
        out_shape=outs,
        in_specs=[hbm_spec()] * 14 + [vmem_spec()] * 4,
        out_specs=(hbm_spec(),) * len(outs),
        scratch_shapes=scratch,
        compiler_params=vmem_params(collective_id=3, has_side_effects=True),
        cost_estimate=cost(flops=30 * 10**9, bytes_accessed=10**8, transcendentals=10**7),
        name="heads_back",
    )(
        grad_attention, qkv, heads, logs, first, qkv_wide, out_wide, branch, sent, own, sums, arrived, chunks,
        qkv_own, cosine, sine, *spreads,
    )


def tables(rows):
    lane = np.arange(LANES)
    entry = lane % (LANES // 2)
    live = (entry < HD // 2).astype(np.float64)
    sign = np.where(lane < LANES // 2, -1.0, 1.0) * live
    inverse = np.where(live > 0, THETA ** (-2.0 * entry / HD), 0.0).astype(np.float32)
    position = np.arange(2 * rows, dtype=np.float32)
    angles = (position[:, None] * inverse[None, :]).astype(np.float32).astype(np.float64)
    both = (np.cos(angles) * live, np.sin(angles) * sign)
    return tuple(jnp.asarray(table.astype(np.float32).reshape(2, rows, LANES)) for table in both)


def norm_factor(rows):
    return lax.rsqrt(jnp.mean(rows * rows, axis=-1, keepdims=True) + EPSILON)


def norm_back(rows, gain, grad):
    factor = norm_factor(rows)
    scaled = grad * gain
    return factor * scaled - rows * factor**3 * jnp.mean(scaled * rows, axis=-1, keepdims=True)


def join(halves):
    return jnp.concatenate([halves[0], halves[1]], axis=1)


def gain_grad(lanes, gain, depth_place):
    piece = lanes.shape[0]
    start = (depth_place * 4 + lax.axis_index("y") * 2 + lax.axis_index("x")) * piece
    return jnp.sum(lanes, axis=1) / lax.dynamic_slice_in_dim(gain, start, piece)


def fast_local(
    tokens,
    cotangent,
    first_gain,
    query_weight,
    key_weight,
    value_weight,
    out_weight,
    second_gain,
    gate_weight,
    up_weight,
    down_weight,
):
    deep = lax.axis_size("z")
    z_place, core = (lax.axis_index(name).astype(jnp.int32) for name in ("z", "c"))
    rows = tokens.shape[0]
    depth_place = z_place * 2 + core
    own_rows = tokens.astype(jnp.float32)
    out_turned, down_turned = out_weight.T, down_weight.T

    def halves(*weights):
        result = []
        for half in range(2):
            pieces = []
            for weight in weights:
                size = weight.shape[1] // 2
                pieces.append(weight[:, half * size : (half + 1) * size])
            result.append(jnp.concatenate(pieces, axis=1))
        return result

    spreads = (spread_heads(3, 1), spread_heads(0, 2))
    cosine, sine = tables(rows)
    gains = jnp.stack([first_gain, second_gain])
    (
        first_all, qkv_all, heads_all, logs_all, qkv_weight, out_wide, middle, second_all, cotangent_all, chunks, qkv_own,
    ) = forward(
        deep,
        cotangent,
        tokens,
        gains,
        jnp.stack(
            halves(gate_weight, up_weight, down_turned, query_weight, key_weight, value_weight, out_turned)
        ),
        (
            gate_weight.shape[1] * 3 // 2,
            query_weight.shape[1] // 2 + key_weight.shape[1],
            out_turned.shape[1] // 2,
        ),
        spreads,
        cosine,
        sine,
    )
    grad_middle, grad_attention, branch, sent, own, sums, arrived = feed_back(
        deep, second_all, cotangent_all, chunks, middle, gains
    )
    first_part, first_core, first_x, branch_x, feed_final, qkv_final, out_final, first_lanes, second_lanes = (
        heads_back(
            deep, grad_attention, qkv_all, heads_all, logs_all, first_all, qkv_weight, out_wide, branch, sent,
            own, sums, arrived, chunks, qkv_own, cosine, sine, spreads,
        )
    )

    def total(*parts):
        return sum(piece.astype(jnp.float32) for piece in parts)

    result = (middle + total(branch[0], branch[2], branch_x)).astype(jnp.bfloat16)
    grad_first = total(first_part, first_core, first_x)
    tokens_grad = grad_middle + norm_back(own_rows, first_gain, grad_first)
    query_end = query_weight.shape[1] // 2
    key_end = query_end + key_weight.shape[1] // 2
    return (
        result,
        tokens_grad,
        join(qkv_final[:, :, :query_end]),
        join(qkv_final[:, :, query_end:key_end]),
        join(qkv_final[:, :, key_end:]),
        join(out_final).T,
        join(feed_final[1]),
        join(feed_final[2]),
        join(feed_final[0]).T,
        gain_grad(first_lanes, first_gain, depth_place),
        gain_grad(second_lanes, second_gain, depth_place),
    )


def specs(depth, width):
    both = depth + width
    rows, inward, outward = P(both, None), P(depth, width), P(width, depth)
    in_specs = (rows, rows, P(), inward, inward, inward, outward, P(), inward, inward, outward)
    out_specs = (rows, rows, inward, inward, inward, outward, inward, inward, outward, P(both), P(both))
    return in_specs, out_specs


def solution(mesh):
    depth, width = mesh.shape["dp"], mesh.shape["tensor"]

    def run(tokens, cotangent, *weights):
        fits = (
            width == 4
            and depth == 8
            and tokens.shape[0] * 2 == SEQ_LEN * depth * width
            and weights[2].shape[1] == 2 * width * HD
            and weights[1].shape[1] == 4 * width * HD
        )
        if fits:
            devices = mesh.devices.reshape(depth // 2, 2, 2, 2)
            fine = jax.sharding.Mesh(devices, ("z", "c", "y", "x"))
            in_specs, out_specs = specs(("z", "c"), ("y", "x"))
            call, over = fast_local, fine
        else:
            in_specs, out_specs = specs(("dp",), ("tensor",))
            call, over = local, mesh
        return jax.shard_map(call, mesh=over, in_specs=in_specs, out_specs=out_specs, check_vma=False)(
            tokens, cotangent, *weights
        )

    return run
```

```python
import functools

import jax
import jax.numpy as jnp
import numpy as np
from jax import lax
from jax.experimental import pallas as pl
from jax.experimental.pallas import tpu as pltpu
from jax.sharding import PartitionSpec as P

HD = 96
SEQ_LEN = 1024


EPSILON = 1e-05
THETA = 100000.0
MASKED = -1e30
LOG2E = 1.4426950408889634
LANES = 128
SHARE = 20
VMEM_BYTES = 63 * 2**20


def normed(inputs, gain):
    factor = lax.rsqrt(jnp.mean(inputs * inputs, axis=-1, keepdims=True) + EPSILON)
    return inputs * factor * gain


def rotate(vectors, direction):
    seq_rows, head_count, head_size = vectors.shape
    half_size = head_size // 2
    position = (jnp.arange(seq_rows, dtype=jnp.int32) % SEQ_LEN).astype(jnp.float32)
    inverse = THETA ** (-2.0 * jnp.arange(half_size, dtype=jnp.float32) / head_size)
    angles = position[:, None] * inverse[None, :]
    cosine = jnp.cos(angles)[:, None, :]
    sine_part = direction * jnp.sin(angles)[:, None, :]
    leading = vectors[..., :half_size]
    trailing = vectors[..., half_size:]
    return jnp.concatenate(
        [leading * cosine - trailing * sine_part, trailing * cosine + leading * sine_part], axis=-1
    )


def times_transposed(left, right):
    return lax.dot_general(
        left, right, (((1,), (1,)), ((), ())), preferred_element_type=jnp.float32
    )


def transposed_times(left, right):
    return lax.dot_general(
        left, right, (((0,), (0,)), ((), ())), preferred_element_type=jnp.float32
    )


def scaled_scores(queries, keys_rot):
    raw_scores = jnp.einsum(
        "qhgd,khd->hgqk", queries, keys_rot, preferred_element_type=jnp.float32
    ) * queries.shape[-1] ** (-0.5)
    length_rows = queries.shape[0]
    causal = jnp.arange(length_rows)[:, None] >= jnp.arange(length_rows)[None, :]
    return jnp.where(causal, raw_scores, MASKED)


def attend_forward(operands):
    queries, keys_rot, values = operands
    scores = scaled_scores(queries, keys_rot)
    row_max = jnp.max(scores, axis=-1, keepdims=True)
    weights = jnp.exp(scores - row_max)
    row_total = jnp.sum(weights, axis=-1, keepdims=True)
    softmax = (weights / row_total).astype(jnp.bfloat16)
    mixed_heads = jnp.einsum("hgqk,khd->qhgd", softmax, values, preferred_element_type=jnp.float32)
    return (mixed_heads.astype(jnp.bfloat16), (row_max + jnp.log(row_total))[..., 0])


def attend_backward(operands):
    queries, keys_rot, values, grad_mixed, log_total = operands
    scores = scaled_scores(queries, keys_rot)
    softmax = jnp.exp(scores - log_total[..., None])
    grad_softmax = jnp.einsum(
        "qhgd,khd->hgqk", grad_mixed, values, preferred_element_type=jnp.float32
    )
    grad_values = jnp.einsum(
        "hgqk,qhgd->khd",
        softmax.astype(jnp.bfloat16),
        grad_mixed,
        preferred_element_type=jnp.float32,
    )
    row_inner = jnp.sum(softmax * grad_softmax, axis=-1, keepdims=True)
    grad_scores = (softmax * (grad_softmax - row_inner)).astype(jnp.bfloat16)
    scale_factor = queries.shape[-1] ** (-0.5)
    grad_queries = (
        jnp.einsum("hgqk,khd->qhgd", grad_scores, keys_rot, preferred_element_type=jnp.float32)
        * scale_factor
    )
    grad_keys = (
        jnp.einsum("hgqk,qhgd->khd", grad_scores, queries, preferred_element_type=jnp.float32)
        * scale_factor
    )
    return (grad_queries, grad_keys, grad_values)


def gather_rows(shard):
    return lax.all_gather(shard, "tensor", axis=0, tiled=True)


def gather_grads(shard):
    return lax.all_gather(shard, "tensor", axis=0, tiled=True)


def sum_outputs(term, row_count):
    return lax.psum_scatter(
        term(jnp.int32(0), row_count * lax.axis_size("tensor")),
        "tensor",
        scatter_dimension=0,
        tiled=True,
    )


def sum_inputs(term, row_count):
    return lax.psum_scatter(
        term(jnp.int32(0), row_count * lax.axis_size("tensor")),
        "tensor",
        scatter_dimension=0,
        tiled=True,
    )


def local(
    tokens,
    cotangent,
    first_gain,
    query_weight,
    key_weight,
    value_weight,
    out_weight,
    second_gain,
    gate_weight,
    up_weight,
    down_weight,
):
    query_weight, key_weight, value_weight, out_weight, gate_weight, up_weight, down_weight = (
        lax.all_gather(query_weight, "dp", axis=0, tiled=True),
        lax.all_gather(key_weight, "dp", axis=0, tiled=True),
        lax.all_gather(value_weight, "dp", axis=0, tiled=True),
        lax.all_gather(out_weight, "dp", axis=1, tiled=True),
        lax.all_gather(gate_weight, "dp", axis=0, tiled=True),
        lax.all_gather(up_weight, "dp", axis=0, tiled=True),
        lax.all_gather(down_weight, "dp", axis=1, tiled=True),
    )
    own_rows = tokens.astype(jnp.float32)
    row_count = own_rows.shape[0]
    pair_count = key_weight.shape[1] // HD
    first_normed = normed(own_rows, first_gain).astype(jnp.bfloat16)
    first_rows = gather_rows(first_normed)
    group_rows = first_rows.shape[0]
    sequences = group_rows // SEQ_LEN
    query_pre = jnp.dot(first_rows, query_weight, preferred_element_type=jnp.float32)
    key_pre = jnp.dot(first_rows, key_weight, preferred_element_type=jnp.float32)
    value_pre = jnp.dot(first_rows, value_weight, preferred_element_type=jnp.float32)
    queries = rotate(query_pre.reshape(group_rows, 2 * pair_count, HD), 1.0).astype(jnp.bfloat16)
    queries = queries.reshape(sequences, SEQ_LEN, pair_count, 2, HD)
    keys_rot = rotate(key_pre.reshape(group_rows, pair_count, HD), 1.0).astype(jnp.bfloat16)
    keys_rot = keys_rot.reshape(sequences, SEQ_LEN, pair_count, HD)
    values = value_pre.astype(jnp.bfloat16).reshape(sequences, SEQ_LEN, pair_count, HD)
    mixed_heads, log_total = lax.map(attend_forward, (queries, keys_rot, values))
    heads_out = mixed_heads.reshape(group_rows, 2 * pair_count * HD)
    heads_rows = lax.all_to_all(heads_out, "tensor", split_axis=0, concat_axis=1, tiled=True)
    out_full = lax.all_gather(out_weight, "tensor", axis=0, tiled=True)
    attention_branch = jnp.dot(heads_rows, out_full, preferred_element_type=jnp.float32)
    middle = own_rows + attention_branch
    second_normed = normed(middle, second_gain).astype(jnp.bfloat16)
    second_rows = gather_rows(second_normed)
    gate_full, up_full, down_full = (gate_weight, up_weight, down_weight)
    gate_value = jnp.dot(second_rows, gate_full, preferred_element_type=jnp.float32)
    up_value = jnp.dot(second_rows, up_full, preferred_element_type=jnp.float32)
    sigmoid_gate = jax.nn.sigmoid(gate_value)
    swish_gate = gate_value * sigmoid_gate
    hidden = (swish_gate * up_value).astype(jnp.bfloat16)

    def project_hidden(start, amount):
        return jnp.dot(hidden, down_full, preferred_element_type=jnp.float32)

    ffn_branch = sum_outputs(project_hidden, row_count)
    grad_branch = gather_grads(cotangent)
    result = (middle + ffn_branch).astype(jnp.bfloat16)
    grad_hidden = times_transposed(grad_branch, down_full)
    down_part = transposed_times(hidden, grad_branch)
    slope = sigmoid_gate + gate_value * sigmoid_gate * (1.0 - sigmoid_gate)
    grad_gate = (grad_hidden * up_value * slope).astype(jnp.bfloat16)
    grad_up = (grad_hidden * swish_gate).astype(jnp.bfloat16)
    gate_part = transposed_times(second_rows, grad_gate)
    up_part = transposed_times(second_rows, grad_up)

    def second_back(start, amount):
        return times_transposed(grad_gate, gate_full) + times_transposed(grad_up, up_full)

    grad_second = sum_inputs(second_back, row_count)
    second_unused, second_pull = jax.vjp(normed, middle, second_gain)
    grad_middle_norm, second_gain_part = second_pull(grad_second)
    grad_middle = cotangent.astype(jnp.float32) + grad_middle_norm
    grad_attention = grad_middle.astype(jnp.bfloat16)
    grad_heads_rows = times_transposed(grad_attention, out_full).astype(jnp.bfloat16)
    grad_heads = lax.all_to_all(grad_heads_rows, "tensor", split_axis=1, concat_axis=0, tiled=True)
    out_part = lax.psum_scatter(
        transposed_times(heads_rows, grad_attention).astype(jnp.bfloat16),
        "tensor",
        scatter_dimension=0,
        tiled=True,
    )
    grad_mixed = grad_heads.reshape(sequences, SEQ_LEN, pair_count, 2, HD)
    grad_queries, grad_keys, grad_values = lax.map(
        attend_backward, (queries, keys_rot, values, grad_mixed, log_total)
    )
    grad_query = (
        rotate(grad_queries.reshape(group_rows, 2 * pair_count, HD), -1.0)
        .reshape(group_rows, -1)
        .astype(jnp.bfloat16)
    )
    grad_key = (
        rotate(grad_keys.reshape(group_rows, pair_count, HD), -1.0)
        .reshape(group_rows, -1)
        .astype(jnp.bfloat16)
    )
    grad_value = grad_values.reshape(group_rows, -1).astype(jnp.bfloat16)
    query_part = transposed_times(first_rows, grad_query)
    key_part = transposed_times(first_rows, grad_key)
    value_part = transposed_times(first_rows, grad_value)

    def first_back(start, amount):
        return (
            times_transposed(grad_query, query_weight)
            + times_transposed(grad_key, key_weight)
            + times_transposed(grad_value, value_weight)
        )

    grad_first = sum_inputs(first_back, row_count)
    first_unused, first_pull = jax.vjp(normed, own_rows, first_gain)
    grad_own_norm, first_gain_part = first_pull(grad_first)
    tokens_grad = grad_middle + grad_own_norm
    query_grad, key_grad, value_grad, out_grad, gate_grad, up_grad, down_grad = (
        lax.psum_scatter(
            query_part.astype(jnp.bfloat16), "dp", scatter_dimension=0, tiled=True
        ).astype(jnp.float32),
        lax.psum_scatter(
            key_part.astype(jnp.bfloat16), "dp", scatter_dimension=0, tiled=True
        ).astype(jnp.float32),
        lax.psum_scatter(
            value_part.astype(jnp.bfloat16), "dp", scatter_dimension=0, tiled=True
        ).astype(jnp.float32),
        lax.psum_scatter(out_part, "dp", scatter_dimension=1, tiled=True).astype(jnp.float32),
        lax.psum_scatter(
            gate_part.astype(jnp.bfloat16), "dp", scatter_dimension=0, tiled=True
        ).astype(jnp.float32),
        lax.psum_scatter(
            up_part.astype(jnp.bfloat16), "dp", scatter_dimension=0, tiled=True
        ).astype(jnp.float32),
        lax.psum_scatter(
            down_part.astype(jnp.bfloat16), "dp", scatter_dimension=1, tiled=True
        ).astype(jnp.float32),
    )
    first_gain_grad, second_gain_grad = (
        lax.psum_scatter(first_gain_part, ("dp", "tensor"), scatter_dimension=0, tiled=True),
        lax.psum_scatter(second_gain_part, ("dp", "tensor"), scatter_dimension=0, tiled=True),
    )
    return (
        result,
        tokens_grad,
        query_grad,
        key_grad,
        value_grad,
        out_grad,
        gate_grad,
        up_grad,
        down_grad,
        first_gain_grad,
        second_gain_grad,
    )


def nn(left, right):
    return jnp.dot(left, right, preferred_element_type=jnp.float32)


def cost(flops, bytes_accessed, transcendentals):
    return pl.CostEstimate(
        flops=flops // SHARE, bytes_accessed=bytes_accessed // SHARE, transcendentals=transcendentals // SHARE
    )


def vmem_params(**more):
    return pltpu.CompilerParams(vmem_limit_bytes=VMEM_BYTES, **more)


def vmem_spec():
    return pl.BlockSpec(memory_space=pltpu.VMEM)


def spread_heads(heads_split, heads_plain):
    columns = (heads_split + heads_plain) * HD
    spread = np.zeros((columns, (heads_split + heads_plain) * LANES), np.float32)
    for head in range(heads_split + heads_plain):
        for entry in range(HD):
            lane = entry
            if head < heads_split and entry >= HD // 2:
                lane = entry - HD // 2 + LANES // 2
            spread[head * HD + entry, head * LANES + lane] = 1.0
    return jnp.asarray(spread, jnp.bfloat16)


def turn(vectors, cosine, sine):
    return vectors * cosine + pltpu.roll(vectors, LANES // 2, 1) * sine


TILE = 256
WIDE = 768


def diagonal_mask():
    row = lax.broadcasted_iota(jnp.int32, (2 * TILE, TILE), 0)
    row = jnp.where(row >= TILE, row - TILE, row)
    return row >= lax.broadcasted_iota(jnp.int32, (2 * TILE, TILE), 1)


def hbm_spec():
    return pl.BlockSpec(memory_space=pltpu.HBM)


def send(source, target, sems, where):
    copy = pltpu.make_async_remote_copy(
        src_ref=source,
        dst_ref=target,
        send_sem=sems[0],
        recv_sem=sems[1],
        device_id=where,
        device_id_type=pl.DeviceIdType.MESH,
    )
    copy.start()
    return copy


def greet(partners):
    barrier = pltpu.get_barrier_semaphore()
    for partner in partners:
        pl.semaphore_signal(barrier, inc=1, device_id=partner, device_id_type=pl.DeviceIdType.MESH)
    pl.semaphore_wait(barrier, len(partners))


def beside():
    core, across, along = (lax.axis_index(name).astype(jnp.int32) for name in ("c", "x", "y"))
    return {"c": 1 - core}, {"x": 1 - across}, {"y": 1 - along}


def grid_offset(slot, rel, deep, part):
    z_place = lax.rem(lax.axis_index("z").astype(jnp.int32) + slot, jnp.int32(deep))
    core = lax.rem(lax.axis_index("c").astype(jnp.int32) + rel, jnp.int32(2))
    return pl.multiple_of((z_place * 2 + core) * part, 64)


def spread_weight(buffer, spread_ref, wide, deep):
    part = buffer.shape[3]
    half = wide.shape[1] // 2

    @pl.loop(0, 4 * deep)
    def _(step):
        rel, slot = lax.rem(step, jnp.int32(2)), lax.rem(step // 2, jnp.int32(deep))
        side = step // (2 * deep)
        rows = pl.ds(grid_offset(slot, rel, deep, part), part)
        lanes = pl.ds(pl.multiple_of(side * half, half), half)
        wide[rows, lanes] = nn(buffer[side, slot, rel], spread_ref[...]).astype(jnp.bfloat16)


def attend_pair(qkv, heads, logs, keys, values, sequence, pair):
    count = qkv.shape[1]
    x_place = lax.axis_index("x").astype(jnp.int32)
    lane0 = pl.multiple_of(pair * 4 * LANES, 4 * LANES)
    mask = diagonal_mask()
    scale = HD ** (-0.5) * LOG2E
    places = [2 * sequence + lax.rem(x_place + position, jnp.int32(2)) for position in range(2)]
    for position, block in enumerate(places):
        rows = slice(position * count, (position + 1) * count)
        keys[rows, :] = qkv[block, :, pl.ds(lane0 + 2 * LANES, LANES)]
        values[rows, :] = qkv[block, :, pl.ds(lane0 + 3 * LANES, LANES)]

    def visit(block, start, before):
        rows = slice(start, start + TILE)
        queries = jnp.concatenate(
            [qkv[block, rows, pl.ds(lane0, LANES)], qkv[block, rows, pl.ds(lane0 + LANES, LANES)]], axis=0
        )
        edge = slice(before, before + TILE)
        near = jnp.where(mask, times_transposed(queries, keys[edge, :]), MASKED)
        top = jnp.max(near, axis=-1, keepdims=True)
        if before:
            far = times_transposed(queries, keys[:before, :])
            top = jnp.maximum(top, jnp.max(far, axis=-1, keepdims=True))
        top = top * scale
        near = jnp.exp2(near * scale - top)
        total = jnp.sum(near, axis=-1, keepdims=True)
        mixed = nn(near.astype(jnp.bfloat16), values[edge, :])
        if before:
            far = jnp.exp2(far * scale - top)
            total = total + jnp.sum(far, axis=-1, keepdims=True)
            mixed = mixed + nn(far.astype(jnp.bfloat16), values[:before, :])
        mixed = (mixed / total).astype(jnp.bfloat16)
        log = top + jnp.log2(total)
        lane = lax.broadcasted_iota(jnp.int32, (TILE, LANES), 1)
        kept = logs[block, rows, :]
        for head in range(2):
            part = slice(head * TILE, (head + 1) * TILE)
            out_lane = pl.multiple_of(pair * 2 * LANES, LANES) + head * LANES
            heads[block, rows, pl.ds(out_lane, LANES)] = mixed[part]
            kept = jnp.where(lane == 2 * pair + head, log[part], kept)
        logs[block, rows, :] = kept

    for position, block in enumerate(places):
        for step in range(count // TILE):
            visit(block, step * TILE, position * count + step * TILE)


def forward_kernel(
    deep, cotangent_ref, tokens_ref, gains_ref, all_halves,
    qkv_spread, out_spread, cosine_ref, sine_ref,
    first_out, qkv_out, heads_out, logs_out, qkv_wide_out, out_wide_out, middle_out, second_out,
    cotangent_out, feed_out, qkv_own_out,
    first_all, qkv_buffer, out_buffer, qkv_wide, out_wide, qkv, heads, logs, keys, values,
    parts, core_parts, outgoing, incoming, middle, second,
    local_sems, row_sems, qkv_sems, out_sems, feed_sems, core_sems,
):
    core, z_place = lax.axis_index("c").astype(jnp.int32), lax.axis_index("z").astype(jnp.int32)
    core_beside, x_beside, y_beside = beside()
    count = tokens_ref.shape[0]
    ring = jnp.int32(deep)
    feed_lanes, qkv_lanes, out_lanes = (
        buffer.shape[-1] for buffer in (feed_out, qkv_buffer, out_buffer)
    )
    feed_halves = all_halves.at[:, :, pl.ds(0, feed_lanes)]
    qkv_halves = all_halves.at[:, :, pl.ds(feed_lanes, qkv_lanes)]
    out_halves = all_halves.at[:, :, pl.ds(feed_lanes + qkv_lanes, out_lanes)]
    z_beside = {way: {"z": lax.rem(z_place + deep + way, ring)} for way in (-1, 1)}
    greet([core_beside, x_beside, y_beside, z_beside[-1], z_beside[1]])

    kept = []
    sent = []

    def keep_local(source, target, index):
        copy = pltpu.make_async_copy(source, target, local_sems.at[index])
        copy.start()
        return copy

    def pair_of(sems, index):
        return sems.at[0, index], sems.at[1, index]

    def move(source, target, sems, index, where):
        copy = send(source, target, pair_of(sems, index), where)
        sent.append(copy)
        return copy

    qkv_core = move(qkv_halves.at[1 - core], qkv_buffer.at[0, 0, 1], qkv_sems, 0, core_beside)
    qkv_kept = keep_local(qkv_halves.at[core], qkv_buffer.at[0, 0, 0], 0)
    step_rows = 128

    @pl.loop(0, count // step_rows)
    def _(step):
        rows = pl.ds(pl.multiple_of(step * step_rows, step_rows), step_rows)
        value = tokens_ref[rows, :].astype(jnp.float32)
        first_all[0, rows, :] = (value * norm_factor(value) * gains_ref[0:1, :]).astype(jnp.bfloat16)

    first_x = move(first_all.at[0], first_all.at[1], row_sems, 0, x_beside)
    out_core = move(out_halves.at[1 - core], out_buffer.at[0, 0, 1], out_sems, 0, core_beside)
    out_kept = keep_local(out_halves.at[core], out_buffer.at[0, 0, 0], 1)
    feed_core = move(feed_halves.at[1 - core], feed_out.at[0, 0, 1], feed_sems, 0, core_beside)
    feed_kept = keep_local(feed_halves.at[core], feed_out.at[0, 0, 0], 2)
    first_core = move(first_all.at[0], first_all.at[2], row_sems, 1, core_beside)
    cotangent_kept = keep_local(cotangent_ref, cotangent_out.at[0], 4)

    last = deep - 1

    def z_copy(buffer, sems, upward, step, rel):
        source, target = ((deep - step) % deep, last - step) if upward else (step, step + 1)
        return pltpu.make_async_remote_copy(
            src_ref=buffer.at[0, source, rel],
            dst_ref=buffer.at[0, target, rel],
            send_sem=sems.at[0, 2 * (1 + upward * last + step) + rel],
            recv_sem=sems.at[1, 2 * target + rel],
            device_id=z_beside[1 if upward else -1],
            device_id_type=pl.DeviceIdType.MESH,
        )

    def z_sends(upward, step):
        if upward:
            return (z_place <= last - 1) & (z_place - step >= 0)
        return (z_place >= 1) & (z_place + step <= last)

    def z_start(buffer, sems, upward, step, rel):
        @pl.when(z_sends(upward, step))
        def _():
            z_copy(buffer, sems, upward, step, rel).start()

    def open_z(buffer, sems):
        for rel in range(2):
            z_start(buffer, sems, False, 0, rel)
            z_start(buffer, sems, True, 0, rel)

    def y_copy(buffer, sems, slot, rel):
        return pltpu.make_async_remote_copy(
            src_ref=buffer.at[0, slot, rel],
            dst_ref=buffer.at[1, slot, rel],
            send_sem=sems.at[0, 2 * (2 * deep + slot) + rel],
            recv_sem=sems.at[1, 2 * (2 * deep + slot) + rel],
            device_id=y_beside,
            device_id_type=pl.DeviceIdType.MESH,
        )

    def open_y(buffer, sems):
        for rel in range(2):
            y_copy(buffer, sems, 0, rel).start()

    def z_part(buffer, sems, step, rel):
        for upward in (False, True):
            slot = last - step if upward else step + 1
            arrives = z_place - step - 1 >= 0 if upward else z_place + step + 1 <= last

            @pl.when(arrives)
            def _(upward=upward, slot=slot):
                z_copy(buffer, sems, upward, step, rel).wait_recv()
                if step + 1 < last:
                    z_start(buffer, sems, upward, step + 1, rel)
                y_copy(buffer, sems, slot, rel).start()

    def z_step(buffer, sems, step):
        for rel in range(2):
            z_part(buffer, sems, step, rel)

    def y_wait(buffer, sems):
        for slot in range(deep):
            for rel in range(2):
                y_copy(buffer, sems, slot, rel).wait_recv()

    def close(buffer, sems):
        for rel in range(2):
            for slot in range(deep):
                y_copy(buffer, sems, slot, rel).wait_send()
            for upward in (False, True):
                for step in range(last):

                    @pl.when(z_sends(upward, step))
                    def _(upward=upward, step=step, rel=rel):
                        z_copy(buffer, sems, upward, step, rel).wait_send()

    qkv_z, out_z, feed_z = (qkv_buffer, qkv_sems), (out_buffer, out_sems), (feed_out, feed_sems)
    qkv_core.wait_recv()
    qkv_kept.wait()
    open_z(*qkv_z)
    open_y(*qkv_z)
    out_core.wait_recv()
    out_kept.wait()
    feed_core.wait_recv()
    feed_kept.wait()
    kept.append(keep_local(qkv_buffer.at[0, 0], qkv_own_out, 13))
    for step in range(last):
        z_step(*qkv_z, step)
        if step == last - 2:
            open_z(*out_z)
    open_y(*out_z)
    for step in range(last):
        z_step(*out_z, step)
    open_z(*feed_z)
    open_y(*feed_z)
    first_x.wait_recv()
    first_far = move(first_all.at[1], first_all.at[3], row_sems, 2, core_beside)
    cotangent_x = move(cotangent_ref, cotangent_out.at[1], row_sems, 3, x_beside)
    cotangent_core = move(cotangent_ref, cotangent_out.at[2], row_sems, 4, core_beside)
    y_wait(*qkv_z)

    spread_weight(qkv_buffer, qkv_spread, qkv_wide, deep)
    kept.append(keep_local(qkv_wide, qkv_wide_out, 5))
    first_core.wait_recv()
    first_far.wait_recv()
    kept.append(keep_local(first_all, first_out, 6))

    @pl.loop(0, 8)
    def _(step):
        block, pair = step // 2, lax.rem(step, jnp.int32(2))
        lane0 = pl.multiple_of(pair * 4 * LANES, 4 * LANES)
        product = nn(first_all[block], qkv_wide[:, pl.ds(lane0, 4 * LANES)])
        position = lax.rem(lax.axis_index("x").astype(jnp.int32) + block, jnp.int32(2))
        cosine, sine = cosine_ref[position], sine_ref[position]
        for head in range(4):
            part = product[:, head * LANES : (head + 1) * LANES]
            if head < 3:
                part = turn(part, cosine, sine)
            qkv[block, :, pl.ds(lane0 + head * LANES, LANES)] = part.astype(jnp.bfloat16)

    kept.append(keep_local(qkv, qkv_out, 7))
    z_part(*feed_z, 0, 0)
    logs[...] = jnp.zeros_like(logs)
    for sequence in range(2):

        @pl.loop(0, 2)
        def _(pair, sequence=sequence):
            attend_pair(qkv, heads, logs, keys, values, sequence, pair)

        if sequence == 0:
            z_part(*feed_z, 0, 1)

    kept.append(keep_local(heads, heads_out, 8))
    kept.append(keep_local(logs, logs_out, 9))
    y_wait(*out_z)
    spread_weight(out_buffer, out_spread, out_wide, deep)
    kept.append(keep_local(out_wide, out_wide_out, 10))

    def out_part(block):
        @pl.loop(0, out_wide.shape[0] // WIDE)
        def _(step):
            lanes = pl.ds(pl.multiple_of(step * WIDE, WIDE), WIDE)
            parts[block, :, lanes] = times_transposed(heads[block], out_wide[lanes, :]).astype(jnp.bfloat16)

    out_part(3)
    core_far = move(parts.at[3], core_parts.at[1], core_sems, 0, core_beside)
    out_part(1)
    core_far.wait_recv()

    @pl.loop(0, count // step_rows)
    def _(step):
        rows = pl.ds(pl.multiple_of(step * step_rows, step_rows), step_rows)
        outgoing[rows, :] = (
            parts[1, rows, :].astype(jnp.float32) + core_parts[1, rows, :].astype(jnp.float32)
        ).astype(jnp.bfloat16)

    branch_x = move(outgoing, incoming, core_sems, 1, x_beside)
    out_part(2)
    core_near = move(parts.at[2], core_parts.at[0], core_sems, 2, core_beside)
    out_part(0)
    core_near.wait_recv()
    z_step(*feed_z, 1)
    branch_x.wait_recv()

    @pl.loop(0, count // step_rows)
    def _(step):
        rows = pl.ds(pl.multiple_of(step * step_rows, step_rows), step_rows)
        total = (
            tokens_ref[rows, :].astype(jnp.float32)
            + parts[0, rows, :].astype(jnp.float32)
            + core_parts[0, rows, :].astype(jnp.float32)
            + incoming[rows, :].astype(jnp.float32)
        )
        middle[rows, :] = total
        second[rows, :] = (total * norm_factor(total) * gains_ref[1:2, :]).astype(jnp.bfloat16)

    kept.append(keep_local(middle, middle_out, 11))
    kept.append(keep_local(second, second_out.at[0], 12))
    second_x = move(second, second_out.at[1], row_sems, 5, x_beside)
    second_core = move(second, second_out.at[2], row_sems, 6, core_beside)
    cotangent_x.wait_recv()
    cotangent_far = move(cotangent_out.at[1], cotangent_out.at[3], row_sems, 7, core_beside)
    z_step(*feed_z, 2)
    second_x.wait_recv()
    second_far = move(second_out.at[1], second_out.at[3], row_sems, 8, core_beside)
    for copy in (second_core, second_far, cotangent_core, cotangent_far):
        copy.wait_recv()
    y_wait(*feed_z)
    for copy in kept + [cotangent_kept]:
        copy.wait()
    for copy in sent:
        copy.wait_send()
    for which in (qkv_z, out_z, feed_z):
        close(*which)


def forward(deep, cotangent, tokens, gains, halves, sizes, spreads, cosine, sine):
    count, width = tokens.shape
    part = halves.shape[1]
    feed_size, qkv_size, out_size = sizes

    def shape(*dims, kind=jnp.bfloat16):
        return jax.ShapeDtypeStruct(dims, kind)

    def room(*dims, kind=jnp.bfloat16):
        return pltpu.VMEM(dims, kind)

    qkv_lanes, out_lanes = 2 * spreads[0].shape[1], 2 * spreads[1].shape[1]
    outs = (
        shape(4, count, width),
        shape(4, count, qkv_lanes),
        shape(4, count, out_lanes),
        shape(4, count, LANES, kind=jnp.float32),
        shape(width, qkv_lanes),
        shape(width, out_lanes),
        shape(count, width, kind=jnp.float32),
        shape(4, count, width),
        shape(4, count, width),
        shape(2, deep, 2, part, feed_size),
        shape(2, part, qkv_size),
    )
    scratch = [
        room(4, count, width),
        room(2, deep, 2, part, qkv_size),
        room(2, deep, 2, part, out_size),
        room(width, qkv_lanes),
        room(width, out_lanes),
        room(4, count, qkv_lanes),
        room(4, count, out_lanes),
        room(4, count, LANES, kind=jnp.float32),
        room(2 * count, LANES),
        room(2 * count, LANES),
        room(4, count, width),
        room(2, count, width),
        room(count, width),
        room(count, width),
        room(count, width, kind=jnp.float32),
        room(count, width),
        pltpu.SemaphoreType.DMA((14,)),
        pltpu.SemaphoreType.DMA((2, 9)),
        pltpu.SemaphoreType.DMA((2, 6 * deep)),
        pltpu.SemaphoreType.DMA((2, 6 * deep)),
        pltpu.SemaphoreType.DMA((2, 6 * deep)),
        pltpu.SemaphoreType.DMA((2, 3)),
    ]
    return pl.pallas_call(
        functools.partial(forward_kernel, deep),
        out_shape=outs,
        in_specs=[hbm_spec(), vmem_spec(), vmem_spec(), hbm_spec()] + [vmem_spec()] * 4,
        out_specs=(hbm_spec(),) * len(outs),
        scratch_shapes=scratch,
        compiler_params=vmem_params(collective_id=1, has_side_effects=True),
        cost_estimate=cost(flops=20 * 10**9, bytes_accessed=10**8, transcendentals=10**7),
        name="forward",
    )(cotangent, tokens, gains, halves, *spreads, cosine, sine)


EARLY = 7
ORDER = (1, 3, 2, 0)
HOPS = {(0, 1): 0, (0, 3): 1, (0, 2): 2, (1, 1): 3}


def ring_row(shift, deep, rows):
    z_place = lax.rem(lax.axis_index("z").astype(jnp.int32) + shift, jnp.int32(deep))
    return pl.multiple_of(z_place * rows, rows)


def add_rows(target, source, step_rows=128):
    @pl.loop(0, target.shape[0] // step_rows)
    def _(step):
        rows = pl.ds(pl.multiple_of(step * step_rows, step_rows), step_rows)
        target[rows, :] = (target[rows, :].astype(jnp.float32) + source[rows, :].astype(jnp.float32)).astype(
            jnp.bfloat16
        )


def ahead(deep):
    z_place = lax.axis_index("z").astype(jnp.int32)
    return [{"z": lax.rem(z_place + shift, jnp.int32(deep))} for shift in range(deep)]


def pieces_of(deep):
    return [(piece, shift) for piece in range(3) for shift in ORDER[:deep]]


def feed_back_kernel(
    deep, rows_hbm, grads_hbm, chunks, middle_hbm, gain_ref,
    grad_middle_out, grad_attention_out, branch_out, sent_out, own_out, sum_out, arrived_out,
    gate, up, down, rows, grads, hidden, grad_gate, grad_up, parts, landing, incoming, middle, stage,
    early_y, load_sems, weight_sems, store_sems, sum_sems, early_sems, core_sems, x_sems, y_sems, z_sems,
):
    core_beside, x_beside, y_beside = beside()
    z_ahead = ahead(deep)
    greet([core_beside, x_beside, y_beside] + z_ahead[1:])
    blocks, count, width = rows.shape
    half = gate.shape[1] // 2
    part = chunks.shape[3]
    piece_rows = 2 * part
    sent = []

    def load(source, target, sem):
        copy = pltpu.make_async_copy(source, target, sem)
        copy.start()
        return copy

    def move(source, target, sems, index, where):
        copy = send(source, target, (sems.at[0, index], sems.at[1, index]), where)
        sent.append(copy)
        return copy

    row_loads = {}
    for block in (3, 1):
        row_loads[block] = [load(rows_hbm.at[block], rows.at[block], load_sems.at[0, block])]
    weight_loads = {}
    for side in range(2):
        here = []
        for matrix, target in enumerate((gate, up, down)):
            for shift in range(deep):
                for rel in range(2):
                    here.append(
                        load(
                            chunks.at[side, shift, rel, :, pl.ds(matrix * half, half)],
                            target.at[pl.ds(grid_offset(shift, rel, deep, part), part), pl.ds(side * half, half)],
                            weight_sems.at[matrix, side, shift, rel],
                        )
                    )
        weight_loads[side] = here
        if side == 0:
            for block in (3, 1):
                row_loads[block].append(load(grads_hbm.at[block], grads.at[block], load_sems.at[1, block]))
    for block in (2, 0):
        row_loads[block] = [
            load(rows_hbm.at[block], rows.at[block], load_sems.at[0, block]),
            load(grads_hbm.at[block], grads.at[block], load_sems.at[1, block]),
        ]
    middle_load = load(middle_hbm, middle, load_sems.at[0, 4])

    def inner(block):
        for side in range(2):
            for copy in weight_loads.pop(side, ()):
                copy.wait()
            lanes = slice(side * half, (side + 1) * half)
            gate_value = nn(rows[block], gate[:, lanes])
            up_value = nn(rows[block], up[:, lanes])
            grad_hidden = nn(grads[block], down[:, lanes])
            sigmoid = 1.0 / (1.0 + jnp.exp(-gate_value))
            swish = gate_value * sigmoid
            slope = sigmoid + swish * (1.0 - sigmoid)
            hidden[block, :, lanes] = (swish * up_value).astype(jnp.bfloat16)
            grad_gate[block, :, lanes] = (grad_hidden * up_value * slope).astype(jnp.bfloat16)
            grad_up[block, :, lanes] = (grad_hidden * swish).astype(jnp.bfloat16)

    def outer(block):
        @pl.loop(0, width // WIDE)
        def _(step):
            lanes = pl.ds(pl.multiple_of(step * WIDE, WIDE), WIDE)
            parts[block, :, lanes] = (
                times_transposed(grad_gate[block], gate[lanes, :])
                + times_transposed(grad_up[block], up[lanes, :])
            ).astype(jnp.bfloat16)

    for block in (3, 1, 2, 0):
        for copy in row_loads[block]:
            copy.wait()
        inner(block)
        if block in (3, 1):
            outer(block)
        if block == 3:
            far = move(parts.at[3], landing.at[1], core_sems, 0, core_beside)
        if block == 1:
            far.wait_recv()
            add_rows(parts.at[1], landing.at[1])
            across = move(parts.at[1], incoming, x_sems, 0, x_beside)

    sources = ((grads, hidden), (rows, grad_gate), (rows, grad_up))

    def weight_part(piece, side, shift):
        left, right = sources[piece]
        row = ring_row(shift, deep, piece_rows)
        lanes = slice(side * half, (side + 1) * half)
        return transposed_times(
            left[:, :, pl.ds(row, piece_rows)].reshape(blocks * count, piece_rows),
            right[:, :, lanes].reshape(blocks * count, half),
        )

    def weight_stage(piece, side, shift):
        row = ring_row(shift, deep, piece_rows)
        stage[piece, pl.ds(row, piece_rows), :] = weight_part(piece, side, shift).astype(jnp.bfloat16)

    def weight_whole(piece, side):
        left, right = sources[piece]
        lanes = slice(side * half, (side + 1) * half)

        @pl.loop(0, width // WIDE)
        def _(step):
            row = pl.multiple_of(step * WIDE, WIDE)
            stage[piece, pl.ds(row, WIDE), :] = transposed_times(
                left[:, :, pl.ds(row, WIDE)].reshape(blocks * count, WIDE),
                right[:, :, lanes].reshape(blocks * count, half),
            ).astype(jnp.bfloat16)

    early = pieces_of(deep)[:EARLY]
    arrivals, stores, pending = [], [], []

    def flush():
        for index, store, target in pending:
            store.wait()
            arrivals.append(move(target, early_y.at[index], y_sems, index, y_beside))
        pending.clear()

    def send_piece(piece):
        if piece:
            weight_whole(piece, 1)
            flush()
        for shift in ORDER:
            if not piece:
                weight_stage(piece, 1, shift)
                flush()
            rows_here = pl.ds(ring_row(shift, deep, piece_rows), piece_rows)
            target = sent_out.at[piece, rows_here, :]
            store = load(stage.at[piece, rows_here, :], target, early_sems.at[piece * deep + shift])
            if (piece, shift) in early:
                pending.append((early.index((piece, shift)), store, target))
            else:
                stores.append(store)

    send_piece(0)
    outer(2)
    flush()
    near = move(parts.at[2], landing.at[0], core_sems, 1, core_beside)
    outer(0)
    send_piece(1)
    send_piece(2)
    flush()
    late_stores = list(stores)
    hops = []

    def join_early(pairs):
        for piece, shift in pairs:
            index = early.index((piece, shift))
            product = weight_part(piece, 0, shift)
            arrivals[index].wait_recv()
            early_y[index] = (product + early_y[index].astype(jnp.float32)).astype(jnp.bfloat16)
            if (piece, shift) in HOPS:
                number = HOPS[piece, shift]
                hops.append(
                    move(early_y.at[index], arrived_out.at[number], z_sems, number, z_ahead[shift])
                )
            else:
                stores.append(load(early_y.at[index], sum_out.at[index], sum_sems.at[index]))

    join_early(early[:2])
    near.wait_recv()
    middle_load.wait()
    across.wait_recv()
    step_rows = 128

    @pl.loop(0, count // step_rows)
    def _(step):
        tile = pl.ds(pl.multiple_of(step * step_rows, step_rows), step_rows)
        grad = (
            parts[0, tile, :].astype(jnp.float32)
            + landing[0, tile, :].astype(jnp.float32)
            + incoming[tile, :].astype(jnp.float32)
        )
        total = grads[0, tile, :].astype(jnp.float32) + norm_back(middle[tile, :], gain_ref[1:2, :], grad)
        middle[tile, :] = total
        incoming[tile, :] = total.astype(jnp.bfloat16)

    attention_x = move(incoming, grad_attention_out.at[1], x_sems, 1, x_beside)
    attention_core = move(incoming, grad_attention_out.at[2], core_sems, 2, core_beside)
    stores.append(load(incoming, grad_attention_out.at[0], store_sems.at[0]))
    stores.append(load(middle, grad_middle_out, store_sems.at[3]))

    join_early(early[2:4])
    far.wait_send()
    across.wait_send()
    near.wait_send()

    def branch(block):
        @pl.loop(0, width // WIDE)
        def _(step):
            lanes = pl.ds(pl.multiple_of(step * WIDE, WIDE), WIDE)
            parts[block, :, lanes] = times_transposed(hidden[block], down[lanes, :]).astype(jnp.bfloat16)

    branch(3)
    attention_core.wait_recv()
    branch_far = move(parts.at[3], landing.at[1], core_sems, 3, core_beside)
    branch(2)
    branch_near = move(parts.at[2], landing.at[0], core_sems, 4, core_beside)
    branch(1)
    branch_far.wait_recv()
    add_rows(parts.at[1], landing.at[1])
    stores.append(load(parts.at[1], branch_out.at[1], store_sems.at[7]))
    branch(0)
    stores.append(load(parts.at[0], branch_out.at[0], store_sems.at[8]))
    branch_near.wait_recv()
    stores.append(load(landing.at[0], branch_out.at[2], store_sems.at[9]))
    for copy in late_stores:
        copy.wait()
    for piece in range(3):
        whole = piece not in [pair[0] for pair in early]
        if whole:
            weight_whole(piece, 0)
        for shift in range(deep):
            if (piece, shift) not in early:
                if not whole:
                    weight_stage(piece, 0, shift)
                rows_here = pl.ds(ring_row(shift, deep, piece_rows), piece_rows)
                stores.append(
                    load(
                        stage.at[piece, rows_here, :],
                        own_out.at[piece, rows_here, :],
                        early_sems.at[(3 + piece) * deep + shift],
                    )
                )
    join_early(early[4:])
    attention_x.wait_recv()
    attention_far = move(grad_attention_out.at[1], grad_attention_out.at[3], core_sems, 5, core_beside)
    attention_far.wait_recv()
    for copy in hops:
        copy.wait_recv()
    for copy in stores[len(late_stores) :]:
        copy.wait()
    for copy in arrivals + hops:
        copy.wait_send()
    for copy in (attention_x, attention_core, branch_far, branch_near, attention_far):
        copy.wait_send()


def feed_back(deep, rows, grads, chunks, middle, gain):
    blocks, count, width = rows.shape
    half = chunks.shape[4] // 3
    part = chunks.shape[3]

    def shape(*dims, kind=jnp.bfloat16):
        return jax.ShapeDtypeStruct(dims, kind)

    def room(*dims, kind=jnp.bfloat16):
        return pltpu.VMEM(dims, kind)

    outs = (
        shape(count, width, kind=jnp.float32),
        shape(blocks, count, width),
        shape(3, count, width),
        shape(3, width, half),
        shape(3, width, half),
        shape(EARLY, 2 * part, half),
        shape(len(HOPS), 2 * part, half),
    )
    dma = pltpu.SemaphoreType.DMA
    return pl.pallas_call(
        functools.partial(feed_back_kernel, deep),
        out_shape=outs,
        in_specs=[hbm_spec()] * 4 + [vmem_spec()],
        out_specs=(hbm_spec(),) * len(outs),
        scratch_shapes=[room(width, 2 * half)] * 3
        + [room(blocks, count, width)] * 2
        + [room(blocks, count, 2 * half)] * 3
        + [room(blocks, count, width), room(2, count, width), room(count, width)]
        + [room(count, width, kind=jnp.float32), room(3, width, half), room(EARLY, 2 * part, half)]
        + [dma((2, 5)), dma((3, 2, deep, 2)), dma((10,)), dma((EARLY,)), dma((6 * deep,)), dma((2, 6)), dma((2, 2)), dma((2, EARLY)), dma((2, EARLY))],
        compiler_params=vmem_params(collective_id=2, has_side_effects=True),
        cost_estimate=cost(flops=80 * 10**9, bytes_accessed=10**8, transcendentals=10**7),
        name="feed_back",
    )(rows, grads, chunks, middle, gain)


def attend_back_pair(
    qkv, grad_heads, heads, logs, cosine_ref, sine_ref, grad_qkv, keys, values, grad_keys, grad_values,
    sequence, pair,
):
    count = qkv.shape[1]
    x_place = lax.axis_index("x").astype(jnp.int32)
    lane0 = pl.multiple_of(pair * 4 * LANES, 4 * LANES)
    head0 = pl.multiple_of(pair * 2 * LANES, 2 * LANES)
    mask = diagonal_mask()
    factor = HD ** (-0.5)
    scale = factor * LOG2E
    places = [2 * sequence + lax.rem(x_place + position, jnp.int32(2)) for position in range(2)]
    for position, block in enumerate(places):
        rows = slice(position * count, (position + 1) * count)
        keys[rows, :] = qkv[block, :, pl.ds(lane0 + 2 * LANES, LANES)]
        values[rows, :] = qkv[block, :, pl.ds(lane0 + 3 * LANES, LANES)]
    grad_keys[...] = jnp.zeros_like(grad_keys)
    grad_values[...] = jnp.zeros_like(grad_values)

    def visit(block, start, before):
        rows = slice(start, start + TILE)

        def both(ref, first):
            return jnp.concatenate(
                [ref[block, rows, pl.ds(first, LANES)], ref[block, rows, pl.ds(first + LANES, LANES)]], axis=0
            )

        queries, grads, outs = both(qkv, lane0), both(grad_heads, head0), both(heads, head0)
        lane = lax.broadcasted_iota(jnp.int32, (TILE, LANES), 1)
        kept = logs[block, rows, :]
        log = jnp.concatenate(
            [
                jnp.sum(jnp.where(lane == 2 * pair + head, kept, 0.0), axis=-1, keepdims=True)
                for head in range(2)
            ],
            axis=0,
        )
        inner = jnp.sum(grads.astype(jnp.float32) * outs.astype(jnp.float32), axis=-1, keepdims=True)

        def span(span_rows, masked):
            softmax = jnp.exp2(times_transposed(queries, keys[span_rows, :]) * scale - log)
            if masked:
                softmax = jnp.where(mask, softmax, 0.0)
            grad_softmax = times_transposed(grads, values[span_rows, :])
            grad_scores = (softmax * (grad_softmax - inner)).astype(jnp.bfloat16)
            grad_values[span_rows, :] += transposed_times(softmax.astype(jnp.bfloat16), grads)
            grad_keys[span_rows, :] += transposed_times(grad_scores, queries)
            return nn(grad_scores, keys[span_rows, :])

        grad_queries = span(slice(before, before + TILE), True)
        if before:
            grad_queries = grad_queries + span(slice(0, before), False)
        position, table_rows = before // count, slice(before % count, before % count + TILE)
        cosine, sine = cosine_ref[position, table_rows, :], -sine_ref[position, table_rows, :]
        for head in range(2):
            piece = grad_queries[head * TILE : (head + 1) * TILE] * factor
            grad_qkv[block, rows, pl.ds(lane0 + head * LANES, LANES)] = turn(piece, cosine, sine).astype(
                jnp.bfloat16
            )

    for position, block in enumerate(places):
        for step in range(count // TILE):
            visit(block, step * TILE, position * count + step * TILE)

    for position, block in enumerate(places):
        rows = slice(position * count, (position + 1) * count)
        grad_qkv[block, :, pl.ds(lane0 + 2 * LANES, LANES)] = turn(
            grad_keys[rows, :] * factor, cosine_ref[position], -sine_ref[position]
        ).astype(jnp.bfloat16)
        grad_qkv[block, :, pl.ds(lane0 + 3 * LANES, LANES)] = grad_values[rows, :].astype(jnp.bfloat16)


def heads_back_kernel(
    deep, grad_attention_hbm, qkv_hbm, heads_hbm, logs_hbm, first_hbm, qkv_wide_hbm, out_wide_hbm,
    branch_hbm, sent_hbm, own_hbm, sum_hbm, arrived_hbm, chunks_hbm, qkv_own_hbm,
    cosine_ref, sine_ref, qkv_spread, out_spread,
    first_part, first_core, first_x, branch_x, feed_final, qkv_final, out_final, first_gain_out, second_gain_out,
    grad_attention, qkv, heads, grad_heads, logs, grad_qkv, qkv_wide, out_wide, keys, values, grad_keys,
    grad_values, slots, landing, feed_sum, feed_y, feed_z, out_sent, out_sum, out_y, out_z, qkv_sent, qkv_sum, qkv_y,
    qkv_z, feed_pass, out_pass, qkv_pass, feed_last, qkv_last, out_last, feed_weight, qkv_weight, gain_part, gain_in, gain_total,
    load_sems, own_sems, tile_sems, core_sems, x_sems, y_sems, z_sems, pass_sems, gain_sems,
):
    blocks, count, width = grad_attention.shape
    core_beside, x_beside, y_beside = beside()
    core = lax.axis_index("c").astype(jnp.int32)
    across, along = lax.axis_index("x").astype(jnp.int32), lax.axis_index("y").astype(jnp.int32)
    z_ahead = ahead(deep)
    cube = {
        (rel, up, over): {"c": (core + rel) % 2, "y": (along + up) % 2, "x": (across + over) % 2}
        for rel in range(2)
        for up in range(2)
        for over in range(2)
    }
    far_cube = [key for key in cube if key != (0, 0, 0)]
    greet([cube[key] for key in far_cube] + z_ahead[1:])
    half = feed_sum.shape[3]
    piece_rows = feed_sum.shape[2]
    part = piece_rows // 2
    step_rows = 128
    sent = []

    def load(source, target, sem):
        copy = pltpu.make_async_copy(source, target, sem)
        copy.start()
        return copy

    def move(source, target, sems, index, where):
        copy = send(source, target, (sems.at[0, index], sems.at[1, index]), where)
        sent.append(copy)
        return copy

    late = pieces_of(deep)[EARLY:]
    attention_load = load(grad_attention_hbm, grad_attention, load_sems.at[0])
    out_load = load(out_wide_hbm, out_wide, load_sems.at[1])
    heads_load = load(heads_hbm, heads, load_sems.at[2])
    late_copies = []
    for index, (piece, shift) in enumerate(late):
        row = ring_row(shift, deep, piece_rows)
        late_copies.append(
            move(
                sent_hbm.at[piece, pl.ds(row, piece_rows), :], feed_y.at[piece, shift], y_sems, index, y_beside
            )
        )
    branch_copy = move(branch_hbm.at[1], branch_x, x_sems, 0, x_beside)
    qkv_load = load(qkv_hbm, qkv, load_sems.at[3])
    logs_load = load(logs_hbm, logs, load_sems.at[4])
    wide_load = load(qkv_wide_hbm, qkv_wide, load_sems.at[5])
    own_loads, z_copies = {}, {}
    early_loads = []
    for index, (piece, shift) in enumerate(pieces_of(deep)):
        if (piece, shift) in late:
            row = ring_row(shift, deep, piece_rows)
            own_loads[piece, shift] = load(
                own_hbm.at[piece, pl.ds(row, piece_rows), :], feed_sum.at[piece, shift], own_sems.at[0, index]
            )
        elif shift == 0:
            early_loads.append(load(sum_hbm.at[index], feed_sum.at[piece, 0], own_sems.at[1, index]))
        elif (piece, shift) in HOPS:
            early_loads.append(
                load(arrived_hbm.at[HOPS[piece, shift]], feed_z.at[piece, shift - 1], own_sems.at[1, index])
            )
        else:
            z_copies[piece, shift] = move(
                sum_hbm.at[index],
                feed_z.at[piece, shift - 1],
                z_sems,
                piece * (deep - 1) + shift - 1,
                z_ahead[shift],
            )
    weight_loads = [
        load(chunks_hbm.at[0, 0, :, :, pl.ds(0, 2 * half)], feed_weight, load_sems.at[6]),
        load(qkv_own_hbm, qkv_weight, load_sems.at[7]),
    ]

    attention_load.wait()
    out_load.wait()

    @pl.loop(0, blocks)
    def _(block):
        grad_heads[block] = nn(grad_attention[block], out_wide[...]).astype(jnp.bfloat16)

    heads_load.wait()

    def weight_tile(left, right, spread, side):
        size = spread.shape[1]
        right = right[:, :, side * size : (side + 1) * size].reshape(blocks * count, size)
        product = transposed_times(left.reshape(blocks * count, piece_rows), right)
        return times_transposed(product.astype(jnp.bfloat16), spread[...]).astype(jnp.bfloat16)

    guarded = []
    z_place = lax.axis_index("z").astype(jnp.int32)
    last = deep - 1
    inside = (z_place > 0) & (z_place < last)
    inward = {"z": jnp.where(z_place == 0, jnp.int32(1), jnp.int32(last - 1))}

    def remote(source, target, sems, index, where):
        return pltpu.make_async_remote_copy(
            src_ref=source,
            dst_ref=target,
            send_sem=sems.at[0, index],
            recv_sem=sems.at[1, index],
            device_id=where,
            device_id_type=pl.DeviceIdType.MESH,
        )

    def begin(copy, condition):
        pl.when(condition)(copy.start)
        guarded.append((copy, condition))

    def clear(target):
        @pl.when(z_place == 0)
        def _():
            target[0] = jnp.zeros(target.shape[1:], target.dtype)

        @pl.when(z_place == last)
        def _():
            target[last - 1] = jnp.zeros(target.shape[1:], target.dtype)

    def join_piece(name, number, total, arrived, target, passing, shift):
        add_rows(total.at[shift], arrived.at[shift])
        if not shift:
            return
        direct = remote(total.at[shift], target.at[shift - 1], z_sems, number * last + shift - 1, z_ahead[shift])
        if passing is None:
            direct.start()
            sent.append(direct)
        else:
            far = z_place == (last if shift == 1 else 0)
            through = remote(total.at[shift], passing, pass_sems, number, inward)
            if shift == 2:

                @pl.when(inside)
                def _():
                    through.wait_recv()
                    add_rows(total.at[shift], passing)

                direct.start()
                sent.append(direct)
            else:
                begin(through, far)
                begin(direct, jnp.logical_not(far))
        z_copies[name, shift] = direct

    def join_feed(piece, shift):
        own_loads[piece, shift].wait()
        join_piece(
            piece, piece, feed_sum.at[piece], feed_y.at[piece], feed_z.at[piece],
            feed_pass if piece == 2 else None, shift,
        )

    for target in (feed_z.at[2], out_z, qkv_z):
        clear(target)

    def join_feed_late(index):
        late_copies[index].wait_recv()
        join_feed(*late[index])

    qkv_load.wait()
    logs_load.wait()
    for sequence in range(2):

        for pair in range(2):
            attend_back_pair(
                qkv, grad_heads, heads, logs, cosine_ref, sine_ref, grad_qkv, keys, values, grad_keys,
                grad_values, sequence, pair,
            )
        join_feed_late(sequence)
    wide_load.wait()

    def first_tile(order):
        row = ring_row(ORDER[order], deep, piece_rows)
        slot = (order % 2) * 512
        return load(
            first_hbm.at[:, :, pl.ds(row, piece_rows)],
            qkv.at[:, :, pl.ds(slot, piece_rows)],
            tile_sems.at[order],
        )

    first_loads = [first_tile(order) for order in range(2)]

    def first_piece(block):
        @pl.loop(0, width // WIDE)
        def _(step):
            lanes = pl.ds(pl.multiple_of(step * WIDE, WIDE), WIDE)
            slots[block % 3, :, lanes] = times_transposed(grad_qkv[block], qkv_wide[lanes, :]).astype(
                jnp.bfloat16
            )

    first_piece(3)
    core_far = move(slots.at[0], landing, core_sems, 0, core_beside)
    first_piece(1)
    core_far.wait_recv()
    add_rows(slots.at[1], landing)
    x_copy = move(slots.at[1], first_x, x_sems, 1, x_beside)
    first_piece(2)
    core_near = move(slots.at[2], first_core, core_sems, 1, core_beside)
    core_far.wait_send()
    sent[:] = [copy for copy in sent if copy is not core_far]
    first_piece(0)
    first_store = load(slots.at[0], first_part, load_sems.at[8])
    join_feed_late(2)
    y_index = len(late)
    out_copies = {}
    for shift in ORDER:
        row = ring_row(shift, deep, piece_rows)
        out_sent[shift] = weight_tile(grad_attention[:, :, pl.ds(row, piece_rows)], heads, out_spread, 1)
        out_copies[shift] = move(out_sent.at[shift], out_y.at[shift], y_sems, y_index + shift, y_beside)

    @pl.loop(0, deep)
    def _(shift):
        row = ring_row(shift, deep, piece_rows)
        out_sum[shift] = weight_tile(grad_attention[:, :, pl.ds(row, piece_rows)], heads, out_spread, 0)

    join_feed_late(3)

    qkv_copies = {}
    y_index += deep
    for order, shift in enumerate(ORDER):
        first_loads[order].wait()
        slot = (order % 2) * 512
        left = qkv[:, :, slot : slot + piece_rows]
        qkv_sent[shift] = weight_tile(left, grad_qkv, qkv_spread, 1)
        qkv_copies[shift] = move(qkv_sent.at[shift], qkv_y.at[shift], y_sems, y_index + shift, y_beside)
        qkv_sum[shift] = weight_tile(left, grad_qkv, qkv_spread, 0)
        if order + 2 < deep:
            first_loads.append(first_tile(order + 2))

    join_feed_late(4)
    for shift in ORDER:
        out_copies[shift].wait_recv()
        join_piece("out", 3, out_sum, out_y, out_z, out_pass, shift)

    finals = []

    def finish(name, number, total, arrived, last, final, weights):
        for shift in range(1, deep):
            if (name, shift) not in z_copies:
                continue
            if name in (0, 1) or shift == 2:
                z_copies[name, shift].wait_recv()
            else:
                pl.when(z_place != (0 if shift == 1 else deep - 1))(z_copies[name, shift].wait_recv)
        size = total.shape[2]
        sums = []
        for rel in range(2):
            row = pl.multiple_of(lax.rem(core + rel, jnp.int32(2)) * part, part)
            value = total[0, pl.ds(row, part), :].astype(jnp.float32)
            for shift in range(deep - 1):
                value = value + arrived[shift, pl.ds(row, part), :].astype(jnp.float32)
            last[rel] = value
            if weights is not None:
                product = value * weights[rel].astype(jnp.float32)
                sums.append(sum(product[:, i * LANES : (i + 1) * LANES] for i in range(size // LANES)))
        finals.append(load(last.at[0], final.at[core], own_sems.at[1, 12 + number]))
        finals.append(move(last.at[1], final.at[core], core_sems, 2 + number, core_beside))
        return sums

    def gain_exchange(which, sums):
        slots = {}
        for rel in range(2):
            gain_part[which, rel] = sums[rel]
        piece = part // 4
        for number, key in enumerate(far_cube):
            rel, up, over = key
            target = ((along + up) % 2) * 2 + (across + over) % 2
            row = pl.multiple_of(target * piece, 8)
            slots[key] = move(
                gain_part.at[which, rel, pl.ds(row, piece), :],
                gain_in.at[which, number],
                gain_sems,
                which * len(far_cube) + number,
                cube[key],
            )
        return slots

    def gain_finish(which, slots, output):
        piece = part // 4
        row = pl.multiple_of((along * 2 + across) * piece, 8)
        value = gain_part[which, 0, pl.ds(row, piece), :]
        for number, key in enumerate(far_cube):
            slots[key].wait_recv()
            value = value + gain_in[which, number]
        gain_total[which] = value
        return load(gain_total.at[which], output, load_sems.at[9 + which])

    for copy in weight_loads + early_loads:
        copy.wait()
    finish(0, 0, feed_sum.at[0], feed_z.at[0], feed_last.at[0], feed_final.at[0], None)
    gate_sums = finish(
        1, 1, feed_sum.at[1], feed_z.at[1], feed_last.at[1], feed_final.at[1], feed_weight.at[:, :, pl.ds(0, half)]
    )
    for shift in ORDER:
        qkv_copies[shift].wait_recv()
        join_piece("qkv", 4, qkv_sum, qkv_y, qkv_z, qkv_pass, shift)
    up_sums = finish(
        2, 2, feed_sum.at[2], feed_z.at[2], feed_last.at[2], feed_final.at[2],
        feed_weight.at[:, :, pl.ds(half, half)],
    )
    second_slots = gain_exchange(1, [one + two for one, two in zip(gate_sums, up_sums)])
    finish("out", 3, out_sum, out_z, out_last, out_final, None)
    sums = finish("qkv", 4, qkv_sum, qkv_z, qkv_last, qkv_final, qkv_weight)
    first_slots = gain_exchange(0, sums)
    second_store = gain_finish(1, second_slots, second_gain_out)
    first_gain_store = gain_finish(0, first_slots, first_gain_out)
    for copy in (branch_copy, x_copy, core_near):
        copy.wait_recv()
    for number in range(5):
        finals[2 * number].wait()
        finals[2 * number + 1].wait_recv()
    for copy in (first_store, second_store, first_gain_store):
        copy.wait()
    for copy in sent:
        copy.wait_send()
    for copy, condition in guarded:
        pl.when(condition)(copy.wait_send)


def heads_back(
    deep, grad_attention, qkv, heads, logs, first, qkv_wide, out_wide, branch, sent, own, sums, arrived, chunks,
    qkv_own, cosine, sine, spreads,
):
    blocks, count, width = grad_attention.shape
    part, half = chunks.shape[3], chunks.shape[4] // 3
    qkv_half, out_half = spreads[0].shape[0], spreads[1].shape[0]
    rows = 2 * part

    def shape(*dims, kind=jnp.bfloat16):
        return jax.ShapeDtypeStruct(dims, kind)

    def room(*dims, kind=jnp.bfloat16):
        return pltpu.VMEM(dims, kind)

    wide = jnp.float32
    outs = (
        shape(count, width),
        shape(count, width),
        shape(count, width),
        shape(count, width),
        shape(3, 2, part, half, kind=wide),
        shape(2, part, qkv_half, kind=wide),
        shape(2, part, out_half, kind=wide),
        shape(part // 4, LANES, kind=wide),
        shape(part // 4, LANES, kind=wide),
    )
    dma = pltpu.SemaphoreType.DMA
    scratch = [
        room(blocks, count, width),
        room(*qkv.shape),
        room(*heads.shape),
        room(*heads.shape),
        room(*logs.shape, kind=wide),
        room(*qkv.shape),
        room(*qkv_wide.shape),
        room(*out_wide.shape),
        room(2 * count, LANES),
        room(2 * count, LANES),
        room(2 * count, LANES, kind=wide),
        room(2 * count, LANES, kind=wide),
        room(3, count, width),
        room(count, width),
        room(3, deep, rows, half),
        room(3, deep, rows, half),
        room(3, deep - 1, rows, half),
        room(deep, rows, out_half),
        room(deep, rows, out_half),
        room(deep, rows, out_half),
        room(deep - 1, rows, out_half),
        room(deep, rows, qkv_half),
        room(deep, rows, qkv_half),
        room(deep, rows, qkv_half),
        room(deep - 1, rows, qkv_half),
        room(rows, half),
        room(rows, out_half),
        room(rows, qkv_half),
        room(3, 2, part, half, kind=wide),
        room(2, part, qkv_half, kind=wide),
        room(2, part, out_half, kind=wide),
        room(2, part, 2 * half),
        room(2, part, qkv_half),
        room(2, 2, part, LANES, kind=wide),
        room(2, 7, part // 4, LANES, kind=wide),
        room(2, part // 4, LANES, kind=wide),
        dma((11,)),
        dma((2, max(3 * deep, 17))),
        dma((deep,)),
        dma((2, 7)),
        dma((2, 2)),
        dma((2, 5 * deep)),
        dma((2, 5 * (deep - 1))),
        dma((2, 5)),
        dma((2, 14)),
    ]
    return pl.pallas_call(
        functools.partial(heads_back_kernel, deep),
        out_shape=outs,
        in_specs=[hbm_spec()] * 14 + [vmem_spec()] * 4,
        out_specs=(hbm_spec(),) * len(outs),
        scratch_shapes=scratch,
        compiler_params=vmem_params(collective_id=3, has_side_effects=True),
        cost_estimate=cost(flops=30 * 10**9, bytes_accessed=10**8, transcendentals=10**7),
        name="heads_back",
    )(
        grad_attention, qkv, heads, logs, first, qkv_wide, out_wide, branch, sent, own, sums, arrived, chunks,
        qkv_own, cosine, sine, *spreads,
    )


def tables(rows):
    lane = np.arange(LANES)
    entry = lane % (LANES // 2)
    live = (entry < HD // 2).astype(np.float64)
    sign = np.where(lane < LANES // 2, -1.0, 1.0) * live
    inverse = np.where(live > 0, THETA ** (-2.0 * entry / HD), 0.0).astype(np.float32)
    position = np.arange(2 * rows, dtype=np.float32)
    angles = (position[:, None] * inverse[None, :]).astype(np.float32).astype(np.float64)
    both = (np.cos(angles) * live, np.sin(angles) * sign)
    return tuple(jnp.asarray(table.astype(np.float32).reshape(2, rows, LANES)) for table in both)


def norm_factor(rows):
    return lax.rsqrt(jnp.mean(rows * rows, axis=-1, keepdims=True) + EPSILON)


def norm_back(rows, gain, grad):
    factor = norm_factor(rows)
    scaled = grad * gain
    return factor * scaled - rows * factor**3 * jnp.mean(scaled * rows, axis=-1, keepdims=True)


def join(halves):
    return jnp.concatenate([halves[0], halves[1]], axis=1)


def gain_grad(lanes, gain, depth_place):
    piece = lanes.shape[0]
    start = (depth_place * 4 + lax.axis_index("y") * 2 + lax.axis_index("x")) * piece
    return jnp.sum(lanes, axis=1) / lax.dynamic_slice_in_dim(gain, start, piece)


def fast_local(
    tokens,
    cotangent,
    first_gain,
    query_weight,
    key_weight,
    value_weight,
    out_weight,
    second_gain,
    gate_weight,
    up_weight,
    down_weight,
):
    deep = lax.axis_size("z")
    z_place, core = (lax.axis_index(name).astype(jnp.int32) for name in ("z", "c"))
    rows = tokens.shape[0]
    depth_place = z_place * 2 + core
    own_rows = tokens.astype(jnp.float32)
    out_turned, down_turned = out_weight.T, down_weight.T

    def halves(*weights):
        result = []
        for half in range(2):
            pieces = []
            for weight in weights:
                size = weight.shape[1] // 2
                pieces.append(weight[:, half * size : (half + 1) * size])
            result.append(jnp.concatenate(pieces, axis=1))
        return result

    spreads = (spread_heads(3, 1), spread_heads(0, 2))
    cosine, sine = tables(rows)
    gains = jnp.stack([first_gain, second_gain])
    (
        first_all, qkv_all, heads_all, logs_all, qkv_weight, out_wide, middle, second_all, cotangent_all, chunks, qkv_own,
    ) = forward(
        deep,
        cotangent,
        tokens,
        gains,
        jnp.stack(
            halves(gate_weight, up_weight, down_turned, query_weight, key_weight, value_weight, out_turned)
        ),
        (
            gate_weight.shape[1] * 3 // 2,
            query_weight.shape[1] // 2 + key_weight.shape[1],
            out_turned.shape[1] // 2,
        ),
        spreads,
        cosine,
        sine,
    )
    grad_middle, grad_attention, branch, sent, own, sums, arrived = feed_back(
        deep, second_all, cotangent_all, chunks, middle, gains
    )
    first_part, first_core, first_x, branch_x, feed_final, qkv_final, out_final, first_lanes, second_lanes = (
        heads_back(
            deep, grad_attention, qkv_all, heads_all, logs_all, first_all, qkv_weight, out_wide, branch, sent,
            own, sums, arrived, chunks, qkv_own, cosine, sine, spreads,
        )
    )

    def total(*parts):
        return sum(piece.astype(jnp.float32) for piece in parts)

    result = (middle + total(branch[0], branch[2], branch_x)).astype(jnp.bfloat16)
    grad_first = total(first_part, first_core, first_x)
    tokens_grad = grad_middle + norm_back(own_rows, first_gain, grad_first)
    query_end = query_weight.shape[1] // 2
    key_end = query_end + key_weight.shape[1] // 2
    return (
        result,
        tokens_grad,
        join(qkv_final[:, :, :query_end]),
        join(qkv_final[:, :, query_end:key_end]),
        join(qkv_final[:, :, key_end:]),
        join(out_final).T,
        join(feed_final[1]),
        join(feed_final[2]),
        join(feed_final[0]).T,
        gain_grad(first_lanes, first_gain, depth_place),
        gain_grad(second_lanes, second_gain, depth_place),
    )


def specs(depth, width):
    both = depth + width
    rows, inward, outward = P(both, None), P(depth, width), P(width, depth)
    in_specs = (rows, rows, P(), inward, inward, inward, outward, P(), inward, inward, outward)
    out_specs = (rows, rows, inward, inward, inward, outward, inward, inward, outward, P(both), P(both))
    return in_specs, out_specs


def solution(mesh):
    depth, width = mesh.shape["dp"], mesh.shape["tensor"]

    def run(tokens, cotangent, *weights):
        fits = (
            width == 4
            and depth == 8
            and tokens.shape[0] * 2 == SEQ_LEN * depth * width
            and weights[2].shape[1] == 2 * width * HD
            and weights[1].shape[1] == 4 * width * HD
        )
        if fits:
            devices = mesh.devices.reshape(depth // 2, 2, 2, 2)
            fine = jax.sharding.Mesh(devices, ("z", "c", "y", "x"))
            in_specs, out_specs = specs(("z", "c"), ("y", "x"))
            call, over = fast_local, fine
        else:
            in_specs, out_specs = specs(("dp",), ("tensor",))
            call, over = local, mesh
        return jax.shard_map(call, mesh=over, in_specs=in_specs, out_specs=out_specs, check_vma=False)(
            tokens, cotangent, *weights
        )

    return run
```

```python
import functools

import jax
import jax.numpy as jnp
import numpy as np
from jax import lax
from jax.experimental import pallas as pl
from jax.experimental.pallas import tpu as pltpu
from jax.sharding import PartitionSpec as P

HD = 96
SEQ_LEN = 1024


EPSILON = 1e-05
THETA = 100000.0
MASKED = -1e30
LOG2E = 1.4426950408889634
LANES = 128
SHARE = 20
VMEM_BYTES = 63 * 2**20


def normed(inputs, gain):
    factor = lax.rsqrt(jnp.mean(inputs * inputs, axis=-1, keepdims=True) + EPSILON)
    return inputs * factor * gain


def rotate(vectors, direction):
    seq_rows, head_count, head_size = vectors.shape
    half_size = head_size // 2
    position = (jnp.arange(seq_rows, dtype=jnp.int32) % SEQ_LEN).astype(jnp.float32)
    inverse = THETA ** (-2.0 * jnp.arange(half_size, dtype=jnp.float32) / head_size)
    angles = position[:, None] * inverse[None, :]
    cosine = jnp.cos(angles)[:, None, :]
    sine_part = direction * jnp.sin(angles)[:, None, :]
    leading = vectors[..., :half_size]
    trailing = vectors[..., half_size:]
    return jnp.concatenate(
        [leading * cosine - trailing * sine_part, trailing * cosine + leading * sine_part], axis=-1
    )


def times_transposed(left, right):
    return lax.dot_general(
        left, right, (((1,), (1,)), ((), ())), preferred_element_type=jnp.float32
    )


def transposed_times(left, right):
    return lax.dot_general(
        left, right, (((0,), (0,)), ((), ())), preferred_element_type=jnp.float32
    )


def scaled_scores(queries, keys_rot):
    raw_scores = jnp.einsum(
        "qhgd,khd->hgqk", queries, keys_rot, preferred_element_type=jnp.float32
    ) * queries.shape[-1] ** (-0.5)
    length_rows = queries.shape[0]
    causal = jnp.arange(length_rows)[:, None] >= jnp.arange(length_rows)[None, :]
    return jnp.where(causal, raw_scores, MASKED)


def attend_forward(operands):
    queries, keys_rot, values = operands
    scores = scaled_scores(queries, keys_rot)
    row_max = jnp.max(scores, axis=-1, keepdims=True)
    weights = jnp.exp(scores - row_max)
    row_total = jnp.sum(weights, axis=-1, keepdims=True)
    softmax = (weights / row_total).astype(jnp.bfloat16)
    mixed_heads = jnp.einsum("hgqk,khd->qhgd", softmax, values, preferred_element_type=jnp.float32)
    return (mixed_heads.astype(jnp.bfloat16), (row_max + jnp.log(row_total))[..., 0])


def attend_backward(operands):
    queries, keys_rot, values, grad_mixed, log_total = operands
    scores = scaled_scores(queries, keys_rot)
    softmax = jnp.exp(scores - log_total[..., None])
    grad_softmax = jnp.einsum(
        "qhgd,khd->hgqk", grad_mixed, values, preferred_element_type=jnp.float32
    )
    grad_values = jnp.einsum(
        "hgqk,qhgd->khd",
        softmax.astype(jnp.bfloat16),
        grad_mixed,
        preferred_element_type=jnp.float32,
    )
    row_inner = jnp.sum(softmax * grad_softmax, axis=-1, keepdims=True)
    grad_scores = (softmax * (grad_softmax - row_inner)).astype(jnp.bfloat16)
    scale_factor = queries.shape[-1] ** (-0.5)
    grad_queries = (
        jnp.einsum("hgqk,khd->qhgd", grad_scores, keys_rot, preferred_element_type=jnp.float32)
        * scale_factor
    )
    grad_keys = (
        jnp.einsum("hgqk,qhgd->khd", grad_scores, queries, preferred_element_type=jnp.float32)
        * scale_factor
    )
    return (grad_queries, grad_keys, grad_values)


def gather_rows(shard):
    return lax.all_gather(shard, "tensor", axis=0, tiled=True)


def gather_grads(shard):
    return lax.all_gather(shard, "tensor", axis=0, tiled=True)


def sum_outputs(term, row_count):
    return lax.psum_scatter(
        term(jnp.int32(0), row_count * lax.axis_size("tensor")),
        "tensor",
        scatter_dimension=0,
        tiled=True,
    )


def sum_inputs(term, row_count):
    return lax.psum_scatter(
        term(jnp.int32(0), row_count * lax.axis_size("tensor")),
        "tensor",
        scatter_dimension=0,
        tiled=True,
    )


def local(
    tokens,
    cotangent,
    first_gain,
    query_weight,
    key_weight,
    value_weight,
    out_weight,
    second_gain,
    gate_weight,
    up_weight,
    down_weight,
):
    query_weight, key_weight, value_weight, out_weight, gate_weight, up_weight, down_weight = (
        lax.all_gather(query_weight, "dp", axis=0, tiled=True),
        lax.all_gather(key_weight, "dp", axis=0, tiled=True),
        lax.all_gather(value_weight, "dp", axis=0, tiled=True),
        lax.all_gather(out_weight, "dp", axis=1, tiled=True),
        lax.all_gather(gate_weight, "dp", axis=0, tiled=True),
        lax.all_gather(up_weight, "dp", axis=0, tiled=True),
        lax.all_gather(down_weight, "dp", axis=1, tiled=True),
    )
    own_rows = tokens.astype(jnp.float32)
    row_count = own_rows.shape[0]
    pair_count = key_weight.shape[1] // HD
    first_normed = normed(own_rows, first_gain).astype(jnp.bfloat16)
    first_rows = gather_rows(first_normed)
    group_rows = first_rows.shape[0]
    sequences = group_rows // SEQ_LEN
    query_pre = jnp.dot(first_rows, query_weight, preferred_element_type=jnp.float32)
    key_pre = jnp.dot(first_rows, key_weight, preferred_element_type=jnp.float32)
    value_pre = jnp.dot(first_rows, value_weight, preferred_element_type=jnp.float32)
    queries = rotate(query_pre.reshape(group_rows, 2 * pair_count, HD), 1.0).astype(jnp.bfloat16)
    queries = queries.reshape(sequences, SEQ_LEN, pair_count, 2, HD)
    keys_rot = rotate(key_pre.reshape(group_rows, pair_count, HD), 1.0).astype(jnp.bfloat16)
    keys_rot = keys_rot.reshape(sequences, SEQ_LEN, pair_count, HD)
    values = value_pre.astype(jnp.bfloat16).reshape(sequences, SEQ_LEN, pair_count, HD)
    mixed_heads, log_total = lax.map(attend_forward, (queries, keys_rot, values))
    heads_out = mixed_heads.reshape(group_rows, 2 * pair_count * HD)
    heads_rows = lax.all_to_all(heads_out, "tensor", split_axis=0, concat_axis=1, tiled=True)
    out_full = lax.all_gather(out_weight, "tensor", axis=0, tiled=True)
    attention_branch = jnp.dot(heads_rows, out_full, preferred_element_type=jnp.float32)
    middle = own_rows + attention_branch
    second_normed = normed(middle, second_gain).astype(jnp.bfloat16)
    second_rows = gather_rows(second_normed)
    gate_full, up_full, down_full = (gate_weight, up_weight, down_weight)
    gate_value = jnp.dot(second_rows, gate_full, preferred_element_type=jnp.float32)
    up_value = jnp.dot(second_rows, up_full, preferred_element_type=jnp.float32)
    sigmoid_gate = jax.nn.sigmoid(gate_value)
    swish_gate = gate_value * sigmoid_gate
    hidden = (swish_gate * up_value).astype(jnp.bfloat16)

    def project_hidden(start, amount):
        return jnp.dot(hidden, down_full, preferred_element_type=jnp.float32)

    ffn_branch = sum_outputs(project_hidden, row_count)
    grad_branch = gather_grads(cotangent)
    result = (middle + ffn_branch).astype(jnp.bfloat16)
    grad_hidden = times_transposed(grad_branch, down_full)
    down_part = transposed_times(hidden, grad_branch)
    slope = sigmoid_gate + gate_value * sigmoid_gate * (1.0 - sigmoid_gate)
    grad_gate = (grad_hidden * up_value * slope).astype(jnp.bfloat16)
    grad_up = (grad_hidden * swish_gate).astype(jnp.bfloat16)
    gate_part = transposed_times(second_rows, grad_gate)
    up_part = transposed_times(second_rows, grad_up)

    def second_back(start, amount):
        return times_transposed(grad_gate, gate_full) + times_transposed(grad_up, up_full)

    grad_second = sum_inputs(second_back, row_count)
    second_unused, second_pull = jax.vjp(normed, middle, second_gain)
    grad_middle_norm, second_gain_part = second_pull(grad_second)
    grad_middle = cotangent.astype(jnp.float32) + grad_middle_norm
    grad_attention = grad_middle.astype(jnp.bfloat16)
    grad_heads_rows = times_transposed(grad_attention, out_full).astype(jnp.bfloat16)
    grad_heads = lax.all_to_all(grad_heads_rows, "tensor", split_axis=1, concat_axis=0, tiled=True)
    out_part = lax.psum_scatter(
        transposed_times(heads_rows, grad_attention).astype(jnp.bfloat16),
        "tensor",
        scatter_dimension=0,
        tiled=True,
    )
    grad_mixed = grad_heads.reshape(sequences, SEQ_LEN, pair_count, 2, HD)
    grad_queries, grad_keys, grad_values = lax.map(
        attend_backward, (queries, keys_rot, values, grad_mixed, log_total)
    )
    grad_query = (
        rotate(grad_queries.reshape(group_rows, 2 * pair_count, HD), -1.0)
        .reshape(group_rows, -1)
        .astype(jnp.bfloat16)
    )
    grad_key = (
        rotate(grad_keys.reshape(group_rows, pair_count, HD), -1.0)
        .reshape(group_rows, -1)
        .astype(jnp.bfloat16)
    )
    grad_value = grad_values.reshape(group_rows, -1).astype(jnp.bfloat16)
    query_part = transposed_times(first_rows, grad_query)
    key_part = transposed_times(first_rows, grad_key)
    value_part = transposed_times(first_rows, grad_value)

    def first_back(start, amount):
        return (
            times_transposed(grad_query, query_weight)
            + times_transposed(grad_key, key_weight)
            + times_transposed(grad_value, value_weight)
        )

    grad_first = sum_inputs(first_back, row_count)
    first_unused, first_pull = jax.vjp(normed, own_rows, first_gain)
    grad_own_norm, first_gain_part = first_pull(grad_first)
    tokens_grad = grad_middle + grad_own_norm
    query_grad, key_grad, value_grad, out_grad, gate_grad, up_grad, down_grad = (
        lax.psum_scatter(
            query_part.astype(jnp.bfloat16), "dp", scatter_dimension=0, tiled=True
        ).astype(jnp.float32),
        lax.psum_scatter(
            key_part.astype(jnp.bfloat16), "dp", scatter_dimension=0, tiled=True
        ).astype(jnp.float32),
        lax.psum_scatter(
            value_part.astype(jnp.bfloat16), "dp", scatter_dimension=0, tiled=True
        ).astype(jnp.float32),
        lax.psum_scatter(out_part, "dp", scatter_dimension=1, tiled=True).astype(jnp.float32),
        lax.psum_scatter(
            gate_part.astype(jnp.bfloat16), "dp", scatter_dimension=0, tiled=True
        ).astype(jnp.float32),
        lax.psum_scatter(
            up_part.astype(jnp.bfloat16), "dp", scatter_dimension=0, tiled=True
        ).astype(jnp.float32),
        lax.psum_scatter(
            down_part.astype(jnp.bfloat16), "dp", scatter_dimension=1, tiled=True
        ).astype(jnp.float32),
    )
    first_gain_grad, second_gain_grad = (
        lax.psum_scatter(first_gain_part, ("dp", "tensor"), scatter_dimension=0, tiled=True),
        lax.psum_scatter(second_gain_part, ("dp", "tensor"), scatter_dimension=0, tiled=True),
    )
    return (
        result,
        tokens_grad,
        query_grad,
        key_grad,
        value_grad,
        out_grad,
        gate_grad,
        up_grad,
        down_grad,
        first_gain_grad,
        second_gain_grad,
    )


def nn(left, right):
    return jnp.dot(left, right, preferred_element_type=jnp.float32)


def cost(flops, bytes_accessed, transcendentals):
    return pl.CostEstimate(
        flops=flops // SHARE, bytes_accessed=bytes_accessed // SHARE, transcendentals=transcendentals // SHARE
    )


def vmem_params(**more):
    return pltpu.CompilerParams(vmem_limit_bytes=VMEM_BYTES, **more)


def vmem_spec():
    return pl.BlockSpec(memory_space=pltpu.VMEM)


def spread_heads(heads_split, heads_plain):
    columns = (heads_split + heads_plain) * HD
    spread = np.zeros((columns, (heads_split + heads_plain) * LANES), np.float32)
    for head in range(heads_split + heads_plain):
        for entry in range(HD):
            lane = entry
            if head < heads_split and entry >= HD // 2:
                lane = entry - HD // 2 + LANES // 2
            spread[head * HD + entry, head * LANES + lane] = 1.0
    return jnp.asarray(spread, jnp.bfloat16)


def turn(vectors, cosine, sine):
    return vectors * cosine + pltpu.roll(vectors, LANES // 2, 1) * sine


TILE = 256
WIDE = 768


def diagonal_mask():
    row = lax.broadcasted_iota(jnp.int32, (2 * TILE, TILE), 0)
    row = jnp.where(row >= TILE, row - TILE, row)
    return row >= lax.broadcasted_iota(jnp.int32, (2 * TILE, TILE), 1)


def hbm_spec():
    return pl.BlockSpec(memory_space=pltpu.HBM)


def send(source, target, sems, where):
    copy = pltpu.make_async_remote_copy(
        src_ref=source,
        dst_ref=target,
        send_sem=sems[0],
        recv_sem=sems[1],
        device_id=where,
        device_id_type=pl.DeviceIdType.MESH,
    )
    copy.start()
    return copy


def greet(partners):
    barrier = pltpu.get_barrier_semaphore()
    for partner in partners:
        pl.semaphore_signal(barrier, inc=1, device_id=partner, device_id_type=pl.DeviceIdType.MESH)
    pl.semaphore_wait(barrier, len(partners))


def beside():
    core, across, along = (lax.axis_index(name).astype(jnp.int32) for name in ("c", "x", "y"))
    return {"c": 1 - core}, {"x": 1 - across}, {"y": 1 - along}


def grid_offset(slot, rel, deep, part):
    z_place = lax.rem(lax.axis_index("z").astype(jnp.int32) + slot, jnp.int32(deep))
    core = lax.rem(lax.axis_index("c").astype(jnp.int32) + rel, jnp.int32(2))
    return pl.multiple_of((z_place * 2 + core) * part, 64)


def spread_weight(buffer, spread_ref, wide, deep, side):
    part = buffer.shape[3]
    half = wide.shape[1] // 2

    @pl.loop(0, 2 * deep)
    def _(step):
        rel, slot = lax.rem(step, jnp.int32(2)), step // 2
        rows = pl.ds(grid_offset(slot, rel, deep, part), part)
        lanes = slice(side * half, (side + 1) * half)
        wide[rows, lanes] = nn(buffer[side, slot, rel], spread_ref[...]).astype(jnp.bfloat16)


def attend_pair(qkv, heads, logs, keys, values, sequence, pair):
    count = qkv.shape[1]
    x_place = lax.axis_index("x").astype(jnp.int32)
    lane0 = pl.multiple_of(pair * 4 * LANES, 4 * LANES)
    mask = diagonal_mask()
    scale = HD ** (-0.5) * LOG2E
    places = [2 * sequence + lax.rem(x_place + position, jnp.int32(2)) for position in range(2)]
    for position, block in enumerate(places):
        rows = slice(position * count, (position + 1) * count)
        keys[rows, :] = qkv[block, :, pl.ds(lane0 + 2 * LANES, LANES)]
        values[rows, :] = qkv[block, :, pl.ds(lane0 + 3 * LANES, LANES)]

    def visit(block, start, before):
        rows = slice(start, start + TILE)
        queries = jnp.concatenate(
            [qkv[block, rows, pl.ds(lane0, LANES)], qkv[block, rows, pl.ds(lane0 + LANES, LANES)]], axis=0
        )
        edge = slice(before, before + TILE)
        near = jnp.where(mask, times_transposed(queries, keys[edge, :]), MASKED)
        top = jnp.max(near, axis=-1, keepdims=True)
        if before:
            far = times_transposed(queries, keys[:before, :])
            top = jnp.maximum(top, jnp.max(far, axis=-1, keepdims=True))
        top = top * scale
        near = jnp.exp2(near * scale - top)
        total = jnp.sum(near, axis=-1, keepdims=True)
        mixed = nn(near.astype(jnp.bfloat16), values[edge, :])
        if before:
            far = jnp.exp2(far * scale - top)
            total = total + jnp.sum(far, axis=-1, keepdims=True)
            mixed = mixed + nn(far.astype(jnp.bfloat16), values[:before, :])
        mixed = (mixed / total).astype(jnp.bfloat16)
        log = top + jnp.log2(total)
        lane = lax.broadcasted_iota(jnp.int32, (TILE, LANES), 1)
        kept = logs[block, rows, :]
        for head in range(2):
            part = slice(head * TILE, (head + 1) * TILE)
            out_lane = pl.multiple_of(pair * 2 * LANES, LANES) + head * LANES
            heads[block, rows, pl.ds(out_lane, LANES)] = mixed[part]
            kept = jnp.where(lane == 2 * pair + head, log[part], kept)
        logs[block, rows, :] = kept

    for position, block in enumerate(places):
        for step in range(count // TILE):
            visit(block, step * TILE, position * count + step * TILE)


def forward_kernel(
    deep, cotangent_ref, tokens_ref, gains_ref, query_ref, key_ref, value_ref, out_ref, gate_ref, up_ref, down_ref,
    qkv_spread, out_spread, cosine_ref, sine_ref,
    first_out, qkv_out, heads_out, logs_out, qkv_wide_out, out_wide_out, middle_out, second_out,
    cotangent_out, feed_out, qkv_own_out,
    qkv_halves, out_halves, feed_halves, first_all, qkv_buffer, out_buffer, qkv_wide, out_wide, qkv, heads, logs, keys, values,
    parts, core_parts, outgoing, incoming, middle, second,
    local_sems, row_sems, qkv_sems, out_sems, feed_sems, core_sems,
):
    core, z_place = lax.axis_index("c").astype(jnp.int32), lax.axis_index("z").astype(jnp.int32)
    core_beside, x_beside, y_beside = beside()
    count = tokens_ref.shape[0]
    ring = jnp.int32(deep)
    z_beside = {way: {"z": lax.rem(z_place + deep + way, ring)} for way in (-1, 1)}
    for half in range(2):
        start = 0
        for ref in (query_ref, key_ref, value_ref):
            size = ref.shape[1] // 2
            qkv_halves[half, :, start : start + size] = ref[:, half * size : (half + 1) * size]
            start += size
    greet([core_beside, x_beside, y_beside, z_beside[-1], z_beside[1]])

    kept = []
    sent = []

    def keep_local(source, target, index):
        copy = pltpu.make_async_copy(source, target, local_sems.at[index])
        copy.start()
        return copy

    def pair_of(sems, index):
        return sems.at[0, index], sems.at[1, index]

    def move(source, target, sems, index, where):
        copy = send(source, target, pair_of(sems, index), where)
        sent.append(copy)
        return copy

    qkv_core = move(qkv_halves.at[1 - core], qkv_buffer.at[0, 0, 1], qkv_sems, 0, core_beside)
    qkv_kept = keep_local(qkv_halves.at[core], qkv_buffer.at[0, 0, 0], 0)
    for half in range(2):
        size = out_ref.shape[1] // 2
        out_halves[half] = out_ref[:, half * size : (half + 1) * size]
        size = gate_ref.shape[1] // 2
        for number, ref in enumerate((gate_ref, up_ref, down_ref)):
            feed_halves[half, :, number * size : (number + 1) * size] = ref[:, half * size : (half + 1) * size]
    step_rows = 128

    @pl.loop(0, count // step_rows)
    def _(step):
        rows = pl.ds(pl.multiple_of(step * step_rows, step_rows), step_rows)
        value = tokens_ref[rows, :].astype(jnp.float32)
        first_all[0, rows, :] = (value * norm_factor(value) * gains_ref[0:1, :]).astype(jnp.bfloat16)

    first_x = move(first_all.at[0], first_all.at[1], row_sems, 0, x_beside)
    out_core = move(out_halves.at[1 - core], out_buffer.at[0, 0, 1], out_sems, 0, core_beside)
    out_kept = keep_local(out_halves.at[core], out_buffer.at[0, 0, 0], 1)
    feed_core = move(feed_halves.at[1 - core], feed_out.at[0, 0, 1], feed_sems, 0, core_beside)
    feed_kept = keep_local(feed_halves.at[core], feed_out.at[0, 0, 0], 2)
    first_core = move(first_all.at[0], first_all.at[2], row_sems, 1, core_beside)
    cotangent_kept = keep_local(cotangent_ref, cotangent_out.at[0], 4)

    last = deep - 1

    def z_copy(buffer, sems, upward, step, rel):
        source, target = ((deep - step) % deep, last - step) if upward else (step, step + 1)
        return pltpu.make_async_remote_copy(
            src_ref=buffer.at[0, source, rel],
            dst_ref=buffer.at[0, target, rel],
            send_sem=sems.at[0, 2 * (1 + upward * last + step) + rel],
            recv_sem=sems.at[1, 2 * target + rel],
            device_id=z_beside[1 if upward else -1],
            device_id_type=pl.DeviceIdType.MESH,
        )

    def z_sends(upward, step):
        if upward:
            return (z_place <= last - 1) & (z_place - step >= 0)
        return (z_place >= 1) & (z_place + step <= last)

    def z_start(buffer, sems, upward, step, rel):
        @pl.when(z_sends(upward, step))
        def _():
            z_copy(buffer, sems, upward, step, rel).start()

    def open_z(buffer, sems):
        for rel in range(2):
            z_start(buffer, sems, False, 0, rel)
            z_start(buffer, sems, True, 0, rel)

    def y_copy(buffer, sems, slot, rel):
        return pltpu.make_async_remote_copy(
            src_ref=buffer.at[0, slot, rel],
            dst_ref=buffer.at[1, slot, rel],
            send_sem=sems.at[0, 2 * (2 * deep + slot) + rel],
            recv_sem=sems.at[1, 2 * (2 * deep + slot) + rel],
            device_id=y_beside,
            device_id_type=pl.DeviceIdType.MESH,
        )

    def open_y(buffer, sems):
        for rel in range(2):
            y_copy(buffer, sems, 0, rel).start()

    def z_part(buffer, sems, step, rel):
        for upward in (False, True):
            slot = last - step if upward else step + 1
            arrives = z_place - step - 1 >= 0 if upward else z_place + step + 1 <= last

            @pl.when(arrives)
            def _(upward=upward, slot=slot):
                z_copy(buffer, sems, upward, step, rel).wait_recv()
                if step + 1 < last:
                    z_start(buffer, sems, upward, step + 1, rel)
                y_copy(buffer, sems, slot, rel).start()

    def z_step(buffer, sems, step):
        for rel in range(2):
            z_part(buffer, sems, step, rel)

    def y_wait(buffer, sems):
        for slot in range(deep):
            for rel in range(2):
                y_copy(buffer, sems, slot, rel).wait_recv()

    def close(buffer, sems):
        for rel in range(2):
            for slot in range(deep):
                y_copy(buffer, sems, slot, rel).wait_send()
            for upward in (False, True):
                for step in range(last):

                    @pl.when(z_sends(upward, step))
                    def _(upward=upward, step=step, rel=rel):
                        z_copy(buffer, sems, upward, step, rel).wait_send()

    qkv_z, out_z, feed_z = (qkv_buffer, qkv_sems), (out_buffer, out_sems), (feed_out, feed_sems)
    qkv_core.wait_recv()
    qkv_kept.wait()
    open_z(*qkv_z)
    open_y(*qkv_z)
    out_core.wait_recv()
    out_kept.wait()
    feed_core.wait_recv()
    feed_kept.wait()
    kept.append(keep_local(qkv_buffer.at[0, 0], qkv_own_out, 13))
    for step in range(last):
        z_step(*qkv_z, step)
        if step == last - 2:
            open_z(*out_z)
    open_y(*out_z)
    for step in range(last):
        z_step(*out_z, step)
    open_z(*feed_z)
    open_y(*feed_z)
    spread_weight(qkv_buffer, qkv_spread, qkv_wide, deep, 0)
    spread_weight(out_buffer, out_spread, out_wide, deep, 0)

    def project(start, stride, amount, pair):
        lane0 = pair * 4 * LANES

        @pl.loop(0, amount)
        def _(step):
            block = start + stride * step
            product = nn(first_all[block], qkv_wide[:, lane0 : lane0 + 4 * LANES])
            position = lax.rem(lax.axis_index("x").astype(jnp.int32) + block, jnp.int32(2))
            cosine, sine = cosine_ref[position], sine_ref[position]
            for head in range(4):
                part = product[:, head * LANES : (head + 1) * LANES]
                if head < 3:
                    part = turn(part, cosine, sine)
                lane = lane0 + head * LANES
                qkv[block, :, lane : lane + LANES] = part.astype(jnp.bfloat16)

    first_core.wait_recv()
    project(0, 2, 2, 0)
    first_x.wait_recv()
    first_far = move(first_all.at[1], first_all.at[3], row_sems, 2, core_beside)
    cotangent_x = move(cotangent_ref, cotangent_out.at[1], row_sems, 3, x_beside)
    cotangent_core = move(cotangent_ref, cotangent_out.at[2], row_sems, 4, core_beside)
    project(1, 2, 1, 0)
    first_far.wait_recv()
    project(3, 2, 1, 0)
    kept.append(keep_local(first_all, first_out, 6))
    y_wait(*qkv_z)
    spread_weight(qkv_buffer, qkv_spread, qkv_wide, deep, 1)
    kept.append(keep_local(qkv_wide, qkv_wide_out, 5))
    project(0, 1, 4, 1)
    kept.append(keep_local(qkv, qkv_out, 7))
    z_part(*feed_z, 0, 0)
    logs[...] = jnp.zeros_like(logs)
    for sequence in range(2):

        @pl.loop(0, 2)
        def _(pair, sequence=sequence):
            attend_pair(qkv, heads, logs, keys, values, sequence, pair)

        if sequence == 0:
            z_part(*feed_z, 0, 1)

    kept.append(keep_local(heads, heads_out, 8))
    kept.append(keep_local(logs, logs_out, 9))
    y_wait(*out_z)
    spread_weight(out_buffer, out_spread, out_wide, deep, 1)
    kept.append(keep_local(out_wide, out_wide_out, 10))

    def out_part(block):
        @pl.loop(0, out_wide.shape[0] // WIDE)
        def _(step):
            lanes = pl.ds(pl.multiple_of(step * WIDE, WIDE), WIDE)
            parts[block, :, lanes] = times_transposed(heads[block], out_wide[lanes, :]).astype(jnp.bfloat16)

    out_part(3)
    core_far = move(parts.at[3], core_parts.at[1], core_sems, 0, core_beside)
    out_part(1)
    core_far.wait_recv()

    @pl.loop(0, count // step_rows)
    def _(step):
        rows = pl.ds(pl.multiple_of(step * step_rows, step_rows), step_rows)
        outgoing[rows, :] = (
            parts[1, rows, :].astype(jnp.float32) + core_parts[1, rows, :].astype(jnp.float32)
        ).astype(jnp.bfloat16)

    branch_x = move(outgoing, incoming, core_sems, 1, x_beside)
    out_part(2)
    core_near = move(parts.at[2], core_parts.at[0], core_sems, 2, core_beside)
    out_part(0)
    core_near.wait_recv()
    z_step(*feed_z, 1)
    branch_x.wait_recv()

    @pl.loop(0, count // step_rows)
    def _(step):
        rows = pl.ds(pl.multiple_of(step * step_rows, step_rows), step_rows)
        total = (
            tokens_ref[rows, :].astype(jnp.float32)
            + parts[0, rows, :].astype(jnp.float32)
            + core_parts[0, rows, :].astype(jnp.float32)
            + incoming[rows, :].astype(jnp.float32)
        )
        middle[rows, :] = total
        second[rows, :] = (total * norm_factor(total) * gains_ref[1:2, :]).astype(jnp.bfloat16)

    kept.append(keep_local(middle, middle_out, 11))
    kept.append(keep_local(second, second_out.at[0], 12))
    second_x = move(second, second_out.at[1], row_sems, 5, x_beside)
    second_core = move(second, second_out.at[2], row_sems, 6, core_beside)
    cotangent_x.wait_recv()
    cotangent_far = move(cotangent_out.at[1], cotangent_out.at[3], row_sems, 7, core_beside)
    z_step(*feed_z, 2)
    second_x.wait_recv()
    second_far = move(second_out.at[1], second_out.at[3], row_sems, 8, core_beside)
    for copy in (second_core, second_far, cotangent_core, cotangent_far):
        copy.wait_recv()
    y_wait(*feed_z)
    for copy in kept + [cotangent_kept]:
        copy.wait()
    for copy in sent:
        copy.wait_send()
    for which in (qkv_z, out_z, feed_z):
        close(*which)


def forward(deep, cotangent, tokens, gains, weights, spreads, cosine, sine):
    count, width = tokens.shape
    query, key, value, out, gate, up, down = weights
    part = query.shape[0]
    feed_size = (gate.shape[1] + up.shape[1] + down.shape[1]) // 2
    qkv_size = (query.shape[1] + key.shape[1] + value.shape[1]) // 2
    out_size = out.shape[1] // 2

    def shape(*dims, kind=jnp.bfloat16):
        return jax.ShapeDtypeStruct(dims, kind)

    def room(*dims, kind=jnp.bfloat16):
        return pltpu.VMEM(dims, kind)

    qkv_lanes, out_lanes = 2 * spreads[0].shape[1], 2 * spreads[1].shape[1]
    outs = (
        shape(4, count, width),
        shape(4, count, qkv_lanes),
        shape(4, count, out_lanes),
        shape(4, count, LANES, kind=jnp.float32),
        shape(width, qkv_lanes),
        shape(width, out_lanes),
        shape(count, width, kind=jnp.float32),
        shape(4, count, width),
        shape(4, count, width),
        shape(2, deep, 2, part, feed_size),
        shape(2, part, qkv_size),
    )
    scratch = [
        room(2, part, qkv_size),
        room(2, part, out_size),
        room(2, part, feed_size),
        room(4, count, width),
        room(2, deep, 2, part, qkv_size),
        room(2, deep, 2, part, out_size),
        room(width, qkv_lanes),
        room(width, out_lanes),
        room(4, count, qkv_lanes),
        room(4, count, out_lanes),
        room(4, count, LANES, kind=jnp.float32),
        room(2 * count, LANES),
        room(2 * count, LANES),
        room(4, count, width),
        room(2, count, width),
        room(count, width),
        room(count, width),
        room(count, width, kind=jnp.float32),
        room(count, width),
        pltpu.SemaphoreType.DMA((14,)),
        pltpu.SemaphoreType.DMA((2, 9)),
        pltpu.SemaphoreType.DMA((2, 6 * deep)),
        pltpu.SemaphoreType.DMA((2, 6 * deep)),
        pltpu.SemaphoreType.DMA((2, 6 * deep)),
        pltpu.SemaphoreType.DMA((2, 3)),
    ]
    return pl.pallas_call(
        functools.partial(forward_kernel, deep),
        out_shape=outs,
        in_specs=[hbm_spec()] + [vmem_spec()] * 13,
        out_specs=(hbm_spec(),) * len(outs),
        scratch_shapes=scratch,
        compiler_params=vmem_params(collective_id=1, has_side_effects=True),
        cost_estimate=cost(flops=20 * 10**9, bytes_accessed=10**8, transcendentals=10**7),
        name="forward",
    )(cotangent, tokens, gains, *weights, *spreads, cosine, sine)


EARLY = 7
ORDER = (1, 3, 2, 0)
HOPS = {(0, 1): 0, (0, 3): 1, (0, 2): 2, (1, 1): 3}


def ring_row(shift, deep, rows):
    z_place = lax.rem(lax.axis_index("z").astype(jnp.int32) + shift, jnp.int32(deep))
    return pl.multiple_of(z_place * rows, rows)


def add_rows(target, source, step_rows=128):
    @pl.loop(0, target.shape[0] // step_rows)
    def _(step):
        rows = pl.ds(pl.multiple_of(step * step_rows, step_rows), step_rows)
        target[rows, :] = (target[rows, :].astype(jnp.float32) + source[rows, :].astype(jnp.float32)).astype(
            jnp.bfloat16
        )


def ahead(deep):
    z_place = lax.axis_index("z").astype(jnp.int32)
    return [{"z": lax.rem(z_place + shift, jnp.int32(deep))} for shift in range(deep)]


def pieces_of(deep):
    return [(piece, shift) for piece in range(3) for shift in ORDER[:deep]]


def feed_back_kernel(
    deep, rows_hbm, grads_hbm, chunks, middle_hbm, gain_ref,
    grad_middle_out, grad_attention_out, branch_out, sent_out, own_out, sum_out, arrived_out,
    gate, up, down, rows, grads, hidden, grad_gate, grad_up, parts, landing, incoming, middle, stage,
    early_y, load_sems, weight_sems, store_sems, sum_sems, early_sems, core_sems, x_sems, y_sems, z_sems,
):
    core_beside, x_beside, y_beside = beside()
    z_ahead = ahead(deep)
    greet([core_beside, x_beside, y_beside] + z_ahead[1:])
    blocks, count, width = rows.shape
    half = gate.shape[1] // 2
    part = chunks.shape[3]
    piece_rows = 2 * part
    sent = []

    def load(source, target, sem):
        copy = pltpu.make_async_copy(source, target, sem)
        copy.start()
        return copy

    def move(source, target, sems, index, where):
        copy = send(source, target, (sems.at[0, index], sems.at[1, index]), where)
        sent.append(copy)
        return copy

    row_loads = {}
    for block in (3, 1):
        row_loads[block] = [load(rows_hbm.at[block], rows.at[block], load_sems.at[0, block])]
    weight_loads = {}
    for side in range(2):
        here = []
        for matrix, target in enumerate((gate, up, down)):
            for shift in range(deep):
                for rel in range(2):
                    here.append(
                        load(
                            chunks.at[side, shift, rel, :, pl.ds(matrix * half, half)],
                            target.at[pl.ds(grid_offset(shift, rel, deep, part), part), pl.ds(side * half, half)],
                            weight_sems.at[matrix, side, shift, rel],
                        )
                    )
        weight_loads[side] = here
        if side == 0:
            for block in (3, 1):
                row_loads[block].append(load(grads_hbm.at[block], grads.at[block], load_sems.at[1, block]))
    for block in (2, 0):
        row_loads[block] = [
            load(rows_hbm.at[block], rows.at[block], load_sems.at[0, block]),
            load(grads_hbm.at[block], grads.at[block], load_sems.at[1, block]),
        ]
    middle_load = load(middle_hbm, middle, load_sems.at[0, 4])

    def inner(block):
        for side in range(2):
            for copy in weight_loads.pop(side, ()):
                copy.wait()
            lanes = slice(side * half, (side + 1) * half)
            gate_value = nn(rows[block], gate[:, lanes])
            up_value = nn(rows[block], up[:, lanes])
            grad_hidden = nn(grads[block], down[:, lanes])
            sigmoid = 1.0 / (1.0 + jnp.exp(-gate_value))
            swish = gate_value * sigmoid
            slope = sigmoid + swish * (1.0 - sigmoid)
            hidden[block, :, lanes] = (swish * up_value).astype(jnp.bfloat16)
            grad_gate[block, :, lanes] = (grad_hidden * up_value * slope).astype(jnp.bfloat16)
            grad_up[block, :, lanes] = (grad_hidden * swish).astype(jnp.bfloat16)

    def outer(block):
        @pl.loop(0, width // WIDE)
        def _(step):
            lanes = pl.ds(pl.multiple_of(step * WIDE, WIDE), WIDE)
            parts[block, :, lanes] = (
                times_transposed(grad_gate[block], gate[lanes, :])
                + times_transposed(grad_up[block], up[lanes, :])
            ).astype(jnp.bfloat16)

    for block in (3, 1, 2, 0):
        for copy in row_loads[block]:
            copy.wait()
        inner(block)
        if block in (3, 1):
            outer(block)
        if block == 3:
            far = move(parts.at[3], landing.at[1], core_sems, 0, core_beside)
        if block == 1:
            far.wait_recv()
            add_rows(parts.at[1], landing.at[1])
            across = move(parts.at[1], incoming, x_sems, 0, x_beside)

    sources = ((grads, hidden), (rows, grad_gate), (rows, grad_up))

    def weight_part(piece, side, shift):
        left, right = sources[piece]
        row = ring_row(shift, deep, piece_rows)
        lanes = slice(side * half, (side + 1) * half)
        return transposed_times(
            left[:, :, pl.ds(row, piece_rows)].reshape(blocks * count, piece_rows),
            right[:, :, lanes].reshape(blocks * count, half),
        )

    def weight_stage(piece, side, shift):
        row = ring_row(shift, deep, piece_rows)
        stage[piece, pl.ds(row, piece_rows), :] = weight_part(piece, side, shift).astype(jnp.bfloat16)

    def weight_whole(piece, side):
        left, right = sources[piece]
        lanes = slice(side * half, (side + 1) * half)

        @pl.loop(0, width // WIDE)
        def _(step):
            row = pl.multiple_of(step * WIDE, WIDE)
            stage[piece, pl.ds(row, WIDE), :] = transposed_times(
                left[:, :, pl.ds(row, WIDE)].reshape(blocks * count, WIDE),
                right[:, :, lanes].reshape(blocks * count, half),
            ).astype(jnp.bfloat16)

    early = pieces_of(deep)[:EARLY]
    arrivals, stores, pending = [], [], []

    def flush():
        for index, store, target in pending:
            store.wait()
            arrivals.append(move(target, early_y.at[index], y_sems, index, y_beside))
        pending.clear()

    def send_piece(piece):
        if piece:
            weight_whole(piece, 1)
            flush()
        for shift in ORDER:
            if not piece:
                weight_stage(piece, 1, shift)
                flush()
            rows_here = pl.ds(ring_row(shift, deep, piece_rows), piece_rows)
            target = sent_out.at[piece, rows_here, :]
            store = load(stage.at[piece, rows_here, :], target, early_sems.at[piece * deep + shift])
            if (piece, shift) in early:
                pending.append((early.index((piece, shift)), store, target))
            else:
                stores.append(store)

    send_piece(0)
    outer(2)
    flush()
    near = move(parts.at[2], landing.at[0], core_sems, 1, core_beside)
    outer(0)
    send_piece(1)
    send_piece(2)
    flush()
    late_stores = list(stores)
    hops = []

    def join_early(pairs):
        for piece, shift in pairs:
            index = early.index((piece, shift))
            product = weight_part(piece, 0, shift)
            arrivals[index].wait_recv()
            early_y[index] = (product + early_y[index].astype(jnp.float32)).astype(jnp.bfloat16)
            if (piece, shift) in HOPS:
                number = HOPS[piece, shift]
                hops.append(
                    move(early_y.at[index], arrived_out.at[number], z_sems, number, z_ahead[shift])
                )
            else:
                stores.append(load(early_y.at[index], sum_out.at[index], sum_sems.at[index]))

    join_early(early[:2])
    near.wait_recv()
    middle_load.wait()
    across.wait_recv()
    step_rows = 128

    @pl.loop(0, count // step_rows)
    def _(step):
        tile = pl.ds(pl.multiple_of(step * step_rows, step_rows), step_rows)
        grad = (
            parts[0, tile, :].astype(jnp.float32)
            + landing[0, tile, :].astype(jnp.float32)
            + incoming[tile, :].astype(jnp.float32)
        )
        total = grads[0, tile, :].astype(jnp.float32) + norm_back(middle[tile, :], gain_ref[1:2, :], grad)
        middle[tile, :] = total
        incoming[tile, :] = total.astype(jnp.bfloat16)

    attention_x = move(incoming, grad_attention_out.at[1], x_sems, 1, x_beside)
    attention_core = move(incoming, grad_attention_out.at[2], core_sems, 2, core_beside)
    stores.append(load(incoming, grad_attention_out.at[0], store_sems.at[0]))
    stores.append(load(middle, grad_middle_out, store_sems.at[3]))

    join_early(early[2:4])
    far.wait_send()
    across.wait_send()
    near.wait_send()

    def branch(block):
        @pl.loop(0, width // WIDE)
        def _(step):
            lanes = pl.ds(pl.multiple_of(step * WIDE, WIDE), WIDE)
            parts[block, :, lanes] = times_transposed(hidden[block], down[lanes, :]).astype(jnp.bfloat16)

    branch(3)
    attention_core.wait_recv()
    branch_far = move(parts.at[3], landing.at[1], core_sems, 3, core_beside)
    branch(2)
    branch_near = move(parts.at[2], landing.at[0], core_sems, 4, core_beside)
    branch(1)
    branch_far.wait_recv()
    add_rows(parts.at[1], landing.at[1])
    stores.append(load(parts.at[1], branch_out.at[1], store_sems.at[7]))
    branch(0)
    stores.append(load(parts.at[0], branch_out.at[0], store_sems.at[8]))
    branch_near.wait_recv()
    stores.append(load(landing.at[0], branch_out.at[2], store_sems.at[9]))
    for copy in late_stores:
        copy.wait()
    for piece in range(3):
        whole = piece not in [pair[0] for pair in early]
        if whole:
            weight_whole(piece, 0)
        for shift in range(deep):
            if (piece, shift) not in early:
                if not whole:
                    weight_stage(piece, 0, shift)
                rows_here = pl.ds(ring_row(shift, deep, piece_rows), piece_rows)
                stores.append(
                    load(
                        stage.at[piece, rows_here, :],
                        own_out.at[piece, rows_here, :],
                        early_sems.at[(3 + piece) * deep + shift],
                    )
                )
    join_early(early[4:])
    attention_x.wait_recv()
    attention_far = move(grad_attention_out.at[1], grad_attention_out.at[3], core_sems, 5, core_beside)
    attention_far.wait_recv()
    for copy in hops:
        copy.wait_recv()
    for copy in stores[len(late_stores) :]:
        copy.wait()
    for copy in arrivals + hops:
        copy.wait_send()
    for copy in (attention_x, attention_core, branch_far, branch_near, attention_far):
        copy.wait_send()


def feed_back(deep, rows, grads, chunks, middle, gain):
    blocks, count, width = rows.shape
    half = chunks.shape[4] // 3
    part = chunks.shape[3]

    def shape(*dims, kind=jnp.bfloat16):
        return jax.ShapeDtypeStruct(dims, kind)

    def room(*dims, kind=jnp.bfloat16):
        return pltpu.VMEM(dims, kind)

    outs = (
        shape(count, width, kind=jnp.float32),
        shape(blocks, count, width),
        shape(3, count, width),
        shape(3, width, half),
        shape(3, width, half),
        shape(EARLY, 2 * part, half),
        shape(len(HOPS), 2 * part, half),
    )
    dma = pltpu.SemaphoreType.DMA
    return pl.pallas_call(
        functools.partial(feed_back_kernel, deep),
        out_shape=outs,
        in_specs=[hbm_spec()] * 4 + [vmem_spec()],
        out_specs=(hbm_spec(),) * len(outs),
        scratch_shapes=[room(width, 2 * half)] * 3
        + [room(blocks, count, width)] * 2
        + [room(blocks, count, 2 * half)] * 3
        + [room(blocks, count, width), room(2, count, width), room(count, width)]
        + [room(count, width, kind=jnp.float32), room(3, width, half), room(EARLY, 2 * part, half)]
        + [dma((2, 5)), dma((3, 2, deep, 2)), dma((10,)), dma((EARLY,)), dma((6 * deep,)), dma((2, 6)), dma((2, 2)), dma((2, EARLY)), dma((2, EARLY))],
        compiler_params=vmem_params(collective_id=2, has_side_effects=True),
        cost_estimate=cost(flops=80 * 10**9, bytes_accessed=10**8, transcendentals=10**7),
        name="feed_back",
    )(rows, grads, chunks, middle, gain)


def attend_back_pair(
    qkv, grad_heads, heads, logs, cosine_ref, sine_ref, grad_qkv, keys, values, grad_keys, grad_values,
    sequence, pair,
):
    count = qkv.shape[1]
    x_place = lax.axis_index("x").astype(jnp.int32)
    lane0 = pl.multiple_of(pair * 4 * LANES, 4 * LANES)
    head0 = pl.multiple_of(pair * 2 * LANES, 2 * LANES)
    mask = diagonal_mask()
    factor = HD ** (-0.5)
    scale = factor * LOG2E
    places = [2 * sequence + lax.rem(x_place + position, jnp.int32(2)) for position in range(2)]
    for position, block in enumerate(places):
        rows = slice(position * count, (position + 1) * count)
        keys[rows, :] = qkv[block, :, pl.ds(lane0 + 2 * LANES, LANES)]
        values[rows, :] = qkv[block, :, pl.ds(lane0 + 3 * LANES, LANES)]
    grad_keys[...] = jnp.zeros_like(grad_keys)
    grad_values[...] = jnp.zeros_like(grad_values)

    def visit(block, start, before):
        rows = slice(start, start + TILE)

        def both(ref, first):
            return jnp.concatenate(
                [ref[block, rows, pl.ds(first, LANES)], ref[block, rows, pl.ds(first + LANES, LANES)]], axis=0
            )

        queries, grads, outs = both(qkv, lane0), both(grad_heads, head0), both(heads, head0)
        lane = lax.broadcasted_iota(jnp.int32, (TILE, LANES), 1)
        kept = logs[block, rows, :]
        log = jnp.concatenate(
            [
                jnp.sum(jnp.where(lane == 2 * pair + head, kept, 0.0), axis=-1, keepdims=True)
                for head in range(2)
            ],
            axis=0,
        )
        inner = jnp.sum(grads.astype(jnp.float32) * outs.astype(jnp.float32), axis=-1, keepdims=True)

        def span(span_rows, masked):
            softmax = jnp.exp2(times_transposed(queries, keys[span_rows, :]) * scale - log)
            if masked:
                softmax = jnp.where(mask, softmax, 0.0)
            grad_softmax = times_transposed(grads, values[span_rows, :])
            grad_scores = (softmax * (grad_softmax - inner)).astype(jnp.bfloat16)
            grad_values[span_rows, :] += transposed_times(softmax.astype(jnp.bfloat16), grads)
            grad_keys[span_rows, :] += transposed_times(grad_scores, queries)
            return nn(grad_scores, keys[span_rows, :])

        grad_queries = span(slice(before, before + TILE), True)
        if before:
            grad_queries = grad_queries + span(slice(0, before), False)
        position, table_rows = before // count, slice(before % count, before % count + TILE)
        cosine, sine = cosine_ref[position, table_rows, :], -sine_ref[position, table_rows, :]
        for head in range(2):
            piece = grad_queries[head * TILE : (head + 1) * TILE] * factor
            grad_qkv[block, rows, pl.ds(lane0 + head * LANES, LANES)] = turn(piece, cosine, sine).astype(
                jnp.bfloat16
            )

    for position, block in enumerate(places):
        for step in range(count // TILE):
            visit(block, step * TILE, position * count + step * TILE)

    for position, block in enumerate(places):
        rows = slice(position * count, (position + 1) * count)
        grad_qkv[block, :, pl.ds(lane0 + 2 * LANES, LANES)] = turn(
            grad_keys[rows, :] * factor, cosine_ref[position], -sine_ref[position]
        ).astype(jnp.bfloat16)
        grad_qkv[block, :, pl.ds(lane0 + 3 * LANES, LANES)] = grad_values[rows, :].astype(jnp.bfloat16)


def heads_back_kernel(
    deep, grad_attention_hbm, qkv_hbm, heads_hbm, logs_hbm, first_hbm, qkv_wide_hbm, out_wide_hbm,
    branch_hbm, sent_hbm, own_hbm, sum_hbm, arrived_hbm, chunks_hbm, qkv_own_hbm,
    cosine_ref, sine_ref, qkv_spread, out_spread,
    first_part, first_core, first_x, branch_x, feed_final, qkv_final, out_final, first_gain_out, second_gain_out,
    grad_attention, qkv, heads, grad_heads, logs, grad_qkv, qkv_wide, out_wide, keys, values, grad_keys,
    grad_values, slots, landing, feed_sum, feed_y, feed_z, out_sent, out_sum, out_y, out_z, qkv_sent, qkv_sum, qkv_y,
    qkv_z, feed_pass, out_pass, qkv_pass, feed_last, qkv_last, out_last, feed_weight, qkv_weight, gain_part, gain_in, gain_total,
    load_sems, own_sems, tile_sems, core_sems, x_sems, y_sems, z_sems, pass_sems, gain_sems,
):
    blocks, count, width = grad_attention.shape
    core_beside, x_beside, y_beside = beside()
    core = lax.axis_index("c").astype(jnp.int32)
    across, along = lax.axis_index("x").astype(jnp.int32), lax.axis_index("y").astype(jnp.int32)
    z_ahead = ahead(deep)
    cube = {
        (rel, up, over): {"c": (core + rel) % 2, "y": (along + up) % 2, "x": (across + over) % 2}
        for rel in range(2)
        for up in range(2)
        for over in range(2)
    }
    far_cube = [key for key in cube if key != (0, 0, 0)]
    greet([cube[key] for key in far_cube] + z_ahead[1:])
    half = feed_sum.shape[3]
    piece_rows = feed_sum.shape[2]
    part = piece_rows // 2
    step_rows = 128
    sent = []

    def load(source, target, sem):
        copy = pltpu.make_async_copy(source, target, sem)
        copy.start()
        return copy

    def move(source, target, sems, index, where):
        copy = send(source, target, (sems.at[0, index], sems.at[1, index]), where)
        sent.append(copy)
        return copy

    late = pieces_of(deep)[EARLY:]
    attention_load = load(grad_attention_hbm, grad_attention, load_sems.at[0])
    out_load = load(out_wide_hbm, out_wide, load_sems.at[1])
    heads_load = load(heads_hbm, heads, load_sems.at[2])
    late_copies = []
    for index, (piece, shift) in enumerate(late):
        row = ring_row(shift, deep, piece_rows)
        late_copies.append(
            move(
                sent_hbm.at[piece, pl.ds(row, piece_rows), :], feed_y.at[piece, shift], y_sems, index, y_beside
            )
        )
    branch_copy = move(branch_hbm.at[1], branch_x, x_sems, 0, x_beside)
    qkv_load = load(qkv_hbm, qkv, load_sems.at[3])
    logs_load = load(logs_hbm, logs, load_sems.at[4])
    wide_load = load(qkv_wide_hbm, qkv_wide, load_sems.at[5])
    own_loads, z_copies = {}, {}
    early_loads = []
    for index, (piece, shift) in enumerate(pieces_of(deep)):
        if (piece, shift) in late:
            row = ring_row(shift, deep, piece_rows)
            own_loads[piece, shift] = load(
                own_hbm.at[piece, pl.ds(row, piece_rows), :], feed_sum.at[piece, shift], own_sems.at[0, index]
            )
        elif shift == 0:
            early_loads.append(load(sum_hbm.at[index], feed_sum.at[piece, 0], own_sems.at[1, index]))
        elif (piece, shift) in HOPS:
            early_loads.append(
                load(arrived_hbm.at[HOPS[piece, shift]], feed_z.at[piece, shift - 1], own_sems.at[1, index])
            )
        else:
            z_copies[piece, shift] = move(
                sum_hbm.at[index],
                feed_z.at[piece, shift - 1],
                z_sems,
                piece * (deep - 1) + shift - 1,
                z_ahead[shift],
            )
    weight_loads = [
        load(chunks_hbm.at[0, 0, :, :, pl.ds(0, 2 * half)], feed_weight, load_sems.at[6]),
        load(qkv_own_hbm, qkv_weight, load_sems.at[7]),
    ]

    attention_load.wait()
    out_load.wait()

    @pl.loop(0, blocks)
    def _(block):
        grad_heads[block] = nn(grad_attention[block], out_wide[...]).astype(jnp.bfloat16)

    heads_load.wait()

    def weight_tile(left, right, spread, side):
        size = spread.shape[1]
        right = right[:, :, side * size : (side + 1) * size].reshape(blocks * count, size)
        product = transposed_times(left.reshape(blocks * count, piece_rows), right)
        return times_transposed(product.astype(jnp.bfloat16), spread[...]).astype(jnp.bfloat16)

    guarded = []
    z_place = lax.axis_index("z").astype(jnp.int32)
    last = deep - 1
    inside = (z_place > 0) & (z_place < last)
    inward = {"z": jnp.where(z_place == 0, jnp.int32(1), jnp.int32(last - 1))}

    def remote(source, target, sems, index, where):
        return pltpu.make_async_remote_copy(
            src_ref=source,
            dst_ref=target,
            send_sem=sems.at[0, index],
            recv_sem=sems.at[1, index],
            device_id=where,
            device_id_type=pl.DeviceIdType.MESH,
        )

    def begin(copy, condition):
        pl.when(condition)(copy.start)
        guarded.append((copy, condition))

    def clear(target):
        @pl.when(z_place == 0)
        def _():
            target[0] = jnp.zeros(target.shape[1:], target.dtype)

        @pl.when(z_place == last)
        def _():
            target[last - 1] = jnp.zeros(target.shape[1:], target.dtype)

    def join_piece(name, number, total, arrived, target, passing, shift):
        add_rows(total.at[shift], arrived.at[shift])
        if not shift:
            return
        direct = remote(total.at[shift], target.at[shift - 1], z_sems, number * last + shift - 1, z_ahead[shift])
        if passing is None:
            direct.start()
            sent.append(direct)
        else:
            far = z_place == (last if shift == 1 else 0)
            through = remote(total.at[shift], passing, pass_sems, number, inward)
            if shift == 2:

                @pl.when(inside)
                def _():
                    through.wait_recv()
                    add_rows(total.at[shift], passing)

                direct.start()
                sent.append(direct)
            else:
                begin(through, far)
                begin(direct, jnp.logical_not(far))
        z_copies[name, shift] = direct

    def join_feed(piece, shift):
        own_loads[piece, shift].wait()
        join_piece(
            piece, piece, feed_sum.at[piece], feed_y.at[piece], feed_z.at[piece],
            feed_pass if piece == 2 else None, shift,
        )

    for target in (feed_z.at[2], out_z, qkv_z):
        clear(target)

    def join_feed_late(index):
        late_copies[index].wait_recv()
        join_feed(*late[index])

    qkv_load.wait()
    logs_load.wait()
    for sequence in range(2):

        for pair in range(2):
            attend_back_pair(
                qkv, grad_heads, heads, logs, cosine_ref, sine_ref, grad_qkv, keys, values, grad_keys,
                grad_values, sequence, pair,
            )
        join_feed_late(sequence)
    wide_load.wait()

    def first_tile(order):
        row = ring_row(ORDER[order], deep, piece_rows)
        slot = (order % 2) * 512
        return load(
            first_hbm.at[:, :, pl.ds(row, piece_rows)],
            qkv.at[:, :, pl.ds(slot, piece_rows)],
            tile_sems.at[order],
        )

    first_loads = [first_tile(order) for order in range(2)]

    def first_piece(block):
        @pl.loop(0, width // WIDE)
        def _(step):
            lanes = pl.ds(pl.multiple_of(step * WIDE, WIDE), WIDE)
            slots[block % 3, :, lanes] = times_transposed(grad_qkv[block], qkv_wide[lanes, :]).astype(
                jnp.bfloat16
            )

    first_piece(3)
    core_far = move(slots.at[0], landing, core_sems, 0, core_beside)
    first_piece(1)
    core_far.wait_recv()
    add_rows(slots.at[1], landing)
    x_copy = move(slots.at[1], first_x, x_sems, 1, x_beside)
    first_piece(2)
    core_near = move(slots.at[2], first_core, core_sems, 1, core_beside)
    core_far.wait_send()
    sent[:] = [copy for copy in sent if copy is not core_far]
    first_piece(0)
    first_store = load(slots.at[0], first_part, load_sems.at[8])
    join_feed_late(2)
    y_index = len(late)
    out_copies = {}
    for shift in ORDER:
        row = ring_row(shift, deep, piece_rows)
        out_sent[shift] = weight_tile(grad_attention[:, :, pl.ds(row, piece_rows)], heads, out_spread, 1)
        out_copies[shift] = move(out_sent.at[shift], out_y.at[shift], y_sems, y_index + shift, y_beside)

    @pl.loop(0, deep)
    def _(shift):
        row = ring_row(shift, deep, piece_rows)
        out_sum[shift] = weight_tile(grad_attention[:, :, pl.ds(row, piece_rows)], heads, out_spread, 0)

    join_feed_late(3)

    qkv_copies = {}
    y_index += deep
    for order, shift in enumerate(ORDER):
        first_loads[order].wait()
        slot = (order % 2) * 512
        left = qkv[:, :, slot : slot + piece_rows]
        qkv_sent[shift] = weight_tile(left, grad_qkv, qkv_spread, 1)
        qkv_copies[shift] = move(qkv_sent.at[shift], qkv_y.at[shift], y_sems, y_index + shift, y_beside)
        qkv_sum[shift] = weight_tile(left, grad_qkv, qkv_spread, 0)
        if order + 2 < deep:
            first_loads.append(first_tile(order + 2))

    join_feed_late(4)
    for shift in ORDER:
        out_copies[shift].wait_recv()
        join_piece("out", 3, out_sum, out_y, out_z, out_pass, shift)

    finals = []

    def finish(name, number, total, arrived, last, final, weights):
        for shift in range(1, deep):
            if (name, shift) not in z_copies:
                continue
            if name in (0, 1) or shift == 2:
                z_copies[name, shift].wait_recv()
            else:
                pl.when(z_place != (0 if shift == 1 else deep - 1))(z_copies[name, shift].wait_recv)
        size = total.shape[2]
        sums = []
        for rel in range(2):
            row = pl.multiple_of(lax.rem(core + rel, jnp.int32(2)) * part, part)
            value = total[0, pl.ds(row, part), :].astype(jnp.float32)
            for shift in range(deep - 1):
                value = value + arrived[shift, pl.ds(row, part), :].astype(jnp.float32)
            last[rel] = value
            if weights is not None:
                product = value * weights[rel].astype(jnp.float32)
                sums.append(sum(product[:, i * LANES : (i + 1) * LANES] for i in range(size // LANES)))
        finals.append(load(last.at[0], final.at[core], own_sems.at[1, 12 + number]))
        finals.append(move(last.at[1], final.at[core], core_sems, 2 + number, core_beside))
        return sums

    def gain_exchange(which, sums):
        slots = {}
        for rel in range(2):
            gain_part[which, rel] = sums[rel]
        piece = part // 4
        for number, key in enumerate(far_cube):
            rel, up, over = key
            target = ((along + up) % 2) * 2 + (across + over) % 2
            row = pl.multiple_of(target * piece, 8)
            slots[key] = move(
                gain_part.at[which, rel, pl.ds(row, piece), :],
                gain_in.at[which, number],
                gain_sems,
                which * len(far_cube) + number,
                cube[key],
            )
        return slots

    def gain_finish(which, slots, output):
        piece = part // 4
        row = pl.multiple_of((along * 2 + across) * piece, 8)
        value = gain_part[which, 0, pl.ds(row, piece), :]
        for number, key in enumerate(far_cube):
            slots[key].wait_recv()
            value = value + gain_in[which, number]
        gain_total[which] = value
        return load(gain_total.at[which], output, load_sems.at[9 + which])

    for copy in weight_loads + early_loads:
        copy.wait()
    finish(0, 0, feed_sum.at[0], feed_z.at[0], feed_last.at[0], feed_final.at[0], None)
    gate_sums = finish(
        1, 1, feed_sum.at[1], feed_z.at[1], feed_last.at[1], feed_final.at[1], feed_weight.at[:, :, pl.ds(0, half)]
    )
    for shift in ORDER:
        qkv_copies[shift].wait_recv()
        join_piece("qkv", 4, qkv_sum, qkv_y, qkv_z, qkv_pass, shift)
    up_sums = finish(
        2, 2, feed_sum.at[2], feed_z.at[2], feed_last.at[2], feed_final.at[2],
        feed_weight.at[:, :, pl.ds(half, half)],
    )
    second_slots = gain_exchange(1, [one + two for one, two in zip(gate_sums, up_sums)])
    finish("out", 3, out_sum, out_z, out_last, out_final, None)
    sums = finish("qkv", 4, qkv_sum, qkv_z, qkv_last, qkv_final, qkv_weight)
    first_slots = gain_exchange(0, sums)
    second_store = gain_finish(1, second_slots, second_gain_out)
    first_gain_store = gain_finish(0, first_slots, first_gain_out)
    for copy in (branch_copy, x_copy, core_near):
        copy.wait_recv()
    for number in range(5):
        finals[2 * number].wait()
        finals[2 * number + 1].wait_recv()
    for copy in (first_store, second_store, first_gain_store):
        copy.wait()
    for copy in sent:
        copy.wait_send()
    for copy, condition in guarded:
        pl.when(condition)(copy.wait_send)


def heads_back(
    deep, grad_attention, qkv, heads, logs, first, qkv_wide, out_wide, branch, sent, own, sums, arrived, chunks,
    qkv_own, cosine, sine, spreads,
):
    blocks, count, width = grad_attention.shape
    part, half = chunks.shape[3], chunks.shape[4] // 3
    qkv_half, out_half = spreads[0].shape[0], spreads[1].shape[0]
    rows = 2 * part

    def shape(*dims, kind=jnp.bfloat16):
        return jax.ShapeDtypeStruct(dims, kind)

    def room(*dims, kind=jnp.bfloat16):
        return pltpu.VMEM(dims, kind)

    wide = jnp.float32
    outs = (
        shape(count, width),
        shape(count, width),
        shape(count, width),
        shape(count, width),
        shape(3, 2, part, half, kind=wide),
        shape(2, part, qkv_half, kind=wide),
        shape(2, part, out_half, kind=wide),
        shape(part // 4, LANES, kind=wide),
        shape(part // 4, LANES, kind=wide),
    )
    dma = pltpu.SemaphoreType.DMA
    scratch = [
        room(blocks, count, width),
        room(*qkv.shape),
        room(*heads.shape),
        room(*heads.shape),
        room(*logs.shape, kind=wide),
        room(*qkv.shape),
        room(*qkv_wide.shape),
        room(*out_wide.shape),
        room(2 * count, LANES),
        room(2 * count, LANES),
        room(2 * count, LANES, kind=wide),
        room(2 * count, LANES, kind=wide),
        room(3, count, width),
        room(count, width),
        room(3, deep, rows, half),
        room(3, deep, rows, half),
        room(3, deep - 1, rows, half),
        room(deep, rows, out_half),
        room(deep, rows, out_half),
        room(deep, rows, out_half),
        room(deep - 1, rows, out_half),
        room(deep, rows, qkv_half),
        room(deep, rows, qkv_half),
        room(deep, rows, qkv_half),
        room(deep - 1, rows, qkv_half),
        room(rows, half),
        room(rows, out_half),
        room(rows, qkv_half),
        room(3, 2, part, half, kind=wide),
        room(2, part, qkv_half, kind=wide),
        room(2, part, out_half, kind=wide),
        room(2, part, 2 * half),
        room(2, part, qkv_half),
        room(2, 2, part, LANES, kind=wide),
        room(2, 7, part // 4, LANES, kind=wide),
        room(2, part // 4, LANES, kind=wide),
        dma((11,)),
        dma((2, max(3 * deep, 17))),
        dma((deep,)),
        dma((2, 7)),
        dma((2, 2)),
        dma((2, 5 * deep)),
        dma((2, 5 * (deep - 1))),
        dma((2, 5)),
        dma((2, 14)),
    ]
    return pl.pallas_call(
        functools.partial(heads_back_kernel, deep),
        out_shape=outs,
        in_specs=[hbm_spec()] * 14 + [vmem_spec()] * 4,
        out_specs=(hbm_spec(),) * len(outs),
        scratch_shapes=scratch,
        compiler_params=vmem_params(collective_id=3, has_side_effects=True),
        cost_estimate=cost(flops=30 * 10**9, bytes_accessed=10**8, transcendentals=10**7),
        name="heads_back",
    )(
        grad_attention, qkv, heads, logs, first, qkv_wide, out_wide, branch, sent, own, sums, arrived, chunks,
        qkv_own, cosine, sine, *spreads,
    )


def tables(rows):
    lane = np.arange(LANES)
    entry = lane % (LANES // 2)
    live = (entry < HD // 2).astype(np.float64)
    sign = np.where(lane < LANES // 2, -1.0, 1.0) * live
    inverse = np.where(live > 0, THETA ** (-2.0 * entry / HD), 0.0).astype(np.float32)
    position = np.arange(2 * rows, dtype=np.float32)
    angles = (position[:, None] * inverse[None, :]).astype(np.float32).astype(np.float64)
    both = (np.cos(angles) * live, np.sin(angles) * sign)
    return tuple(jnp.asarray(table.astype(np.float32).reshape(2, rows, LANES)) for table in both)


def norm_factor(rows):
    return lax.rsqrt(jnp.mean(rows * rows, axis=-1, keepdims=True) + EPSILON)


def norm_back(rows, gain, grad):
    factor = norm_factor(rows)
    scaled = grad * gain
    return factor * scaled - rows * factor**3 * jnp.mean(scaled * rows, axis=-1, keepdims=True)


def finish_kernel(
    middle, branch_near, branch_core, branch_x, grad_middle, first_part, first_core, first_x, tokens, gains,
    gate_final, up_final, down_final, qkv_final, out_final, first_lanes, second_lanes,
    result, tokens_grad, query_grad, key_grad, value_grad, out_grad, gate_grad, up_grad, down_grad,
    first_gain, second_gain,
):
    def total(*parts):
        return sum(part[...].astype(jnp.float32) for part in parts)

    result[...] = (middle[...] + total(branch_near, branch_core, branch_x)).astype(jnp.bfloat16)
    rows = tokens[...].astype(jnp.float32)
    grad_first = total(first_part, first_core, first_x)
    tokens_grad[...] = grad_middle[...] + norm_back(rows, gains[0:1, :], grad_first)
    for half in range(2):
        start = 0
        for target in (query_grad, key_grad, value_grad):
            size = target.shape[1] // 2
            target[:, half * size : (half + 1) * size] = qkv_final[half, :, start : start + size]
            start += size
        for target, source in (
            (gate_grad, gate_final), (up_grad, up_final), (down_grad, down_final), (out_grad, out_final)
        ):
            size = target.shape[1] // 2
            target[:, half * size : (half + 1) * size] = source[half]

    @pl.when(pl.program_id(0) == 0)
    def _():
        piece = first_lanes.shape[0]
        place = 0
        for name in ("z", "c", "y", "x"):
            place = place * lax.axis_size(name) + lax.axis_index(name).astype(jnp.int32)
        shape = (piece, gains.shape[1])
        lane = lax.broadcasted_iota(jnp.int32, shape, 1) - place * piece
        chosen = lane == lax.broadcasted_iota(jnp.int32, shape, 0)
        square = (piece, LANES)
        corner = lax.broadcasted_iota(jnp.int32, square, 1) == lax.broadcasted_iota(jnp.int32, square, 0)
        for which, (source, target) in enumerate(((first_lanes, first_gain), (second_lanes, second_gain))):
            gain = jnp.sum(jnp.where(chosen, gains[which : which + 1, :], 0.0), axis=1, keepdims=True)
            value = jnp.sum(source[...], axis=1, keepdims=True) / gain
            target[...] = jnp.sum(jnp.where(corner, value, 0.0), axis=0, keepdims=True)[:, :piece]


def finish_all(
    middle, branch, branch_x, grad_middle, firsts, tokens, gains, feed_final, qkv_final, out_final, lanes,
):
    steps = 4
    count, width = tokens.shape
    part, half = feed_final.shape[2:]
    query = qkv_final.shape[2] // 2
    wide = jnp.float32

    def rows(third=None):
        if third is None:
            return pl.BlockSpec((count // steps, width), lambda i: (i, 0))
        return pl.BlockSpec((None, count // steps, width), lambda i: (third, i, 0))

    def piece(columns):
        return pl.BlockSpec((part // steps, columns), lambda i: (i, 0))

    def halves(columns):
        return pl.BlockSpec((2, part // steps, columns), lambda i: (0, i, 0))

    def feed_halves(third):
        return pl.BlockSpec((None, 2, part // steps, half), lambda i: (third, 0, i, 0))

    out_lanes = out_final.shape[2]
    return pl.pallas_call(
        finish_kernel,
        grid=(steps,),
        out_shape=(
            jax.ShapeDtypeStruct((count, width), jnp.bfloat16),
            jax.ShapeDtypeStruct((count, width), wide),
            jax.ShapeDtypeStruct((part, 2 * query), wide),
            jax.ShapeDtypeStruct((part, query), wide),
            jax.ShapeDtypeStruct((part, query), wide),
            jax.ShapeDtypeStruct((part, 2 * out_lanes), wide),
            jax.ShapeDtypeStruct((part, 2 * half), wide),
            jax.ShapeDtypeStruct((part, 2 * half), wide),
            jax.ShapeDtypeStruct((part, 2 * half), wide),
            jax.ShapeDtypeStruct((1, part // 4), wide),
            jax.ShapeDtypeStruct((1, part // 4), wide),
        ),
        in_specs=[rows(), rows(0), rows(2), rows(), rows(), rows(), rows(), rows(), rows()]
        + [
            pl.BlockSpec(gains.shape, lambda i: (0, 0)),
            feed_halves(1),
            feed_halves(2),
            feed_halves(0),
            halves(2 * query),
            halves(out_lanes),
            pl.BlockSpec(lanes[0].shape, lambda i: (0, 0)),
            pl.BlockSpec(lanes[1].shape, lambda i: (0, 0)),
        ],
        out_specs=(
            rows(),
            rows(),
            piece(2 * query),
            piece(query),
            piece(query),
            piece(2 * out_lanes),
            piece(2 * half),
            piece(2 * half),
            piece(2 * half),
            pl.BlockSpec((1, part // 4), lambda i: (0, 0)),
            pl.BlockSpec((1, part // 4), lambda i: (0, 0)),
        ),
        compiler_params=vmem_params(),
        cost_estimate=cost(flops=10**7, bytes_accessed=3 * 10**7, transcendentals=0),
        name="finish_all",
    )(
        middle, branch, branch, branch_x, grad_middle, *firsts, tokens, gains, feed_final, feed_final, feed_final,
        qkv_final, out_final, *lanes,
    )


def fast_local(
    tokens,
    cotangent,
    first_gain,
    query_weight,
    key_weight,
    value_weight,
    out_weight,
    second_gain,
    gate_weight,
    up_weight,
    down_weight,
):
    deep = lax.axis_size("z")
    rows = tokens.shape[0]
    own_rows = tokens.astype(jnp.float32)
    spreads = (spread_heads(3, 1), spread_heads(0, 2))
    cosine, sine = tables(rows)
    gains = jnp.stack([first_gain, second_gain])
    (
        first_all, qkv_all, heads_all, logs_all, qkv_weight, out_wide, middle, second_all, cotangent_all, chunks, qkv_own,
    ) = forward(
        deep,
        cotangent,
        tokens,
        gains,
        (query_weight, key_weight, value_weight, out_weight.T, gate_weight, up_weight, down_weight.T),
        spreads,
        cosine,
        sine,
    )
    grad_middle, grad_attention, branch, sent, own, sums, arrived = feed_back(
        deep, second_all, cotangent_all, chunks, middle, gains
    )
    first_part, first_core, first_x, branch_x, feed_final, qkv_final, out_final, first_lanes, second_lanes = (
        heads_back(
            deep, grad_attention, qkv_all, heads_all, logs_all, first_all, qkv_weight, out_wide, branch, sent,
            own, sums, arrived, chunks, qkv_own, cosine, sine, spreads,
        )
    )

    (
        result, tokens_grad, query_grad, key_grad, value_grad, out_grad, gate_grad, up_grad, down_grad,
        first_gain_grad, second_gain_grad,
    ) = finish_all(
        middle, branch, branch_x, grad_middle, (first_part, first_core, first_x), tokens, gains, feed_final,
        qkv_final, out_final, (first_lanes, second_lanes),
    )
    return (
        result,
        tokens_grad,
        query_grad,
        key_grad,
        value_grad,
        out_grad.T,
        gate_grad,
        up_grad,
        down_grad.T,
        first_gain_grad[0],
        second_gain_grad[0],
    )


def specs(depth, width):
    both = depth + width
    rows, inward, outward = P(both, None), P(depth, width), P(width, depth)
    in_specs = (rows, rows, P(), inward, inward, inward, outward, P(), inward, inward, outward)
    out_specs = (rows, rows, inward, inward, inward, outward, inward, inward, outward, P(both), P(both))
    return in_specs, out_specs


def solution(mesh):
    depth, width = mesh.shape["dp"], mesh.shape["tensor"]

    def run(tokens, cotangent, *weights):
        fits = (
            width == 4
            and depth == 8
            and tokens.shape[0] * 2 == SEQ_LEN * depth * width
            and weights[2].shape[1] == 2 * width * HD
            and weights[1].shape[1] == 4 * width * HD
        )
        if fits:
            devices = mesh.devices.reshape(depth // 2, 2, 2, 2)
            fine = jax.sharding.Mesh(devices, ("z", "c", "y", "x"))
            in_specs, out_specs = specs(("z", "c"), ("y", "x"))
            call, over = fast_local, fine
        else:
            in_specs, out_specs = specs(("dp",), ("tensor",))
            call, over = local, mesh
        return jax.shard_map(call, mesh=over, in_specs=in_specs, out_specs=out_specs, check_vma=False)(
            tokens, cotangent, *weights
        )

    return run
```

```python
import functools

import jax
import jax.numpy as jnp
import numpy as np
from jax import lax
from jax.experimental import pallas as pl
from jax.experimental.pallas import tpu as pltpu
from jax.sharding import PartitionSpec as P

HD = 96
SEQ_LEN = 1024


EPSILON = 1e-05
THETA = 100000.0
MASKED = -1e30
LOG2E = 1.4426950408889634
LANES = 128
SHARE = 20
VMEM_BYTES = 63 * 2**20


def normed(inputs, gain):
    factor = lax.rsqrt(jnp.mean(inputs * inputs, axis=-1, keepdims=True) + EPSILON)
    return inputs * factor * gain


def rotate(vectors, direction):
    seq_rows, head_count, head_size = vectors.shape
    half_size = head_size // 2
    position = (jnp.arange(seq_rows, dtype=jnp.int32) % SEQ_LEN).astype(jnp.float32)
    inverse = THETA ** (-2.0 * jnp.arange(half_size, dtype=jnp.float32) / head_size)
    angles = position[:, None] * inverse[None, :]
    cosine = jnp.cos(angles)[:, None, :]
    sine_part = direction * jnp.sin(angles)[:, None, :]
    leading = vectors[..., :half_size]
    trailing = vectors[..., half_size:]
    return jnp.concatenate(
        [leading * cosine - trailing * sine_part, trailing * cosine + leading * sine_part], axis=-1
    )


def times_transposed(left, right):
    return lax.dot_general(
        left, right, (((1,), (1,)), ((), ())), preferred_element_type=jnp.float32
    )


def transposed_times(left, right):
    return lax.dot_general(
        left, right, (((0,), (0,)), ((), ())), preferred_element_type=jnp.float32
    )


def scaled_scores(queries, keys_rot):
    raw_scores = jnp.einsum(
        "qhgd,khd->hgqk", queries, keys_rot, preferred_element_type=jnp.float32
    ) * queries.shape[-1] ** (-0.5)
    length_rows = queries.shape[0]
    causal = jnp.arange(length_rows)[:, None] >= jnp.arange(length_rows)[None, :]
    return jnp.where(causal, raw_scores, MASKED)


def attend_forward(operands):
    queries, keys_rot, values = operands
    scores = scaled_scores(queries, keys_rot)
    row_max = jnp.max(scores, axis=-1, keepdims=True)
    weights = jnp.exp(scores - row_max)
    row_total = jnp.sum(weights, axis=-1, keepdims=True)
    softmax = (weights / row_total).astype(jnp.bfloat16)
    mixed_heads = jnp.einsum("hgqk,khd->qhgd", softmax, values, preferred_element_type=jnp.float32)
    return (mixed_heads.astype(jnp.bfloat16), (row_max + jnp.log(row_total))[..., 0])


def attend_backward(operands):
    queries, keys_rot, values, grad_mixed, log_total = operands
    scores = scaled_scores(queries, keys_rot)
    softmax = jnp.exp(scores - log_total[..., None])
    grad_softmax = jnp.einsum(
        "qhgd,khd->hgqk", grad_mixed, values, preferred_element_type=jnp.float32
    )
    grad_values = jnp.einsum(
        "hgqk,qhgd->khd",
        softmax.astype(jnp.bfloat16),
        grad_mixed,
        preferred_element_type=jnp.float32,
    )
    row_inner = jnp.sum(softmax * grad_softmax, axis=-1, keepdims=True)
    grad_scores = (softmax * (grad_softmax - row_inner)).astype(jnp.bfloat16)
    scale_factor = queries.shape[-1] ** (-0.5)
    grad_queries = (
        jnp.einsum("hgqk,khd->qhgd", grad_scores, keys_rot, preferred_element_type=jnp.float32)
        * scale_factor
    )
    grad_keys = (
        jnp.einsum("hgqk,qhgd->khd", grad_scores, queries, preferred_element_type=jnp.float32)
        * scale_factor
    )
    return (grad_queries, grad_keys, grad_values)


def gather_rows(shard):
    return lax.all_gather(shard, "tensor", axis=0, tiled=True)


def gather_grads(shard):
    return lax.all_gather(shard, "tensor", axis=0, tiled=True)


def sum_outputs(term, row_count):
    return lax.psum_scatter(
        term(jnp.int32(0), row_count * lax.axis_size("tensor")),
        "tensor",
        scatter_dimension=0,
        tiled=True,
    )


def sum_inputs(term, row_count):
    return lax.psum_scatter(
        term(jnp.int32(0), row_count * lax.axis_size("tensor")),
        "tensor",
        scatter_dimension=0,
        tiled=True,
    )


def local(
    tokens,
    cotangent,
    first_gain,
    query_weight,
    key_weight,
    value_weight,
    out_weight,
    second_gain,
    gate_weight,
    up_weight,
    down_weight,
):
    query_weight, key_weight, value_weight, out_weight, gate_weight, up_weight, down_weight = (
        lax.all_gather(query_weight, "dp", axis=0, tiled=True),
        lax.all_gather(key_weight, "dp", axis=0, tiled=True),
        lax.all_gather(value_weight, "dp", axis=0, tiled=True),
        lax.all_gather(out_weight, "dp", axis=1, tiled=True),
        lax.all_gather(gate_weight, "dp", axis=0, tiled=True),
        lax.all_gather(up_weight, "dp", axis=0, tiled=True),
        lax.all_gather(down_weight, "dp", axis=1, tiled=True),
    )
    own_rows = tokens.astype(jnp.float32)
    row_count = own_rows.shape[0]
    pair_count = key_weight.shape[1] // HD
    first_normed = normed(own_rows, first_gain).astype(jnp.bfloat16)
    first_rows = gather_rows(first_normed)
    group_rows = first_rows.shape[0]
    sequences = group_rows // SEQ_LEN
    query_pre = jnp.dot(first_rows, query_weight, preferred_element_type=jnp.float32)
    key_pre = jnp.dot(first_rows, key_weight, preferred_element_type=jnp.float32)
    value_pre = jnp.dot(first_rows, value_weight, preferred_element_type=jnp.float32)
    queries = rotate(query_pre.reshape(group_rows, 2 * pair_count, HD), 1.0).astype(jnp.bfloat16)
    queries = queries.reshape(sequences, SEQ_LEN, pair_count, 2, HD)
    keys_rot = rotate(key_pre.reshape(group_rows, pair_count, HD), 1.0).astype(jnp.bfloat16)
    keys_rot = keys_rot.reshape(sequences, SEQ_LEN, pair_count, HD)
    values = value_pre.astype(jnp.bfloat16).reshape(sequences, SEQ_LEN, pair_count, HD)
    mixed_heads, log_total = lax.map(attend_forward, (queries, keys_rot, values))
    heads_out = mixed_heads.reshape(group_rows, 2 * pair_count * HD)
    heads_rows = lax.all_to_all(heads_out, "tensor", split_axis=0, concat_axis=1, tiled=True)
    out_full = lax.all_gather(out_weight, "tensor", axis=0, tiled=True)
    attention_branch = jnp.dot(heads_rows, out_full, preferred_element_type=jnp.float32)
    middle = own_rows + attention_branch
    second_normed = normed(middle, second_gain).astype(jnp.bfloat16)
    second_rows = gather_rows(second_normed)
    gate_full, up_full, down_full = (gate_weight, up_weight, down_weight)
    gate_value = jnp.dot(second_rows, gate_full, preferred_element_type=jnp.float32)
    up_value = jnp.dot(second_rows, up_full, preferred_element_type=jnp.float32)
    sigmoid_gate = jax.nn.sigmoid(gate_value)
    swish_gate = gate_value * sigmoid_gate
    hidden = (swish_gate * up_value).astype(jnp.bfloat16)

    def project_hidden(start, amount):
        return jnp.dot(hidden, down_full, preferred_element_type=jnp.float32)

    ffn_branch = sum_outputs(project_hidden, row_count)
    grad_branch = gather_grads(cotangent)
    result = (middle + ffn_branch).astype(jnp.bfloat16)
    grad_hidden = times_transposed(grad_branch, down_full)
    down_part = transposed_times(hidden, grad_branch)
    slope = sigmoid_gate + gate_value * sigmoid_gate * (1.0 - sigmoid_gate)
    grad_gate = (grad_hidden * up_value * slope).astype(jnp.bfloat16)
    grad_up = (grad_hidden * swish_gate).astype(jnp.bfloat16)
    gate_part = transposed_times(second_rows, grad_gate)
    up_part = transposed_times(second_rows, grad_up)

    def second_back(start, amount):
        return times_transposed(grad_gate, gate_full) + times_transposed(grad_up, up_full)

    grad_second = sum_inputs(second_back, row_count)
    second_unused, second_pull = jax.vjp(normed, middle, second_gain)
    grad_middle_norm, second_gain_part = second_pull(grad_second)
    grad_middle = cotangent.astype(jnp.float32) + grad_middle_norm
    grad_attention = grad_middle.astype(jnp.bfloat16)
    grad_heads_rows = times_transposed(grad_attention, out_full).astype(jnp.bfloat16)
    grad_heads = lax.all_to_all(grad_heads_rows, "tensor", split_axis=1, concat_axis=0, tiled=True)
    out_part = lax.psum_scatter(
        transposed_times(heads_rows, grad_attention).astype(jnp.bfloat16),
        "tensor",
        scatter_dimension=0,
        tiled=True,
    )
    grad_mixed = grad_heads.reshape(sequences, SEQ_LEN, pair_count, 2, HD)
    grad_queries, grad_keys, grad_values = lax.map(
        attend_backward, (queries, keys_rot, values, grad_mixed, log_total)
    )
    grad_query = (
        rotate(grad_queries.reshape(group_rows, 2 * pair_count, HD), -1.0)
        .reshape(group_rows, -1)
        .astype(jnp.bfloat16)
    )
    grad_key = (
        rotate(grad_keys.reshape(group_rows, pair_count, HD), -1.0)
        .reshape(group_rows, -1)
        .astype(jnp.bfloat16)
    )
    grad_value = grad_values.reshape(group_rows, -1).astype(jnp.bfloat16)
    query_part = transposed_times(first_rows, grad_query)
    key_part = transposed_times(first_rows, grad_key)
    value_part = transposed_times(first_rows, grad_value)

    def first_back(start, amount):
        return (
            times_transposed(grad_query, query_weight)
            + times_transposed(grad_key, key_weight)
            + times_transposed(grad_value, value_weight)
        )

    grad_first = sum_inputs(first_back, row_count)
    first_unused, first_pull = jax.vjp(normed, own_rows, first_gain)
    grad_own_norm, first_gain_part = first_pull(grad_first)
    tokens_grad = grad_middle + grad_own_norm
    query_grad, key_grad, value_grad, out_grad, gate_grad, up_grad, down_grad = (
        lax.psum_scatter(
            query_part.astype(jnp.bfloat16), "dp", scatter_dimension=0, tiled=True
        ).astype(jnp.float32),
        lax.psum_scatter(
            key_part.astype(jnp.bfloat16), "dp", scatter_dimension=0, tiled=True
        ).astype(jnp.float32),
        lax.psum_scatter(
            value_part.astype(jnp.bfloat16), "dp", scatter_dimension=0, tiled=True
        ).astype(jnp.float32),
        lax.psum_scatter(out_part, "dp", scatter_dimension=1, tiled=True).astype(jnp.float32),
        lax.psum_scatter(
            gate_part.astype(jnp.bfloat16), "dp", scatter_dimension=0, tiled=True
        ).astype(jnp.float32),
        lax.psum_scatter(
            up_part.astype(jnp.bfloat16), "dp", scatter_dimension=0, tiled=True
        ).astype(jnp.float32),
        lax.psum_scatter(
            down_part.astype(jnp.bfloat16), "dp", scatter_dimension=1, tiled=True
        ).astype(jnp.float32),
    )
    first_gain_grad, second_gain_grad = (
        lax.psum_scatter(first_gain_part, ("dp", "tensor"), scatter_dimension=0, tiled=True),
        lax.psum_scatter(second_gain_part, ("dp", "tensor"), scatter_dimension=0, tiled=True),
    )
    return (
        result,
        tokens_grad,
        query_grad,
        key_grad,
        value_grad,
        out_grad,
        gate_grad,
        up_grad,
        down_grad,
        first_gain_grad,
        second_gain_grad,
    )


def nn(left, right):
    return jnp.dot(left, right, preferred_element_type=jnp.float32)


def cost(flops, bytes_accessed, transcendentals):
    return pl.CostEstimate(
        flops=flops // SHARE, bytes_accessed=bytes_accessed // SHARE, transcendentals=transcendentals // SHARE
    )


def vmem_params(**more):
    return pltpu.CompilerParams(vmem_limit_bytes=VMEM_BYTES, **more)


def vmem_spec():
    return pl.BlockSpec(memory_space=pltpu.VMEM)


def spread_heads(heads_split, heads_plain):
    columns = (heads_split + heads_plain) * HD
    spread = np.zeros((columns, (heads_split + heads_plain) * LANES), np.float32)
    for head in range(heads_split + heads_plain):
        for entry in range(HD):
            lane = entry
            if head < heads_split and entry >= HD // 2:
                lane = entry - HD // 2 + LANES // 2
            spread[head * HD + entry, head * LANES + lane] = 1.0
    return jnp.asarray(spread, jnp.bfloat16)


def turn(vectors, cosine, sine):
    return vectors * cosine + pltpu.roll(vectors, LANES // 2, 1) * sine


TILE = 256
WIDE = 768


def diagonal_mask():
    row = lax.broadcasted_iota(jnp.int32, (2 * TILE, TILE), 0)
    row = jnp.where(row >= TILE, row - TILE, row)
    return row >= lax.broadcasted_iota(jnp.int32, (2 * TILE, TILE), 1)


def hbm_spec():
    return pl.BlockSpec(memory_space=pltpu.HBM)


def send(source, target, sems, where):
    copy = pltpu.make_async_remote_copy(
        src_ref=source,
        dst_ref=target,
        send_sem=sems[0],
        recv_sem=sems[1],
        device_id=where,
        device_id_type=pl.DeviceIdType.MESH,
    )
    copy.start()
    return copy


def greet(partners):
    barrier = pltpu.get_barrier_semaphore()
    for partner in partners:
        pl.semaphore_signal(barrier, inc=1, device_id=partner, device_id_type=pl.DeviceIdType.MESH)
    pl.semaphore_wait(barrier, len(partners))


def beside():
    core, across, along = (lax.axis_index(name).astype(jnp.int32) for name in ("c", "x", "y"))
    return {"c": 1 - core}, {"x": 1 - across}, {"y": 1 - along}


def grid_offset(slot, rel, deep, part):
    z_place = lax.rem(lax.axis_index("z").astype(jnp.int32) + slot, jnp.int32(deep))
    core = lax.rem(lax.axis_index("c").astype(jnp.int32) + rel, jnp.int32(2))
    return pl.multiple_of((z_place * 2 + core) * part, 64)


def spread_weight(buffer, spread_ref, wide, deep, side):
    part = buffer.shape[3]
    half = wide.shape[1] // 2

    @pl.loop(0, 2 * deep)
    def _(step):
        rel, slot = lax.rem(step, jnp.int32(2)), step // 2
        rows = pl.ds(grid_offset(slot, rel, deep, part), part)
        lanes = slice(side * half, (side + 1) * half)
        wide[rows, lanes] = nn(buffer[side, slot, rel], spread_ref[...]).astype(jnp.bfloat16)


def attend_pair(qkv, heads, logs, keys, values, sequence, pair):
    count = qkv.shape[1]
    x_place = lax.axis_index("x").astype(jnp.int32)
    lane0 = pl.multiple_of(pair * 4 * LANES, 4 * LANES)
    mask = diagonal_mask()
    scale = HD ** (-0.5) * LOG2E
    places = [2 * sequence + lax.rem(x_place + position, jnp.int32(2)) for position in range(2)]
    for position, block in enumerate(places):
        rows = slice(position * count, (position + 1) * count)
        keys[rows, :] = qkv[block, :, pl.ds(lane0 + 2 * LANES, LANES)]
        values[rows, :] = qkv[block, :, pl.ds(lane0 + 3 * LANES, LANES)]

    def visit(block, start, before):
        rows = slice(start, start + TILE)
        queries = jnp.concatenate(
            [qkv[block, rows, pl.ds(lane0, LANES)], qkv[block, rows, pl.ds(lane0 + LANES, LANES)]], axis=0
        )
        edge = slice(before, before + TILE)
        near = jnp.where(mask, times_transposed(queries, keys[edge, :]), MASKED)
        top = jnp.max(near, axis=-1, keepdims=True)
        if before:
            far = times_transposed(queries, keys[:before, :])
            top = jnp.maximum(top, jnp.max(far, axis=-1, keepdims=True))
        top = top * scale
        near = jnp.exp2(near * scale - top)
        total = jnp.sum(near, axis=-1, keepdims=True)
        mixed = nn(near.astype(jnp.bfloat16), values[edge, :])
        if before:
            far = jnp.exp2(far * scale - top)
            total = total + jnp.sum(far, axis=-1, keepdims=True)
            mixed = mixed + nn(far.astype(jnp.bfloat16), values[:before, :])
        mixed = (mixed / total).astype(jnp.bfloat16)
        log = top + jnp.log2(total)
        lane = lax.broadcasted_iota(jnp.int32, (TILE, LANES), 1)
        kept = logs[block, rows, :]
        for head in range(2):
            part = slice(head * TILE, (head + 1) * TILE)
            out_lane = pl.multiple_of(pair * 2 * LANES, LANES) + head * LANES
            heads[block, rows, pl.ds(out_lane, LANES)] = mixed[part]
            kept = jnp.where(lane == 2 * pair + head, log[part], kept)
        logs[block, rows, :] = kept

    for position, block in enumerate(places):
        for step in range(count // TILE):
            visit(block, step * TILE, position * count + step * TILE)


def forward_kernel(
    deep, cotangent_ref, tokens_ref, gains_ref, query_ref, key_ref, value_ref, out_ref, gate_ref, up_ref, down_ref,
    qkv_spread, out_spread, cosine_ref, sine_ref,
    first_out, qkv_out, heads_out, logs_out, qkv_wide_out, out_wide_out, middle_out, second_out,
    cotangent_out, feed_out, qkv_own_out,
    qkv_halves, out_halves, feed_halves, first_all, qkv_buffer, out_buffer, qkv_wide, out_wide, qkv, heads, logs, keys, values,
    parts, core_parts, outgoing, incoming, middle, second,
    local_sems, row_sems, qkv_sems, out_sems, feed_sems, core_sems,
):
    core, z_place = lax.axis_index("c").astype(jnp.int32), lax.axis_index("z").astype(jnp.int32)
    core_beside, x_beside, y_beside = beside()
    count = tokens_ref.shape[0]
    ring = jnp.int32(deep)
    z_beside = {way: {"z": lax.rem(z_place + deep + way, ring)} for way in (-1, 1)}
    for half in range(2):
        start = 0
        for ref in (query_ref, key_ref, value_ref):
            size = ref.shape[1] // 2
            qkv_halves[half, :, start : start + size] = ref[:, half * size : (half + 1) * size]
            start += size
    greet([core_beside, x_beside, y_beside, z_beside[-1], z_beside[1]])

    kept = []
    sent = []

    def keep_local(source, target, index):
        copy = pltpu.make_async_copy(source, target, local_sems.at[index])
        copy.start()
        return copy

    def pair_of(sems, index):
        return sems.at[0, index], sems.at[1, index]

    def move(source, target, sems, index, where):
        copy = send(source, target, pair_of(sems, index), where)
        sent.append(copy)
        return copy

    qkv_core = move(qkv_halves.at[1 - core], qkv_buffer.at[0, 0, 1], qkv_sems, 0, core_beside)
    qkv_kept = keep_local(qkv_halves.at[core], qkv_buffer.at[0, 0, 0], 0)
    for half in range(2):
        size = out_ref.shape[1] // 2
        out_halves[half] = out_ref[:, half * size : (half + 1) * size]
        size = gate_ref.shape[1] // 2
        for number, ref in enumerate((gate_ref, up_ref, down_ref)):
            feed_halves[half, :, number * size : (number + 1) * size] = ref[:, half * size : (half + 1) * size]
    step_rows = 128

    @pl.loop(0, count // step_rows)
    def _(step):
        rows = pl.ds(pl.multiple_of(step * step_rows, step_rows), step_rows)
        value = tokens_ref[rows, :].astype(jnp.float32)
        first_all[0, rows, :] = (value * norm_factor(value) * gains_ref[0:1, :]).astype(jnp.bfloat16)

    first_x = move(first_all.at[0], first_all.at[1], row_sems, 0, x_beside)
    out_core = move(out_halves.at[1 - core], out_buffer.at[0, 0, 1], out_sems, 0, core_beside)
    out_kept = keep_local(out_halves.at[core], out_buffer.at[0, 0, 0], 1)
    feed_core = move(feed_halves.at[1 - core], feed_out.at[0, 0, 1], feed_sems, 0, core_beside)
    feed_kept = keep_local(feed_halves.at[core], feed_out.at[0, 0, 0], 2)
    first_core = move(first_all.at[0], first_all.at[2], row_sems, 1, core_beside)
    cotangent_kept = keep_local(cotangent_ref, cotangent_out.at[0], 4)

    last = deep - 1

    def z_copy(buffer, sems, upward, step, rel):
        source, target = ((deep - step) % deep, last - step) if upward else (step, step + 1)
        return pltpu.make_async_remote_copy(
            src_ref=buffer.at[0, source, rel],
            dst_ref=buffer.at[0, target, rel],
            send_sem=sems.at[0, 2 * (1 + upward * last + step) + rel],
            recv_sem=sems.at[1, 2 * target + rel],
            device_id=z_beside[1 if upward else -1],
            device_id_type=pl.DeviceIdType.MESH,
        )

    def z_sends(upward, step):
        if upward:
            return (z_place <= last - 1) & (z_place - step >= 0)
        return (z_place >= 1) & (z_place + step <= last)

    def z_start(buffer, sems, upward, step, rel):
        @pl.when(z_sends(upward, step))
        def _():
            z_copy(buffer, sems, upward, step, rel).start()

    def open_z(buffer, sems):
        for rel in range(2):
            z_start(buffer, sems, False, 0, rel)
            z_start(buffer, sems, True, 0, rel)

    def y_copy(buffer, sems, slot, rel):
        return pltpu.make_async_remote_copy(
            src_ref=buffer.at[0, slot, rel],
            dst_ref=buffer.at[1, slot, rel],
            send_sem=sems.at[0, 2 * (2 * deep + slot) + rel],
            recv_sem=sems.at[1, 2 * (2 * deep + slot) + rel],
            device_id=y_beside,
            device_id_type=pl.DeviceIdType.MESH,
        )

    def open_y(buffer, sems):
        for rel in range(2):
            y_copy(buffer, sems, 0, rel).start()

    def z_part(buffer, sems, step, rel):
        for upward in (False, True):
            slot = last - step if upward else step + 1
            arrives = z_place - step - 1 >= 0 if upward else z_place + step + 1 <= last

            @pl.when(arrives)
            def _(upward=upward, slot=slot):
                z_copy(buffer, sems, upward, step, rel).wait_recv()
                if step + 1 < last:
                    z_start(buffer, sems, upward, step + 1, rel)
                y_copy(buffer, sems, slot, rel).start()

    def z_step(buffer, sems, step):
        for rel in range(2):
            z_part(buffer, sems, step, rel)

    def y_wait(buffer, sems):
        for slot in range(deep):
            for rel in range(2):
                y_copy(buffer, sems, slot, rel).wait_recv()

    def close(buffer, sems):
        for rel in range(2):
            for slot in range(deep):
                y_copy(buffer, sems, slot, rel).wait_send()
            for upward in (False, True):
                for step in range(last):

                    @pl.when(z_sends(upward, step))
                    def _(upward=upward, step=step, rel=rel):
                        z_copy(buffer, sems, upward, step, rel).wait_send()

    qkv_z, out_z, feed_z = (qkv_buffer, qkv_sems), (out_buffer, out_sems), (feed_out, feed_sems)
    qkv_core.wait_recv()
    qkv_kept.wait()
    open_z(*qkv_z)
    open_y(*qkv_z)
    out_core.wait_recv()
    out_kept.wait()
    feed_core.wait_recv()
    feed_kept.wait()
    kept.append(keep_local(qkv_buffer.at[0, 0], qkv_own_out, 13))
    for step in range(last):
        z_step(*qkv_z, step)
        if step == last - 2:
            open_z(*out_z)
    open_y(*out_z)
    for step in range(last):
        z_step(*out_z, step)
    open_z(*feed_z)
    open_y(*feed_z)
    spread_weight(qkv_buffer, qkv_spread, qkv_wide, deep, 0)
    spread_weight(out_buffer, out_spread, out_wide, deep, 0)

    def project(start, stride, amount, pair):
        lane0 = pair * 4 * LANES

        @pl.loop(0, amount)
        def _(step):
            block = start + stride * step
            product = nn(first_all[block], qkv_wide[:, lane0 : lane0 + 4 * LANES])
            position = lax.rem(lax.axis_index("x").astype(jnp.int32) + block, jnp.int32(2))
            cosine, sine = cosine_ref[position], sine_ref[position]
            for head in range(4):
                part = product[:, head * LANES : (head + 1) * LANES]
                if head < 3:
                    part = turn(part, cosine, sine)
                lane = lane0 + head * LANES
                qkv[block, :, lane : lane + LANES] = part.astype(jnp.bfloat16)

    first_core.wait_recv()
    project(0, 2, 2, 0)
    first_x.wait_recv()
    first_far = move(first_all.at[1], first_all.at[3], row_sems, 2, core_beside)
    cotangent_x = move(cotangent_ref, cotangent_out.at[1], row_sems, 3, x_beside)
    cotangent_core = move(cotangent_ref, cotangent_out.at[2], row_sems, 4, core_beside)
    project(1, 2, 1, 0)
    first_far.wait_recv()
    project(3, 2, 1, 0)
    kept.append(keep_local(first_all, first_out, 6))
    y_wait(*qkv_z)
    spread_weight(qkv_buffer, qkv_spread, qkv_wide, deep, 1)
    kept.append(keep_local(qkv_wide, qkv_wide_out, 5))
    project(0, 1, 4, 1)
    kept.append(keep_local(qkv, qkv_out, 7))
    z_part(*feed_z, 0, 0)
    logs[...] = jnp.zeros_like(logs)
    for sequence in range(2):

        @pl.loop(0, 2)
        def _(pair, sequence=sequence):
            attend_pair(qkv, heads, logs, keys, values, sequence, pair)

        if sequence == 0:
            z_part(*feed_z, 0, 1)

    kept.append(keep_local(heads, heads_out, 8))
    kept.append(keep_local(logs, logs_out, 9))
    y_wait(*out_z)
    spread_weight(out_buffer, out_spread, out_wide, deep, 1)
    kept.append(keep_local(out_wide, out_wide_out, 10))

    def out_part(block):
        @pl.loop(0, out_wide.shape[0] // WIDE)
        def _(step):
            lanes = pl.ds(pl.multiple_of(step * WIDE, WIDE), WIDE)
            parts[block, :, lanes] = times_transposed(heads[block], out_wide[lanes, :]).astype(jnp.bfloat16)

    out_part(3)
    core_far = move(parts.at[3], core_parts.at[1], core_sems, 0, core_beside)
    out_part(1)
    core_far.wait_recv()

    @pl.loop(0, count // step_rows)
    def _(step):
        rows = pl.ds(pl.multiple_of(step * step_rows, step_rows), step_rows)
        outgoing[rows, :] = (
            parts[1, rows, :].astype(jnp.float32) + core_parts[1, rows, :].astype(jnp.float32)
        ).astype(jnp.bfloat16)

    branch_x = move(outgoing, incoming, core_sems, 1, x_beside)
    out_part(2)
    core_near = move(parts.at[2], core_parts.at[0], core_sems, 2, core_beside)
    out_part(0)
    core_near.wait_recv()
    z_step(*feed_z, 1)
    branch_x.wait_recv()

    @pl.loop(0, count // step_rows)
    def _(step):
        rows = pl.ds(pl.multiple_of(step * step_rows, step_rows), step_rows)
        total = (
            tokens_ref[rows, :].astype(jnp.float32)
            + parts[0, rows, :].astype(jnp.float32)
            + core_parts[0, rows, :].astype(jnp.float32)
            + incoming[rows, :].astype(jnp.float32)
        )
        middle[rows, :] = total
        second[rows, :] = (total * norm_factor(total) * gains_ref[1:2, :]).astype(jnp.bfloat16)

    kept.append(keep_local(middle, middle_out, 11))
    kept.append(keep_local(second, second_out.at[0], 12))
    second_x = move(second, second_out.at[1], row_sems, 5, x_beside)
    second_core = move(second, second_out.at[2], row_sems, 6, core_beside)
    cotangent_x.wait_recv()
    cotangent_far = move(cotangent_out.at[1], cotangent_out.at[3], row_sems, 7, core_beside)
    z_step(*feed_z, 2)
    second_x.wait_recv()
    second_far = move(second_out.at[1], second_out.at[3], row_sems, 8, core_beside)
    for copy in (second_core, second_far, cotangent_core, cotangent_far):
        copy.wait_recv()
    y_wait(*feed_z)
    for copy in kept + [cotangent_kept]:
        copy.wait()
    for copy in sent:
        copy.wait_send()
    for which in (qkv_z, out_z, feed_z):
        close(*which)


def forward(deep, cotangent, tokens, gains, weights, spreads, cosine, sine):
    count, width = tokens.shape
    query, key, value, out, gate, up, down = weights
    part = query.shape[0]
    feed_size = (gate.shape[1] + up.shape[1] + down.shape[1]) // 2
    qkv_size = (query.shape[1] + key.shape[1] + value.shape[1]) // 2
    out_size = out.shape[1] // 2

    def shape(*dims, kind=jnp.bfloat16):
        return jax.ShapeDtypeStruct(dims, kind)

    def room(*dims, kind=jnp.bfloat16):
        return pltpu.VMEM(dims, kind)

    qkv_lanes, out_lanes = 2 * spreads[0].shape[1], 2 * spreads[1].shape[1]
    outs = (
        shape(4, count, width),
        shape(4, count, qkv_lanes),
        shape(4, count, out_lanes),
        shape(4, count, LANES, kind=jnp.float32),
        shape(width, qkv_lanes),
        shape(width, out_lanes),
        shape(count, width, kind=jnp.float32),
        shape(4, count, width),
        shape(4, count, width),
        shape(2, deep, 2, part, feed_size),
        shape(2, part, qkv_size),
    )
    scratch = [
        room(2, part, qkv_size),
        room(2, part, out_size),
        room(2, part, feed_size),
        room(4, count, width),
        room(2, deep, 2, part, qkv_size),
        room(2, deep, 2, part, out_size),
        room(width, qkv_lanes),
        room(width, out_lanes),
        room(4, count, qkv_lanes),
        room(4, count, out_lanes),
        room(4, count, LANES, kind=jnp.float32),
        room(2 * count, LANES),
        room(2 * count, LANES),
        room(4, count, width),
        room(2, count, width),
        room(count, width),
        room(count, width),
        room(count, width, kind=jnp.float32),
        room(count, width),
        pltpu.SemaphoreType.DMA((14,)),
        pltpu.SemaphoreType.DMA((2, 9)),
        pltpu.SemaphoreType.DMA((2, 6 * deep)),
        pltpu.SemaphoreType.DMA((2, 6 * deep)),
        pltpu.SemaphoreType.DMA((2, 6 * deep)),
        pltpu.SemaphoreType.DMA((2, 3)),
    ]
    return pl.pallas_call(
        functools.partial(forward_kernel, deep),
        out_shape=outs,
        in_specs=[hbm_spec()] + [vmem_spec()] * 13,
        out_specs=(hbm_spec(),) * len(outs),
        scratch_shapes=scratch,
        compiler_params=vmem_params(collective_id=1, has_side_effects=True),
        cost_estimate=cost(flops=20 * 10**9, bytes_accessed=10**8, transcendentals=10**7),
        name="forward",
    )(cotangent, tokens, gains, *weights, *spreads, cosine, sine)


EARLY = 7
ORDER = (1, 3, 2, 0)
HOPS = {(0, 1): 0, (0, 3): 1, (0, 2): 2, (1, 1): 3}


def ring_row(shift, deep, rows):
    z_place = lax.rem(lax.axis_index("z").astype(jnp.int32) + shift, jnp.int32(deep))
    return pl.multiple_of(z_place * rows, rows)


def add_rows(target, source, step_rows=128):
    @pl.loop(0, target.shape[0] // step_rows)
    def _(step):
        rows = pl.ds(pl.multiple_of(step * step_rows, step_rows), step_rows)
        target[rows, :] = (target[rows, :].astype(jnp.float32) + source[rows, :].astype(jnp.float32)).astype(
            jnp.bfloat16
        )


def ahead(deep):
    z_place = lax.axis_index("z").astype(jnp.int32)
    return [{"z": lax.rem(z_place + shift, jnp.int32(deep))} for shift in range(deep)]


def pieces_of(deep):
    return [(piece, shift) for piece in range(3) for shift in ORDER[:deep]]


def feed_back_kernel(
    deep, rows_hbm, grads_hbm, chunks, middle_hbm, gain_ref,
    grad_middle_out, grad_attention_out, branch_out, sent_out, own_out, sum_out, arrived_out,
    gate, up, down, rows, grads, hidden, grad_gate, grad_up, parts, landing, incoming, middle, stage,
    early_y, load_sems, weight_sems, store_sems, sum_sems, early_sems, core_sems, x_sems, y_sems, z_sems,
):
    core_beside, x_beside, y_beside = beside()
    z_ahead = ahead(deep)
    greet([core_beside, x_beside, y_beside] + z_ahead[1:])
    blocks, count, width = rows.shape
    half = gate.shape[1] // 2
    part = chunks.shape[3]
    piece_rows = 2 * part
    sent = []

    def load(source, target, sem):
        copy = pltpu.make_async_copy(source, target, sem)
        copy.start()
        return copy

    def move(source, target, sems, index, where):
        copy = send(source, target, (sems.at[0, index], sems.at[1, index]), where)
        sent.append(copy)
        return copy

    row_loads = {}
    for block in (3, 1):
        row_loads[block] = [load(rows_hbm.at[block], rows.at[block], load_sems.at[0, block])]
    weight_loads = {}
    for side in range(2):
        here = []
        for matrix, target in enumerate((gate, up, down)):
            for shift in range(deep):
                for rel in range(2):
                    here.append(
                        load(
                            chunks.at[side, shift, rel, :, pl.ds(matrix * half, half)],
                            target.at[pl.ds(grid_offset(shift, rel, deep, part), part), pl.ds(side * half, half)],
                            weight_sems.at[matrix, side, shift, rel],
                        )
                    )
        weight_loads[side] = here
        if side == 0:
            for block in (3, 1):
                row_loads[block].append(load(grads_hbm.at[block], grads.at[block], load_sems.at[1, block]))
    for block in (2, 0):
        row_loads[block] = [
            load(rows_hbm.at[block], rows.at[block], load_sems.at[0, block]),
            load(grads_hbm.at[block], grads.at[block], load_sems.at[1, block]),
        ]
    middle_load = load(middle_hbm, middle, load_sems.at[0, 4])

    def inner(block):
        for side in range(2):
            for copy in weight_loads.pop(side, ()):
                copy.wait()
            lanes = slice(side * half, (side + 1) * half)
            gate_value = nn(rows[block], gate[:, lanes])
            up_value = nn(rows[block], up[:, lanes])
            grad_hidden = nn(grads[block], down[:, lanes])
            sigmoid = 1.0 / (1.0 + jnp.exp(-gate_value))
            swish = gate_value * sigmoid
            slope = sigmoid + swish * (1.0 - sigmoid)
            hidden[block, :, lanes] = (swish * up_value).astype(jnp.bfloat16)
            grad_gate[block, :, lanes] = (grad_hidden * up_value * slope).astype(jnp.bfloat16)
            grad_up[block, :, lanes] = (grad_hidden * swish).astype(jnp.bfloat16)

    def outer(block):
        @pl.loop(0, width // WIDE)
        def _(step):
            lanes = pl.ds(pl.multiple_of(step * WIDE, WIDE), WIDE)
            parts[block, :, lanes] = (
                times_transposed(grad_gate[block], gate[lanes, :])
                + times_transposed(grad_up[block], up[lanes, :])
            ).astype(jnp.bfloat16)

    for block in (3, 1, 2, 0):
        for copy in row_loads[block]:
            copy.wait()
        inner(block)
        if block in (3, 1):
            outer(block)
        if block == 3:
            far = move(parts.at[3], landing.at[1], core_sems, 0, core_beside)
        if block == 1:
            far.wait_recv()
            add_rows(parts.at[1], landing.at[1])
            across = move(parts.at[1], incoming, x_sems, 0, x_beside)

    sources = ((grads, hidden), (rows, grad_gate), (rows, grad_up))

    def weight_part(piece, side, shift):
        left, right = sources[piece]
        row = ring_row(shift, deep, piece_rows)
        lanes = slice(side * half, (side + 1) * half)
        return transposed_times(
            left[:, :, pl.ds(row, piece_rows)].reshape(blocks * count, piece_rows),
            right[:, :, lanes].reshape(blocks * count, half),
        )

    def weight_stage(piece, side, shift):
        row = ring_row(shift, deep, piece_rows)
        stage[piece, pl.ds(row, piece_rows), :] = weight_part(piece, side, shift).astype(jnp.bfloat16)

    def weight_whole(piece, side):
        left, right = sources[piece]
        lanes = slice(side * half, (side + 1) * half)

        @pl.loop(0, width // WIDE)
        def _(step):
            row = pl.multiple_of(step * WIDE, WIDE)
            stage[piece, pl.ds(row, WIDE), :] = transposed_times(
                left[:, :, pl.ds(row, WIDE)].reshape(blocks * count, WIDE),
                right[:, :, lanes].reshape(blocks * count, half),
            ).astype(jnp.bfloat16)

    early = pieces_of(deep)[:EARLY]
    arrivals, stores, pending = [], [], []

    def flush():
        for index, store, target in pending:
            store.wait()
            arrivals.append(move(target, early_y.at[index], y_sems, index, y_beside))
        pending.clear()

    def send_piece(piece):
        if piece:
            weight_whole(piece, 1)
            flush()
        for shift in ORDER:
            if not piece:
                weight_stage(piece, 1, shift)
                flush()
            rows_here = pl.ds(ring_row(shift, deep, piece_rows), piece_rows)
            target = sent_out.at[piece, rows_here, :]
            store = load(stage.at[piece, rows_here, :], target, early_sems.at[piece * deep + shift])
            if (piece, shift) in early:
                pending.append((early.index((piece, shift)), store, target))
            else:
                stores.append(store)

    send_piece(0)
    outer(2)
    flush()
    near = move(parts.at[2], landing.at[0], core_sems, 1, core_beside)
    outer(0)
    send_piece(1)
    send_piece(2)
    flush()
    late_stores = list(stores)
    hops = []

    def join_early(pairs):
        for piece, shift in pairs:
            index = early.index((piece, shift))
            product = weight_part(piece, 0, shift)
            arrivals[index].wait_recv()
            early_y[index] = (product + early_y[index].astype(jnp.float32)).astype(jnp.bfloat16)
            if (piece, shift) in HOPS:
                number = HOPS[piece, shift]
                hops.append(
                    move(early_y.at[index], arrived_out.at[number], z_sems, number, z_ahead[shift])
                )
            else:
                stores.append(load(early_y.at[index], sum_out.at[index], sum_sems.at[index]))

    join_early(early[:2])
    near.wait_recv()
    middle_load.wait()
    across.wait_recv()
    step_rows = 128

    @pl.loop(0, count // step_rows)
    def _(step):
        tile = pl.ds(pl.multiple_of(step * step_rows, step_rows), step_rows)
        grad = (
            parts[0, tile, :].astype(jnp.float32)
            + landing[0, tile, :].astype(jnp.float32)
            + incoming[tile, :].astype(jnp.float32)
        )
        total = grads[0, tile, :].astype(jnp.float32) + norm_back(middle[tile, :], gain_ref[1:2, :], grad)
        middle[tile, :] = total
        incoming[tile, :] = total.astype(jnp.bfloat16)

    attention_x = move(incoming, grad_attention_out.at[1], x_sems, 1, x_beside)
    attention_core = move(incoming, grad_attention_out.at[2], core_sems, 2, core_beside)
    stores.append(load(incoming, grad_attention_out.at[0], store_sems.at[0]))
    stores.append(load(middle, grad_middle_out, store_sems.at[3]))

    join_early(early[2:4])
    far.wait_send()
    across.wait_send()
    near.wait_send()

    def branch(block):
        @pl.loop(0, width // WIDE)
        def _(step):
            lanes = pl.ds(pl.multiple_of(step * WIDE, WIDE), WIDE)
            parts[block, :, lanes] = times_transposed(hidden[block], down[lanes, :]).astype(jnp.bfloat16)

    branch(3)
    attention_core.wait_recv()
    branch_far = move(parts.at[3], landing.at[1], core_sems, 3, core_beside)
    branch(2)
    branch_near = move(parts.at[2], landing.at[0], core_sems, 4, core_beside)
    branch(1)
    branch_far.wait_recv()
    add_rows(parts.at[1], landing.at[1])
    stores.append(load(parts.at[1], branch_out.at[1], store_sems.at[7]))
    branch(0)
    stores.append(load(parts.at[0], branch_out.at[0], store_sems.at[8]))
    branch_near.wait_recv()
    stores.append(load(landing.at[0], branch_out.at[2], store_sems.at[9]))
    for copy in late_stores:
        copy.wait()
    for piece in range(3):
        whole = piece not in [pair[0] for pair in early]
        if whole:
            weight_whole(piece, 0)
        for shift in range(deep):
            if (piece, shift) not in early:
                if not whole:
                    weight_stage(piece, 0, shift)
                rows_here = pl.ds(ring_row(shift, deep, piece_rows), piece_rows)
                stores.append(
                    load(
                        stage.at[piece, rows_here, :],
                        own_out.at[piece, rows_here, :],
                        early_sems.at[(3 + piece) * deep + shift],
                    )
                )
    join_early(early[4:])
    attention_x.wait_recv()
    attention_far = move(grad_attention_out.at[1], grad_attention_out.at[3], core_sems, 5, core_beside)
    attention_far.wait_recv()
    for copy in hops:
        copy.wait_recv()
    for copy in stores[len(late_stores) :]:
        copy.wait()
    for copy in arrivals + hops:
        copy.wait_send()
    for copy in (attention_x, attention_core, branch_far, branch_near, attention_far):
        copy.wait_send()


def feed_back(deep, rows, grads, chunks, middle, gain):
    blocks, count, width = rows.shape
    half = chunks.shape[4] // 3
    part = chunks.shape[3]

    def shape(*dims, kind=jnp.bfloat16):
        return jax.ShapeDtypeStruct(dims, kind)

    def room(*dims, kind=jnp.bfloat16):
        return pltpu.VMEM(dims, kind)

    outs = (
        shape(count, width, kind=jnp.float32),
        shape(blocks, count, width),
        shape(3, count, width),
        shape(3, width, half),
        shape(3, width, half),
        shape(EARLY, 2 * part, half),
        shape(len(HOPS), 2 * part, half),
    )
    dma = pltpu.SemaphoreType.DMA
    return pl.pallas_call(
        functools.partial(feed_back_kernel, deep),
        out_shape=outs,
        in_specs=[hbm_spec()] * 4 + [vmem_spec()],
        out_specs=(hbm_spec(),) * len(outs),
        scratch_shapes=[room(width, 2 * half)] * 3
        + [room(blocks, count, width)] * 2
        + [room(blocks, count, 2 * half)] * 3
        + [room(blocks, count, width), room(2, count, width), room(count, width)]
        + [room(count, width, kind=jnp.float32), room(3, width, half), room(EARLY, 2 * part, half)]
        + [dma((2, 5)), dma((3, 2, deep, 2)), dma((10,)), dma((EARLY,)), dma((6 * deep,)), dma((2, 6)), dma((2, 2)), dma((2, EARLY)), dma((2, EARLY))],
        compiler_params=vmem_params(collective_id=2, has_side_effects=True),
        cost_estimate=cost(flops=80 * 10**9, bytes_accessed=10**8, transcendentals=10**7),
        name="feed_back",
    )(rows, grads, chunks, middle, gain)


def attend_back_pair(
    qkv, grad_heads, heads, logs, cosine_ref, sine_ref, grad_qkv, keys, values, grad_keys, grad_values,
    sequence, pair,
):
    count = qkv.shape[1]
    x_place = lax.axis_index("x").astype(jnp.int32)
    lane0 = pl.multiple_of(pair * 4 * LANES, 4 * LANES)
    head0 = pl.multiple_of(pair * 2 * LANES, 2 * LANES)
    mask = diagonal_mask()
    factor = HD ** (-0.5)
    scale = factor * LOG2E
    places = [2 * sequence + lax.rem(x_place + position, jnp.int32(2)) for position in range(2)]
    for position, block in enumerate(places):
        rows = slice(position * count, (position + 1) * count)
        keys[rows, :] = qkv[block, :, pl.ds(lane0 + 2 * LANES, LANES)]
        values[rows, :] = qkv[block, :, pl.ds(lane0 + 3 * LANES, LANES)]
    grad_keys[...] = jnp.zeros_like(grad_keys)
    grad_values[...] = jnp.zeros_like(grad_values)

    def visit(block, start, before):
        rows = slice(start, start + TILE)

        def both(ref, first):
            return jnp.concatenate(
                [ref[block, rows, pl.ds(first, LANES)], ref[block, rows, pl.ds(first + LANES, LANES)]], axis=0
            )

        queries, grads, outs = both(qkv, lane0), both(grad_heads, head0), both(heads, head0)
        lane = lax.broadcasted_iota(jnp.int32, (TILE, LANES), 1)
        kept = logs[block, rows, :]
        log = jnp.concatenate(
            [
                jnp.sum(jnp.where(lane == 2 * pair + head, kept, 0.0), axis=-1, keepdims=True)
                for head in range(2)
            ],
            axis=0,
        )
        inner = jnp.sum(grads.astype(jnp.float32) * outs.astype(jnp.float32), axis=-1, keepdims=True)

        def span(span_rows, masked):
            softmax = jnp.exp2(times_transposed(queries, keys[span_rows, :]) * scale - log)
            if masked:
                softmax = jnp.where(mask, softmax, 0.0)
            grad_softmax = times_transposed(grads, values[span_rows, :])
            grad_scores = (softmax * (grad_softmax - inner)).astype(jnp.bfloat16)
            grad_values[span_rows, :] += transposed_times(softmax.astype(jnp.bfloat16), grads)
            grad_keys[span_rows, :] += transposed_times(grad_scores, queries)
            return nn(grad_scores, keys[span_rows, :])

        grad_queries = span(slice(before, before + TILE), True)
        if before:
            grad_queries = grad_queries + span(slice(0, before), False)
        position, table_rows = before // count, slice(before % count, before % count + TILE)
        cosine, sine = cosine_ref[position, table_rows, :], -sine_ref[position, table_rows, :]
        for head in range(2):
            piece = grad_queries[head * TILE : (head + 1) * TILE] * factor
            grad_qkv[block, rows, pl.ds(lane0 + head * LANES, LANES)] = turn(piece, cosine, sine).astype(
                jnp.bfloat16
            )

    for position, block in enumerate(places):
        for step in range(count // TILE):
            visit(block, step * TILE, position * count + step * TILE)

    for position, block in enumerate(places):
        rows = slice(position * count, (position + 1) * count)
        grad_qkv[block, :, pl.ds(lane0 + 2 * LANES, LANES)] = turn(
            grad_keys[rows, :] * factor, cosine_ref[position], -sine_ref[position]
        ).astype(jnp.bfloat16)
        grad_qkv[block, :, pl.ds(lane0 + 3 * LANES, LANES)] = grad_values[rows, :].astype(jnp.bfloat16)


def heads_back_kernel(
    deep, grad_attention_hbm, qkv_hbm, heads_hbm, logs_hbm, first_hbm, qkv_wide_hbm, out_wide_hbm,
    branch_hbm, sent_hbm, own_hbm, sum_hbm, arrived_hbm, chunks_hbm, qkv_own_hbm,
    cosine_ref, sine_ref, qkv_spread, out_spread,
    first_part, first_core, first_x, branch_x, feed_final, qkv_final, out_final, first_gain_out, second_gain_out,
    grad_attention, qkv, heads, grad_heads, logs, grad_qkv, qkv_wide, out_wide, keys, values, grad_keys,
    grad_values, slots, landing, feed_sum, feed_y, feed_z, out_sent, out_sum, out_y, out_z, qkv_sent, qkv_sum, qkv_y,
    qkv_z, feed_pass, out_pass, qkv_pass, feed_last, qkv_last, out_last, feed_weight, qkv_weight, gain_part, gain_in, gain_total,
    load_sems, own_sems, tile_sems, core_sems, x_sems, y_sems, z_sems, pass_sems, gain_sems,
):
    blocks, count, width = grad_attention.shape
    core_beside, x_beside, y_beside = beside()
    core = lax.axis_index("c").astype(jnp.int32)
    across, along = lax.axis_index("x").astype(jnp.int32), lax.axis_index("y").astype(jnp.int32)
    z_ahead = ahead(deep)
    cube = {
        (rel, up, over): {"c": (core + rel) % 2, "y": (along + up) % 2, "x": (across + over) % 2}
        for rel in range(2)
        for up in range(2)
        for over in range(2)
    }
    far_cube = [key for key in cube if key != (0, 0, 0)]
    greet([cube[key] for key in far_cube] + z_ahead[1:])
    half = feed_sum.shape[3]
    piece_rows = feed_sum.shape[2]
    part = piece_rows // 2
    step_rows = 128
    sent = []

    def load(source, target, sem):
        copy = pltpu.make_async_copy(source, target, sem)
        copy.start()
        return copy

    def move(source, target, sems, index, where):
        copy = send(source, target, (sems.at[0, index], sems.at[1, index]), where)
        sent.append(copy)
        return copy

    late = pieces_of(deep)[EARLY:]
    attention_load = load(grad_attention_hbm, grad_attention, load_sems.at[0])
    out_load = load(out_wide_hbm, out_wide, load_sems.at[1])
    heads_load = load(heads_hbm, heads, load_sems.at[2])
    late_copies = []
    for index, (piece, shift) in enumerate(late):
        row = ring_row(shift, deep, piece_rows)
        late_copies.append(
            move(
                sent_hbm.at[piece, pl.ds(row, piece_rows), :], feed_y.at[piece, shift], y_sems, index, y_beside
            )
        )
    branch_copy = move(branch_hbm.at[1], branch_x, x_sems, 0, x_beside)
    qkv_load = load(qkv_hbm, qkv, load_sems.at[3])
    logs_load = load(logs_hbm, logs, load_sems.at[4])
    wide_load = load(qkv_wide_hbm, qkv_wide, load_sems.at[5])
    own_loads, z_copies = {}, {}
    early_loads = []
    for index, (piece, shift) in enumerate(pieces_of(deep)):
        if (piece, shift) in late:
            row = ring_row(shift, deep, piece_rows)
            own_loads[piece, shift] = load(
                own_hbm.at[piece, pl.ds(row, piece_rows), :], feed_sum.at[piece, shift], own_sems.at[0, index]
            )
        elif shift == 0:
            early_loads.append(load(sum_hbm.at[index], feed_sum.at[piece, 0], own_sems.at[1, index]))
        elif (piece, shift) in HOPS:
            early_loads.append(
                load(arrived_hbm.at[HOPS[piece, shift]], feed_z.at[piece, shift - 1], own_sems.at[1, index])
            )
        else:
            z_copies[piece, shift] = move(
                sum_hbm.at[index],
                feed_z.at[piece, shift - 1],
                z_sems,
                piece * (deep - 1) + shift - 1,
                z_ahead[shift],
            )
    weight_loads = [
        load(chunks_hbm.at[0, 0, :, :, pl.ds(0, 2 * half)], feed_weight, load_sems.at[6]),
        load(qkv_own_hbm, qkv_weight, load_sems.at[7]),
    ]

    attention_load.wait()
    out_load.wait()

    @pl.loop(0, blocks)
    def _(block):
        grad_heads[block] = nn(grad_attention[block], out_wide[...]).astype(jnp.bfloat16)

    heads_load.wait()

    def weight_tile(left, right, spread, side):
        size = spread.shape[1]
        right = right[:, :, side * size : (side + 1) * size].reshape(blocks * count, size)
        product = transposed_times(left.reshape(blocks * count, piece_rows), right)
        return times_transposed(product.astype(jnp.bfloat16), spread[...]).astype(jnp.bfloat16)

    guarded = []
    z_place = lax.axis_index("z").astype(jnp.int32)
    last = deep - 1
    inside = (z_place > 0) & (z_place < last)
    inward = {"z": jnp.where(z_place == 0, jnp.int32(1), jnp.int32(last - 1))}

    def remote(source, target, sems, index, where):
        return pltpu.make_async_remote_copy(
            src_ref=source,
            dst_ref=target,
            send_sem=sems.at[0, index],
            recv_sem=sems.at[1, index],
            device_id=where,
            device_id_type=pl.DeviceIdType.MESH,
        )

    def begin(copy, condition):
        pl.when(condition)(copy.start)
        guarded.append((copy, condition))

    def clear(target):
        @pl.when(z_place == 0)
        def _():
            target[0] = jnp.zeros(target.shape[1:], target.dtype)

        @pl.when(z_place == last)
        def _():
            target[last - 1] = jnp.zeros(target.shape[1:], target.dtype)

    def join_piece(name, number, total, arrived, target, passing, shift):
        add_rows(total.at[shift], arrived.at[shift])
        if not shift:
            return
        direct = remote(total.at[shift], target.at[shift - 1], z_sems, number * last + shift - 1, z_ahead[shift])
        if passing is None:
            direct.start()
            sent.append(direct)
        else:
            far = z_place == (last if shift == 1 else 0)
            through = remote(total.at[shift], passing, pass_sems, number, inward)
            if shift == 2:

                @pl.when(inside)
                def _():
                    through.wait_recv()
                    add_rows(total.at[shift], passing)

                direct.start()
                sent.append(direct)
            else:
                begin(through, far)
                begin(direct, jnp.logical_not(far))
        z_copies[name, shift] = direct

    def join_feed(piece, shift):
        own_loads[piece, shift].wait()
        join_piece(
            piece, piece, feed_sum.at[piece], feed_y.at[piece], feed_z.at[piece],
            feed_pass if piece == 2 else None, shift,
        )

    for target in (feed_z.at[2], out_z, qkv_z):
        clear(target)

    def join_feed_late(index):
        late_copies[index].wait_recv()
        join_feed(*late[index])

    qkv_load.wait()
    logs_load.wait()
    for sequence in range(2):

        for pair in range(2):
            attend_back_pair(
                qkv, grad_heads, heads, logs, cosine_ref, sine_ref, grad_qkv, keys, values, grad_keys,
                grad_values, sequence, pair,
            )
        join_feed_late(sequence)
    wide_load.wait()

    def first_tile(order):
        row = ring_row(ORDER[order], deep, piece_rows)
        slot = (order % 2) * 512
        return load(
            first_hbm.at[:, :, pl.ds(row, piece_rows)],
            qkv.at[:, :, pl.ds(slot, piece_rows)],
            tile_sems.at[order],
        )

    first_loads = [first_tile(order) for order in range(2)]

    def first_piece(block):
        @pl.loop(0, width // WIDE)
        def _(step):
            lanes = pl.ds(pl.multiple_of(step * WIDE, WIDE), WIDE)
            slots[block % 3, :, lanes] = times_transposed(grad_qkv[block], qkv_wide[lanes, :]).astype(
                jnp.bfloat16
            )

    first_piece(3)
    core_far = move(slots.at[0], landing, core_sems, 0, core_beside)
    first_piece(1)
    core_far.wait_recv()
    add_rows(slots.at[1], landing)
    x_copy = move(slots.at[1], first_x, x_sems, 1, x_beside)
    join_feed_late(2)
    y_index = len(late)
    qkv_copies = {}
    for order, shift in enumerate(ORDER):
        first_loads[order].wait()
        slot = (order % 2) * 512
        left = qkv[:, :, slot : slot + piece_rows]
        qkv_sent[shift] = weight_tile(left, grad_qkv, qkv_spread, 1)
        qkv_copies[shift] = move(qkv_sent.at[shift], qkv_y.at[shift], y_sems, y_index + shift, y_beside)
        qkv_sum[shift] = weight_tile(left, grad_qkv, qkv_spread, 0)
        if order + 2 < deep:
            first_loads.append(first_tile(order + 2))
    join_feed_late(3)
    first_piece(2)
    core_near = move(slots.at[2], first_core, core_sems, 1, core_beside)
    core_far.wait_send()
    sent[:] = [copy for copy in sent if copy is not core_far]
    first_piece(0)
    first_store = load(slots.at[0], first_part, load_sems.at[8])
    join_feed_late(4)
    y_index += deep
    out_copies = {}
    for shift in ORDER:
        row = ring_row(shift, deep, piece_rows)
        out_sent[shift] = weight_tile(grad_attention[:, :, pl.ds(row, piece_rows)], heads, out_spread, 1)
        out_copies[shift] = move(out_sent.at[shift], out_y.at[shift], y_sems, y_index + shift, y_beside)

    @pl.loop(0, deep)
    def _(shift):
        row = ring_row(shift, deep, piece_rows)
        out_sum[shift] = weight_tile(grad_attention[:, :, pl.ds(row, piece_rows)], heads, out_spread, 0)


    finals = []

    def finish(name, number, total, arrived, last, final, weights):
        for shift in range(1, deep):
            if (name, shift) not in z_copies:
                continue
            if name in (0, 1) or shift == 2:
                z_copies[name, shift].wait_recv()
            else:
                pl.when(z_place != (0 if shift == 1 else deep - 1))(z_copies[name, shift].wait_recv)
        size = total.shape[2]
        sums = []
        for rel in range(2):
            row = pl.multiple_of(lax.rem(core + rel, jnp.int32(2)) * part, part)
            value = total[0, pl.ds(row, part), :].astype(jnp.float32)
            for shift in range(deep - 1):
                value = value + arrived[shift, pl.ds(row, part), :].astype(jnp.float32)
            last[rel] = value
            if weights is not None:
                product = value * weights[rel].astype(jnp.float32)
                sums.append(sum(product[:, i * LANES : (i + 1) * LANES] for i in range(size // LANES)))
        finals.append(load(last.at[0], final.at[core], own_sems.at[1, 12 + number]))
        finals.append(move(last.at[1], final.at[core], core_sems, 2 + number, core_beside))
        return sums

    def gain_exchange(which, sums):
        slots = {}
        for rel in range(2):
            gain_part[which, rel] = sums[rel]
        piece = part // 4
        for number, key in enumerate(far_cube):
            rel, up, over = key
            target = ((along + up) % 2) * 2 + (across + over) % 2
            row = pl.multiple_of(target * piece, 8)
            slots[key] = move(
                gain_part.at[which, rel, pl.ds(row, piece), :],
                gain_in.at[which, number],
                gain_sems,
                which * len(far_cube) + number,
                cube[key],
            )
        return slots

    def gain_finish(which, slots, output):
        piece = part // 4
        row = pl.multiple_of((along * 2 + across) * piece, 8)
        value = gain_part[which, 0, pl.ds(row, piece), :]
        for number, key in enumerate(far_cube):
            slots[key].wait_recv()
            value = value + gain_in[which, number]
        gain_total[which] = value
        return load(gain_total.at[which], output, load_sems.at[9 + which])

    for copy in weight_loads + early_loads:
        copy.wait()
    finish(0, 0, feed_sum.at[0], feed_z.at[0], feed_last.at[0], feed_final.at[0], None)
    gate_sums = finish(
        1, 1, feed_sum.at[1], feed_z.at[1], feed_last.at[1], feed_final.at[1], feed_weight.at[:, :, pl.ds(0, half)]
    )
    for shift in ORDER:
        qkv_copies[shift].wait_recv()
        join_piece("qkv", 4, qkv_sum, qkv_y, qkv_z, qkv_pass, shift)
    for shift in ORDER:
        out_copies[shift].wait_recv()
        join_piece("out", 3, out_sum, out_y, out_z, out_pass, shift)
    up_sums = finish(
        2, 2, feed_sum.at[2], feed_z.at[2], feed_last.at[2], feed_final.at[2],
        feed_weight.at[:, :, pl.ds(half, half)],
    )
    second_slots = gain_exchange(1, [one + two for one, two in zip(gate_sums, up_sums)])
    sums = finish("qkv", 4, qkv_sum, qkv_z, qkv_last, qkv_final, qkv_weight)
    first_slots = gain_exchange(0, sums)
    finish("out", 3, out_sum, out_z, out_last, out_final, None)
    second_store = gain_finish(1, second_slots, second_gain_out)
    first_gain_store = gain_finish(0, first_slots, first_gain_out)
    for copy in (branch_copy, x_copy, core_near):
        copy.wait_recv()
    for number in range(5):
        finals[2 * number].wait()
        finals[2 * number + 1].wait_recv()
    for copy in (first_store, second_store, first_gain_store):
        copy.wait()
    for copy in sent:
        copy.wait_send()
    for copy, condition in guarded:
        pl.when(condition)(copy.wait_send)


def heads_back(
    deep, grad_attention, qkv, heads, logs, first, qkv_wide, out_wide, branch, sent, own, sums, arrived, chunks,
    qkv_own, cosine, sine, spreads,
):
    blocks, count, width = grad_attention.shape
    part, half = chunks.shape[3], chunks.shape[4] // 3
    qkv_half, out_half = spreads[0].shape[0], spreads[1].shape[0]
    rows = 2 * part

    def shape(*dims, kind=jnp.bfloat16):
        return jax.ShapeDtypeStruct(dims, kind)

    def room(*dims, kind=jnp.bfloat16):
        return pltpu.VMEM(dims, kind)

    wide = jnp.float32
    outs = (
        shape(count, width),
        shape(count, width),
        shape(count, width),
        shape(count, width),
        shape(3, 2, part, half, kind=wide),
        shape(2, part, qkv_half, kind=wide),
        shape(2, part, out_half, kind=wide),
        shape(part // 4, LANES, kind=wide),
        shape(part // 4, LANES, kind=wide),
    )
    dma = pltpu.SemaphoreType.DMA
    scratch = [
        room(blocks, count, width),
        room(*qkv.shape),
        room(*heads.shape),
        room(*heads.shape),
        room(*logs.shape, kind=wide),
        room(*qkv.shape),
        room(*qkv_wide.shape),
        room(*out_wide.shape),
        room(2 * count, LANES),
        room(2 * count, LANES),
        room(2 * count, LANES, kind=wide),
        room(2 * count, LANES, kind=wide),
        room(3, count, width),
        room(count, width),
        room(3, deep, rows, half),
        room(3, deep, rows, half),
        room(3, deep - 1, rows, half),
        room(deep, rows, out_half),
        room(deep, rows, out_half),
        room(deep, rows, out_half),
        room(deep - 1, rows, out_half),
        room(deep, rows, qkv_half),
        room(deep, rows, qkv_half),
        room(deep, rows, qkv_half),
        room(deep - 1, rows, qkv_half),
        room(rows, half),
        room(rows, out_half),
        room(rows, qkv_half),
        room(3, 2, part, half, kind=wide),
        room(2, part, qkv_half, kind=wide),
        room(2, part, out_half, kind=wide),
        room(2, part, 2 * half),
        room(2, part, qkv_half),
        room(2, 2, part, LANES, kind=wide),
        room(2, 7, part // 4, LANES, kind=wide),
        room(2, part // 4, LANES, kind=wide),
        dma((11,)),
        dma((2, max(3 * deep, 17))),
        dma((deep,)),
        dma((2, 7)),
        dma((2, 2)),
        dma((2, 5 * deep)),
        dma((2, 5 * (deep - 1))),
        dma((2, 5)),
        dma((2, 14)),
    ]
    return pl.pallas_call(
        functools.partial(heads_back_kernel, deep),
        out_shape=outs,
        in_specs=[hbm_spec()] * 14 + [vmem_spec()] * 4,
        out_specs=(hbm_spec(),) * len(outs),
        scratch_shapes=scratch,
        compiler_params=vmem_params(collective_id=3, has_side_effects=True),
        cost_estimate=cost(flops=30 * 10**9, bytes_accessed=10**8, transcendentals=10**7),
        name="heads_back",
    )(
        grad_attention, qkv, heads, logs, first, qkv_wide, out_wide, branch, sent, own, sums, arrived, chunks,
        qkv_own, cosine, sine, *spreads,
    )


def tables(rows):
    lane = np.arange(LANES)
    entry = lane % (LANES // 2)
    live = (entry < HD // 2).astype(np.float64)
    sign = np.where(lane < LANES // 2, -1.0, 1.0) * live
    inverse = np.where(live > 0, THETA ** (-2.0 * entry / HD), 0.0).astype(np.float32)
    position = np.arange(2 * rows, dtype=np.float32)
    angles = (position[:, None] * inverse[None, :]).astype(np.float32).astype(np.float64)
    both = (np.cos(angles) * live, np.sin(angles) * sign)
    return tuple(jnp.asarray(table.astype(np.float32).reshape(2, rows, LANES)) for table in both)


def norm_factor(rows):
    return lax.rsqrt(jnp.mean(rows * rows, axis=-1, keepdims=True) + EPSILON)


def norm_back(rows, gain, grad):
    factor = norm_factor(rows)
    scaled = grad * gain
    return factor * scaled - rows * factor**3 * jnp.mean(scaled * rows, axis=-1, keepdims=True)


def finish_kernel(
    middle, branch_near, branch_core, branch_x, grad_middle, first_part, first_core, first_x, tokens, gains,
    gate_final, up_final, down_final, qkv_final, out_final, first_lanes, second_lanes,
    result, tokens_grad, query_grad, key_grad, value_grad, out_grad, gate_grad, up_grad, down_grad,
    first_gain, second_gain,
):
    def total(*parts):
        return sum(part[...].astype(jnp.float32) for part in parts)

    result[...] = (middle[...] + total(branch_near, branch_core, branch_x)).astype(jnp.bfloat16)
    rows = tokens[...].astype(jnp.float32)
    grad_first = total(first_part, first_core, first_x)
    tokens_grad[...] = grad_middle[...] + norm_back(rows, gains[0:1, :], grad_first)
    for half in range(2):
        start = 0
        for target in (query_grad, key_grad, value_grad):
            size = target.shape[1] // 2
            target[:, half * size : (half + 1) * size] = qkv_final[half, :, start : start + size]
            start += size
        for target, source in (
            (gate_grad, gate_final), (up_grad, up_final), (down_grad, down_final), (out_grad, out_final)
        ):
            size = target.shape[1] // 2
            target[:, half * size : (half + 1) * size] = source[half]

    @pl.when(pl.program_id(0) == 0)
    def _():
        piece = first_lanes.shape[0]
        place = 0
        for name in ("z", "c", "y", "x"):
            place = place * lax.axis_size(name) + lax.axis_index(name).astype(jnp.int32)
        shape = (piece, gains.shape[1])
        lane = lax.broadcasted_iota(jnp.int32, shape, 1) - place * piece
        chosen = lane == lax.broadcasted_iota(jnp.int32, shape, 0)
        square = (piece, LANES)
        corner = lax.broadcasted_iota(jnp.int32, square, 1) == lax.broadcasted_iota(jnp.int32, square, 0)
        for which, (source, target) in enumerate(((first_lanes, first_gain), (second_lanes, second_gain))):
            gain = jnp.sum(jnp.where(chosen, gains[which : which + 1, :], 0.0), axis=1, keepdims=True)
            value = jnp.sum(source[...], axis=1, keepdims=True) / gain
            target[...] = jnp.sum(jnp.where(corner, value, 0.0), axis=0, keepdims=True)[:, :piece]


def finish_all(
    middle, branch, branch_x, grad_middle, firsts, tokens, gains, feed_final, qkv_final, out_final, lanes,
):
    steps = 4
    count, width = tokens.shape
    part, half = feed_final.shape[2:]
    query = qkv_final.shape[2] // 2
    wide = jnp.float32

    def rows(third=None):
        if third is None:
            return pl.BlockSpec((count // steps, width), lambda i: (i, 0))
        return pl.BlockSpec((None, count // steps, width), lambda i: (third, i, 0))

    def piece(columns):
        return pl.BlockSpec((part // steps, columns), lambda i: (i, 0))

    def halves(columns):
        return pl.BlockSpec((2, part // steps, columns), lambda i: (0, i, 0))

    def feed_halves(third):
        return pl.BlockSpec((None, 2, part // steps, half), lambda i: (third, 0, i, 0))

    out_lanes = out_final.shape[2]
    return pl.pallas_call(
        finish_kernel,
        grid=(steps,),
        out_shape=(
            jax.ShapeDtypeStruct((count, width), jnp.bfloat16),
            jax.ShapeDtypeStruct((count, width), wide),
            jax.ShapeDtypeStruct((part, 2 * query), wide),
            jax.ShapeDtypeStruct((part, query), wide),
            jax.ShapeDtypeStruct((part, query), wide),
            jax.ShapeDtypeStruct((part, 2 * out_lanes), wide),
            jax.ShapeDtypeStruct((part, 2 * half), wide),
            jax.ShapeDtypeStruct((part, 2 * half), wide),
            jax.ShapeDtypeStruct((part, 2 * half), wide),
            jax.ShapeDtypeStruct((1, part // 4), wide),
            jax.ShapeDtypeStruct((1, part // 4), wide),
        ),
        in_specs=[rows(), rows(0), rows(2), rows(), rows(), rows(), rows(), rows(), rows()]
        + [
            pl.BlockSpec(gains.shape, lambda i: (0, 0)),
            feed_halves(1),
            feed_halves(2),
            feed_halves(0),
            halves(2 * query),
            halves(out_lanes),
            pl.BlockSpec(lanes[0].shape, lambda i: (0, 0)),
            pl.BlockSpec(lanes[1].shape, lambda i: (0, 0)),
        ],
        out_specs=(
            rows(),
            rows(),
            piece(2 * query),
            piece(query),
            piece(query),
            piece(2 * out_lanes),
            piece(2 * half),
            piece(2 * half),
            piece(2 * half),
            pl.BlockSpec((1, part // 4), lambda i: (0, 0)),
            pl.BlockSpec((1, part // 4), lambda i: (0, 0)),
        ),
        compiler_params=vmem_params(),
        cost_estimate=cost(flops=10**7, bytes_accessed=3 * 10**7, transcendentals=0),
        name="finish_all",
    )(
        middle, branch, branch, branch_x, grad_middle, *firsts, tokens, gains, feed_final, feed_final, feed_final,
        qkv_final, out_final, *lanes,
    )


def fast_local(
    tokens,
    cotangent,
    first_gain,
    query_weight,
    key_weight,
    value_weight,
    out_weight,
    second_gain,
    gate_weight,
    up_weight,
    down_weight,
):
    deep = lax.axis_size("z")
    rows = tokens.shape[0]
    own_rows = tokens.astype(jnp.float32)
    spreads = (spread_heads(3, 1), spread_heads(0, 2))
    cosine, sine = tables(rows)
    gains = jnp.stack([first_gain, second_gain])
    (
        first_all, qkv_all, heads_all, logs_all, qkv_weight, out_wide, middle, second_all, cotangent_all, chunks, qkv_own,
    ) = forward(
        deep,
        cotangent,
        tokens,
        gains,
        (query_weight, key_weight, value_weight, out_weight.T, gate_weight, up_weight, down_weight.T),
        spreads,
        cosine,
        sine,
    )
    grad_middle, grad_attention, branch, sent, own, sums, arrived = feed_back(
        deep, second_all, cotangent_all, chunks, middle, gains
    )
    first_part, first_core, first_x, branch_x, feed_final, qkv_final, out_final, first_lanes, second_lanes = (
        heads_back(
            deep, grad_attention, qkv_all, heads_all, logs_all, first_all, qkv_weight, out_wide, branch, sent,
            own, sums, arrived, chunks, qkv_own, cosine, sine, spreads,
        )
    )

    (
        result, tokens_grad, query_grad, key_grad, value_grad, out_grad, gate_grad, up_grad, down_grad,
        first_gain_grad, second_gain_grad,
    ) = finish_all(
        middle, branch, branch_x, grad_middle, (first_part, first_core, first_x), tokens, gains, feed_final,
        qkv_final, out_final, (first_lanes, second_lanes),
    )
    return (
        result,
        tokens_grad,
        query_grad,
        key_grad,
        value_grad,
        out_grad.T,
        gate_grad,
        up_grad,
        down_grad.T,
        first_gain_grad[0],
        second_gain_grad[0],
    )


def specs(depth, width):
    both = depth + width
    rows, inward, outward = P(both, None), P(depth, width), P(width, depth)
    in_specs = (rows, rows, P(), inward, inward, inward, outward, P(), inward, inward, outward)
    out_specs = (rows, rows, inward, inward, inward, outward, inward, inward, outward, P(both), P(both))
    return in_specs, out_specs


def solution(mesh):
    depth, width = mesh.shape["dp"], mesh.shape["tensor"]

    def run(tokens, cotangent, *weights):
        fits = (
            width == 4
            and depth == 8
            and tokens.shape[0] * 2 == SEQ_LEN * depth * width
            and weights[2].shape[1] == 2 * width * HD
            and weights[1].shape[1] == 4 * width * HD
        )
        if fits:
            devices = mesh.devices.reshape(depth // 2, 2, 2, 2)
            fine = jax.sharding.Mesh(devices, ("z", "c", "y", "x"))
            in_specs, out_specs = specs(("z", "c"), ("y", "x"))
            call, over = fast_local, fine
        else:
            in_specs, out_specs = specs(("dp",), ("tensor",))
            call, over = local, mesh
        return jax.shard_map(call, mesh=over, in_specs=in_specs, out_specs=out_specs, check_vma=False)(
            tokens, cotangent, *weights
        )

    return run
```

```python
import functools

import jax
import jax.numpy as jnp
import numpy as np
from jax import lax
from jax.experimental import pallas as pl
from jax.experimental.pallas import tpu as pltpu
from jax.sharding import PartitionSpec as P

HD = 96
SEQ_LEN = 1024


EPSILON = 1e-05
THETA = 100000.0
MASKED = -1e30
LOG2E = 1.4426950408889634
LANES = 128
SHARE = 20
VMEM_BYTES = 63 * 2**20


def normed(inputs, gain):
    factor = lax.rsqrt(jnp.mean(inputs * inputs, axis=-1, keepdims=True) + EPSILON)
    return inputs * factor * gain


def rotate(vectors, direction):
    seq_rows, head_count, head_size = vectors.shape
    half_size = head_size // 2
    position = (jnp.arange(seq_rows, dtype=jnp.int32) % SEQ_LEN).astype(jnp.float32)
    inverse = THETA ** (-2.0 * jnp.arange(half_size, dtype=jnp.float32) / head_size)
    angles = position[:, None] * inverse[None, :]
    cosine = jnp.cos(angles)[:, None, :]
    sine_part = direction * jnp.sin(angles)[:, None, :]
    leading = vectors[..., :half_size]
    trailing = vectors[..., half_size:]
    return jnp.concatenate(
        [leading * cosine - trailing * sine_part, trailing * cosine + leading * sine_part], axis=-1
    )


def times_transposed(left, right):
    return lax.dot_general(
        left, right, (((1,), (1,)), ((), ())), preferred_element_type=jnp.float32
    )


def transposed_times(left, right):
    return lax.dot_general(
        left, right, (((0,), (0,)), ((), ())), preferred_element_type=jnp.float32
    )


def scaled_scores(queries, keys_rot):
    raw_scores = jnp.einsum(
        "qhgd,khd->hgqk", queries, keys_rot, preferred_element_type=jnp.float32
    ) * queries.shape[-1] ** (-0.5)
    length_rows = queries.shape[0]
    causal = jnp.arange(length_rows)[:, None] >= jnp.arange(length_rows)[None, :]
    return jnp.where(causal, raw_scores, MASKED)


def attend_forward(operands):
    queries, keys_rot, values = operands
    scores = scaled_scores(queries, keys_rot)
    row_max = jnp.max(scores, axis=-1, keepdims=True)
    weights = jnp.exp(scores - row_max)
    row_total = jnp.sum(weights, axis=-1, keepdims=True)
    softmax = (weights / row_total).astype(jnp.bfloat16)
    mixed_heads = jnp.einsum("hgqk,khd->qhgd", softmax, values, preferred_element_type=jnp.float32)
    return (mixed_heads.astype(jnp.bfloat16), (row_max + jnp.log(row_total))[..., 0])


def attend_backward(operands):
    queries, keys_rot, values, grad_mixed, log_total = operands
    scores = scaled_scores(queries, keys_rot)
    softmax = jnp.exp(scores - log_total[..., None])
    grad_softmax = jnp.einsum(
        "qhgd,khd->hgqk", grad_mixed, values, preferred_element_type=jnp.float32
    )
    grad_values = jnp.einsum(
        "hgqk,qhgd->khd",
        softmax.astype(jnp.bfloat16),
        grad_mixed,
        preferred_element_type=jnp.float32,
    )
    row_inner = jnp.sum(softmax * grad_softmax, axis=-1, keepdims=True)
    grad_scores = (softmax * (grad_softmax - row_inner)).astype(jnp.bfloat16)
    scale_factor = queries.shape[-1] ** (-0.5)
    grad_queries = (
        jnp.einsum("hgqk,khd->qhgd", grad_scores, keys_rot, preferred_element_type=jnp.float32)
        * scale_factor
    )
    grad_keys = (
        jnp.einsum("hgqk,qhgd->khd", grad_scores, queries, preferred_element_type=jnp.float32)
        * scale_factor
    )
    return (grad_queries, grad_keys, grad_values)


def gather_rows(shard):
    return lax.all_gather(shard, "tensor", axis=0, tiled=True)


def gather_grads(shard):
    return lax.all_gather(shard, "tensor", axis=0, tiled=True)


def sum_outputs(term, row_count):
    return lax.psum_scatter(
        term(jnp.int32(0), row_count * lax.axis_size("tensor")),
        "tensor",
        scatter_dimension=0,
        tiled=True,
    )


def sum_inputs(term, row_count):
    return lax.psum_scatter(
        term(jnp.int32(0), row_count * lax.axis_size("tensor")),
        "tensor",
        scatter_dimension=0,
        tiled=True,
    )


def local(
    tokens,
    cotangent,
    first_gain,
    query_weight,
    key_weight,
    value_weight,
    out_weight,
    second_gain,
    gate_weight,
    up_weight,
    down_weight,
):
    query_weight, key_weight, value_weight, out_weight, gate_weight, up_weight, down_weight = (
        lax.all_gather(query_weight, "dp", axis=0, tiled=True),
        lax.all_gather(key_weight, "dp", axis=0, tiled=True),
        lax.all_gather(value_weight, "dp", axis=0, tiled=True),
        lax.all_gather(out_weight, "dp", axis=1, tiled=True),
        lax.all_gather(gate_weight, "dp", axis=0, tiled=True),
        lax.all_gather(up_weight, "dp", axis=0, tiled=True),
        lax.all_gather(down_weight, "dp", axis=1, tiled=True),
    )
    own_rows = tokens.astype(jnp.float32)
    row_count = own_rows.shape[0]
    pair_count = key_weight.shape[1] // HD
    first_normed = normed(own_rows, first_gain).astype(jnp.bfloat16)
    first_rows = gather_rows(first_normed)
    group_rows = first_rows.shape[0]
    sequences = group_rows // SEQ_LEN
    query_pre = jnp.dot(first_rows, query_weight, preferred_element_type=jnp.float32)
    key_pre = jnp.dot(first_rows, key_weight, preferred_element_type=jnp.float32)
    value_pre = jnp.dot(first_rows, value_weight, preferred_element_type=jnp.float32)
    queries = rotate(query_pre.reshape(group_rows, 2 * pair_count, HD), 1.0).astype(jnp.bfloat16)
    queries = queries.reshape(sequences, SEQ_LEN, pair_count, 2, HD)
    keys_rot = rotate(key_pre.reshape(group_rows, pair_count, HD), 1.0).astype(jnp.bfloat16)
    keys_rot = keys_rot.reshape(sequences, SEQ_LEN, pair_count, HD)
    values = value_pre.astype(jnp.bfloat16).reshape(sequences, SEQ_LEN, pair_count, HD)
    mixed_heads, log_total = lax.map(attend_forward, (queries, keys_rot, values))
    heads_out = mixed_heads.reshape(group_rows, 2 * pair_count * HD)
    heads_rows = lax.all_to_all(heads_out, "tensor", split_axis=0, concat_axis=1, tiled=True)
    out_full = lax.all_gather(out_weight, "tensor", axis=0, tiled=True)
    attention_branch = jnp.dot(heads_rows, out_full, preferred_element_type=jnp.float32)
    middle = own_rows + attention_branch
    second_normed = normed(middle, second_gain).astype(jnp.bfloat16)
    second_rows = gather_rows(second_normed)
    gate_full, up_full, down_full = (gate_weight, up_weight, down_weight)
    gate_value = jnp.dot(second_rows, gate_full, preferred_element_type=jnp.float32)
    up_value = jnp.dot(second_rows, up_full, preferred_element_type=jnp.float32)
    sigmoid_gate = jax.nn.sigmoid(gate_value)
    swish_gate = gate_value * sigmoid_gate
    hidden = (swish_gate * up_value).astype(jnp.bfloat16)

    def project_hidden(start, amount):
        return jnp.dot(hidden, down_full, preferred_element_type=jnp.float32)

    ffn_branch = sum_outputs(project_hidden, row_count)
    grad_branch = gather_grads(cotangent)
    result = (middle + ffn_branch).astype(jnp.bfloat16)
    grad_hidden = times_transposed(grad_branch, down_full)
    down_part = transposed_times(hidden, grad_branch)
    slope = sigmoid_gate + gate_value * sigmoid_gate * (1.0 - sigmoid_gate)
    grad_gate = (grad_hidden * up_value * slope).astype(jnp.bfloat16)
    grad_up = (grad_hidden * swish_gate).astype(jnp.bfloat16)
    gate_part = transposed_times(second_rows, grad_gate)
    up_part = transposed_times(second_rows, grad_up)

    def second_back(start, amount):
        return times_transposed(grad_gate, gate_full) + times_transposed(grad_up, up_full)

    grad_second = sum_inputs(second_back, row_count)
    second_unused, second_pull = jax.vjp(normed, middle, second_gain)
    grad_middle_norm, second_gain_part = second_pull(grad_second)
    grad_middle = cotangent.astype(jnp.float32) + grad_middle_norm
    grad_attention = grad_middle.astype(jnp.bfloat16)
    grad_heads_rows = times_transposed(grad_attention, out_full).astype(jnp.bfloat16)
    grad_heads = lax.all_to_all(grad_heads_rows, "tensor", split_axis=1, concat_axis=0, tiled=True)
    out_part = lax.psum_scatter(
        transposed_times(heads_rows, grad_attention).astype(jnp.bfloat16),
        "tensor",
        scatter_dimension=0,
        tiled=True,
    )
    grad_mixed = grad_heads.reshape(sequences, SEQ_LEN, pair_count, 2, HD)
    grad_queries, grad_keys, grad_values = lax.map(
        attend_backward, (queries, keys_rot, values, grad_mixed, log_total)
    )
    grad_query = (
        rotate(grad_queries.reshape(group_rows, 2 * pair_count, HD), -1.0)
        .reshape(group_rows, -1)
        .astype(jnp.bfloat16)
    )
    grad_key = (
        rotate(grad_keys.reshape(group_rows, pair_count, HD), -1.0)
        .reshape(group_rows, -1)
        .astype(jnp.bfloat16)
    )
    grad_value = grad_values.reshape(group_rows, -1).astype(jnp.bfloat16)
    query_part = transposed_times(first_rows, grad_query)
    key_part = transposed_times(first_rows, grad_key)
    value_part = transposed_times(first_rows, grad_value)

    def first_back(start, amount):
        return (
            times_transposed(grad_query, query_weight)
            + times_transposed(grad_key, key_weight)
            + times_transposed(grad_value, value_weight)
        )

    grad_first = sum_inputs(first_back, row_count)
    first_unused, first_pull = jax.vjp(normed, own_rows, first_gain)
    grad_own_norm, first_gain_part = first_pull(grad_first)
    tokens_grad = grad_middle + grad_own_norm
    query_grad, key_grad, value_grad, out_grad, gate_grad, up_grad, down_grad = (
        lax.psum_scatter(
            query_part.astype(jnp.bfloat16), "dp", scatter_dimension=0, tiled=True
        ).astype(jnp.float32),
        lax.psum_scatter(
            key_part.astype(jnp.bfloat16), "dp", scatter_dimension=0, tiled=True
        ).astype(jnp.float32),
        lax.psum_scatter(
            value_part.astype(jnp.bfloat16), "dp", scatter_dimension=0, tiled=True
        ).astype(jnp.float32),
        lax.psum_scatter(out_part, "dp", scatter_dimension=1, tiled=True).astype(jnp.float32),
        lax.psum_scatter(
            gate_part.astype(jnp.bfloat16), "dp", scatter_dimension=0, tiled=True
        ).astype(jnp.float32),
        lax.psum_scatter(
            up_part.astype(jnp.bfloat16), "dp", scatter_dimension=0, tiled=True
        ).astype(jnp.float32),
        lax.psum_scatter(
            down_part.astype(jnp.bfloat16), "dp", scatter_dimension=1, tiled=True
        ).astype(jnp.float32),
    )
    first_gain_grad, second_gain_grad = (
        lax.psum_scatter(first_gain_part, ("dp", "tensor"), scatter_dimension=0, tiled=True),
        lax.psum_scatter(second_gain_part, ("dp", "tensor"), scatter_dimension=0, tiled=True),
    )
    return (
        result,
        tokens_grad,
        query_grad,
        key_grad,
        value_grad,
        out_grad,
        gate_grad,
        up_grad,
        down_grad,
        first_gain_grad,
        second_gain_grad,
    )


def nn(left, right):
    return jnp.dot(left, right, preferred_element_type=jnp.float32)


def cost(flops, bytes_accessed, transcendentals):
    return pl.CostEstimate(
        flops=flops // SHARE, bytes_accessed=bytes_accessed // SHARE, transcendentals=transcendentals // SHARE
    )


def vmem_params(**more):
    return pltpu.CompilerParams(vmem_limit_bytes=VMEM_BYTES, **more)


def vmem_spec():
    return pl.BlockSpec(memory_space=pltpu.VMEM)


def spread_heads(heads_split, heads_plain):
    columns = (heads_split + heads_plain) * HD
    spread = np.zeros((columns, (heads_split + heads_plain) * LANES), np.float32)
    for head in range(heads_split + heads_plain):
        for entry in range(HD):
            lane = entry
            if head < heads_split and entry >= HD // 2:
                lane = entry - HD // 2 + LANES // 2
            spread[head * HD + entry, head * LANES + lane] = 1.0
    return jnp.asarray(spread, jnp.bfloat16)


def turn(vectors, cosine, sine):
    return vectors * cosine + pltpu.roll(vectors, LANES // 2, 1) * sine


TILE = 256
WIDE = 768


def diagonal_mask():
    row = lax.broadcasted_iota(jnp.int32, (2 * TILE, TILE), 0)
    row = jnp.where(row >= TILE, row - TILE, row)
    return row >= lax.broadcasted_iota(jnp.int32, (2 * TILE, TILE), 1)


def hbm_spec():
    return pl.BlockSpec(memory_space=pltpu.HBM)


def send(source, target, sems, where):
    copy = pltpu.make_async_remote_copy(
        src_ref=source,
        dst_ref=target,
        send_sem=sems[0],
        recv_sem=sems[1],
        device_id=where,
        device_id_type=pl.DeviceIdType.MESH,
    )
    copy.start()
    return copy


def greet(partners):
    barrier = pltpu.get_barrier_semaphore()
    for partner in partners:
        pl.semaphore_signal(barrier, inc=1, device_id=partner, device_id_type=pl.DeviceIdType.MESH)
    pl.semaphore_wait(barrier, len(partners))


def beside():
    core, across, along = (lax.axis_index(name).astype(jnp.int32) for name in ("c", "x", "y"))
    return {"c": 1 - core}, {"x": 1 - across}, {"y": 1 - along}


def grid_offset(slot, rel, deep, part):
    z_place = lax.rem(lax.axis_index("z").astype(jnp.int32) + slot, jnp.int32(deep))
    core = lax.rem(lax.axis_index("c").astype(jnp.int32) + rel, jnp.int32(2))
    return pl.multiple_of((z_place * 2 + core) * part, 64)


def spread_weight(buffer, spread_ref, wide, deep, side):
    part = buffer.shape[3]
    half = wide.shape[1] // 2

    @pl.loop(0, 2 * deep)
    def _(step):
        rel, slot = lax.rem(step, jnp.int32(2)), step // 2
        rows = pl.ds(grid_offset(slot, rel, deep, part), part)
        lanes = slice(side * half, (side + 1) * half)
        wide[rows, lanes] = nn(buffer[side, slot, rel], spread_ref[...]).astype(jnp.bfloat16)


def attend_pair(qkv, heads, logs, keys, values, sequence, pair):
    count = qkv.shape[1]
    x_place = lax.axis_index("x").astype(jnp.int32)
    lane0 = pl.multiple_of(pair * 4 * LANES, 4 * LANES)
    mask = diagonal_mask()
    scale = HD ** (-0.5) * LOG2E
    places = [2 * sequence + lax.rem(x_place + position, jnp.int32(2)) for position in range(2)]
    for position, block in enumerate(places):
        rows = slice(position * count, (position + 1) * count)
        keys[rows, :] = qkv[block, :, pl.ds(lane0 + 2 * LANES, LANES)]
        values[rows, :] = qkv[block, :, pl.ds(lane0 + 3 * LANES, LANES)]

    def visit(block, start, before):
        rows = slice(start, start + TILE)
        queries = jnp.concatenate(
            [qkv[block, rows, pl.ds(lane0, LANES)], qkv[block, rows, pl.ds(lane0 + LANES, LANES)]], axis=0
        )
        edge = slice(before, before + TILE)
        near = jnp.where(mask, times_transposed(queries, keys[edge, :]), MASKED)
        top = jnp.max(near, axis=-1, keepdims=True)
        if before:
            far = times_transposed(queries, keys[:before, :])
            top = jnp.maximum(top, jnp.max(far, axis=-1, keepdims=True))
        top = top * scale
        near = jnp.exp2(near * scale - top)
        total = jnp.sum(near, axis=-1, keepdims=True)
        mixed = nn(near.astype(jnp.bfloat16), values[edge, :])
        if before:
            far = jnp.exp2(far * scale - top)
            total = total + jnp.sum(far, axis=-1, keepdims=True)
            mixed = mixed + nn(far.astype(jnp.bfloat16), values[:before, :])
        mixed = (mixed / total).astype(jnp.bfloat16)
        log = top + jnp.log2(total)
        lane = lax.broadcasted_iota(jnp.int32, (TILE, LANES), 1)
        kept = logs[block, rows, :]
        for head in range(2):
            part = slice(head * TILE, (head + 1) * TILE)
            out_lane = pl.multiple_of(pair * 2 * LANES, LANES) + head * LANES
            heads[block, rows, pl.ds(out_lane, LANES)] = mixed[part]
            kept = jnp.where(lane == 2 * pair + head, log[part], kept)
        logs[block, rows, :] = kept

    for position, block in enumerate(places):
        for step in range(count // TILE):
            visit(block, step * TILE, position * count + step * TILE)


def forward_kernel(
    deep, cotangent_ref, tokens_ref, first_gain_ref, second_gain_ref, query_ref, key_ref, value_ref, out_ref, gate_ref, up_ref, down_ref,
    qkv_spread, out_spread, cosine_ref, sine_ref,
    first_out, qkv_out, heads_out, logs_out, qkv_wide_out, out_wide_out, middle_out, second_out,
    cotangent_out, feed_out, qkv_own_out,
    qkv_halves, out_halves, feed_halves, first_all, qkv_buffer, out_buffer, qkv_wide, out_wide, qkv, heads, logs, keys, values,
    parts, core_parts, outgoing, incoming, middle, second,
    local_sems, row_sems, qkv_sems, out_sems, feed_sems, core_sems,
):
    core, z_place = lax.axis_index("c").astype(jnp.int32), lax.axis_index("z").astype(jnp.int32)
    core_beside, x_beside, y_beside = beside()
    count = tokens_ref.shape[0]
    ring = jnp.int32(deep)
    z_beside = {way: {"z": lax.rem(z_place + deep + way, ring)} for way in (-1, 1)}
    for half in range(2):
        start = 0
        for ref in (query_ref, key_ref, value_ref):
            size = ref.shape[1] // 2
            qkv_halves[half, :, start : start + size] = ref[:, half * size : (half + 1) * size]
            start += size
    greet([core_beside, x_beside, y_beside, z_beside[-1], z_beside[1]])

    kept = []
    sent = []

    def keep_local(source, target, index):
        copy = pltpu.make_async_copy(source, target, local_sems.at[index])
        copy.start()
        return copy

    def pair_of(sems, index):
        return sems.at[0, index], sems.at[1, index]

    def move(source, target, sems, index, where):
        copy = send(source, target, pair_of(sems, index), where)
        sent.append(copy)
        return copy

    qkv_core = move(qkv_halves.at[1 - core], qkv_buffer.at[0, 0, 1], qkv_sems, 0, core_beside)
    qkv_kept = keep_local(qkv_halves.at[core], qkv_buffer.at[0, 0, 0], 0)
    for half in range(2):
        size = out_ref.shape[1] // 2
        out_halves[half] = out_ref[:, half * size : (half + 1) * size]
        size = gate_ref.shape[1] // 2
        for number, ref in enumerate((gate_ref, up_ref, down_ref)):
            feed_halves[half, :, number * size : (number + 1) * size] = ref[:, half * size : (half + 1) * size]
    step_rows = 128

    @pl.loop(0, count // step_rows)
    def _(step):
        rows = pl.ds(pl.multiple_of(step * step_rows, step_rows), step_rows)
        value = tokens_ref[rows, :].astype(jnp.float32)
        first_all[0, rows, :] = (value * norm_factor(value) * first_gain_ref[...][None]).astype(jnp.bfloat16)

    first_x = move(first_all.at[0], first_all.at[1], row_sems, 0, x_beside)
    out_core = move(out_halves.at[1 - core], out_buffer.at[0, 0, 1], out_sems, 0, core_beside)
    out_kept = keep_local(out_halves.at[core], out_buffer.at[0, 0, 0], 1)
    feed_core = move(feed_halves.at[1 - core], feed_out.at[0, 0, 1], feed_sems, 0, core_beside)
    feed_kept = keep_local(feed_halves.at[core], feed_out.at[0, 0, 0], 2)
    first_core = move(first_all.at[0], first_all.at[2], row_sems, 1, core_beside)
    cotangent_kept = keep_local(cotangent_ref, cotangent_out.at[0], 4)

    last = deep - 1

    def z_copy(buffer, sems, upward, step, rel):
        source, target = ((deep - step) % deep, last - step) if upward else (step, step + 1)
        return pltpu.make_async_remote_copy(
            src_ref=buffer.at[0, source, rel],
            dst_ref=buffer.at[0, target, rel],
            send_sem=sems.at[0, 2 * (1 + upward * last + step) + rel],
            recv_sem=sems.at[1, 2 * target + rel],
            device_id=z_beside[1 if upward else -1],
            device_id_type=pl.DeviceIdType.MESH,
        )

    def z_sends(upward, step):
        if upward:
            return (z_place <= last - 1) & (z_place - step >= 0)
        return (z_place >= 1) & (z_place + step <= last)

    def z_start(buffer, sems, upward, step, rel):
        @pl.when(z_sends(upward, step))
        def _():
            z_copy(buffer, sems, upward, step, rel).start()

    def open_z(buffer, sems):
        for rel in range(2):
            z_start(buffer, sems, False, 0, rel)
            z_start(buffer, sems, True, 0, rel)

    def y_copy(buffer, sems, slot, rel):
        return pltpu.make_async_remote_copy(
            src_ref=buffer.at[0, slot, rel],
            dst_ref=buffer.at[1, slot, rel],
            send_sem=sems.at[0, 2 * (2 * deep + slot) + rel],
            recv_sem=sems.at[1, 2 * (2 * deep + slot) + rel],
            device_id=y_beside,
            device_id_type=pl.DeviceIdType.MESH,
        )

    def open_y(buffer, sems):
        for rel in range(2):
            y_copy(buffer, sems, 0, rel).start()

    def z_part(buffer, sems, step, rel):
        for upward in (False, True):
            slot = last - step if upward else step + 1
            arrives = z_place - step - 1 >= 0 if upward else z_place + step + 1 <= last

            @pl.when(arrives)
            def _(upward=upward, slot=slot):
                z_copy(buffer, sems, upward, step, rel).wait_recv()
                if step + 1 < last:
                    z_start(buffer, sems, upward, step + 1, rel)
                y_copy(buffer, sems, slot, rel).start()

    def z_step(buffer, sems, step):
        for rel in range(2):
            z_part(buffer, sems, step, rel)

    def y_wait(buffer, sems):
        for slot in range(deep):
            for rel in range(2):
                y_copy(buffer, sems, slot, rel).wait_recv()

    def close(buffer, sems):
        for rel in range(2):
            for slot in range(deep):
                y_copy(buffer, sems, slot, rel).wait_send()
            for upward in (False, True):
                for step in range(last):

                    @pl.when(z_sends(upward, step))
                    def _(upward=upward, step=step, rel=rel):
                        z_copy(buffer, sems, upward, step, rel).wait_send()

    qkv_z, out_z, feed_z = (qkv_buffer, qkv_sems), (out_buffer, out_sems), (feed_out, feed_sems)
    qkv_core.wait_recv()
    qkv_kept.wait()
    open_z(*qkv_z)
    open_y(*qkv_z)
    out_core.wait_recv()
    out_kept.wait()
    feed_core.wait_recv()
    feed_kept.wait()
    kept.append(keep_local(qkv_buffer.at[0, 0], qkv_own_out, 13))
    for step in range(last):
        z_step(*qkv_z, step)
        if step == last - 2:
            open_z(*out_z)
    open_y(*out_z)
    for step in range(last):
        z_step(*out_z, step)
    open_z(*feed_z)
    open_y(*feed_z)
    spread_weight(qkv_buffer, qkv_spread, qkv_wide, deep, 0)
    spread_weight(out_buffer, out_spread, out_wide, deep, 0)

    def project(start, stride, amount, pair):
        lane0 = pair * 4 * LANES

        @pl.loop(0, amount)
        def _(step):
            block = start + stride * step
            product = nn(first_all[block], qkv_wide[:, lane0 : lane0 + 4 * LANES])
            position = lax.rem(lax.axis_index("x").astype(jnp.int32) + block, jnp.int32(2))
            cosine, sine = cosine_ref[position], sine_ref[position]
            for head in range(4):
                part = product[:, head * LANES : (head + 1) * LANES]
                if head < 3:
                    part = turn(part, cosine, sine)
                lane = lane0 + head * LANES
                qkv[block, :, lane : lane + LANES] = part.astype(jnp.bfloat16)

    first_core.wait_recv()
    project(0, 2, 2, 0)
    first_x.wait_recv()
    first_far = move(first_all.at[1], first_all.at[3], row_sems, 2, core_beside)
    cotangent_x = move(cotangent_ref, cotangent_out.at[1], row_sems, 3, x_beside)
    cotangent_core = move(cotangent_ref, cotangent_out.at[2], row_sems, 4, core_beside)
    project(1, 2, 1, 0)
    first_far.wait_recv()
    project(3, 2, 1, 0)
    kept.append(keep_local(first_all, first_out, 6))
    y_wait(*qkv_z)
    spread_weight(qkv_buffer, qkv_spread, qkv_wide, deep, 1)
    kept.append(keep_local(qkv_wide, qkv_wide_out, 5))
    project(0, 1, 4, 1)
    kept.append(keep_local(qkv, qkv_out, 7))
    z_part(*feed_z, 0, 0)
    logs[...] = jnp.zeros_like(logs)
    for sequence in range(2):

        @pl.loop(0, 2)
        def _(pair, sequence=sequence):
            attend_pair(qkv, heads, logs, keys, values, sequence, pair)

        if sequence == 0:
            z_part(*feed_z, 0, 1)

    kept.append(keep_local(heads, heads_out, 8))
    kept.append(keep_local(logs, logs_out, 9))
    y_wait(*out_z)
    spread_weight(out_buffer, out_spread, out_wide, deep, 1)
    kept.append(keep_local(out_wide, out_wide_out, 10))

    def out_part(block):
        @pl.loop(0, out_wide.shape[0] // WIDE)
        def _(step):
            lanes = pl.ds(pl.multiple_of(step * WIDE, WIDE), WIDE)
            parts[block, :, lanes] = times_transposed(heads[block], out_wide[lanes, :]).astype(jnp.bfloat16)

    out_part(3)
    core_far = move(parts.at[3], core_parts.at[1], core_sems, 0, core_beside)
    out_part(1)
    core_far.wait_recv()

    @pl.loop(0, count // step_rows)
    def _(step):
        rows = pl.ds(pl.multiple_of(step * step_rows, step_rows), step_rows)
        outgoing[rows, :] = (
            parts[1, rows, :].astype(jnp.float32) + core_parts[1, rows, :].astype(jnp.float32)
        ).astype(jnp.bfloat16)

    branch_x = move(outgoing, incoming, core_sems, 1, x_beside)
    out_part(2)
    core_near = move(parts.at[2], core_parts.at[0], core_sems, 2, core_beside)
    out_part(0)
    core_near.wait_recv()
    z_step(*feed_z, 1)
    branch_x.wait_recv()

    @pl.loop(0, count // step_rows)
    def _(step):
        rows = pl.ds(pl.multiple_of(step * step_rows, step_rows), step_rows)
        total = (
            tokens_ref[rows, :].astype(jnp.float32)
            + parts[0, rows, :].astype(jnp.float32)
            + core_parts[0, rows, :].astype(jnp.float32)
            + incoming[rows, :].astype(jnp.float32)
        )
        middle[rows, :] = total
        second[rows, :] = (total * norm_factor(total) * second_gain_ref[...][None]).astype(jnp.bfloat16)

    kept.append(keep_local(middle, middle_out, 11))
    kept.append(keep_local(second, second_out.at[0], 12))
    second_x = move(second, second_out.at[1], row_sems, 5, x_beside)
    second_core = move(second, second_out.at[2], row_sems, 6, core_beside)
    cotangent_x.wait_recv()
    cotangent_far = move(cotangent_out.at[1], cotangent_out.at[3], row_sems, 7, core_beside)
    z_step(*feed_z, 2)
    second_x.wait_recv()
    second_far = move(second_out.at[1], second_out.at[3], row_sems, 8, core_beside)
    for copy in (second_core, second_far, cotangent_core, cotangent_far):
        copy.wait_recv()
    y_wait(*feed_z)
    for copy in kept + [cotangent_kept]:
        copy.wait()
    for copy in sent:
        copy.wait_send()
    for which in (qkv_z, out_z, feed_z):
        close(*which)


def forward(deep, cotangent, tokens, gains, weights, spreads, cosine, sine):
    count, width = tokens.shape
    query, key, value, out, gate, up, down = weights
    part = query.shape[0]
    feed_size = (gate.shape[1] + up.shape[1] + down.shape[1]) // 2
    qkv_size = (query.shape[1] + key.shape[1] + value.shape[1]) // 2
    out_size = out.shape[1] // 2

    def shape(*dims, kind=jnp.bfloat16):
        return jax.ShapeDtypeStruct(dims, kind)

    def room(*dims, kind=jnp.bfloat16):
        return pltpu.VMEM(dims, kind)

    qkv_lanes, out_lanes = 2 * spreads[0].shape[1], 2 * spreads[1].shape[1]
    outs = (
        shape(4, count, width),
        shape(4, count, qkv_lanes),
        shape(4, count, out_lanes),
        shape(4, count, LANES, kind=jnp.float32),
        shape(width, qkv_lanes),
        shape(width, out_lanes),
        shape(count, width, kind=jnp.float32),
        shape(4, count, width),
        shape(4, count, width),
        shape(2, deep, 2, part, feed_size),
        shape(2, part, qkv_size),
    )
    scratch = [
        room(2, part, qkv_size),
        room(2, part, out_size),
        room(2, part, feed_size),
        room(4, count, width),
        room(2, deep, 2, part, qkv_size),
        room(2, deep, 2, part, out_size),
        room(width, qkv_lanes),
        room(width, out_lanes),
        room(4, count, qkv_lanes),
        room(4, count, out_lanes),
        room(4, count, LANES, kind=jnp.float32),
        room(2 * count, LANES),
        room(2 * count, LANES),
        room(4, count, width),
        room(2, count, width),
        room(count, width),
        room(count, width),
        room(count, width, kind=jnp.float32),
        room(count, width),
        pltpu.SemaphoreType.DMA((14,)),
        pltpu.SemaphoreType.DMA((2, 9)),
        pltpu.SemaphoreType.DMA((2, 6 * deep)),
        pltpu.SemaphoreType.DMA((2, 6 * deep)),
        pltpu.SemaphoreType.DMA((2, 6 * deep)),
        pltpu.SemaphoreType.DMA((2, 3)),
    ]
    return pl.pallas_call(
        functools.partial(forward_kernel, deep),
        out_shape=outs,
        in_specs=[hbm_spec()] + [vmem_spec()] * 14,
        out_specs=(hbm_spec(),) * len(outs),
        scratch_shapes=scratch,
        compiler_params=vmem_params(collective_id=1, has_side_effects=True),
        cost_estimate=cost(flops=20 * 10**9, bytes_accessed=10**8, transcendentals=10**7),
        name="forward",
    )(cotangent, tokens, *gains, *weights, *spreads, cosine, sine)


EARLY = 7
ORDER = (1, 3, 2, 0)
HOPS = {(0, 1): 0, (0, 3): 1, (0, 2): 2, (1, 1): 3}


def ring_row(shift, deep, rows):
    z_place = lax.rem(lax.axis_index("z").astype(jnp.int32) + shift, jnp.int32(deep))
    return pl.multiple_of(z_place * rows, rows)


def add_rows(target, source, step_rows=128):
    @pl.loop(0, target.shape[0] // step_rows)
    def _(step):
        rows = pl.ds(pl.multiple_of(step * step_rows, step_rows), step_rows)
        target[rows, :] = (target[rows, :].astype(jnp.float32) + source[rows, :].astype(jnp.float32)).astype(
            jnp.bfloat16
        )


def ahead(deep):
    z_place = lax.axis_index("z").astype(jnp.int32)
    return [{"z": lax.rem(z_place + shift, jnp.int32(deep))} for shift in range(deep)]


def pieces_of(deep):
    return [(piece, shift) for piece in range(3) for shift in ORDER[:deep]]


def feed_back_kernel(
    deep, rows_hbm, grads_hbm, chunks, middle_hbm, gain_ref,
    grad_middle_out, grad_attention_out, branch_out, sent_out, own_out, sum_out, arrived_out,
    gate, up, down, rows, grads, hidden, grad_gate, grad_up, parts, landing, incoming, middle, stage,
    early_y, load_sems, weight_sems, store_sems, sum_sems, early_sems, core_sems, x_sems, y_sems, z_sems,
):
    core_beside, x_beside, y_beside = beside()
    z_ahead = ahead(deep)
    greet([core_beside, x_beside, y_beside] + z_ahead[1:])
    blocks, count, width = rows.shape
    half = gate.shape[1] // 2
    part = chunks.shape[3]
    piece_rows = 2 * part
    sent = []

    def load(source, target, sem):
        copy = pltpu.make_async_copy(source, target, sem)
        copy.start()
        return copy

    def move(source, target, sems, index, where):
        copy = send(source, target, (sems.at[0, index], sems.at[1, index]), where)
        sent.append(copy)
        return copy

    row_loads = {}
    for block in (3, 1):
        row_loads[block] = [load(rows_hbm.at[block], rows.at[block], load_sems.at[0, block])]
    weight_loads = {}
    for side in range(2):
        here = []
        for matrix, target in enumerate((gate, up, down)):
            for shift in range(deep):
                for rel in range(2):
                    here.append(
                        load(
                            chunks.at[side, shift, rel, :, pl.ds(matrix * half, half)],
                            target.at[pl.ds(grid_offset(shift, rel, deep, part), part), pl.ds(side * half, half)],
                            weight_sems.at[matrix, side, shift, rel],
                        )
                    )
        weight_loads[side] = here
        if side == 0:
            for block in (3, 1):
                row_loads[block].append(load(grads_hbm.at[block], grads.at[block], load_sems.at[1, block]))
    for block in (2, 0):
        row_loads[block] = [
            load(rows_hbm.at[block], rows.at[block], load_sems.at[0, block]),
            load(grads_hbm.at[block], grads.at[block], load_sems.at[1, block]),
        ]
    middle_load = load(middle_hbm, middle, load_sems.at[0, 4])

    def inner(block):
        for side in range(2):
            for copy in weight_loads.pop(side, ()):
                copy.wait()
            lanes = slice(side * half, (side + 1) * half)
            gate_value = nn(rows[block], gate[:, lanes])
            up_value = nn(rows[block], up[:, lanes])
            grad_hidden = nn(grads[block], down[:, lanes])
            sigmoid = 1.0 / (1.0 + jnp.exp(-gate_value))
            swish = gate_value * sigmoid
            slope = sigmoid + swish * (1.0 - sigmoid)
            hidden[block, :, lanes] = (swish * up_value).astype(jnp.bfloat16)
            grad_gate[block, :, lanes] = (grad_hidden * up_value * slope).astype(jnp.bfloat16)
            grad_up[block, :, lanes] = (grad_hidden * swish).astype(jnp.bfloat16)

    def outer(block):
        @pl.loop(0, width // WIDE)
        def _(step):
            lanes = pl.ds(pl.multiple_of(step * WIDE, WIDE), WIDE)
            parts[block, :, lanes] = (
                times_transposed(grad_gate[block], gate[lanes, :])
                + times_transposed(grad_up[block], up[lanes, :])
            ).astype(jnp.bfloat16)

    for block in (3, 1, 2, 0):
        for copy in row_loads[block]:
            copy.wait()
        inner(block)
        if block in (3, 1):
            outer(block)
        if block == 3:
            far = move(parts.at[3], landing.at[1], core_sems, 0, core_beside)
        if block == 1:
            far.wait_recv()
            add_rows(parts.at[1], landing.at[1])
            across = move(parts.at[1], incoming, x_sems, 0, x_beside)

    sources = ((grads, hidden), (rows, grad_gate), (rows, grad_up))

    def weight_part(piece, side, shift):
        left, right = sources[piece]
        row = ring_row(shift, deep, piece_rows)
        lanes = slice(side * half, (side + 1) * half)
        return transposed_times(
            left[:, :, pl.ds(row, piece_rows)].reshape(blocks * count, piece_rows),
            right[:, :, lanes].reshape(blocks * count, half),
        )

    def weight_stage(piece, side, shift):
        row = ring_row(shift, deep, piece_rows)
        stage[piece, pl.ds(row, piece_rows), :] = weight_part(piece, side, shift).astype(jnp.bfloat16)

    def weight_whole(piece, side):
        left, right = sources[piece]
        lanes = slice(side * half, (side + 1) * half)

        @pl.loop(0, width // WIDE)
        def _(step):
            row = pl.multiple_of(step * WIDE, WIDE)
            stage[piece, pl.ds(row, WIDE), :] = transposed_times(
                left[:, :, pl.ds(row, WIDE)].reshape(blocks * count, WIDE),
                right[:, :, lanes].reshape(blocks * count, half),
            ).astype(jnp.bfloat16)

    early = pieces_of(deep)[:EARLY]
    arrivals, stores, pending = [], [], []

    def flush():
        for index, store, target in pending:
            store.wait()
            arrivals.append(move(target, early_y.at[index], y_sems, index, y_beside))
        pending.clear()

    def send_piece(piece):
        if piece:
            weight_whole(piece, 1)
            flush()
        for shift in ORDER:
            if not piece:
                weight_stage(piece, 1, shift)
                flush()
            rows_here = pl.ds(ring_row(shift, deep, piece_rows), piece_rows)
            target = sent_out.at[piece, rows_here, :]
            store = load(stage.at[piece, rows_here, :], target, early_sems.at[piece * deep + shift])
            if (piece, shift) in early:
                pending.append((early.index((piece, shift)), store, target))
            else:
                stores.append(store)

    send_piece(0)
    outer(2)
    flush()
    near = move(parts.at[2], landing.at[0], core_sems, 1, core_beside)
    outer(0)
    send_piece(1)
    send_piece(2)
    flush()
    late_stores = list(stores)
    hops = []

    def join_early(pairs):
        for piece, shift in pairs:
            index = early.index((piece, shift))
            product = weight_part(piece, 0, shift)
            arrivals[index].wait_recv()
            early_y[index] = (product + early_y[index].astype(jnp.float32)).astype(jnp.bfloat16)
            if (piece, shift) in HOPS:
                number = HOPS[piece, shift]
                hops.append(
                    move(early_y.at[index], arrived_out.at[number], z_sems, number, z_ahead[shift])
                )
            else:
                stores.append(load(early_y.at[index], sum_out.at[index], sum_sems.at[index]))

    join_early(early[:2])
    near.wait_recv()
    middle_load.wait()
    across.wait_recv()
    step_rows = 128

    @pl.loop(0, count // step_rows)
    def _(step):
        tile = pl.ds(pl.multiple_of(step * step_rows, step_rows), step_rows)
        grad = (
            parts[0, tile, :].astype(jnp.float32)
            + landing[0, tile, :].astype(jnp.float32)
            + incoming[tile, :].astype(jnp.float32)
        )
        total = grads[0, tile, :].astype(jnp.float32) + norm_back(middle[tile, :], gain_ref[...][None], grad)
        middle[tile, :] = total
        incoming[tile, :] = total.astype(jnp.bfloat16)

    attention_x = move(incoming, grad_attention_out.at[1], x_sems, 1, x_beside)
    attention_core = move(incoming, grad_attention_out.at[2], core_sems, 2, core_beside)
    stores.append(load(incoming, grad_attention_out.at[0], store_sems.at[0]))
    stores.append(load(middle, grad_middle_out, store_sems.at[3]))

    join_early(early[2:4])
    far.wait_send()
    across.wait_send()
    near.wait_send()

    def branch(block):
        @pl.loop(0, width // WIDE)
        def _(step):
            lanes = pl.ds(pl.multiple_of(step * WIDE, WIDE), WIDE)
            parts[block, :, lanes] = times_transposed(hidden[block], down[lanes, :]).astype(jnp.bfloat16)

    branch(3)
    attention_core.wait_recv()
    branch_far = move(parts.at[3], landing.at[1], core_sems, 3, core_beside)
    branch(2)
    branch_near = move(parts.at[2], landing.at[0], core_sems, 4, core_beside)
    branch(1)
    branch_far.wait_recv()
    add_rows(parts.at[1], landing.at[1])
    stores.append(load(parts.at[1], branch_out.at[1], store_sems.at[7]))
    branch(0)
    stores.append(load(parts.at[0], branch_out.at[0], store_sems.at[8]))
    branch_near.wait_recv()
    stores.append(load(landing.at[0], branch_out.at[2], store_sems.at[9]))
    for copy in late_stores:
        copy.wait()
    for piece in range(3):
        whole = piece not in [pair[0] for pair in early]
        if whole:
            weight_whole(piece, 0)
        for shift in range(deep):
            if (piece, shift) not in early:
                if not whole:
                    weight_stage(piece, 0, shift)
                rows_here = pl.ds(ring_row(shift, deep, piece_rows), piece_rows)
                stores.append(
                    load(
                        stage.at[piece, rows_here, :],
                        own_out.at[piece, rows_here, :],
                        early_sems.at[(3 + piece) * deep + shift],
                    )
                )
    join_early(early[4:])
    attention_x.wait_recv()
    attention_far = move(grad_attention_out.at[1], grad_attention_out.at[3], core_sems, 5, core_beside)
    attention_far.wait_recv()
    for copy in hops:
        copy.wait_recv()
    for copy in stores[len(late_stores) :]:
        copy.wait()
    for copy in arrivals + hops:
        copy.wait_send()
    for copy in (attention_x, attention_core, branch_far, branch_near, attention_far):
        copy.wait_send()


def feed_back(deep, rows, grads, chunks, middle, gain):
    blocks, count, width = rows.shape
    half = chunks.shape[4] // 3
    part = chunks.shape[3]

    def shape(*dims, kind=jnp.bfloat16):
        return jax.ShapeDtypeStruct(dims, kind)

    def room(*dims, kind=jnp.bfloat16):
        return pltpu.VMEM(dims, kind)

    outs = (
        shape(count, width, kind=jnp.float32),
        shape(blocks, count, width),
        shape(3, count, width),
        shape(3, width, half),
        shape(3, width, half),
        shape(EARLY, 2 * part, half),
        shape(len(HOPS), 2 * part, half),
    )
    dma = pltpu.SemaphoreType.DMA
    return pl.pallas_call(
        functools.partial(feed_back_kernel, deep),
        out_shape=outs,
        in_specs=[hbm_spec()] * 4 + [vmem_spec()],
        out_specs=(hbm_spec(),) * len(outs),
        scratch_shapes=[room(width, 2 * half)] * 3
        + [room(blocks, count, width)] * 2
        + [room(blocks, count, 2 * half)] * 3
        + [room(blocks, count, width), room(2, count, width), room(count, width)]
        + [room(count, width, kind=jnp.float32), room(3, width, half), room(EARLY, 2 * part, half)]
        + [dma((2, 5)), dma((3, 2, deep, 2)), dma((10,)), dma((EARLY,)), dma((6 * deep,)), dma((2, 6)), dma((2, 2)), dma((2, EARLY)), dma((2, EARLY))],
        compiler_params=vmem_params(collective_id=2, has_side_effects=True),
        cost_estimate=cost(flops=80 * 10**9, bytes_accessed=10**8, transcendentals=10**7),
        name="feed_back",
    )(rows, grads, chunks, middle, gain)


def attend_back_pair(
    qkv, grad_heads, heads, logs, cosine_ref, sine_ref, grad_qkv, keys, values, grad_keys, grad_values,
    sequence, pair,
):
    count = qkv.shape[1]
    x_place = lax.axis_index("x").astype(jnp.int32)
    lane0 = pl.multiple_of(pair * 4 * LANES, 4 * LANES)
    head0 = pl.multiple_of(pair * 2 * LANES, 2 * LANES)
    mask = diagonal_mask()
    factor = HD ** (-0.5)
    scale = factor * LOG2E
    places = [2 * sequence + lax.rem(x_place + position, jnp.int32(2)) for position in range(2)]
    for position, block in enumerate(places):
        rows = slice(position * count, (position + 1) * count)
        keys[rows, :] = qkv[block, :, pl.ds(lane0 + 2 * LANES, LANES)]
        values[rows, :] = qkv[block, :, pl.ds(lane0 + 3 * LANES, LANES)]
    grad_keys[...] = jnp.zeros_like(grad_keys)
    grad_values[...] = jnp.zeros_like(grad_values)

    def visit(block, start, before):
        rows = slice(start, start + TILE)

        def both(ref, first):
            return jnp.concatenate(
                [ref[block, rows, pl.ds(first, LANES)], ref[block, rows, pl.ds(first + LANES, LANES)]], axis=0
            )

        queries, grads, outs = both(qkv, lane0), both(grad_heads, head0), both(heads, head0)
        lane = lax.broadcasted_iota(jnp.int32, (TILE, LANES), 1)
        kept = logs[block, rows, :]
        log = jnp.concatenate(
            [
                jnp.sum(jnp.where(lane == 2 * pair + head, kept, 0.0), axis=-1, keepdims=True)
                for head in range(2)
            ],
            axis=0,
        )
        inner = jnp.sum(grads.astype(jnp.float32) * outs.astype(jnp.float32), axis=-1, keepdims=True)

        def span(span_rows, masked):
            softmax = jnp.exp2(times_transposed(queries, keys[span_rows, :]) * scale - log)
            if masked:
                softmax = jnp.where(mask, softmax, 0.0)
            grad_softmax = times_transposed(grads, values[span_rows, :])
            grad_scores = (softmax * (grad_softmax - inner)).astype(jnp.bfloat16)
            grad_values[span_rows, :] += transposed_times(softmax.astype(jnp.bfloat16), grads)
            grad_keys[span_rows, :] += transposed_times(grad_scores, queries)
            return nn(grad_scores, keys[span_rows, :])

        grad_queries = span(slice(before, before + TILE), True)
        if before:
            grad_queries = grad_queries + span(slice(0, before), False)
        position, table_rows = before // count, slice(before % count, before % count + TILE)
        cosine, sine = cosine_ref[position, table_rows, :], -sine_ref[position, table_rows, :]
        for head in range(2):
            piece = grad_queries[head * TILE : (head + 1) * TILE] * factor
            grad_qkv[block, rows, pl.ds(lane0 + head * LANES, LANES)] = turn(piece, cosine, sine).astype(
                jnp.bfloat16
            )

    for position, block in enumerate(places):
        for step in range(count // TILE):
            visit(block, step * TILE, position * count + step * TILE)

    for position, block in enumerate(places):
        rows = slice(position * count, (position + 1) * count)
        grad_qkv[block, :, pl.ds(lane0 + 2 * LANES, LANES)] = turn(
            grad_keys[rows, :] * factor, cosine_ref[position], -sine_ref[position]
        ).astype(jnp.bfloat16)
        grad_qkv[block, :, pl.ds(lane0 + 3 * LANES, LANES)] = grad_values[rows, :].astype(jnp.bfloat16)


def heads_back_kernel(
    deep, grad_attention_hbm, qkv_hbm, heads_hbm, logs_hbm, first_hbm, qkv_wide_hbm, out_wide_hbm,
    branch_hbm, sent_hbm, own_hbm, sum_hbm, arrived_hbm, chunks_hbm, qkv_own_hbm,
    cosine_ref, sine_ref, qkv_spread, out_spread,
    first_part, first_core, first_x, branch_x, feed_final, qkv_final, out_final, first_gain_out, second_gain_out,
    grad_attention, qkv, heads, grad_heads, logs, grad_qkv, qkv_wide, out_wide, keys, values, grad_keys,
    grad_values, slots, landing, feed_sum, feed_y, feed_z, out_sent, out_sum, out_y, out_z, qkv_sent, qkv_sum, qkv_y,
    qkv_z, feed_pass, out_pass, qkv_pass, feed_last, qkv_last, out_last, feed_weight, qkv_weight, gain_part, gain_in, gain_total,
    load_sems, own_sems, tile_sems, core_sems, x_sems, y_sems, z_sems, pass_sems, gain_sems,
):
    blocks, count, width = grad_attention.shape
    core_beside, x_beside, y_beside = beside()
    core = lax.axis_index("c").astype(jnp.int32)
    across, along = lax.axis_index("x").astype(jnp.int32), lax.axis_index("y").astype(jnp.int32)
    z_ahead = ahead(deep)
    cube = {
        (rel, up, over): {"c": (core + rel) % 2, "y": (along + up) % 2, "x": (across + over) % 2}
        for rel in range(2)
        for up in range(2)
        for over in range(2)
    }
    far_cube = [key for key in cube if key != (0, 0, 0)]
    greet([cube[key] for key in far_cube] + z_ahead[1:])
    half = feed_sum.shape[3]
    piece_rows = feed_sum.shape[2]
    part = piece_rows // 2
    step_rows = 128
    sent = []

    def load(source, target, sem):
        copy = pltpu.make_async_copy(source, target, sem)
        copy.start()
        return copy

    def move(source, target, sems, index, where):
        copy = send(source, target, (sems.at[0, index], sems.at[1, index]), where)
        sent.append(copy)
        return copy

    late = pieces_of(deep)[EARLY:]
    attention_load = load(grad_attention_hbm, grad_attention, load_sems.at[0])
    out_load = load(out_wide_hbm, out_wide, load_sems.at[1])
    heads_load = load(heads_hbm, heads, load_sems.at[2])
    late_copies = []
    for index, (piece, shift) in enumerate(late):
        row = ring_row(shift, deep, piece_rows)
        late_copies.append(
            move(
                sent_hbm.at[piece, pl.ds(row, piece_rows), :], feed_y.at[piece, shift], y_sems, index, y_beside
            )
        )
    branch_copy = move(branch_hbm.at[1], branch_x, x_sems, 0, x_beside)
    qkv_load = load(qkv_hbm, qkv, load_sems.at[3])
    logs_load = load(logs_hbm, logs, load_sems.at[4])
    wide_load = load(qkv_wide_hbm, qkv_wide, load_sems.at[5])
    own_loads, z_copies = {}, {}
    early_loads = []
    for index, (piece, shift) in enumerate(pieces_of(deep)):
        if (piece, shift) in late:
            row = ring_row(shift, deep, piece_rows)
            own_loads[piece, shift] = load(
                own_hbm.at[piece, pl.ds(row, piece_rows), :], feed_sum.at[piece, shift], own_sems.at[0, index]
            )
        elif shift == 0:
            early_loads.append(load(sum_hbm.at[index], feed_sum.at[piece, 0], own_sems.at[1, index]))
        elif (piece, shift) in HOPS:
            early_loads.append(
                load(arrived_hbm.at[HOPS[piece, shift]], feed_z.at[piece, shift - 1], own_sems.at[1, index])
            )
        else:
            z_copies[piece, shift] = move(
                sum_hbm.at[index],
                feed_z.at[piece, shift - 1],
                z_sems,
                piece * (deep - 1) + shift - 1,
                z_ahead[shift],
            )
    weight_loads = [
        load(chunks_hbm.at[0, 0, :, :, pl.ds(0, 2 * half)], feed_weight, load_sems.at[6]),
        load(qkv_own_hbm, qkv_weight, load_sems.at[7]),
    ]

    attention_load.wait()
    out_load.wait()

    @pl.loop(0, blocks)
    def _(block):
        grad_heads[block] = nn(grad_attention[block], out_wide[...]).astype(jnp.bfloat16)

    heads_load.wait()

    def weight_tile(left, right, spread, side):
        size = spread.shape[1]
        right = right[:, :, side * size : (side + 1) * size].reshape(blocks * count, size)
        product = transposed_times(left.reshape(blocks * count, piece_rows), right)
        return times_transposed(product.astype(jnp.bfloat16), spread[...]).astype(jnp.bfloat16)

    guarded = []
    z_place = lax.axis_index("z").astype(jnp.int32)
    last = deep - 1
    inside = (z_place > 0) & (z_place < last)
    inward = {"z": jnp.where(z_place == 0, jnp.int32(1), jnp.int32(last - 1))}

    def remote(source, target, sems, index, where):
        return pltpu.make_async_remote_copy(
            src_ref=source,
            dst_ref=target,
            send_sem=sems.at[0, index],
            recv_sem=sems.at[1, index],
            device_id=where,
            device_id_type=pl.DeviceIdType.MESH,
        )

    def begin(copy, condition):
        pl.when(condition)(copy.start)
        guarded.append((copy, condition))

    def clear(target):
        @pl.when(z_place == 0)
        def _():
            target[0] = jnp.zeros(target.shape[1:], target.dtype)

        @pl.when(z_place == last)
        def _():
            target[last - 1] = jnp.zeros(target.shape[1:], target.dtype)

    def join_piece(name, number, total, arrived, target, passing, shift):
        add_rows(total.at[shift], arrived.at[shift])
        if not shift:
            return
        direct = remote(total.at[shift], target.at[shift - 1], z_sems, number * last + shift - 1, z_ahead[shift])
        if passing is None:
            direct.start()
            sent.append(direct)
        else:
            far = z_place == (last if shift == 1 else 0)
            through = remote(total.at[shift], passing, pass_sems, number, inward)
            if shift == 2:

                @pl.when(inside)
                def _():
                    through.wait_recv()
                    add_rows(total.at[shift], passing)

                direct.start()
                sent.append(direct)
            else:
                begin(through, far)
                begin(direct, jnp.logical_not(far))
        z_copies[name, shift] = direct

    def join_feed(piece, shift):
        own_loads[piece, shift].wait()
        join_piece(
            piece, piece, feed_sum.at[piece], feed_y.at[piece], feed_z.at[piece],
            feed_pass if piece == 2 else None, shift,
        )

    for target in (feed_z.at[2], out_z, qkv_z):
        clear(target)

    def join_feed_late(index):
        late_copies[index].wait_recv()
        join_feed(*late[index])

    qkv_load.wait()
    logs_load.wait()
    for sequence in range(2):

        for pair in range(2):
            attend_back_pair(
                qkv, grad_heads, heads, logs, cosine_ref, sine_ref, grad_qkv, keys, values, grad_keys,
                grad_values, sequence, pair,
            )
        join_feed_late(sequence)
    wide_load.wait()

    def first_tile(order):
        row = ring_row(ORDER[order], deep, piece_rows)
        slot = (order % 2) * 512
        return load(
            first_hbm.at[:, :, pl.ds(row, piece_rows)],
            qkv.at[:, :, pl.ds(slot, piece_rows)],
            tile_sems.at[order],
        )

    first_loads = [first_tile(order) for order in range(2)]

    def first_piece(block):
        @pl.loop(0, width // WIDE)
        def _(step):
            lanes = pl.ds(pl.multiple_of(step * WIDE, WIDE), WIDE)
            slots[block % 3, :, lanes] = times_transposed(grad_qkv[block], qkv_wide[lanes, :]).astype(
                jnp.bfloat16
            )

    first_piece(3)
    core_far = move(slots.at[0], landing, core_sems, 0, core_beside)
    first_piece(1)
    core_far.wait_recv()
    add_rows(slots.at[1], landing)
    x_copy = move(slots.at[1], first_x, x_sems, 1, x_beside)
    join_feed_late(2)
    y_index = len(late)
    qkv_copies = {}
    for order, shift in enumerate(ORDER):
        first_loads[order].wait()
        slot = (order % 2) * 512
        left = qkv[:, :, slot : slot + piece_rows]
        qkv_sent[shift] = weight_tile(left, grad_qkv, qkv_spread, 1)
        qkv_copies[shift] = move(qkv_sent.at[shift], qkv_y.at[shift], y_sems, y_index + shift, y_beside)
        qkv_sum[shift] = weight_tile(left, grad_qkv, qkv_spread, 0)
        if order + 2 < deep:
            first_loads.append(first_tile(order + 2))
    join_feed_late(3)
    first_piece(2)
    core_near = move(slots.at[2], first_core, core_sems, 1, core_beside)
    core_far.wait_send()
    sent[:] = [copy for copy in sent if copy is not core_far]
    first_piece(0)
    first_store = load(slots.at[0], first_part, load_sems.at[8])
    join_feed_late(4)
    y_index += deep
    out_copies = {}
    for shift in ORDER:
        row = ring_row(shift, deep, piece_rows)
        out_sent[shift] = weight_tile(grad_attention[:, :, pl.ds(row, piece_rows)], heads, out_spread, 1)
        out_copies[shift] = move(out_sent.at[shift], out_y.at[shift], y_sems, y_index + shift, y_beside)

    @pl.loop(0, deep)
    def _(shift):
        row = ring_row(shift, deep, piece_rows)
        out_sum[shift] = weight_tile(grad_attention[:, :, pl.ds(row, piece_rows)], heads, out_spread, 0)


    finals = []

    def finish(name, number, total, arrived, last, final, weights):
        for shift in range(1, deep):
            if (name, shift) not in z_copies:
                continue
            if name in (0, 1) or shift == 2:
                z_copies[name, shift].wait_recv()
            else:
                pl.when(z_place != (0 if shift == 1 else deep - 1))(z_copies[name, shift].wait_recv)
        size = total.shape[2]
        sums = []
        for rel in range(2):
            row = pl.multiple_of(lax.rem(core + rel, jnp.int32(2)) * part, part)
            value = total[0, pl.ds(row, part), :].astype(jnp.float32)
            for shift in range(deep - 1):
                value = value + arrived[shift, pl.ds(row, part), :].astype(jnp.float32)
            last[rel] = value
            if weights is not None:
                product = value * weights[rel].astype(jnp.float32)
                sums.append(sum(product[:, i * LANES : (i + 1) * LANES] for i in range(size // LANES)))
        finals.append(load(last.at[0], final.at[core], own_sems.at[1, 12 + number]))
        finals.append(move(last.at[1], final.at[core], core_sems, 2 + number, core_beside))
        return sums

    def gain_exchange(which, sums):
        slots = {}
        for rel in range(2):
            gain_part[which, rel] = sums[rel]
        piece = part // 4
        for number, key in enumerate(far_cube):
            rel, up, over = key
            target = ((along + up) % 2) * 2 + (across + over) % 2
            row = pl.multiple_of(target * piece, 8)
            slots[key] = move(
                gain_part.at[which, rel, pl.ds(row, piece), :],
                gain_in.at[which, number],
                gain_sems,
                which * len(far_cube) + number,
                cube[key],
            )
        return slots

    def gain_finish(which, slots, output):
        piece = part // 4
        row = pl.multiple_of((along * 2 + across) * piece, 8)
        value = gain_part[which, 0, pl.ds(row, piece), :]
        for number, key in enumerate(far_cube):
            slots[key].wait_recv()
            value = value + gain_in[which, number]
        gain_total[which] = value
        return load(gain_total.at[which], output, load_sems.at[9 + which])

    for copy in weight_loads + early_loads:
        copy.wait()
    finish(0, 0, feed_sum.at[0], feed_z.at[0], feed_last.at[0], feed_final.at[0], None)
    gate_sums = finish(
        1, 1, feed_sum.at[1], feed_z.at[1], feed_last.at[1], feed_final.at[1], feed_weight.at[:, :, pl.ds(0, half)]
    )
    for shift in ORDER:
        qkv_copies[shift].wait_recv()
        join_piece("qkv", 4, qkv_sum, qkv_y, qkv_z, qkv_pass, shift)
    for shift in ORDER:
        out_copies[shift].wait_recv()
        join_piece("out", 3, out_sum, out_y, out_z, out_pass, shift)
    up_sums = finish(
        2, 2, feed_sum.at[2], feed_z.at[2], feed_last.at[2], feed_final.at[2],
        feed_weight.at[:, :, pl.ds(half, half)],
    )
    second_slots = gain_exchange(1, [one + two for one, two in zip(gate_sums, up_sums)])
    sums = finish("qkv", 4, qkv_sum, qkv_z, qkv_last, qkv_final, qkv_weight)
    first_slots = gain_exchange(0, sums)
    finish("out", 3, out_sum, out_z, out_last, out_final, None)
    second_store = gain_finish(1, second_slots, second_gain_out)
    first_gain_store = gain_finish(0, first_slots, first_gain_out)
    for copy in (branch_copy, x_copy, core_near):
        copy.wait_recv()
    for number in range(5):
        finals[2 * number].wait()
        finals[2 * number + 1].wait_recv()
    for copy in (first_store, second_store, first_gain_store):
        copy.wait()
    for copy in sent:
        copy.wait_send()
    for copy, condition in guarded:
        pl.when(condition)(copy.wait_send)


def heads_back(
    deep, grad_attention, qkv, heads, logs, first, qkv_wide, out_wide, branch, sent, own, sums, arrived, chunks,
    qkv_own, cosine, sine, spreads,
):
    blocks, count, width = grad_attention.shape
    part, half = chunks.shape[3], chunks.shape[4] // 3
    qkv_half, out_half = spreads[0].shape[0], spreads[1].shape[0]
    rows = 2 * part

    def shape(*dims, kind=jnp.bfloat16):
        return jax.ShapeDtypeStruct(dims, kind)

    def room(*dims, kind=jnp.bfloat16):
        return pltpu.VMEM(dims, kind)

    wide = jnp.float32
    outs = (
        shape(count, width),
        shape(count, width),
        shape(count, width),
        shape(count, width),
        shape(3, 2, part, half, kind=wide),
        shape(2, part, qkv_half, kind=wide),
        shape(2, part, out_half, kind=wide),
        shape(part // 4, LANES, kind=wide),
        shape(part // 4, LANES, kind=wide),
    )
    dma = pltpu.SemaphoreType.DMA
    scratch = [
        room(blocks, count, width),
        room(*qkv.shape),
        room(*heads.shape),
        room(*heads.shape),
        room(*logs.shape, kind=wide),
        room(*qkv.shape),
        room(*qkv_wide.shape),
        room(*out_wide.shape),
        room(2 * count, LANES),
        room(2 * count, LANES),
        room(2 * count, LANES, kind=wide),
        room(2 * count, LANES, kind=wide),
        room(3, count, width),
        room(count, width),
        room(3, deep, rows, half),
        room(3, deep, rows, half),
        room(3, deep - 1, rows, half),
        room(deep, rows, out_half),
        room(deep, rows, out_half),
        room(deep, rows, out_half),
        room(deep - 1, rows, out_half),
        room(deep, rows, qkv_half),
        room(deep, rows, qkv_half),
        room(deep, rows, qkv_half),
        room(deep - 1, rows, qkv_half),
        room(rows, half),
        room(rows, out_half),
        room(rows, qkv_half),
        room(3, 2, part, half, kind=wide),
        room(2, part, qkv_half, kind=wide),
        room(2, part, out_half, kind=wide),
        room(2, part, 2 * half),
        room(2, part, qkv_half),
        room(2, 2, part, LANES, kind=wide),
        room(2, 7, part // 4, LANES, kind=wide),
        room(2, part // 4, LANES, kind=wide),
        dma((11,)),
        dma((2, max(3 * deep, 17))),
        dma((deep,)),
        dma((2, 7)),
        dma((2, 2)),
        dma((2, 5 * deep)),
        dma((2, 5 * (deep - 1))),
        dma((2, 5)),
        dma((2, 14)),
    ]
    return pl.pallas_call(
        functools.partial(heads_back_kernel, deep),
        out_shape=outs,
        in_specs=[hbm_spec()] * 14 + [vmem_spec()] * 4,
        out_specs=(hbm_spec(),) * len(outs),
        scratch_shapes=scratch,
        compiler_params=vmem_params(collective_id=3, has_side_effects=True),
        cost_estimate=cost(flops=30 * 10**9, bytes_accessed=10**8, transcendentals=10**7),
        name="heads_back",
    )(
        grad_attention, qkv, heads, logs, first, qkv_wide, out_wide, branch, sent, own, sums, arrived, chunks,
        qkv_own, cosine, sine, *spreads,
    )


def tables(rows):
    lane = np.arange(LANES)
    entry = lane % (LANES // 2)
    live = (entry < HD // 2).astype(np.float64)
    sign = np.where(lane < LANES // 2, -1.0, 1.0) * live
    inverse = np.where(live > 0, THETA ** (-2.0 * entry / HD), 0.0).astype(np.float32)
    position = np.arange(2 * rows, dtype=np.float32)
    angles = (position[:, None] * inverse[None, :]).astype(np.float32).astype(np.float64)
    both = (np.cos(angles) * live, np.sin(angles) * sign)
    return tuple(jnp.asarray(table.astype(np.float32).reshape(2, rows, LANES)) for table in both)


def norm_factor(rows):
    return lax.rsqrt(jnp.mean(rows * rows, axis=-1, keepdims=True) + EPSILON)


def norm_back(rows, gain, grad):
    factor = norm_factor(rows)
    scaled = grad * gain
    return factor * scaled - rows * factor**3 * jnp.mean(scaled * rows, axis=-1, keepdims=True)


def finish_kernel(
    middle, branch_near, branch_core, branch_x, grad_middle, first_part, first_core, first_x, tokens, first_scale, second_scale,
    gate_final, up_final, down_final, qkv_final, out_final, first_lanes, second_lanes,
    result, tokens_grad, query_grad, key_grad, value_grad, out_grad, gate_grad, up_grad, down_grad,
    first_gain, second_gain,
):
    def total(*parts):
        return sum(part[...].astype(jnp.float32) for part in parts)

    result[...] = (middle[...] + total(branch_near, branch_core, branch_x)).astype(jnp.bfloat16)
    rows = tokens[...].astype(jnp.float32)
    grad_first = total(first_part, first_core, first_x)
    tokens_grad[...] = grad_middle[...] + norm_back(rows, first_scale[...][None], grad_first)
    for half in range(2):
        start = 0
        for target in (query_grad, key_grad, value_grad):
            size = target.shape[1] // 2
            target[:, half * size : (half + 1) * size] = qkv_final[half, :, start : start + size]
            start += size
        for target, source in (
            (gate_grad, gate_final), (up_grad, up_final), (down_grad, down_final), (out_grad, out_final)
        ):
            size = target.shape[1] // 2
            target[:, half * size : (half + 1) * size] = source[half]

    @pl.when(pl.program_id(0) == 0)
    def _():
        piece = first_lanes.shape[0]
        place = 0
        for name in ("z", "c", "y", "x"):
            place = place * lax.axis_size(name) + lax.axis_index(name).astype(jnp.int32)
        shape = (piece, first_scale.shape[0])
        lane = lax.broadcasted_iota(jnp.int32, shape, 1) - place * piece
        chosen = lane == lax.broadcasted_iota(jnp.int32, shape, 0)
        square = (piece, LANES)
        corner = lax.broadcasted_iota(jnp.int32, square, 1) == lax.broadcasted_iota(jnp.int32, square, 0)
        for scale, source, target in (
            (first_scale, first_lanes, first_gain),
            (second_scale, second_lanes, second_gain),
        ):
            gain = jnp.sum(jnp.where(chosen, scale[...][None], 0.0), axis=1, keepdims=True)
            value = jnp.sum(source[...], axis=1, keepdims=True) / gain
            target[...] = jnp.sum(jnp.where(corner, value, 0.0), axis=0, keepdims=True)[:, :piece]


def finish_all(
    middle, branch, branch_x, grad_middle, firsts, tokens, gains, feed_final, qkv_final, out_final, lanes,
):
    steps = 4
    count, width = tokens.shape
    part, half = feed_final.shape[2:]
    query = qkv_final.shape[2] // 2
    wide = jnp.float32

    def rows(third=None):
        if third is None:
            return pl.BlockSpec((count // steps, width), lambda i: (i, 0))
        return pl.BlockSpec((None, count // steps, width), lambda i: (third, i, 0))

    def piece(columns):
        return pl.BlockSpec((part // steps, columns), lambda i: (i, 0))

    def halves(columns):
        return pl.BlockSpec((2, part // steps, columns), lambda i: (0, i, 0))

    def feed_halves(third):
        return pl.BlockSpec((None, 2, part // steps, half), lambda i: (third, 0, i, 0))

    out_lanes = out_final.shape[2]
    return pl.pallas_call(
        finish_kernel,
        grid=(steps,),
        out_shape=(
            jax.ShapeDtypeStruct((count, width), jnp.bfloat16),
            jax.ShapeDtypeStruct((count, width), wide),
            jax.ShapeDtypeStruct((part, 2 * query), wide),
            jax.ShapeDtypeStruct((part, query), wide),
            jax.ShapeDtypeStruct((part, query), wide),
            jax.ShapeDtypeStruct((part, 2 * out_lanes), wide),
            jax.ShapeDtypeStruct((part, 2 * half), wide),
            jax.ShapeDtypeStruct((part, 2 * half), wide),
            jax.ShapeDtypeStruct((part, 2 * half), wide),
            jax.ShapeDtypeStruct((1, part // 4), wide),
            jax.ShapeDtypeStruct((1, part // 4), wide),
        ),
        in_specs=[rows(), rows(0), rows(2), rows(), rows(), rows(), rows(), rows(), rows()]
        + [
            pl.BlockSpec(gains[0].shape, lambda i: (0,)),
            pl.BlockSpec(gains[1].shape, lambda i: (0,)),
            feed_halves(1),
            feed_halves(2),
            feed_halves(0),
            halves(2 * query),
            halves(out_lanes),
            pl.BlockSpec(lanes[0].shape, lambda i: (0, 0)),
            pl.BlockSpec(lanes[1].shape, lambda i: (0, 0)),
        ],
        out_specs=(
            rows(),
            rows(),
            piece(2 * query),
            piece(query),
            piece(query),
            piece(2 * out_lanes),
            piece(2 * half),
            piece(2 * half),
            piece(2 * half),
            pl.BlockSpec((1, part // 4), lambda i: (0, 0)),
            pl.BlockSpec((1, part // 4), lambda i: (0, 0)),
        ),
        compiler_params=vmem_params(),
        cost_estimate=cost(flops=10**7, bytes_accessed=3 * 10**7, transcendentals=0),
        name="finish_all",
    )(
        middle, branch, branch, branch_x, grad_middle, *firsts, tokens, *gains, feed_final, feed_final, feed_final,
        qkv_final, out_final, *lanes,
    )


def fast_local(
    tokens,
    cotangent,
    first_gain,
    query_weight,
    key_weight,
    value_weight,
    out_weight,
    second_gain,
    gate_weight,
    up_weight,
    down_weight,
):
    deep = lax.axis_size("z")
    rows = tokens.shape[0]
    own_rows = tokens.astype(jnp.float32)
    spreads = (spread_heads(3, 1), spread_heads(0, 2))
    cosine, sine = tables(rows)
    gains = (first_gain, second_gain)
    (
        first_all, qkv_all, heads_all, logs_all, qkv_weight, out_wide, middle, second_all, cotangent_all, chunks, qkv_own,
    ) = forward(
        deep,
        cotangent,
        tokens,
        gains,
        (query_weight, key_weight, value_weight, out_weight.T, gate_weight, up_weight, down_weight.T),
        spreads,
        cosine,
        sine,
    )
    grad_middle, grad_attention, branch, sent, own, sums, arrived = feed_back(
        deep, second_all, cotangent_all, chunks, middle, second_gain
    )
    first_part, first_core, first_x, branch_x, feed_final, qkv_final, out_final, first_lanes, second_lanes = (
        heads_back(
            deep, grad_attention, qkv_all, heads_all, logs_all, first_all, qkv_weight, out_wide, branch, sent,
            own, sums, arrived, chunks, qkv_own, cosine, sine, spreads,
        )
    )

    (
        result, tokens_grad, query_grad, key_grad, value_grad, out_grad, gate_grad, up_grad, down_grad,
        first_gain_grad, second_gain_grad,
    ) = finish_all(
        middle, branch, branch_x, grad_middle, (first_part, first_core, first_x), tokens, gains, feed_final,
        qkv_final, out_final, (first_lanes, second_lanes),
    )
    return (
        result,
        tokens_grad,
        query_grad,
        key_grad,
        value_grad,
        out_grad.T,
        gate_grad,
        up_grad,
        down_grad.T,
        first_gain_grad[0],
        second_gain_grad[0],
    )


def specs(depth, width):
    both = depth + width
    rows, inward, outward = P(both, None), P(depth, width), P(width, depth)
    in_specs = (rows, rows, P(), inward, inward, inward, outward, P(), inward, inward, outward)
    out_specs = (rows, rows, inward, inward, inward, outward, inward, inward, outward, P(both), P(both))
    return in_specs, out_specs


def solution(mesh):
    depth, width = mesh.shape["dp"], mesh.shape["tensor"]

    def run(tokens, cotangent, *weights):
        fits = (
            width == 4
            and depth == 8
            and tokens.shape[0] * 2 == SEQ_LEN * depth * width
            and weights[2].shape[1] == 2 * width * HD
            and weights[1].shape[1] == 4 * width * HD
        )
        if fits:
            devices = mesh.devices.reshape(depth // 2, 2, 2, 2)
            fine = jax.sharding.Mesh(devices, ("z", "c", "y", "x"))
            in_specs, out_specs = specs(("z", "c"), ("y", "x"))
            call, over = fast_local, fine
        else:
            in_specs, out_specs = specs(("dp",), ("tensor",))
            call, over = local, mesh
        return jax.shard_map(call, mesh=over, in_specs=in_specs, out_specs=out_specs, check_vma=False)(
            tokens, cotangent, *weights
        )

    return run
```
